32 devices in a mesh: fsdp: 4 (over y, x), ctx: 2 (over core), tp: 4 (over z).
Axes of the slice: x: 2, y: 2, z: 4, core: 2. Of those that a mesh axis runs over, the one named last changes fastest.
Arguments:
- tokens: bfloat16 [8, 4096, 512], P('fsdp', ('ctx', 'tp')), may hold values from -6 to 6
- timesteps: int32 [8], P('fsdp'), may hold values from 0 to 49
- time_table: bfloat16 [50, 512], replicated, may hold values from -6 to 6
- prefix: int32 [8], P('fsdp'), may hold values from 409 to 2048, as said below
- encoder: bfloat16 [8, 256, 512], P('fsdp'), may hold values from -6 to 6
- self_qkv: bfloat16 [3, 512, 512], P(None, 'fsdp', 'tp'), may hold values from -0.375 to 0.375
- cross_q: bfloat16 [512, 512], P('fsdp', 'tp'), may hold values from -0.375 to 0.375
- cross_kv: bfloat16 [2, 512, 512], P(None, 'fsdp', 'tp'), may hold values from -0.375 to 0.375
- self_out: bfloat16 [512, 512], P('tp', 'fsdp'), may hold values from -2 to 2
- cross_out: bfloat16 [512, 512], P('tp', 'fsdp'), may hold values from -0.5 to 0.5
- ffn_up: bfloat16 [512, 2048], P('fsdp', 'tp'), may hold values from -0.25 to 0.25
- ffn_down: bfloat16 [2048, 512], P('tp', 'fsdp'), may hold values from -0.125 to 0.125
- norm_gain: float32 [3, 512], replicated, may hold values from 0.5 to 1.5
- norm_bias: float32 [3, 512], replicated, may hold values from -1.25 to 1.25
- cotangent: bfloat16 [8, 4096, 512], P('fsdp', ('ctx', 'tp')), may hold values from -6 to 6
Outputs:
- output: float32 [8, 4096, 512], P('fsdp', ('ctx', 'tp'))
- input_grad: float32 [8, 4096, 512], P('fsdp', ('ctx', 'tp'))
- encoder_grad: float32 [8, 256, 512], P('fsdp', ('ctx', 'tp'))
- self_qkv_grad: float32 [3, 512, 512], P(None, 'fsdp', 'tp')
- cross_q_grad: float32 [512, 512], P('fsdp', 'tp')
- cross_kv_grad: float32 [2, 512, 512], P(None, 'fsdp', 'tp')
- self_out_grad: float32 [512, 512], P('tp', 'fsdp')
- cross_out_grad: float32 [512, 512], P('tp', 'fsdp')
- ffn_up_grad: float32 [512, 2048], P('fsdp', 'tp')
- ffn_down_grad: float32 [2048, 512], P('tp', 'fsdp')
- gain_grad: float32 [3, 512], replicated
- bias_grad: float32 [2, 512], replicated
- ffn_bias_grad: float32 [512], replicated
- norms: float32 [4], replicated
The draws below stay inside these ranges and needn't reach their ends.
Inputs may be any that keep to these rules, and one draw needn't show every extreme that they name: Each sequence's prefix; some sequence has exactly 409 and some exactly 2048.
All inputs are finite; a program needn't handle non-finite values.
Results may differ from the reference program's by a relative error of at most 0.035.
Values may be sent and summed in bfloat16 or wider, within the bound.
A program may use at most 192 MiB of HBM per device.

```python
import jax
import jax.numpy as jnp
from jax import lax

D = 512
HEADS = 8
HEAD_DIM = 64
FF = 2048
LEN = 4096
ENC = 256
TSTEPS = 50
SEQS = 8


def draw_prefix(key, part):
    values = jax.random.randint(jax.random.fold_in(key, 11), (SEQS,), LEN // 10, LEN // 2 + 1, dtype=jnp.int32)
    order = jax.random.permutation(jax.random.fold_in(key, 12), SEQS)
    values = values.at[order[0]].set(LEN // 2)
    return values.at[order[1]].set(LEN // 10)


def set_ends(array, rng, least, top_value):
    longest = array.shape.index(max(array.shape))
    spots = []
    for shift in (0, 1):
        where = [jax.random.randint(jax.random.fold_in(rng, axis), (), 0, length) for axis, length in enumerate(array.shape)]
        where[longest] = (where[longest] + shift) % array.shape[longest]
        spots.append(tuple(where))
    return array.at[spots[0]].set(least).at[spots[1]].set(top_value)


def block_levels(rng, extent, split, low, high):
    level = 1.0
    for dim, blocks in split:
        steps = jax.random.uniform(jax.random.fold_in(jax.random.fold_in(rng, 6), dim), (blocks,), jnp.float32, low / len(split), high / len(split))
        level = level * jnp.repeat(jnp.exp(steps), extent[dim] // blocks).reshape((-1,) + (1,) * (len(extent) - 1 - dim))
    return level


def noise(key, shape, scale, bound, pieces=(), kind=jnp.bfloat16):
    level = block_levels(key, shape, pieces, -0.22, 0.18) if pieces else 1.0
    entries = jax.random.normal(key, shape, jnp.float32) * scale * level
    return jnp.minimum(jnp.maximum(entries, -bound), bound).astype(kind)


def setup_inputs(seed: int = 0) -> dict:
    splits = jax.random.split(jax.random.key(seed), 16)
    return {
        "tokens": noise(splits[0], (SEQS, LEN, D), 1.0, 6.0, ((0, 4), (1, 8))),
        "timesteps": set_ends(jax.random.randint(splits[1], (SEQS,), 0, TSTEPS), jax.random.fold_in(splits[1], 1), 0, TSTEPS - 1).astype(jnp.int32),
        "time_table": noise(splits[2], (TSTEPS, D), 1.0, 6.0),
        "prefix": draw_prefix(jax.random.fold_in(splits[15], 71), 0),
        "encoder": noise(splits[4], (SEQS, ENC, D), 1.0, 6.0, ((0, 4),)),
        "self_qkv": noise(splits[5], (3, D, D), (D // 2) ** -0.5, 0.375, ((1, 4), (2, 4))),
        "cross_q": noise(splits[6], (D, D), (D // 2) ** -0.5, 0.375, ((0, 4), (1, 4))),
        "cross_kv": noise(splits[7], (2, D, D), (D // 2) ** -0.5, 0.375, ((1, 4), (2, 4))),
        "self_out": noise(splits[8], (D, D), (max(1, D * 64 // LEN)) ** -0.5, 2.0, ((0, 4), (1, 4))),
        "cross_out": noise(splits[9], (D, D), (D // 4) ** -0.5, 0.5, ((0, 4), (1, 4))),
        "ffn_up": noise(splits[10], (D, FF), D ** -0.5, 0.25, ((0, 4), (1, 4))),
        "ffn_down": noise(splits[11], (FF, D), FF ** -0.5, 0.125, ((0, 4), (1, 4))),
        "norm_gain": jnp.clip(1.0 + 0.1 * jax.random.normal(splits[12], (3, D), jnp.float32), 0.5, 1.5),
        "norm_bias": noise(splits[13], (3, D), 0.2, 1.25, (), jnp.float32),
        "cotangent": noise(splits[14], (SEQS, LEN, D), 1.0, 6.0, ((0, 4), (1, 8))),
    }


HIGH = lax.Precision.HIGHEST
EPS = 1e-05
NEG = -1e+30

@jax.custom_vjp
def low(v):
    return lax.optimization_barrier(v.astype(jnp.bfloat16)).astype(jnp.float32)

@jax.custom_vjp
def low_back(v):
    return v

def low_keep(v):
    return (low(v), None)

def low_pass(kept, grad):
    return (grad,)

def back_keep(v):
    return (v, None)

def back_low(kept, grad):
    return (low(grad),)
low.defvjp(low_keep, low_pass)
low_back.defvjp(back_keep, back_low)

def product(left, right):
    return jnp.dot(left, right, precision=HIGH)

def layer_norm(hidden, scaling, offsets):
    centre = hidden - lax.optimization_barrier(jnp.mean(hidden, -1, keepdims=True))
    inverse = lax.rsqrt(lax.optimization_barrier(jnp.mean(centre * centre, -1, keepdims=True)) + EPS)
    return centre * inverse * scaling + offsets

def self_attention(queries, key_rows, value_rows, lengths):
    length = queries.shape[0]
    row_span = min(512, length)
    factor = HEAD_DIM ** (-0.5)
    query_blocks = queries.reshape(length // row_span, row_span, HEADS, HEAD_DIM)
    key_heads = key_rows.reshape(length, HEADS, HEAD_DIM)
    value_heads = value_rows.reshape(length, HEADS, HEAD_DIM)
    key_pos = jnp.arange(length, dtype=jnp.int32)

    def one_block(inputs):
        rows, offset = inputs
        scores = jnp.einsum('qhe,khe->hqk', rows, key_heads, precision=HIGH) * factor
        scores = low_back(scores)
        query_pos = offset + jnp.arange(row_span, dtype=jnp.int32)
        visible = (key_pos[None, :] <= query_pos[:, None]) | (key_pos[None, :] < lengths)
        probs = jax.nn.softmax(jnp.where(visible[None], scores, NEG), axis=-1)
        probs = low(probs)
        result = jnp.einsum('hqk,khe->qhe', probs, value_heads, precision=HIGH)
        return result.reshape(row_span, HEADS * HEAD_DIM)
    offsets = jnp.arange(length // row_span, dtype=jnp.int32) * row_span
    result = lax.map(jax.checkpoint(one_block), (query_blocks, offsets))
    return result.reshape(length, HEADS * HEAD_DIM)

def cross_attention(queries, key_rows, value_rows):
    length = queries.shape[0]
    enc_count = key_rows.shape[0]
    factor = HEAD_DIM ** (-0.5)
    query_heads = queries.reshape(length, HEADS, HEAD_DIM)
    key_heads = key_rows.reshape(enc_count, HEADS, HEAD_DIM)
    value_heads = value_rows.reshape(enc_count, HEADS, HEAD_DIM)
    scores = low_back(jnp.einsum('qhe,khe->hqk', query_heads, key_heads, precision=HIGH) * factor)
    probs = low(jax.nn.softmax(scores, axis=-1))
    result = jnp.einsum('hqk,khe->qhe', probs, value_heads, precision=HIGH)
    return result.reshape(length, HEADS * HEAD_DIM)

def sequence_forward(params, inputs, enc_rows, embedded, lengths):
    proj_self, proj_query, proj_pair, back_self, back_cross, expand_full, shrink_full, gains, shifts = params
    start_sum = inputs + embedded[None, :]
    normed_one = low(layer_norm(start_sum, gains[0], shifts[0]))
    queries = low_back(low(product(normed_one, proj_self[0])))
    key_rows = low_back(low(product(normed_one, proj_self[1])))
    value_rows = low_back(low(product(normed_one, proj_self[2])))
    context_one = low_back(low(self_attention(queries, key_rows, value_rows, lengths)))
    branch_one = low_back(product(context_one, back_self))
    after_one = start_sum + branch_one
    normed_two = low(layer_norm(after_one, gains[1], shifts[1]))
    cross_queries = low_back(low(product(normed_two, proj_query)))
    cross_keys = low_back(low(product(enc_rows, proj_pair[0])))
    cross_values = low_back(low(product(enc_rows, proj_pair[1])))
    context_two = low_back(low(cross_attention(cross_queries, cross_keys, cross_values)))
    branch_two = low_back(product(context_two, back_cross))
    after_two = after_one + branch_two
    normed_three = low(layer_norm(after_two, gains[2], shifts[2]))
    pre_act = low_back(product(normed_three, expand_full))
    hidden = low(jax.nn.gelu(pre_act, approximate=False))
    branch_three = low_back(product(hidden, shrink_full))
    final_sum = after_two + branch_three
    squares = jnp.stack([jnp.sum(final_sum * final_sum), jnp.sum(branch_one * branch_one), jnp.sum(branch_two * branch_two), jnp.sum(branch_three * branch_three)])
    return (final_sum, squares)

def reference(tokens, timesteps, time_table, prefix, encoder, self_qkv, cross_q, cross_kv, self_out, cross_out, ffn_up, ffn_down, norm_gain, norm_bias, cotangent):
    params = (self_qkv.astype(jnp.float32), cross_q.astype(jnp.float32), cross_kv.astype(jnp.float32), self_out.astype(jnp.float32), cross_out.astype(jnp.float32), ffn_up.astype(jnp.float32), ffn_down.astype(jnp.float32), norm_gain, norm_bias)
    embedded_all = time_table.astype(jnp.float32)[timesteps]

    def one_sequence(running, inputs):
        token_rows, enc_rows, embedded, lengths, grad_rows = inputs

        def forward(weights, token_values, enc_values):
            return sequence_forward(weights, token_values, enc_values, embedded, lengths)
        result, pull, squares = jax.vjp(forward, params, token_rows.astype(jnp.float32), enc_rows.astype(jnp.float32), has_aux=True)
        grad_params, grad_tokens, grad_enc = pull(grad_rows.astype(jnp.float32))
        totals, sums = running
        totals = jax.tree.map(lambda left, right: left + right, totals, grad_params)
        return ((totals, sums + squares), (result, grad_tokens, grad_enc))
    zeros = jax.tree.map(jnp.zeros_like, params)
    (totals, sums), (output, input_grad, encoder_grad) = lax.scan(one_sequence, (zeros, jnp.zeros((4,), jnp.float32)), (tokens, encoder, embedded_all, prefix, cotangent))
    norms = jnp.sqrt(sums / (SEQS * LEN * D))
    return (output, input_grad, encoder_grad, totals[0], totals[1], totals[2], totals[3], totals[4], totals[5], totals[6], totals[7], totals[8][:2], totals[8][2], norms)
```

```python
import functools
import math

import jax
import jax.numpy as jnp
from jax import lax
from jax.experimental import pallas as pl
from jax.experimental.pallas import tpu as pltpu
from jax.sharding import PartitionSpec as P

HEAD_DIM = 64


EPS = 1e-05
NEG = -1e30
ROOT_HALF = 1.0 / math.sqrt(2.0)
INV_ROOT_TWO_PI = 1.0 / math.sqrt(2.0 * math.pi)
VMEM_LIMIT = 56 * 2**20


def norm_rows(hidden, scaling, offsets):
    centre = hidden - jnp.mean(hidden, -1, keepdims=True)
    inverse = lax.rsqrt(jnp.mean(centre * centre, -1, keepdims=True) + EPS)
    unit_rows = centre * inverse
    return (unit_rows * scaling + offsets, unit_rows, inverse)


def norm_back(upstream, unit_rows, inverse, scaling):
    scaled = upstream * scaling
    result = inverse * (
        scaled
        - jnp.mean(scaled, -1, keepdims=True)
        - unit_rows * jnp.mean(scaled * unit_rows, -1, keepdims=True)
    )
    return (result, jnp.sum(upstream * unit_rows, (0, 1)), jnp.sum(upstream, (0, 1)))


def gelu_parts(inputs):
    normal_cdf = 0.5 * (1.0 + lax.erf(inputs * ROOT_HALF))
    return (
        inputs * normal_cdf,
        normal_cdf + inputs * jnp.exp(-0.5 * inputs * inputs) * INV_ROOT_TWO_PI,
    )


def spread_rows(rows):
    return lax.all_gather(rows, "tp", axis=1, tiled=True)


def spread_grads(grad_rows):
    return lax.all_gather(grad_rows, "tp", axis=1, tiled=True)


def finish_branch(local_in, local_weight):
    return lax.psum_scatter(
        jnp.einsum("scw,wd->scd", local_in, local_weight, preferred_element_type=jnp.float32),
        "tp",
        scatter_dimension=1,
        tiled=True,
    )


def finish_grad(local_grad, local_weight):
    return lax.psum_scatter(
        jnp.einsum("scw,dw->scd", local_grad, local_weight, preferred_element_type=jnp.float32),
        "tp",
        scatter_dimension=1,
        tiled=True,
    )


def block_scores(queries, key_block, query_pos, key_pos, lengths, factor):
    scores = (
        jnp.einsum("sqhe,skhe->sqhk", queries, key_block, preferred_element_type=jnp.float32)
        * factor
    )
    visible = (key_pos[None, None, :] <= query_pos[None, :, None]) | (
        key_pos[None, None, :] < lengths[:, None, None]
    )
    return jnp.where(visible[:, :, None, :], scores, NEG)


def attend_forward(queries, key_rows, value_rows, query_pos, lengths, key_span, factor):
    length = key_rows.shape[1]

    def attend_advance(running, offset):
        highest, totals, summed = running
        key_block = lax.dynamic_slice_in_dim(key_rows, offset, key_span, 1)
        value_block = lax.dynamic_slice_in_dim(value_rows, offset, key_span, 1)
        scores = block_scores(
            queries, key_block, query_pos, offset + lax.iota(jnp.int32, key_span), lengths, factor
        )
        new_high = jnp.maximum(highest, jnp.max(scores, -1))
        weights = jnp.exp(scores - new_high[..., None])
        fading = jnp.exp(highest - new_high)
        totals = totals * fading + jnp.sum(weights, -1)
        summed = summed * fading[..., None] + jnp.einsum(
            "sqhk,skhe->sqhe",
            weights.astype(jnp.bfloat16),
            value_block,
            preferred_element_type=jnp.float32,
        )
        return ((new_high, totals, summed), None)

    stat_shape = queries.shape[:3]
    initial = (
        jnp.full(stat_shape, NEG, jnp.float32),
        jnp.zeros(stat_shape, jnp.float32),
        jnp.zeros(queries.shape, jnp.float32),
    )
    offsets = jnp.arange(length // key_span, dtype=jnp.int32) * key_span
    (highest, totals, summed), unused = lax.scan(attend_advance, initial, offsets)
    return (summed / totals[..., None], highest + jnp.log(totals))


def attend_block(
    queries,
    grad_out,
    log_rows,
    delta_rows,
    key_block,
    value_block,
    query_pos,
    key_pos,
    lengths,
    factor,
):
    scores = block_scores(queries, key_block, query_pos, key_pos, lengths, factor)
    probs = jnp.exp(scores - log_rows[..., None])
    grad_probs = jnp.einsum(
        "sqhe,skhe->sqhk", grad_out, value_block, preferred_element_type=jnp.float32
    )
    grad_scores = (probs * (grad_probs - delta_rows[..., None])).astype(jnp.bfloat16)
    return (probs.astype(jnp.bfloat16), grad_scores)


def key_sweep(
    queries,
    grad_out,
    log_rows,
    delta_rows,
    key_rows,
    value_rows,
    query_pos,
    lengths,
    key_span,
    factor,
):
    batches, row_count, head_count, head_depth = queries.shape
    length = key_rows.shape[1]

    def key_advance(grad_query, offset):
        key_block = lax.dynamic_slice_in_dim(key_rows, offset, key_span, 1)
        value_block = lax.dynamic_slice_in_dim(value_rows, offset, key_span, 1)
        key_pos = offset + lax.iota(jnp.int32, key_span)
        probs_low, grad_scores = attend_block(
            queries,
            grad_out,
            log_rows,
            delta_rows,
            key_block,
            value_block,
            query_pos,
            key_pos,
            lengths,
            factor,
        )
        grad_query = (
            grad_query
            + jnp.einsum(
                "sqhk,skhe->sqhe", grad_scores, key_block, preferred_element_type=jnp.float32
            )
            * factor
        )
        grad_key = (
            jnp.einsum("sqhk,sqhe->kshe", grad_scores, queries, preferred_element_type=jnp.float32)
            * factor
        )
        grad_value = jnp.einsum(
            "sqhk,sqhe->kshe", probs_low, grad_out, preferred_element_type=jnp.float32
        )
        return (grad_query, (grad_key, grad_value))

    offsets = jnp.arange(length // key_span, dtype=jnp.int32) * key_span
    grad_query, stacked = lax.scan(key_advance, jnp.zeros(queries.shape, jnp.float32), offsets)
    flat_shape = (length, batches, head_count * head_depth)
    return (grad_query, stacked[0].reshape(flat_shape), stacked[1].reshape(flat_shape))


def local(
    tokens,
    timesteps,
    time_table,
    prefix,
    encoder,
    self_qkv,
    cross_q,
    cross_kv,
    self_out,
    cross_out,
    ffn_up,
    ffn_down,
    norm_gain,
    norm_bias,
    cotangent,
):
    proj_self, proj_query, proj_pair, back_self, back_cross, expand_full, shrink_full = (
        lax.all_gather(self_qkv, "fsdp", axis=1, tiled=True),
        lax.all_gather(cross_q, "fsdp", axis=0, tiled=True),
        lax.all_gather(cross_kv, "fsdp", axis=1, tiled=True),
        lax.all_gather(self_out, "fsdp", axis=1, tiled=True),
        lax.all_gather(cross_out, "fsdp", axis=1, tiled=True),
        lax.all_gather(ffn_up, "fsdp", axis=0, tiled=True),
        lax.all_gather(ffn_down, "fsdp", axis=1, tiled=True),
    )
    batches = tokens.shape[0]
    model_width = tokens.shape[2]
    local_width = proj_query.shape[1]
    head_count = local_width // HEAD_DIM
    factor = HEAD_DIM ** (-0.5)
    ctx_index = lax.axis_index("ctx")
    local_stack = jnp.transpose(proj_self, (1, 0, 2)).reshape(model_width, 3 * local_width)
    steps_onehot = (timesteps[:, None] == lax.iota(jnp.int32, time_table.shape[0])[None, :]).astype(
        jnp.bfloat16
    )
    embedded = jnp.dot(steps_onehot, time_table, preferred_element_type=jnp.float32)
    start_sum = tokens.astype(jnp.float32) + embedded[:, None, :]
    normed_one, unit_one, inverse_one = norm_rows(start_sum, norm_gain[0], norm_bias[0])
    rows_self = spread_rows(normed_one.astype(jnp.bfloat16))
    row_count = rows_self.shape[1]
    head_shape = (batches, row_count, head_count, HEAD_DIM)
    projected = jnp.einsum(
        "scd,kdw->kscw", rows_self, proj_self, preferred_element_type=jnp.float32
    ).astype(jnp.bfloat16)
    queries, key_local, value_local = (projected[0], projected[1], projected[2])
    key_all, value_all = (
        lax.all_gather(key_local, "ctx", axis=1, tiled=True),
        lax.all_gather(value_local, "ctx", axis=1, tiled=True),
    )
    length = key_all.shape[1]
    key_span = min(512, length)
    query_pos = ctx_index * row_count + lax.iota(jnp.int32, row_count)
    keys_four = key_all.reshape(batches, length, head_count, HEAD_DIM)
    values_four = value_all.reshape(batches, length, head_count, HEAD_DIM)
    queries_four = queries.reshape(head_shape)
    attended, log_total = attend_forward(
        queries_four, keys_four, values_four, query_pos, prefix, key_span, factor
    )
    context_one = attended.reshape(batches, row_count, local_width).astype(jnp.bfloat16)
    branch_one = finish_branch(context_one, back_self)
    after_one = start_sum + branch_one
    normed_two, unit_two, inverse_two = norm_rows(after_one, norm_gain[1], norm_bias[1])
    rows_cross = spread_rows(normed_two.astype(jnp.bfloat16))
    cross_queries = jnp.einsum(
        "scd,dw->scw", rows_cross, proj_query, preferred_element_type=jnp.float32
    ).astype(jnp.bfloat16)
    enc_pair = jnp.einsum(
        "sed,kdw->ksew", encoder, proj_pair, preferred_element_type=jnp.float32
    ).astype(jnp.bfloat16)
    enc_count = encoder.shape[1]
    cross_keys = enc_pair[0].reshape(batches, enc_count, head_count, HEAD_DIM)
    cross_values = enc_pair[1].reshape(batches, enc_count, head_count, HEAD_DIM)
    cross_four = cross_queries.reshape(head_shape)
    cross_probs = jax.nn.softmax(
        jnp.einsum("sqhe,skhe->sqhk", cross_four, cross_keys, preferred_element_type=jnp.float32)
        * factor,
        axis=-1,
    )
    cross_low = cross_probs.astype(jnp.bfloat16)
    context_two = (
        jnp.einsum("sqhk,skhe->sqhe", cross_low, cross_values, preferred_element_type=jnp.float32)
        .reshape(batches, row_count, local_width)
        .astype(jnp.bfloat16)
    )
    branch_two = finish_branch(context_two, back_cross)
    after_two = after_one + branch_two
    normed_three, unit_three, inverse_three = norm_rows(after_two, norm_gain[2], norm_bias[2])
    rows_ffn = spread_rows(normed_three.astype(jnp.bfloat16))
    pre_act = jnp.einsum("scd,df->scf", rows_ffn, expand_full, preferred_element_type=jnp.float32)
    activated, slopes = gelu_parts(pre_act)
    hidden_low = activated.astype(jnp.bfloat16)
    branch_three = finish_branch(hidden_low, shrink_full)
    final_sum = after_two + branch_three
    grad_three = spread_grads(cotangent)
    grad_shrink = jnp.einsum(
        "scf,scd->fd", hidden_low, grad_three, preferred_element_type=jnp.float32
    )
    grad_pre = (
        jnp.einsum("scd,fd->scf", grad_three, shrink_full, preferred_element_type=jnp.float32)
        * slopes
    ).astype(jnp.bfloat16)
    grad_expand = jnp.einsum("scd,scf->df", rows_ffn, grad_pre, preferred_element_type=jnp.float32)
    back_three, gain_three, shift_three = norm_back(
        finish_grad(grad_pre, expand_full), unit_three, inverse_three, norm_gain[2]
    )
    grad_after_two = cotangent.astype(jnp.float32) + back_three
    grad_two = spread_grads(grad_after_two.astype(jnp.bfloat16))
    grad_back_cross = jnp.einsum(
        "scw,scd->wd", context_two, grad_two, preferred_element_type=jnp.float32
    )
    grad_context_two = jnp.einsum(
        "scd,wd->scw", grad_two, back_cross, preferred_element_type=jnp.float32
    ).astype(jnp.bfloat16)
    grad_cross_four = grad_context_two.reshape(head_shape)
    grad_cross_probs = jnp.einsum(
        "sqhe,skhe->sqhk", grad_cross_four, cross_values, preferred_element_type=jnp.float32
    )
    grad_cross_scores = (
        cross_probs
        * (grad_cross_probs - jnp.sum(cross_probs * grad_cross_probs, -1, keepdims=True))
    ).astype(jnp.bfloat16)
    grad_cross_q = (
        (
            jnp.einsum(
                "sqhk,skhe->sqhe", grad_cross_scores, cross_keys, preferred_element_type=jnp.float32
            )
            * factor
        )
        .reshape(batches, row_count, local_width)
        .astype(jnp.bfloat16)
    )
    part_keys = (
        jnp.einsum(
            "sqhk,sqhe->skhe", grad_cross_scores, cross_four, preferred_element_type=jnp.float32
        )
        * factor
    ).reshape(batches, enc_count, local_width)
    part_values = jnp.einsum(
        "sqhk,sqhe->skhe", cross_low, grad_cross_four, preferred_element_type=jnp.float32
    ).reshape(batches, enc_count, local_width)
    enc_keys, enc_values = (
        lax.psum_scatter(part_keys, "ctx", scatter_dimension=1, tiled=True),
        lax.psum_scatter(part_values, "ctx", scatter_dimension=1, tiled=True),
    )
    enc_keys = enc_keys.astype(jnp.bfloat16)
    enc_values = enc_values.astype(jnp.bfloat16)
    enc_share = enc_keys.shape[1]
    enc_rows = lax.dynamic_slice_in_dim(encoder, ctx_index * enc_share, enc_share, 1)
    grad_pair = jnp.stack(
        [
            jnp.einsum("sed,sew->dw", enc_rows, enc_keys, preferred_element_type=jnp.float32),
            jnp.einsum("sed,sew->dw", enc_rows, enc_values, preferred_element_type=jnp.float32),
        ]
    )
    encoder_grad = lax.psum_scatter(
        jnp.einsum("sew,dw->sed", enc_keys, proj_pair[0], preferred_element_type=jnp.float32)
        + jnp.einsum("sew,dw->sed", enc_values, proj_pair[1], preferred_element_type=jnp.float32),
        "tp",
        scatter_dimension=1,
        tiled=True,
    )
    grad_query_proj = jnp.einsum(
        "scd,scw->dw", rows_cross, grad_cross_q, preferred_element_type=jnp.float32
    )
    back_two, gain_two, shift_two = norm_back(
        finish_grad(grad_cross_q, proj_query), unit_two, inverse_two, norm_gain[1]
    )
    grad_after_one = grad_after_two + back_two
    grad_one = spread_grads(grad_after_one.astype(jnp.bfloat16))
    grad_back_self = jnp.einsum(
        "scw,scd->wd", context_one, grad_one, preferred_element_type=jnp.float32
    )
    grad_context_one = jnp.einsum(
        "scd,wd->scw", grad_one, back_self, preferred_element_type=jnp.float32
    ).astype(jnp.bfloat16)
    grad_ctx_four = grad_context_one.reshape(head_shape)
    delta_rows = jnp.sum(grad_ctx_four.astype(jnp.float32) * attended, -1)
    grad_query, grad_key_all, grad_value_all = key_sweep(
        queries_four,
        grad_ctx_four,
        log_total,
        delta_rows,
        keys_four,
        values_four,
        query_pos,
        prefix,
        key_span,
        factor,
    )
    own_keys, own_values = (
        lax.psum_scatter(grad_key_all, "ctx", scatter_dimension=0, tiled=True),
        lax.psum_scatter(grad_value_all, "ctx", scatter_dimension=0, tiled=True),
    )
    own_keys = jnp.transpose(own_keys, (1, 0, 2))
    own_values = jnp.transpose(own_values, (1, 0, 2))
    grad_joined = jnp.concatenate(
        [grad_query.reshape(batches, row_count, local_width), own_keys, own_values], -1
    ).astype(jnp.bfloat16)
    grad_proj_self = jnp.transpose(
        jnp.einsum(
            "scd,scw->dw", rows_self, grad_joined, preferred_element_type=jnp.float32
        ).reshape(model_width, 3, local_width),
        (1, 0, 2),
    )
    back_one, gain_one, shift_one = norm_back(
        finish_grad(grad_joined, local_stack), unit_one, inverse_one, norm_gain[0]
    )
    input_grad = grad_after_one + back_one
    shard_grads = (
        lax.psum_scatter(grad_proj_self, "fsdp", scatter_dimension=1, tiled=True),
        lax.psum_scatter(grad_query_proj, "fsdp", scatter_dimension=0, tiled=True),
        lax.psum_scatter(grad_pair, "fsdp", scatter_dimension=1, tiled=True),
        lax.psum_scatter(grad_back_self, "fsdp", scatter_dimension=1, tiled=True),
        lax.psum_scatter(grad_back_cross, "fsdp", scatter_dimension=1, tiled=True),
        lax.psum_scatter(grad_expand, "fsdp", scatter_dimension=0, tiled=True),
        lax.psum_scatter(grad_shrink, "fsdp", scatter_dimension=1, tiled=True),
    )
    full_grads = lax.psum(
        (
            shard_grads[0],
            shard_grads[1],
            shard_grads[2],
            shard_grads[3],
            shard_grads[4],
            shard_grads[5],
            shard_grads[6],
        ),
        "ctx",
    )
    squares = jnp.stack(
        [
            jnp.sum(final_sum * final_sum),
            jnp.sum(branch_one * branch_one),
            jnp.sum(branch_two * branch_two),
            jnp.sum(branch_three * branch_three),
        ]
    )
    gain_grad, bias_grad, square_totals = lax.psum(
        (
            jnp.stack([gain_one, gain_two, gain_three]),
            jnp.stack([shift_one, shift_two, shift_three]),
            squares,
        ),
        ("fsdp", "ctx", "tp"),
    )
    entries = (
        tokens.shape[0]
        * tokens.shape[1]
        * tokens.shape[2]
        * lax.axis_size("fsdp")
        * lax.axis_size("ctx")
        * lax.axis_size("tp")
    )
    norms = jnp.sqrt(square_totals / entries)
    return (
        final_sum,
        input_grad,
        encoder_grad,
        full_grads[0],
        full_grads[1],
        full_grads[2],
        full_grads[3],
        full_grads[4],
        full_grads[5],
        full_grads[6],
        gain_grad,
        bias_grad[:2],
        bias_grad[2],
        norms,
    )


def dot_of(left, right, left_dim, right_dim):
    return lax.dot_general(
        left, right, (((left_dim,), (right_dim,)), ((), ())), preferred_element_type=jnp.float32
    )


def bounds(prefix, start, query_span, key_span):
    whole = jnp.maximum(prefix, start + 1) // key_span
    every = (jnp.maximum(prefix, start + query_span) + key_span - 1) // key_span
    return whole, every


def hide(scores, limit, offset):
    return jnp.where(lax.broadcasted_iota(jnp.int32, scores.shape, 0) < limit - offset, scores, NEG)


def forward_kernel(scalars, weight_ref, *refs, span, chunk, slots, group):
    chunk_refs, refs = refs[:slots], refs[slots:]
    qkv_ref, wide_ref, log_ref = refs[:3]
    out_refs, refs = refs[3 : 3 + group], refs[3 + group :]
    queries_ref, keys_ref, values_ref, low_ref = refs
    step = pl.program_id(0)
    prefix, me = scalars[0], scalars[1]
    factor = HEAD_DIM**-0.5

    @pl.when(step == 0)
    def project():
        values_ref[HEAD_DIM:, :] = jnp.ones_like(values_ref[HEAD_DIM:, :])
        for slot in range(slots):
            place = scalars[2 + slot]

            @pl.when(place >= 0)
            def one_chunk(slot=slot, place=place):
                rows = chunk_refs[slot][...]
                joined = dot_of(weight_ref[...], rows, 1, 1).astype(jnp.bfloat16)
                here = pl.ds(pl.multiple_of(place * chunk, chunk), chunk)
                scaled = joined[:HEAD_DIM, :] * jnp.bfloat16(factor)
                queries_ref[:, here] = scaled
                values_ref[:HEAD_DIM, here] = joined[2 * HEAD_DIM :, :]
                keys_ref[here, :] = dot_of(
                    rows, weight_ref[HEAD_DIM : 2 * HEAD_DIM, :], 1, 1
                ).astype(jnp.bfloat16)
                qkv_ref[:HEAD_DIM, here] = scaled
                qkv_ref[HEAD_DIM:, here] = joined[HEAD_DIM:, :]

    start = pl.multiple_of(step * span, span)
    queries = queries_ref[:, pl.ds(start, span)]
    limit = jnp.maximum(prefix, start + 1 + lax.broadcasted_iota(jnp.int32, (1, span), 1))
    whole, every = bounds(prefix, start, span, span)

    def advance(block, carry, masked):
        highest, total = carry
        offset = pl.multiple_of(block * span, span)
        scores = dot_of(keys_ref[pl.ds(offset, span), :], queries, 1, 0)
        if masked:
            scores = hide(scores, limit, offset)
        higher = jnp.maximum(highest, jnp.max(scores, axis=0, keepdims=True))
        weights = jnp.exp(scores - higher).astype(jnp.bfloat16)
        fading = jnp.exp(highest - higher)
        total = total * fading + dot_of(values_ref[:, pl.ds(offset, span)], weights, 1, 0)
        return higher, total

    carry = (
        jnp.full((1, span), NEG, jnp.float32),
        jnp.zeros((values_ref.shape[0], span), jnp.float32),
    )
    carry = lax.fori_loop(0, whole, lambda j, c: advance(j, c, False), carry)
    highest, total = lax.fori_loop(whole, every, lambda j, c: advance(j, c, True), carry)
    weight_sum = total[HEAD_DIM : HEAD_DIM + 1, :]
    attended = total[:HEAD_DIM, :] / weight_sum
    wide_ref[...] = attended
    log_ref[...] = highest + jnp.log(weight_sum)
    low = attended.astype(jnp.bfloat16)
    for part in range(span // chunk):
        low_ref[(step * (span // chunk) + part) ^ me] = low[:, part * chunk : (part + 1) * chunk]

    @pl.when(step == pl.num_programs(0) - 1)
    def finish():
        for slot in range(group):
            out_refs[slot][...] = low_ref[slot]


def forward_attention(scalars, weight, chunks, length, span, group):
    slots = len(chunks)
    chunk = chunks[0].shape[0]
    whole = lambda *shape: pl.BlockSpec(shape, lambda i, s: (0,) * len(shape))
    bf16, f32 = jnp.bfloat16, jnp.float32
    struct = jax.ShapeDtypeStruct
    outs = pl.pallas_call(
        functools.partial(forward_kernel, span=span, chunk=chunk, slots=slots, group=group),
        grid_spec=pltpu.PrefetchScalarGridSpec(
            num_scalar_prefetch=1,
            grid=(length // span,),
            in_specs=[whole(*weight.shape)] + [whole(*c.shape) for c in chunks],
            out_specs=[
                whole(3 * HEAD_DIM, length),
                pl.BlockSpec((HEAD_DIM, span), lambda i, s: (0, i)),
                pl.BlockSpec((1, span), lambda i, s: (0, i)),
            ]
            + [whole(HEAD_DIM, chunk)] * group,
            scratch_shapes=[
                pltpu.VMEM((HEAD_DIM, length), bf16),
                pltpu.VMEM((length, HEAD_DIM), bf16),
                pltpu.VMEM((HEAD_DIM + 16, length), bf16),
                pltpu.VMEM((group, HEAD_DIM, chunk), bf16),
            ],
        ),
        out_shape=[
            struct((3 * HEAD_DIM, length), bf16),
            struct((HEAD_DIM, length), f32),
            struct((1, length), f32),
        ]
        + [struct((HEAD_DIM, chunk), bf16)] * group,
        compiler_params=pltpu.CompilerParams(vmem_limit_bytes=VMEM_LIMIT),
        cost_estimate=pl.CostEstimate(
            flops=20_000_000_000, bytes_accessed=10_000_000, transcendentals=10_000_000
        ),
        name="attention_forward",
    )(scalars, weight, *chunks)
    return outs[0], outs[1], outs[2], outs[3:]


def backward_kernel(scalars, qkv_ref, wide_ref, log_ref, *refs, span, chunk, group):
    grad_refs, refs = refs[:group], refs[group:]
    out_refs, refs = refs[:group], refs[group:]
    (
        queries_ref,
        keys_ref,
        values_ref,
        gradt_ref,
        grad_ref,
        delta_ref,
        grad_keys_ref,
        grad_values_ref,
        low_ref,
    ) = refs
    step = pl.program_id(0)
    prefix, me = scalars[0], scalars[1]
    factor = HEAD_DIM**-0.5
    length = qkv_ref.shape[1]

    @pl.when(step == 0)
    def prepare():
        for slot in range(group):
            here = pl.ds(pl.multiple_of((me ^ slot) * chunk, chunk), chunk)
            gradt_ref[:, here] = grad_refs[slot][...]
            grad_ref[here, :] = grad_refs[slot][...].T
        delta_ref[...] = jnp.sum(
            gradt_ref[...].astype(jnp.float32) * wide_ref[...], axis=0, keepdims=True
        )
        queries_ref[...] = qkv_ref[:HEAD_DIM, :].T
        keys_ref[...] = qkv_ref[HEAD_DIM : 2 * HEAD_DIM, :].T
        values_ref[...] = qkv_ref[2 * HEAD_DIM :, :].T
        grad_keys_ref[...] = jnp.zeros_like(grad_keys_ref)
        grad_values_ref[...] = jnp.zeros_like(grad_values_ref)

    start = pl.multiple_of(step * span, span)
    here = pl.ds(start, span)
    queries_t, queries = qkv_ref[:HEAD_DIM, here], queries_ref[here, :]
    grads_t, grads = gradt_ref[:, here], grad_ref[here, :]
    logs, deltas = log_ref[:, here], delta_ref[:, here]
    limit = jnp.maximum(prefix, start + 1 + lax.broadcasted_iota(jnp.int32, (1, span), 1))
    whole, every = bounds(prefix, start, span, span)

    def advance(block, grad_queries, masked):
        there = pl.ds(pl.multiple_of(block * span, span), span)
        scores = dot_of(keys_ref[there, :], queries_t, 1, 0)
        if masked:
            scores = hide(scores, limit, block * span)
        probs = jnp.exp(scores - logs)
        grad_probs = dot_of(values_ref[there, :], grads_t, 1, 0)
        grad_scores = (probs * (grad_probs - deltas)).astype(jnp.bfloat16)
        grad_values_ref[there, :] += dot_of(probs.astype(jnp.bfloat16), grads, 1, 0)
        grad_keys_ref[there, :] += dot_of(grad_scores, queries, 1, 0)
        return grad_queries + dot_of(
            qkv_ref[HEAD_DIM : 2 * HEAD_DIM, there], grad_scores, 1, 0
        )

    grad_queries = jnp.zeros((HEAD_DIM, span), jnp.float32)
    grad_queries = lax.fori_loop(0, whole, lambda j, c: advance(j, c, False), grad_queries)
    grad_queries = lax.fori_loop(whole, every, lambda j, c: advance(j, c, True), grad_queries)
    low = (grad_queries * factor).astype(jnp.bfloat16)
    for part in range(span // chunk):
        low_ref[(step * (span // chunk) + part) ^ me, :HEAD_DIM, :] = low[
            :, part * chunk : (part + 1) * chunk
        ]

    @pl.when(step == pl.num_programs(0) - 1)
    def finish():
        for place in range(length // chunk):
            rows = pl.ds(place * chunk, chunk)
            low_ref[place ^ me, HEAD_DIM : 2 * HEAD_DIM, :] = grad_keys_ref[rows, :].T.astype(
                jnp.bfloat16
            )
            low_ref[place ^ me, 2 * HEAD_DIM :, :] = grad_values_ref[rows, :].T.astype(jnp.bfloat16)
        for slot in range(group):
            out_refs[slot][...] = low_ref[slot]


def backward_attention(scalars, qkv, wide, logs, grads, span):
    group = len(grads)
    length = qkv.shape[1]
    chunk = grads[0].shape[1]
    whole = lambda *shape: pl.BlockSpec(shape, lambda i, s: (0,) * len(shape))
    bf16, f32 = jnp.bfloat16, jnp.float32
    return pl.pallas_call(
        functools.partial(backward_kernel, span=span, chunk=chunk, group=group),
        grid_spec=pltpu.PrefetchScalarGridSpec(
            num_scalar_prefetch=1,
            grid=(length // span,),
            in_specs=[whole(*qkv.shape), whole(*wide.shape), whole(*logs.shape)]
            + [whole(*g.shape) for g in grads],
            out_specs=[whole(3 * HEAD_DIM, chunk)] * group,
            scratch_shapes=[
                pltpu.VMEM((length, HEAD_DIM), bf16),
                pltpu.VMEM((length, HEAD_DIM), bf16),
                pltpu.VMEM((length, HEAD_DIM), bf16),
                pltpu.VMEM((HEAD_DIM, length), bf16),
                pltpu.VMEM((length, HEAD_DIM), bf16),
                pltpu.VMEM((1, length), f32),
                pltpu.VMEM((length, HEAD_DIM), f32),
                pltpu.VMEM((length, HEAD_DIM), f32),
                pltpu.VMEM((group, 3 * HEAD_DIM, chunk), bf16),
            ],
        ),
        out_shape=[jax.ShapeDtypeStruct((3 * HEAD_DIM, chunk), bf16)] * group,
        compiler_params=pltpu.CompilerParams(vmem_limit_bytes=VMEM_LIMIT),
        cost_estimate=pl.CostEstimate(
            flops=40_000_000_000, bytes_accessed=10_000_000, transcendentals=10_000_000
        ),
        name="attention_backward",
    )(scalars, qkv, wide, logs, *grads)


def swap_cores(value):
    return lax.ppermute(value, "ctx", [(0, 1), (1, 0)])


def trade(parts):
    group = len(parts)
    return [parts[0]] + [
        lax.ppermute(parts[k], ("ctx", "tp"), [(i, i ^ k) for i in range(group)])
        for k in range(1, group)
    ]


def gather_rows(rows):
    up = lax.ppermute(rows, "tp", [(0, 1), (1, 2), (2, 3)])
    down = lax.ppermute(rows, "tp", [(1, 0), (2, 1), (3, 2)])
    up_two = lax.ppermute(up, "tp", [(1, 2), (2, 3)])
    down_two = lax.ppermute(down, "tp", [(2, 1), (1, 0)])
    far = lax.ppermute(rows, "tp", [(0, 3), (3, 0)])
    mine = [rows, up, down, up_two, down_two, far]
    return mine + [swap_cores(piece) for piece in mine]


def slot_places(ctx_index, tp_index):
    offsets = [0, -1, 1, -2, 2]
    places = []
    for core in (ctx_index, 1 - ctx_index):
        for offset in offsets:
            chip = tp_index + offset
            places.append(jnp.where((chip >= 0) & (chip < 4), core * 4 + chip, -1))
        places.append(jnp.where((tp_index == 0) | (tp_index == 3), core * 4 + 3 - tp_index, -1))
    return places


def norm_back_rows(upstream, unit_rows, inverse, scaling):
    scaled = upstream * scaling
    result = inverse * (
        scaled
        - jnp.mean(scaled, -1, keepdims=True)
        - unit_rows * jnp.mean(scaled * unit_rows, -1, keepdims=True)
    )
    return result, jnp.sum(upstream * unit_rows, 0), jnp.sum(upstream, 0)


def low(value):
    return value.astype(jnp.bfloat16)


def head_parts(value):
    return value.reshape(value.shape[0], -1, HEAD_DIM)


def local_heads(
    tokens,
    timesteps,
    time_table,
    prefix,
    encoder,
    self_qkv,
    cross_q,
    cross_kv,
    self_out,
    cross_out,
    ffn_up,
    ffn_down,
    norm_gain,
    norm_bias,
    cotangent,
):
    batches, chunk, width = tokens.shape
    group = 8
    length = group * chunk
    enc_count = encoder.shape[1]
    factor = HEAD_DIM ** (-0.5)
    ctx_index, tp_index = lax.axis_index("ctx"), lax.axis_index("tp")
    me = ctx_index * 4 + tp_index
    span = 1024
    piece = width // 4
    blocks = jnp.concatenate(
        [
            self_qkv,
            cross_q[None],
            cross_kv,
            self_out[None],
            cross_out[None],
            jnp.transpose(ffn_up.reshape(piece, 4, piece), (1, 0, 2)),
            ffn_down.reshape(4, piece, piece),
        ]
    )
    count = blocks.shape[0]
    half = piece // 2
    own_half = lax.dynamic_slice_in_dim(blocks, ctx_index * half, half, 1)
    gathered = lax.all_gather(own_half, ("fsdp", "tp"), axis=0, tiled=False)
    mine = lax.dynamic_slice_in_dim(self_qkv, ctx_index * HEAD_DIM, HEAD_DIM, 2)
    mine = jnp.transpose(mine, (0, 2, 1)).reshape(3 * HEAD_DIM, piece)
    columns = [mine] + [
        lax.ppermute(mine, "fsdp", [(i, i ^ k) for i in range(4)]) for k in range(1, 4)
    ]
    fsdp_index = lax.axis_index("fsdp")
    columns = jnp.stack(columns)
    head_weight = jnp.concatenate(
        [lax.dynamic_index_in_dim(columns, fsdp_index ^ f, 0, False) for f in range(4)], 1
    )
    steps_onehot = (timesteps[:, None] == lax.iota(jnp.int32, time_table.shape[0])[None, :]).astype(
        jnp.bfloat16
    )
    embedded = jnp.dot(steps_onehot, time_table, preferred_element_type=jnp.float32)
    places = slot_places(ctx_index, tp_index)
    start_sums, units_one, kept, arrived = [], [], [], []
    for s in range(batches):
        start_sum = tokens[s].astype(jnp.float32) + embedded[s][None, :]
        normed, unit, inverse = norm_rows(start_sum, norm_gain[0], norm_bias[0])
        start_sums.append(start_sum)
        units_one.append((unit, inverse))
        chunks = gather_rows(low(normed))
        scalars = jnp.stack([prefix[s], me] + places).astype(jnp.int32)
        qkv, wide, logs, outs = forward_attention(
            scalars, head_weight, chunks, length, span, group
        )
        kept.append((chunks, scalars, qkv, wide, logs))
        arrived.append(trade(outs))
    other = swap_cores(gathered)
    first = jnp.where(ctx_index == 0, gathered, other)
    second = jnp.where(ctx_index == 0, other, gathered)
    whole = jnp.concatenate([first, second], 2).reshape(4, 4, count, piece, piece)
    square = lambda b: jnp.transpose(whole[:, :, b], (0, 2, 1, 3)).reshape(width, width)
    flipped = lambda b: jnp.transpose(whole[:, :, b], (1, 2, 0, 3)).reshape(width, width)
    full_qkv = [square(b) for b in range(3)]
    full_q, full_k, full_v = square(3), square(4), square(5)
    full_out, full_cross = flipped(6), flipped(7)
    full_up = jnp.transpose(whole[:, :, 8:12], (0, 3, 1, 2, 4)).reshape(width, 4 * width)
    full_down = jnp.transpose(whole[:, :, 12:16], (1, 2, 3, 0, 4)).reshape(4 * width, width)
    slot_heads = [((me ^ k) % 4) * 2 + (me ^ k) // 4 for k in range(group)]
    out_heads = full_out.reshape(group, HEAD_DIM, width)
    out_slots = jnp.concatenate(
        [lax.dynamic_index_in_dim(out_heads, h, 0, False) for h in slot_heads]
    )
    qkv_heads = jnp.stack(full_qkv).reshape(3, width, group, HEAD_DIM)
    qkv_heads = jnp.transpose(qkv_heads, (2, 0, 3, 1))
    qkv_slots = jnp.concatenate(
        [lax.dynamic_index_in_dim(qkv_heads, h, 0, False) for h in slot_heads]
    ).reshape(group * 3 * HEAD_DIM, width)

    results, sums, returns, early = [], [], [], []
    for s in range(batches):
        context_t = jnp.concatenate(arrived[s])
        branch_one = dot_of(context_t, out_slots, 0, 0)
        after_one = start_sums[s] + branch_one
        normed_two, unit_two, inverse_two = norm_rows(after_one, norm_gain[1], norm_bias[1])
        normed_two = low(normed_two)
        cross_queries = low(dot_of(normed_two, full_q, 1, 0))
        cross_keys = low(dot_of(encoder[s], full_k, 1, 0))
        cross_values = low(dot_of(encoder[s], full_v, 1, 0))
        queries, keys, values = (
            head_parts(cross_queries),
            head_parts(cross_keys),
            head_parts(cross_values),
        )
        probs = jax.nn.softmax(
            jnp.einsum("qhe,khe->hqk", queries, keys, preferred_element_type=jnp.float32) * factor,
            axis=-1,
        )
        probs_low = low(probs)
        context_two = low(
            jnp.einsum("hqk,khe->qhe", probs_low, values, preferred_element_type=jnp.float32)
        ).reshape(chunk, width)
        branch_two = dot_of(context_two, full_cross, 1, 0)
        after_two = after_one + branch_two
        normed_three, unit_three, inverse_three = norm_rows(after_two, norm_gain[2], norm_bias[2])
        normed_three = low(normed_three)
        activated, slopes = gelu_parts(dot_of(normed_three, full_up, 1, 0))
        hidden = low(activated)
        branch_three = dot_of(hidden, full_down, 1, 0)
        final_sum = after_two + branch_three
        squares = jnp.stack(
            [jnp.sum(v * v) for v in (final_sum, branch_one, branch_two, branch_three)]
        )
        grad_three = cotangent[s]
        grad_pre = low(dot_of(grad_three, full_down, 1, 1) * slopes)
        back_three, gain_three, shift_three = norm_back_rows(
            dot_of(grad_pre, full_up, 1, 1), unit_three, inverse_three, norm_gain[2]
        )
        grad_after_two = grad_three.astype(jnp.float32) + back_three
        grad_two = low(grad_after_two)
        grad_context = low(dot_of(grad_two, full_cross, 1, 1))
        grad_heads = head_parts(grad_context)
        grad_probs = jnp.einsum(
            "qhe,khe->hqk", grad_heads, values, preferred_element_type=jnp.float32
        )
        grad_scores = low(
            probs * (grad_probs - jnp.sum(probs * grad_probs, -1, keepdims=True))
        )
        grad_cross_q = low(
            jnp.einsum("hqk,khe->qhe", grad_scores, keys, preferred_element_type=jnp.float32)
            * factor
        ).reshape(chunk, width)
        part_keys = (
            jnp.einsum("hqk,qhe->khe", grad_scores, queries, preferred_element_type=jnp.float32)
            * factor
        ).reshape(enc_count, width)
        part_values = jnp.einsum(
            "hqk,qhe->khe", probs_low, grad_heads, preferred_element_type=jnp.float32
        ).reshape(enc_count, width)
        back_two, gain_two, shift_two = norm_back_rows(
            dot_of(grad_cross_q, full_q, 1, 1), unit_two, inverse_two, norm_gain[1]
        )
        grad_after_one = grad_after_two + back_two
        grad_one = low(grad_after_one)
        grad_context_t = low(dot_of(out_slots, grad_one, 1, 1))
        returns.append(
            trade([grad_context_t[k * HEAD_DIM : (k + 1) * HEAD_DIM] for k in range(group)])
        )
        results.append((final_sum, grad_after_one))
        sums.append((squares, gain_two, shift_two, gain_three, shift_three))
        early.append(
            (
                dot_of(normed_two, grad_cross_q, 0, 0),
                dot_of(context_t, grad_one, 1, 0),
                dot_of(context_two, grad_two, 0, 0),
                dot_of(normed_three, grad_pre, 0, 0),
                dot_of(hidden, grad_three, 0, 0),
                low(jnp.concatenate([part_keys, part_values], 1)),
            )
        )
    share = enc_count // group
    parts = jnp.stack([e[5] for e in early]).reshape(batches, group, share, 2 * width)
    parts = [lax.dynamic_index_in_dim(parts, me ^ k, 1, False) for k in range(group)]
    enc_grads = low(sum(p.astype(jnp.float32) for p in trade(parts)))
    enc_rows = lax.dynamic_slice_in_dim(encoder, me * share, share, 1)
    enc_rows = enc_rows.reshape(batches * share, width)
    enc_flat = enc_grads.reshape(batches * share, 2 * width)
    encoder_grad = (
        dot_of(enc_flat[:, :width], full_k, 1, 1) + dot_of(enc_flat[:, width:], full_v, 1, 1)
    ).reshape(batches, share, width)
    grad_pair = dot_of(enc_rows, enc_flat, 0, 0)
    grads_back, head_grads = [], 0.0
    for s in range(batches):
        chunks, scalars, qkv, wide, logs = kept[s]
        outs = backward_attention(scalars, qkv, wide, logs, returns[s], span)
        grads_back.append(trade(outs))
        kept[s] = kept[s] + (outs,)
    add = lambda n: sum(e[n] for e in early)
    grad_q = add(0)
    slot_out = add(1).reshape(group, HEAD_DIM, width)
    head_slots = [((h % 2) * 4 + h // 2) ^ me for h in range(group)]
    grad_out = jnp.concatenate(
        [lax.dynamic_index_in_dim(slot_out, k, 0, False) for k in head_slots]
    )
    cut = lambda g: jnp.transpose(g.reshape(4, piece, 4, piece), (0, 2, 1, 3))[:, :, None]
    cut_flipped = lambda g: jnp.transpose(g.reshape(4, piece, 4, piece), (2, 0, 1, 3))[:, :, None]
    packed = jnp.concatenate(
        [
            cut(grad_q),
            cut(grad_pair[:, :width]),
            cut(grad_pair[:, width:]),
            cut_flipped(grad_out),
            cut_flipped(add(2)),
            jnp.transpose(add(3).reshape(4, piece, 4, 4, piece), (0, 2, 3, 1, 4)),
            jnp.transpose(add(4).reshape(4, 4, piece, 4, piece), (3, 0, 1, 2, 4)),
        ],
        2,
    ).reshape(16, -1, 2, half, piece)
    packed = low(packed)
    keep_half = lax.dynamic_index_in_dim(packed, ctx_index, 2, False)
    send_half = lax.dynamic_index_in_dim(packed, 1 - ctx_index, 2, False)
    halved = keep_half.astype(jnp.float32) + swap_cores(send_half).astype(jnp.float32)
    scattered = lax.psum_scatter(low(halved), ("fsdp", "tp"), scatter_dimension=0, tiled=False)
    scattered = scattered.astype(jnp.float32)
    other_half = swap_cores(scattered)
    shards = jnp.concatenate(
        [
            jnp.where(ctx_index == 0, scattered, other_half),
            jnp.where(ctx_index == 0, other_half, scattered),
        ],
        1,
    )
    for s in range(batches):
        chunks, outs = kept[s][0], kept[s][5]
        joined = jnp.stack(outs)
        for slot, rows in enumerate(chunks):
            place = places[slot]
            index = jnp.where(place >= 0, place, me) ^ me
            part = dot_of(lax.dynamic_index_in_dim(joined, index, 0, False), rows, 1, 0)
            head_grads = head_grads + jnp.where(place >= 0, part, 0.0)
    head_grads = head_grads.reshape(3 * HEAD_DIM, 4, piece)
    pieces = [lax.dynamic_index_in_dim(head_grads, fsdp_index ^ k, 1, False) for k in range(4)]
    head_shard = pieces[0] + sum(
        lax.ppermute(pieces[k], "fsdp", [(i, i ^ k) for i in range(4)]) for k in range(1, 4)
    )
    head_shard = jnp.transpose(head_shard.reshape(3, HEAD_DIM, piece), (0, 2, 1))
    other_shard = swap_cores(head_shard)
    grad_self = jnp.concatenate(
        [
            jnp.where(ctx_index == 0, head_shard, other_shard),
            jnp.where(ctx_index == 0, other_shard, head_shard),
        ],
        2,
    )
    input_grads, gains_one, shifts_one = [], 0.0, 0.0
    for s in range(batches):
        upstream = dot_of(jnp.concatenate(grads_back[s]), qkv_slots, 0, 0)
        unit, inverse = units_one[s]
        back, gain, shift = norm_back_rows(upstream, unit, inverse, norm_gain[0])
        input_grads.append(results[s][1] + back)
        gains_one, shifts_one = gains_one + gain, shifts_one + shift
    total = lambda n: sum(v[n] for v in sums)
    gain_grad, bias_grad, square_totals = lax.psum(
        (
            jnp.stack([gains_one, total(1), total(3)]),
            jnp.stack([shifts_one, total(2), total(4)]),
            total(0),
        ),
        ("fsdp", "ctx", "tp"),
    )
    entries = (
        tokens.shape[0]
        * tokens.shape[1]
        * tokens.shape[2]
        * lax.axis_size("fsdp")
        * lax.axis_size("ctx")
        * lax.axis_size("tp")
    )
    return (
        jnp.stack([r[0] for r in results]),
        jnp.stack(input_grads),
        encoder_grad,
        grad_self,
        shards[0],
        shards[1:3],
        shards[3],
        shards[4],
        jnp.transpose(shards[5:9], (1, 0, 2)).reshape(piece, width),
        shards[9:13].reshape(width, piece),
        gain_grad,
        bias_grad[:2],
        bias_grad[2],
        jnp.sqrt(square_totals / entries),
    )


def solution(mesh):
    placed = (
        P("fsdp", ("ctx", "tp"), None),
        P("fsdp"),
        P(),
        P("fsdp"),
        P("fsdp", None, None),
        P(None, "fsdp", "tp"),
        P("fsdp", "tp"),
        P(None, "fsdp", "tp"),
        P("tp", "fsdp"),
        P("tp", "fsdp"),
        P("fsdp", "tp"),
        P("tp", "fsdp"),
        P(),
        P(),
        P("fsdp", ("ctx", "tp"), None),
    )
    heads_fit = dict(mesh.shape) == {"fsdp": 4, "ctx": 2, "tp": 4}
    return jax.shard_map(
        local_heads if heads_fit else local,
        mesh=mesh,
        in_specs=placed,
        out_specs=(
            P("fsdp", ("ctx", "tp"), None),
            P("fsdp", ("ctx", "tp"), None),
            P("fsdp", ("ctx", "tp"), None),
            P(None, "fsdp", "tp"),
            P("fsdp", "tp"),
            P(None, "fsdp", "tp"),
            P("tp", "fsdp"),
            P("tp", "fsdp"),
            P("fsdp", "tp"),
            P("tp", "fsdp"),
            P(),
            P(),
            P(),
            P(),
        ),
        check_vma=False,
    )
```

```python
import functools
import math

import jax
import jax.numpy as jnp
from jax import lax
from jax.experimental import pallas as pl
from jax.experimental.pallas import tpu as pltpu
from jax.sharding import PartitionSpec as P

HEAD_DIM = 64


EPS = 1e-05
NEG = -1e30
ROOT_HALF = 1.0 / math.sqrt(2.0)
INV_ROOT_TWO_PI = 1.0 / math.sqrt(2.0 * math.pi)
VMEM_LIMIT = 56 * 2**20


def norm_rows(hidden, scaling, offsets):
    centre = hidden - jnp.mean(hidden, -1, keepdims=True)
    inverse = lax.rsqrt(jnp.mean(centre * centre, -1, keepdims=True) + EPS)
    unit_rows = centre * inverse
    return (unit_rows * scaling + offsets, unit_rows, inverse)


def norm_back(upstream, unit_rows, inverse, scaling):
    scaled = upstream * scaling
    result = inverse * (
        scaled
        - jnp.mean(scaled, -1, keepdims=True)
        - unit_rows * jnp.mean(scaled * unit_rows, -1, keepdims=True)
    )
    return (result, jnp.sum(upstream * unit_rows, (0, 1)), jnp.sum(upstream, (0, 1)))


def gelu_parts(inputs):
    normal_cdf = 0.5 * (1.0 + lax.erf(inputs * ROOT_HALF))
    return (
        inputs * normal_cdf,
        normal_cdf + inputs * jnp.exp(-0.5 * inputs * inputs) * INV_ROOT_TWO_PI,
    )


def spread_rows(rows):
    return lax.all_gather(rows, "tp", axis=1, tiled=True)


def spread_grads(grad_rows):
    return lax.all_gather(grad_rows, "tp", axis=1, tiled=True)


def finish_branch(local_in, local_weight):
    return lax.psum_scatter(
        jnp.einsum("scw,wd->scd", local_in, local_weight, preferred_element_type=jnp.float32),
        "tp",
        scatter_dimension=1,
        tiled=True,
    )


def finish_grad(local_grad, local_weight):
    return lax.psum_scatter(
        jnp.einsum("scw,dw->scd", local_grad, local_weight, preferred_element_type=jnp.float32),
        "tp",
        scatter_dimension=1,
        tiled=True,
    )


def block_scores(queries, key_block, query_pos, key_pos, lengths, factor):
    scores = (
        jnp.einsum("sqhe,skhe->sqhk", queries, key_block, preferred_element_type=jnp.float32)
        * factor
    )
    visible = (key_pos[None, None, :] <= query_pos[None, :, None]) | (
        key_pos[None, None, :] < lengths[:, None, None]
    )
    return jnp.where(visible[:, :, None, :], scores, NEG)


def attend_forward(queries, key_rows, value_rows, query_pos, lengths, key_span, factor):
    length = key_rows.shape[1]

    def attend_advance(running, offset):
        highest, totals, summed = running
        key_block = lax.dynamic_slice_in_dim(key_rows, offset, key_span, 1)
        value_block = lax.dynamic_slice_in_dim(value_rows, offset, key_span, 1)
        scores = block_scores(
            queries, key_block, query_pos, offset + lax.iota(jnp.int32, key_span), lengths, factor
        )
        new_high = jnp.maximum(highest, jnp.max(scores, -1))
        weights = jnp.exp(scores - new_high[..., None])
        fading = jnp.exp(highest - new_high)
        totals = totals * fading + jnp.sum(weights, -1)
        summed = summed * fading[..., None] + jnp.einsum(
            "sqhk,skhe->sqhe",
            weights.astype(jnp.bfloat16),
            value_block,
            preferred_element_type=jnp.float32,
        )
        return ((new_high, totals, summed), None)

    stat_shape = queries.shape[:3]
    initial = (
        jnp.full(stat_shape, NEG, jnp.float32),
        jnp.zeros(stat_shape, jnp.float32),
        jnp.zeros(queries.shape, jnp.float32),
    )
    offsets = jnp.arange(length // key_span, dtype=jnp.int32) * key_span
    (highest, totals, summed), unused = lax.scan(attend_advance, initial, offsets)
    return (summed / totals[..., None], highest + jnp.log(totals))


def attend_block(
    queries,
    grad_out,
    log_rows,
    delta_rows,
    key_block,
    value_block,
    query_pos,
    key_pos,
    lengths,
    factor,
):
    scores = block_scores(queries, key_block, query_pos, key_pos, lengths, factor)
    probs = jnp.exp(scores - log_rows[..., None])
    grad_probs = jnp.einsum(
        "sqhe,skhe->sqhk", grad_out, value_block, preferred_element_type=jnp.float32
    )
    grad_scores = (probs * (grad_probs - delta_rows[..., None])).astype(jnp.bfloat16)
    return (probs.astype(jnp.bfloat16), grad_scores)


def key_sweep(
    queries,
    grad_out,
    log_rows,
    delta_rows,
    key_rows,
    value_rows,
    query_pos,
    lengths,
    key_span,
    factor,
):
    batches, row_count, head_count, head_depth = queries.shape
    length = key_rows.shape[1]

    def key_advance(grad_query, offset):
        key_block = lax.dynamic_slice_in_dim(key_rows, offset, key_span, 1)
        value_block = lax.dynamic_slice_in_dim(value_rows, offset, key_span, 1)
        key_pos = offset + lax.iota(jnp.int32, key_span)
        probs_low, grad_scores = attend_block(
            queries,
            grad_out,
            log_rows,
            delta_rows,
            key_block,
            value_block,
            query_pos,
            key_pos,
            lengths,
            factor,
        )
        grad_query = (
            grad_query
            + jnp.einsum(
                "sqhk,skhe->sqhe", grad_scores, key_block, preferred_element_type=jnp.float32
            )
            * factor
        )
        grad_key = (
            jnp.einsum("sqhk,sqhe->kshe", grad_scores, queries, preferred_element_type=jnp.float32)
            * factor
        )
        grad_value = jnp.einsum(
            "sqhk,sqhe->kshe", probs_low, grad_out, preferred_element_type=jnp.float32
        )
        return (grad_query, (grad_key, grad_value))

    offsets = jnp.arange(length // key_span, dtype=jnp.int32) * key_span
    grad_query, stacked = lax.scan(key_advance, jnp.zeros(queries.shape, jnp.float32), offsets)
    flat_shape = (length, batches, head_count * head_depth)
    return (grad_query, stacked[0].reshape(flat_shape), stacked[1].reshape(flat_shape))


def local(
    tokens,
    timesteps,
    time_table,
    prefix,
    encoder,
    self_qkv,
    cross_q,
    cross_kv,
    self_out,
    cross_out,
    ffn_up,
    ffn_down,
    norm_gain,
    norm_bias,
    cotangent,
):
    proj_self, proj_query, proj_pair, back_self, back_cross, expand_full, shrink_full = (
        lax.all_gather(self_qkv, "fsdp", axis=1, tiled=True),
        lax.all_gather(cross_q, "fsdp", axis=0, tiled=True),
        lax.all_gather(cross_kv, "fsdp", axis=1, tiled=True),
        lax.all_gather(self_out, "fsdp", axis=1, tiled=True),
        lax.all_gather(cross_out, "fsdp", axis=1, tiled=True),
        lax.all_gather(ffn_up, "fsdp", axis=0, tiled=True),
        lax.all_gather(ffn_down, "fsdp", axis=1, tiled=True),
    )
    batches = tokens.shape[0]
    model_width = tokens.shape[2]
    local_width = proj_query.shape[1]
    head_count = local_width // HEAD_DIM
    factor = HEAD_DIM ** (-0.5)
    ctx_index = lax.axis_index("ctx")
    local_stack = jnp.transpose(proj_self, (1, 0, 2)).reshape(model_width, 3 * local_width)
    steps_onehot = (timesteps[:, None] == lax.iota(jnp.int32, time_table.shape[0])[None, :]).astype(
        jnp.bfloat16
    )
    embedded = jnp.dot(steps_onehot, time_table, preferred_element_type=jnp.float32)
    start_sum = tokens.astype(jnp.float32) + embedded[:, None, :]
    normed_one, unit_one, inverse_one = norm_rows(start_sum, norm_gain[0], norm_bias[0])
    rows_self = spread_rows(normed_one.astype(jnp.bfloat16))
    row_count = rows_self.shape[1]
    head_shape = (batches, row_count, head_count, HEAD_DIM)
    projected = jnp.einsum(
        "scd,kdw->kscw", rows_self, proj_self, preferred_element_type=jnp.float32
    ).astype(jnp.bfloat16)
    queries, key_local, value_local = (projected[0], projected[1], projected[2])
    key_all, value_all = (
        lax.all_gather(key_local, "ctx", axis=1, tiled=True),
        lax.all_gather(value_local, "ctx", axis=1, tiled=True),
    )
    length = key_all.shape[1]
    key_span = min(512, length)
    query_pos = ctx_index * row_count + lax.iota(jnp.int32, row_count)
    keys_four = key_all.reshape(batches, length, head_count, HEAD_DIM)
    values_four = value_all.reshape(batches, length, head_count, HEAD_DIM)
    queries_four = queries.reshape(head_shape)
    attended, log_total = attend_forward(
        queries_four, keys_four, values_four, query_pos, prefix, key_span, factor
    )
    context_one = attended.reshape(batches, row_count, local_width).astype(jnp.bfloat16)
    branch_one = finish_branch(context_one, back_self)
    after_one = start_sum + branch_one
    normed_two, unit_two, inverse_two = norm_rows(after_one, norm_gain[1], norm_bias[1])
    rows_cross = spread_rows(normed_two.astype(jnp.bfloat16))
    cross_queries = jnp.einsum(
        "scd,dw->scw", rows_cross, proj_query, preferred_element_type=jnp.float32
    ).astype(jnp.bfloat16)
    enc_pair = jnp.einsum(
        "sed,kdw->ksew", encoder, proj_pair, preferred_element_type=jnp.float32
    ).astype(jnp.bfloat16)
    enc_count = encoder.shape[1]
    cross_keys = enc_pair[0].reshape(batches, enc_count, head_count, HEAD_DIM)
    cross_values = enc_pair[1].reshape(batches, enc_count, head_count, HEAD_DIM)
    cross_four = cross_queries.reshape(head_shape)
    cross_probs = jax.nn.softmax(
        jnp.einsum("sqhe,skhe->sqhk", cross_four, cross_keys, preferred_element_type=jnp.float32)
        * factor,
        axis=-1,
    )
    cross_low = cross_probs.astype(jnp.bfloat16)
    context_two = (
        jnp.einsum("sqhk,skhe->sqhe", cross_low, cross_values, preferred_element_type=jnp.float32)
        .reshape(batches, row_count, local_width)
        .astype(jnp.bfloat16)
    )
    branch_two = finish_branch(context_two, back_cross)
    after_two = after_one + branch_two
    normed_three, unit_three, inverse_three = norm_rows(after_two, norm_gain[2], norm_bias[2])
    rows_ffn = spread_rows(normed_three.astype(jnp.bfloat16))
    pre_act = jnp.einsum("scd,df->scf", rows_ffn, expand_full, preferred_element_type=jnp.float32)
    activated, slopes = gelu_parts(pre_act)
    hidden_low = activated.astype(jnp.bfloat16)
    branch_three = finish_branch(hidden_low, shrink_full)
    final_sum = after_two + branch_three
    grad_three = spread_grads(cotangent)
    grad_shrink = jnp.einsum(
        "scf,scd->fd", hidden_low, grad_three, preferred_element_type=jnp.float32
    )
    grad_pre = (
        jnp.einsum("scd,fd->scf", grad_three, shrink_full, preferred_element_type=jnp.float32)
        * slopes
    ).astype(jnp.bfloat16)
    grad_expand = jnp.einsum("scd,scf->df", rows_ffn, grad_pre, preferred_element_type=jnp.float32)
    back_three, gain_three, shift_three = norm_back(
        finish_grad(grad_pre, expand_full), unit_three, inverse_three, norm_gain[2]
    )
    grad_after_two = cotangent.astype(jnp.float32) + back_three
    grad_two = spread_grads(grad_after_two.astype(jnp.bfloat16))
    grad_back_cross = jnp.einsum(
        "scw,scd->wd", context_two, grad_two, preferred_element_type=jnp.float32
    )
    grad_context_two = jnp.einsum(
        "scd,wd->scw", grad_two, back_cross, preferred_element_type=jnp.float32
    ).astype(jnp.bfloat16)
    grad_cross_four = grad_context_two.reshape(head_shape)
    grad_cross_probs = jnp.einsum(
        "sqhe,skhe->sqhk", grad_cross_four, cross_values, preferred_element_type=jnp.float32
    )
    grad_cross_scores = (
        cross_probs
        * (grad_cross_probs - jnp.sum(cross_probs * grad_cross_probs, -1, keepdims=True))
    ).astype(jnp.bfloat16)
    grad_cross_q = (
        (
            jnp.einsum(
                "sqhk,skhe->sqhe", grad_cross_scores, cross_keys, preferred_element_type=jnp.float32
            )
            * factor
        )
        .reshape(batches, row_count, local_width)
        .astype(jnp.bfloat16)
    )
    part_keys = (
        jnp.einsum(
            "sqhk,sqhe->skhe", grad_cross_scores, cross_four, preferred_element_type=jnp.float32
        )
        * factor
    ).reshape(batches, enc_count, local_width)
    part_values = jnp.einsum(
        "sqhk,sqhe->skhe", cross_low, grad_cross_four, preferred_element_type=jnp.float32
    ).reshape(batches, enc_count, local_width)
    enc_keys, enc_values = (
        lax.psum_scatter(part_keys, "ctx", scatter_dimension=1, tiled=True),
        lax.psum_scatter(part_values, "ctx", scatter_dimension=1, tiled=True),
    )
    enc_keys = enc_keys.astype(jnp.bfloat16)
    enc_values = enc_values.astype(jnp.bfloat16)
    enc_share = enc_keys.shape[1]
    enc_rows = lax.dynamic_slice_in_dim(encoder, ctx_index * enc_share, enc_share, 1)
    grad_pair = jnp.stack(
        [
            jnp.einsum("sed,sew->dw", enc_rows, enc_keys, preferred_element_type=jnp.float32),
            jnp.einsum("sed,sew->dw", enc_rows, enc_values, preferred_element_type=jnp.float32),
        ]
    )
    encoder_grad = lax.psum_scatter(
        jnp.einsum("sew,dw->sed", enc_keys, proj_pair[0], preferred_element_type=jnp.float32)
        + jnp.einsum("sew,dw->sed", enc_values, proj_pair[1], preferred_element_type=jnp.float32),
        "tp",
        scatter_dimension=1,
        tiled=True,
    )
    grad_query_proj = jnp.einsum(
        "scd,scw->dw", rows_cross, grad_cross_q, preferred_element_type=jnp.float32
    )
    back_two, gain_two, shift_two = norm_back(
        finish_grad(grad_cross_q, proj_query), unit_two, inverse_two, norm_gain[1]
    )
    grad_after_one = grad_after_two + back_two
    grad_one = spread_grads(grad_after_one.astype(jnp.bfloat16))
    grad_back_self = jnp.einsum(
        "scw,scd->wd", context_one, grad_one, preferred_element_type=jnp.float32
    )
    grad_context_one = jnp.einsum(
        "scd,wd->scw", grad_one, back_self, preferred_element_type=jnp.float32
    ).astype(jnp.bfloat16)
    grad_ctx_four = grad_context_one.reshape(head_shape)
    delta_rows = jnp.sum(grad_ctx_four.astype(jnp.float32) * attended, -1)
    grad_query, grad_key_all, grad_value_all = key_sweep(
        queries_four,
        grad_ctx_four,
        log_total,
        delta_rows,
        keys_four,
        values_four,
        query_pos,
        prefix,
        key_span,
        factor,
    )
    own_keys, own_values = (
        lax.psum_scatter(grad_key_all, "ctx", scatter_dimension=0, tiled=True),
        lax.psum_scatter(grad_value_all, "ctx", scatter_dimension=0, tiled=True),
    )
    own_keys = jnp.transpose(own_keys, (1, 0, 2))
    own_values = jnp.transpose(own_values, (1, 0, 2))
    grad_joined = jnp.concatenate(
        [grad_query.reshape(batches, row_count, local_width), own_keys, own_values], -1
    ).astype(jnp.bfloat16)
    grad_proj_self = jnp.transpose(
        jnp.einsum(
            "scd,scw->dw", rows_self, grad_joined, preferred_element_type=jnp.float32
        ).reshape(model_width, 3, local_width),
        (1, 0, 2),
    )
    back_one, gain_one, shift_one = norm_back(
        finish_grad(grad_joined, local_stack), unit_one, inverse_one, norm_gain[0]
    )
    input_grad = grad_after_one + back_one
    shard_grads = (
        lax.psum_scatter(grad_proj_self, "fsdp", scatter_dimension=1, tiled=True),
        lax.psum_scatter(grad_query_proj, "fsdp", scatter_dimension=0, tiled=True),
        lax.psum_scatter(grad_pair, "fsdp", scatter_dimension=1, tiled=True),
        lax.psum_scatter(grad_back_self, "fsdp", scatter_dimension=1, tiled=True),
        lax.psum_scatter(grad_back_cross, "fsdp", scatter_dimension=1, tiled=True),
        lax.psum_scatter(grad_expand, "fsdp", scatter_dimension=0, tiled=True),
        lax.psum_scatter(grad_shrink, "fsdp", scatter_dimension=1, tiled=True),
    )
    full_grads = lax.psum(
        (
            shard_grads[0],
            shard_grads[1],
            shard_grads[2],
            shard_grads[3],
            shard_grads[4],
            shard_grads[5],
            shard_grads[6],
        ),
        "ctx",
    )
    squares = jnp.stack(
        [
            jnp.sum(final_sum * final_sum),
            jnp.sum(branch_one * branch_one),
            jnp.sum(branch_two * branch_two),
            jnp.sum(branch_three * branch_three),
        ]
    )
    gain_grad, bias_grad, square_totals = lax.psum(
        (
            jnp.stack([gain_one, gain_two, gain_three]),
            jnp.stack([shift_one, shift_two, shift_three]),
            squares,
        ),
        ("fsdp", "ctx", "tp"),
    )
    entries = (
        tokens.shape[0]
        * tokens.shape[1]
        * tokens.shape[2]
        * lax.axis_size("fsdp")
        * lax.axis_size("ctx")
        * lax.axis_size("tp")
    )
    norms = jnp.sqrt(square_totals / entries)
    return (
        final_sum,
        input_grad,
        encoder_grad,
        full_grads[0],
        full_grads[1],
        full_grads[2],
        full_grads[3],
        full_grads[4],
        full_grads[5],
        full_grads[6],
        gain_grad,
        bias_grad[:2],
        bias_grad[2],
        norms,
    )


def dot_of(left, right, left_dim, right_dim):
    return lax.dot_general(
        left, right, (((left_dim,), (right_dim,)), ((), ())), preferred_element_type=jnp.float32
    )


def bounds(prefix, start, query_span, key_span):
    whole = jnp.maximum(prefix, start + 1) // key_span
    every = (jnp.maximum(prefix, start + query_span) + key_span - 1) // key_span
    return whole, every


def hide(scores, limit, offset):
    return jnp.where(lax.broadcasted_iota(jnp.int32, scores.shape, 0) < limit - offset, scores, NEG)


def backward_kernel(scalars, qkv_ref, wide_ref, log_ref, *refs, span, chunk, group):
    grad_refs, refs = refs[:group], refs[group:]
    out_refs, refs = refs[:group], refs[group:]
    (
        queries_ref,
        keys_ref,
        values_ref,
        gradt_ref,
        grad_ref,
        delta_ref,
        grad_keys_ref,
        grad_values_ref,
        low_ref,
    ) = refs
    step = pl.program_id(0)
    prefix, me = scalars[0], scalars[1]
    factor = HEAD_DIM**-0.5
    length = qkv_ref.shape[1]

    @pl.when(step == 0)
    def prepare():
        for slot in range(group):
            here = pl.ds(pl.multiple_of((me ^ slot) * chunk, chunk), chunk)
            gradt_ref[:, here] = grad_refs[slot][...]
            grad_ref[here, :] = grad_refs[slot][...].T
        delta_ref[...] = jnp.sum(
            gradt_ref[...].astype(jnp.float32) * wide_ref[...], axis=0, keepdims=True
        )
        queries_ref[...] = qkv_ref[:HEAD_DIM, :].T
        keys_ref[...] = qkv_ref[HEAD_DIM : 2 * HEAD_DIM, :].T
        values_ref[...] = qkv_ref[2 * HEAD_DIM :, :].T
        grad_keys_ref[...] = jnp.zeros_like(grad_keys_ref)
        grad_values_ref[...] = jnp.zeros_like(grad_values_ref)

    start = pl.multiple_of(step * span, span)
    here = pl.ds(start, span)
    queries_t, queries = qkv_ref[:HEAD_DIM, here], queries_ref[here, :]
    grads_t, grads = gradt_ref[:, here], grad_ref[here, :]
    logs, deltas = log_ref[:, here], delta_ref[:, here]
    limit = jnp.maximum(prefix, start + 1 + lax.broadcasted_iota(jnp.int32, (1, span), 1))
    whole, every = bounds(prefix, start, span, span)

    def advance(block, grad_queries, masked):
        there = pl.ds(pl.multiple_of(block * span, span), span)
        scores = dot_of(keys_ref[there, :], queries_t, 1, 0)
        if masked:
            scores = hide(scores, limit, block * span)
        probs = jnp.exp(scores - logs)
        grad_probs = dot_of(values_ref[there, :], grads_t, 1, 0)
        grad_scores = (probs * (grad_probs - deltas)).astype(jnp.bfloat16)
        grad_values_ref[there, :] += dot_of(probs.astype(jnp.bfloat16), grads, 1, 0)
        grad_keys_ref[there, :] += dot_of(grad_scores, queries, 1, 0)
        return grad_queries + dot_of(
            qkv_ref[HEAD_DIM : 2 * HEAD_DIM, there], grad_scores, 1, 0
        )

    grad_queries = jnp.zeros((HEAD_DIM, span), jnp.float32)
    grad_queries = lax.fori_loop(0, whole, lambda j, c: advance(j, c, False), grad_queries)
    grad_queries = lax.fori_loop(whole, every, lambda j, c: advance(j, c, True), grad_queries)
    low = (grad_queries * factor).astype(jnp.bfloat16)
    for part in range(span // chunk):
        low_ref[(step * (span // chunk) + part) ^ me, :HEAD_DIM, :] = low[
            :, part * chunk : (part + 1) * chunk
        ]

    @pl.when(step == pl.num_programs(0) - 1)
    def finish():
        for place in range(length // chunk):
            rows = pl.ds(place * chunk, chunk)
            low_ref[place ^ me, HEAD_DIM : 2 * HEAD_DIM, :] = grad_keys_ref[rows, :].T.astype(
                jnp.bfloat16
            )
            low_ref[place ^ me, 2 * HEAD_DIM :, :] = grad_values_ref[rows, :].T.astype(jnp.bfloat16)
        for slot in range(group):
            out_refs[slot][...] = low_ref[slot]


def backward_attention(scalars, qkv, wide, logs, grads, span):
    group = len(grads)
    length = qkv.shape[1]
    chunk = grads[0].shape[1]
    whole = lambda *shape: pl.BlockSpec(shape, lambda i, s: (0,) * len(shape))
    bf16, f32 = jnp.bfloat16, jnp.float32
    return pl.pallas_call(
        functools.partial(backward_kernel, span=span, chunk=chunk, group=group),
        grid_spec=pltpu.PrefetchScalarGridSpec(
            num_scalar_prefetch=1,
            grid=(length // span,),
            in_specs=[whole(*qkv.shape), whole(*wide.shape), whole(*logs.shape)]
            + [whole(*g.shape) for g in grads],
            out_specs=[whole(3 * HEAD_DIM, chunk)] * group,
            scratch_shapes=[
                pltpu.VMEM((length, HEAD_DIM), bf16),
                pltpu.VMEM((length, HEAD_DIM), bf16),
                pltpu.VMEM((length, HEAD_DIM), bf16),
                pltpu.VMEM((HEAD_DIM, length), bf16),
                pltpu.VMEM((length, HEAD_DIM), bf16),
                pltpu.VMEM((1, length), f32),
                pltpu.VMEM((length, HEAD_DIM), f32),
                pltpu.VMEM((length, HEAD_DIM), f32),
                pltpu.VMEM((group, 3 * HEAD_DIM, chunk), bf16),
            ],
        ),
        out_shape=[jax.ShapeDtypeStruct((3 * HEAD_DIM, chunk), bf16)] * group,
        compiler_params=pltpu.CompilerParams(vmem_limit_bytes=VMEM_LIMIT),
        cost_estimate=pl.CostEstimate(
            flops=40_000_000_000, bytes_accessed=10_000_000, transcendentals=10_000_000
        ),
        name="attention_backward",
    )(scalars, qkv, wide, logs, *grads)


def swap_cores(value):
    return lax.ppermute(value, "ctx", [(0, 1), (1, 0)])


def trade(parts):
    group = len(parts)
    return [parts[0]] + [
        lax.ppermute(parts[k], ("ctx", "tp"), [(i, i ^ k) for i in range(group)])
        for k in range(1, group)
    ]


def norm_back_rows(upstream, unit_rows, inverse, scaling):
    scaled = upstream * scaling
    result = inverse * (
        scaled
        - jnp.mean(scaled, -1, keepdims=True)
        - unit_rows * jnp.mean(scaled * unit_rows, -1, keepdims=True)
    )
    return result, jnp.sum(upstream * unit_rows, 0), jnp.sum(upstream, 0)


def low(value):
    return value.astype(jnp.bfloat16)


def head_parts(value):
    return value.reshape(value.shape[0], -1, HEAD_DIM)


def rows_norm(hidden, scaling, offsets):
    centre = hidden - jnp.mean(hidden, -1, keepdims=True)
    inverse = lax.rsqrt(jnp.mean(centre * centre, -1, keepdims=True) + EPS)
    unit_rows = centre * inverse
    return low(unit_rows * scaling + offsets), unit_rows, inverse


def rows_back(upstream, unit_rows, inverse, scaling):
    scaled = upstream * scaling
    result = inverse * (
        scaled
        - jnp.mean(scaled, -1, keepdims=True)
        - unit_rows * jnp.mean(scaled * unit_rows, -1, keepdims=True)
    )
    return (
        result,
        jnp.sum(upstream * unit_rows, 0, keepdims=True),
        jnp.sum(upstream, 0, keepdims=True),
    )


MESH = pl.DeviceIdType.MESH


def meet(group, tp, fsdp):
    here, core, chip = lax.axis_index("fsdp"), lax.axis_index("ctx"), lax.axis_index("tp")
    me = core * tp + chip
    barrier = pltpu.get_barrier_semaphore()
    for k in range(1, group):
        other = me ^ k
        pl.semaphore_signal(
            barrier, inc=1, device_id={"ctx": other // tp, "tp": other % tp}, device_id_type=MESH
        )
    for k in range(1, fsdp):
        pl.semaphore_signal(barrier, inc=1, device_id={"fsdp": here ^ k}, device_id_type=MESH)
    pl.semaphore_wait(barrier, group - 1 + fsdp - 1)


def forward_kernel(
    prefix_ref,
    tokens_ref,
    step_ref,
    gain_ref,
    bias_ref,
    mine_ref,
    rows_out,
    qkv_ref,
    wide_ref,
    log_ref,
    ctx_ref,
    weight_ref,
    rows_ref,
    columns,
    weight,
    keys_ref,
    values_ref,
    low_ref,
    landing,
    w_send,
    w_recv,
    x_send,
    x_recv,
    c_send,
    c_recv,
    keep_sem,
    *,
    span,
    tp,
    fsdp,
):
    batches, chunk, width = tokens_ref.shape
    group = rows_ref.shape[1]
    length = group * chunk
    blocks, ratio = length // span, span // chunk
    wide_blocks = max(1, length // 2 // span)
    factor = HEAD_DIM**-0.5
    here, core, chip = lax.axis_index("fsdp"), lax.axis_index("ctx"), lax.axis_index("tp")
    me = core * tp + chip
    meet(group, tp, fsdp)

    def w_copy(k):
        return pltpu.make_async_remote_copy(
            src_ref=mine_ref,
            dst_ref=columns.at[k],
            send_sem=w_send.at[k],
            recv_sem=w_recv.at[k],
            device_id={"fsdp": here ^ k},
            device_id_type=MESH,
        )

    for k in range(1, fsdp):
        w_copy(k).start()

    def x_copy(seq, origin, kind):
        target = ({"tp": chip + 1}, {"tp": chip - 1}, {"ctx": 1 - core})[kind]
        block = rows_ref.at[seq, core * tp + origin]
        return pltpu.make_async_remote_copy(
            src_ref=block,
            dst_ref=block,
            send_sem=x_send.at[seq, origin, kind],
            recv_sem=x_recv.at[seq, core * tp + origin],
            device_id=target,
            device_id_type=MESH,
        )

    def x_wait(seq, place):
        pltpu.make_async_remote_copy(
            src_ref=rows_ref.at[seq, place],
            dst_ref=rows_ref.at[seq, place],
            send_sem=x_send.at[seq, 0, 0],
            recv_sem=x_recv.at[seq, place],
            device_id={"ctx": 1 - core},
            device_id_type=MESH,
        ).wait_recv()

    def own_sends(seq):
        @pl.when(chip < tp - 1)
        def upward():
            x_copy(seq, chip, 0).start()

        @pl.when(chip > 0)
        def downward():
            x_copy(seq, chip, 1).start()

        x_copy(seq, chip, 2).start()

    def normalise(seq):
        start_sum = tokens_ref[seq].astype(jnp.float32) + step_ref[seq]
        normed, unused, unused_too = rows_norm(start_sum, gain_ref[...], bias_ref[...])
        rows_ref[seq, me] = normed

    normalise(0)
    own_sends(0)
    normalise(1)
    values_ref[:, HEAD_DIM:, :] = jnp.ones_like(values_ref[:, HEAD_DIM:, :])
    piece = mine_ref.shape[1]
    for k in range(fsdp):
        if k:
            w_copy(k).wait_recv()
        part = columns[k] if k else mine_ref[...]
        for f in range(fsdp):

            @pl.when((here ^ k) == f)
            def place(f=f, part=part):
                weight[:, f * piece : (f + 1) * piece] = part

    weight_ref[...] = weight[...]

    def project(seq, place):
        rows = rows_ref[seq, place]
        joined = low(dot_of(weight[...], rows, 1, 1))
        at = pl.ds(pl.multiple_of(place * chunk, chunk), chunk)
        qkv_ref[seq, :HEAD_DIM, at] = joined[:HEAD_DIM] * jnp.bfloat16(factor)
        qkv_ref[seq, HEAD_DIM:, at] = joined[HEAD_DIM:]
        values_ref[seq, :HEAD_DIM, at] = joined[2 * HEAD_DIM :]
        keys_ref[seq, at, :] = low(dot_of(rows, weight[HEAD_DIM : 2 * HEAD_DIM, :], 1, 1))

    def stage(seq, hop):
        @pl.when(chip >= hop)
        def from_below():
            x_wait(seq, core * tp + chip - hop)

            @pl.when(chip < tp - 1)
            def onward():
                x_copy(seq, chip - hop, 0).start()

            x_copy(seq, chip - hop, 2).start()

        @pl.when(chip + hop < tp)
        def from_above():
            x_wait(seq, core * tp + chip + hop)

            @pl.when(chip > 0)
            def onward():
                x_copy(seq, chip + hop, 1).start()

            x_copy(seq, chip + hop, 2).start()

    def project_some(seq, first, count):
        def one(k, unused):
            project(seq, first + k)
            return unused

        lax.fori_loop(0, count, one, 0)

    def complete(seq):
        def one(k, unused):
            x_wait(seq, (1 - core) * tp + k)
            return unused

        project_some(seq, core * tp, tp)
        lax.fori_loop(0, tp, one, 0)
        project_some(seq, (1 - core) * tp, tp)

    for hop in range(1, tp):
        stage(0, hop)
        if hop == tp - 2:
            own_sends(1)
    complete(0)

    def c_copy(seq, place):
        return pltpu.make_async_remote_copy(
            src_ref=low_ref.at[seq, place],
            dst_ref=landing.at[seq, me],
            send_sem=c_send.at[seq, place],
            recv_sem=c_recv.at[seq, me],
            device_id={"ctx": place // tp, "tp": place % tp},
            device_id_type=MESH,
        )

    def c_wait(seq, place):
        pltpu.make_async_remote_copy(
            src_ref=low_ref.at[seq, place],
            dst_ref=landing.at[seq, place],
            send_sem=c_send.at[seq, place],
            recv_sem=c_recv.at[seq, place],
            device_id={"ctx": place // tp, "tp": place % tp},
            device_id_type=MESH,
        ).wait_recv()

    def attend(index, unused):
        seq, block = index // blocks, index % blocks

        @pl.when(index == blocks - 1)
        def pass_on():
            stage(1, 1)

        @pl.when(index == blocks)
        def receive():
            for hop in range(3, tp):
                stage(1, hop)
            complete(1)

        start = pl.multiple_of(block * span, span)
        queries = qkv_ref[seq, :HEAD_DIM, pl.ds(start, span)]
        limit = jnp.maximum(
            prefix_ref[seq], start + 1 + lax.broadcasted_iota(jnp.int32, (1, span), 1)
        )

        def advance(other, carry, masked):
            highest, total = carry
            offset = pl.multiple_of(other * span, span)
            scores = dot_of(keys_ref[seq, pl.ds(offset, span), :], queries, 1, 0)
            if masked:
                scores = hide(scores, limit, offset)
            higher = jnp.maximum(highest, jnp.max(scores, axis=0, keepdims=True))
            weights = low(jnp.exp(scores - higher))
            fading = jnp.exp(highest - higher)
            total = total * fading + dot_of(values_ref[seq, :, pl.ds(offset, span)], weights, 1, 0)
            return higher, total

        carry = (
            jnp.full((1, span), NEG, jnp.float32),
            jnp.zeros((values_ref.shape[1], span), jnp.float32),
        )
        carry = lax.fori_loop(0, block, lambda j, c: advance(j, c, False), carry)
        highest, total = lax.fori_loop(
            block, jnp.maximum(block + 1, wide_blocks), lambda j, c: advance(j, c, True), carry
        )
        weight_sum = total[HEAD_DIM : HEAD_DIM + 1, :]
        attended = total[:HEAD_DIM, :] / weight_sum
        wide_ref[seq, :, pl.ds(start, span)] = attended
        log_ref[seq, :, pl.ds(start, span)] = highest + jnp.log(weight_sum)
        attended = low(attended)
        for part in range(ratio):
            place = block * ratio + part
            low_ref[seq, place] = attended[:, part * chunk : (part + 1) * chunk]

            @pl.when(place != me)
            def send(place=place):
                c_copy(seq, place).start()

        @pl.when(index == blocks - 1)
        def pass_on_two():
            stage(1, 2)

        return unused

    lax.fori_loop(0, batches * blocks, attend, 0)
    keep = pltpu.make_async_copy(rows_ref, rows_out, keep_sem)
    keep.start()
    for seq in range(batches):

        def collect(k, unused, seq=seq):
            c_wait(seq, me ^ k)
            ctx_ref[seq, me ^ k] = landing[seq, me ^ k]
            return unused

        lax.fori_loop(1, group, collect, 0)
        ctx_ref[seq, me] = low_ref[seq, me]
    for k in range(1, fsdp):
        w_copy(k).wait_send()
    for seq in range(batches):
        for hop in range(tp):

            @pl.when(chip >= hop)
            def sent_up(seq=seq, hop=hop):
                @pl.when(chip < tp - 1)
                def onward():
                    x_copy(seq, chip - hop, 0).wait_send()

                x_copy(seq, chip - hop, 2).wait_send()

            @pl.when(chip + hop < tp)
            def sent_down(seq=seq, hop=hop):
                @pl.when(chip > 0)
                def onward():
                    x_copy(seq, chip + hop, 1).wait_send()

                if hop:
                    x_copy(seq, chip + hop, 2).wait_send()

        def sent(k, unused, seq=seq):
            c_copy(seq, me ^ k).wait_send()
            return unused

        lax.fori_loop(1, group, sent, 0)
    keep.wait()


def forward_group(prefix, tokens, steps, gain, bias, mine, span, group, tp, fsdp):
    batches, chunk, width = tokens.shape
    length = group * chunk
    bf16, f32 = jnp.bfloat16, jnp.float32
    struct = jax.ShapeDtypeStruct
    inside = pl.BlockSpec(memory_space=pltpu.VMEM)
    dma = pltpu.SemaphoreType.DMA
    return pl.pallas_call(
        functools.partial(forward_kernel, span=span, tp=tp, fsdp=fsdp),
        in_specs=[pl.BlockSpec(memory_space=pltpu.SMEM)] + [inside] * 5,
        out_specs=[pl.BlockSpec(memory_space=pl.ANY)] + [inside] * 5,
        out_shape=[
            struct((batches, group, chunk, width), bf16),
            struct((batches, 3 * HEAD_DIM, length), bf16),
            struct((batches, HEAD_DIM, length), f32),
            struct((batches, 1, length), f32),
            struct((batches, group, HEAD_DIM, chunk), bf16),
            struct((3 * HEAD_DIM, width), bf16),
        ],
        scratch_shapes=[
            pltpu.VMEM((batches, group, chunk, width), bf16),
            pltpu.VMEM((fsdp,) + mine.shape, bf16),
            pltpu.VMEM((3 * HEAD_DIM, width), bf16),
            pltpu.VMEM((batches, length, HEAD_DIM), bf16),
            pltpu.VMEM((batches, HEAD_DIM + 16, length), bf16),
            pltpu.VMEM((batches, group, HEAD_DIM, chunk), bf16),
            pltpu.VMEM((batches, group, HEAD_DIM, chunk), bf16),
            dma((fsdp,)),
            dma((fsdp,)),
            dma((batches, tp, 3)),
            dma((batches, group)),
            dma((batches, group)),
            dma((batches, group)),
            dma,
        ],
        compiler_params=pltpu.CompilerParams(
            vmem_limit_bytes=VMEM_LIMIT, collective_id=1, has_side_effects=True
        ),
        cost_estimate=pl.CostEstimate(
            flops=60_000_000_000, bytes_accessed=30_000_000, transcendentals=20_000_000
        ),
        name="forward_group",
    )(prefix, tokens, steps, gain, bias, mine)


QUERY, KEY, VALUE, SELF_OUT, CROSS_OUT, UP, DOWN = 0, 1, 2, 3, 4, 5, 9


def middle_kernel(
    scalars,
    gathered,
    tokens_ref,
    step_ref,
    enc_ref,
    cot_ref,
    gain_ref,
    bias_ref,
    ctx_ref,
    final_ref,
    after_ref,
    back_ref,
    enc_grad_ref,
    stats_ref,
    packed_ref,
    weights,
    totals,
    context,
    queries,
    keys,
    values,
    probs,
    context_two,
    grad_heads,
    grad_queries,
    grad_keys,
    grad_values,
    sem,
    *,
    tp,
    group,
):
    me = scalars[0]
    seq = pl.program_id(0)
    chunk, width = tokens_ref.shape[1:]
    piece = gathered.shape[-1]
    factor = HEAD_DIM**-0.5
    heads = width // HEAD_DIM

    @pl.when(seq == 0)
    def assemble():
        copies = []
        for f in range(width // piece):
            for c in range(group // tp):
                for t in range(tp):
                    head = t * (group // tp) + c
                    copies.append(
                        pltpu.make_async_copy(
                            gathered.at[f, c, t, pl.ds(3, weights.shape[0])],
                            weights.at[
                                :, pl.ds(head * HEAD_DIM, HEAD_DIM), pl.ds(f * piece, piece)
                            ],
                            sem.at[(f * group // tp + c) * tp + t],
                        )
                    )
        for copy in copies:
            copy.start()
        totals[...] = jnp.zeros_like(totals)
        stats_ref[...] = jnp.zeros_like(stats_ref)
        for copy in copies:
            copy.wait()

    for other in range(group):
        head = (other % tp) * (group // tp) + other // tp
        context[head * HEAD_DIM : (head + 1) * HEAD_DIM, :] = ctx_ref[0, other]
    start_sum = tokens_ref[0].astype(jnp.float32) + step_ref[0]
    branch_one = dot_of(context[...], weights[SELF_OUT], 0, 0)
    after_one = start_sum + branch_one
    stats_ref[1:2, :] += jnp.sum(branch_one * branch_one, 0, keepdims=True)
    normed_two, unit_two, inverse_two = rows_norm(after_one, gain_ref[1:2], bias_ref[1:2])
    queries[...] = low(dot_of(weights[QUERY], normed_two, 1, 1))
    keys[...] = low(dot_of(weights[KEY], enc_ref[0], 1, 1))
    values[...] = low(dot_of(weights[VALUE], enc_ref[0], 1, 1))

    def attend(head, unused):
        rows = pl.ds(pl.multiple_of(head * HEAD_DIM, HEAD_DIM), HEAD_DIM)
        scores = dot_of(keys[rows, :].T, queries[rows, :], 1, 0) * factor
        powers = jnp.exp(scores - jnp.max(scores, 0, keepdims=True))
        attn = powers / jnp.sum(powers, 0, keepdims=True)
        probs[head] = attn
        context_two[rows, :] = low(dot_of(values[rows, :], low(attn), 1, 0))
        return unused

    lax.fori_loop(0, heads, attend, 0, unroll=2)
    branch_two = dot_of(context_two[...], weights[CROSS_OUT], 0, 0)
    after_two = after_one + branch_two
    stats_ref[2:3, :] += jnp.sum(branch_two * branch_two, 0, keepdims=True)
    normed_three, unit_three, inverse_three = rows_norm(after_two, gain_ref[2:3], bias_ref[2:3])
    grad_three = cot_ref[0]

    def feed(part, carry):
        branch, grad = carry
        up, down = weights[UP + part], weights[DOWN + part]
        inputs = dot_of(up, normed_three, 1, 1)
        activated, slopes = gelu_parts(inputs)
        hidden = low(activated)
        branch = branch + dot_of(hidden, down, 0, 0)
        totals[DOWN - 2 + part] += dot_of(hidden, grad_three, 1, 0)
        grad_pre = low(dot_of(down, grad_three, 1, 1) * slopes)
        totals[UP - 2 + part] += dot_of(grad_pre, normed_three, 1, 0)
        return branch, grad + dot_of(grad_pre, up, 0, 0)

    blank = jnp.zeros((chunk, width), jnp.float32)
    branch_three, grad_norm = lax.fori_loop(0, DOWN - UP, feed, (blank, blank))
    final_sum = after_two + branch_three
    final_ref[0] = final_sum
    stats_ref[0:1, :] += jnp.sum(final_sum * final_sum, 0, keepdims=True)
    stats_ref[3:4, :] += jnp.sum(branch_three * branch_three, 0, keepdims=True)
    back, gain_sum, bias_sum = rows_back(grad_norm, unit_three, inverse_three, gain_ref[2:3])
    stats_ref[6:7, :] += gain_sum
    stats_ref[7:8, :] += bias_sum
    grad_after_two = grad_three.astype(jnp.float32) + back
    grad_two = low(grad_after_two)
    totals[2] += dot_of(context_two[...], grad_two, 1, 0)
    grad_heads[...] = low(dot_of(weights[CROSS_OUT], grad_two, 1, 1))

    def attend_back(head, unused):
        rows = pl.ds(pl.multiple_of(head * HEAD_DIM, HEAD_DIM), HEAD_DIM)
        grads = grad_heads[rows, :]
        attn = probs[head]
        grad_probs = dot_of(values[rows, :].T, grads, 1, 0)
        grad_scores = low(
            attn * (grad_probs - jnp.sum(attn * grad_probs, 0, keepdims=True))
        )
        grad_queries[rows, :] = low(dot_of(keys[rows, :], grad_scores, 1, 0) * factor)
        grad_keys[rows, :] = dot_of(queries[rows, :], grad_scores, 1, 1) * factor
        grad_values[rows, :] = dot_of(grads, low(attn), 1, 1)
        return unused

    lax.fori_loop(0, heads, attend_back, 0, unroll=2)
    enc_grad_ref[0, :, :width] = low(grad_keys[...].T)
    enc_grad_ref[0, :, width:] = low(grad_values[...].T)
    totals[0] += dot_of(grad_queries[...], normed_two, 1, 0)
    upstream = dot_of(grad_queries[...], weights[QUERY], 0, 0)
    back, gain_sum, bias_sum = rows_back(upstream, unit_two, inverse_two, gain_ref[1:2])
    stats_ref[4:5, :] += gain_sum
    stats_ref[5:6, :] += bias_sum
    grad_after_one = grad_after_two + back
    after_ref[0] = grad_after_one
    grad_one = low(grad_after_one)
    totals[1] += dot_of(context[...], grad_one, 1, 0)
    context[...] = low(dot_of(weights[SELF_OUT], grad_one, 1, 1))
    for slot in range(group):
        other = me ^ slot
        head = (other % tp) * (group // tp) + other // tp
        back_ref[0, slot] = context[
            pl.ds(pl.multiple_of(head * HEAD_DIM, HEAD_DIM), HEAD_DIM), :
        ]

    @pl.when(seq == pl.num_programs(0) - 1)
    def pack():
        for f in range(width // piece):
            for c in range(group // tp):
                for t in range(tp):
                    head = t * (group // tp) + c
                    packed_ref[f, c, t] = low(
                        totals[
                            :,
                            head * HEAD_DIM : (head + 1) * HEAD_DIM,
                            f * piece : (f + 1) * piece,
                        ]
                    )


def middle(scalars, gathered, tokens, steps, encoder, cotangent, gains, biases, contexts, tp):
    batches, chunk, width = tokens.shape
    group = contexts.shape[1]
    enc_count = encoder.shape[1]
    heads = width // HEAD_DIM
    bf16, f32 = jnp.bfloat16, jnp.float32
    struct = jax.ShapeDtypeStruct
    each = lambda *shape: pl.BlockSpec((1,) + shape, lambda i, s: (i,) + (0,) * len(shape))
    once = lambda *shape: pl.BlockSpec(
        shape, lambda i, s: (0,) * len(shape), pipeline_mode=pl.Buffered(1)
    )
    count = gathered.shape[3] - 3
    packed = gathered.shape[:3] + (count - 2,) + gathered.shape[4:]
    return pl.pallas_call(
        functools.partial(middle_kernel, tp=tp, group=group),
        grid_spec=pltpu.PrefetchScalarGridSpec(
            num_scalar_prefetch=1,
            grid=(batches,),
            in_specs=[
                pl.BlockSpec(memory_space=pl.ANY),
                each(chunk, width),
                each(1, width),
                each(enc_count, width),
                each(chunk, width),
                once(3, width),
                once(3, width),
                each(group, HEAD_DIM, chunk),
            ],
            out_specs=[
                each(chunk, width),
                each(chunk, width),
                each(group, HEAD_DIM, chunk),
                each(enc_count, 2 * width),
                once(8, width),
                once(*packed),
            ],
            scratch_shapes=[
                pltpu.VMEM((count, width, width), bf16),
                pltpu.VMEM((count - 2, width, width), f32),
                pltpu.VMEM((width, chunk), bf16),
                pltpu.VMEM((width, chunk), bf16),
                pltpu.VMEM((width, enc_count), bf16),
                pltpu.VMEM((width, enc_count), bf16),
                pltpu.VMEM((heads, enc_count, chunk), f32),
                pltpu.VMEM((width, chunk), bf16),
                pltpu.VMEM((width, chunk), bf16),
                pltpu.VMEM((width, chunk), bf16),
                pltpu.VMEM((width, enc_count), f32),
                pltpu.VMEM((width, enc_count), f32),
                pltpu.SemaphoreType.DMA((32,)),
            ],
        ),
        out_shape=[
            struct((batches, chunk, width), f32),
            struct((batches, chunk, width), f32),
            struct((batches, group, HEAD_DIM, chunk), bf16),
            struct((batches, enc_count, 2 * width), bf16),
            struct((8, width), f32),
            struct(packed, bf16),
        ],
        compiler_params=pltpu.CompilerParams(vmem_limit_bytes=VMEM_LIMIT),
        cost_estimate=pl.CostEstimate(
            flops=30_000_000_000, bytes_accessed=30_000_000, transcendentals=10_000_000
        ),
        name="middle",
    )(scalars, gathered, tokens, steps, encoder, cotangent, gains, biases, contexts)


def local_heads(
    tokens,
    timesteps,
    time_table,
    prefix,
    encoder,
    self_qkv,
    cross_q,
    cross_kv,
    self_out,
    cross_out,
    ffn_up,
    ffn_down,
    norm_gain,
    norm_bias,
    cotangent,
):
    batches, chunk, width = tokens.shape
    group = 8
    length = group * chunk
    enc_count = encoder.shape[1]
    factor = HEAD_DIM ** (-0.5)
    ctx_index, tp_index = lax.axis_index("ctx"), lax.axis_index("tp")
    me = ctx_index * 4 + tp_index
    span = 1024
    piece = width // 4
    flip = lambda w: jnp.swapaxes(w, -1, -2)
    blocks = jnp.concatenate(
        [
            flip(self_qkv),
            flip(cross_q)[None],
            flip(cross_kv),
            self_out[None],
            cross_out[None],
            flip(ffn_up).reshape(4, piece, piece),
            ffn_down.reshape(4, piece, piece),
        ]
    )
    count = blocks.shape[0]
    half = piece // 2
    own_half = lax.dynamic_slice_in_dim(blocks, ctx_index * half, half, 1)
    gathered = lax.all_gather(own_half, ("fsdp", "ctx", "tp"), axis=0, tiled=False)
    gathered = gathered.reshape(4, 2, 4, count, half, piece)
    mine = own_half[:3].reshape(3 * HEAD_DIM, piece)
    fsdp_index = lax.axis_index("fsdp")
    steps_onehot = (timesteps[:, None] == lax.iota(jnp.int32, time_table.shape[0])[None, :]).astype(
        jnp.bfloat16
    )
    embedded = jnp.dot(steps_onehot, time_table, preferred_element_type=jnp.float32)[:, None, :]
    rows, qkv, wide, logs, contexts, head_weight = forward_group(
        prefix, tokens, embedded, norm_gain[:1], norm_bias[:1], mine, span, group, 4, 4
    )
    final, grad_after, returned, enc_parts, stats, packed = middle(
        me[None].astype(jnp.int32),
        gathered,
        tokens,
        embedded,
        encoder,
        cotangent,
        norm_gain,
        norm_bias,
        contexts,
        4,
    )
    returns = [trade([returned[s, k] for k in range(group)]) for s in range(batches)]
    whole_block = lambda b: jnp.transpose(gathered[:, :, :, b], (2, 1, 3, 0, 4)).reshape(
        width, width
    )
    full_k, full_v = whole_block(4), whole_block(5)
    qkv_heads = jnp.transpose(gathered[:, :, :, :3], (1, 2, 3, 4, 0, 5)).reshape(
        group, 3 * HEAD_DIM, width
    )
    qkv_slots = jnp.concatenate(
        [lax.dynamic_index_in_dim(qkv_heads, me ^ k, 0, False) for k in range(group)]
    )
    share = enc_count // group
    parts = enc_parts.reshape(batches, group, share, 2 * width)
    parts = [lax.dynamic_index_in_dim(parts, me ^ k, 1, False) for k in range(group)]
    enc_grads = low(sum(p.astype(jnp.float32) for p in trade(parts)))
    enc_rows = lax.dynamic_slice_in_dim(encoder, me * share, share, 1)
    enc_rows = enc_rows.reshape(batches * share, width)
    enc_flat = enc_grads.reshape(batches * share, 2 * width)
    encoder_grad = (
        dot_of(enc_flat[:, :width], full_k, 1, 0) + dot_of(enc_flat[:, width:], full_v, 1, 0)
    ).reshape(batches, share, width)
    grad_pair = dot_of(enc_flat, enc_rows, 0, 0)
    grads_back, head_grads = [], 0.0
    for s in range(batches):
        scalars = jnp.stack([prefix[s], me]).astype(jnp.int32)
        outs = backward_attention(scalars, qkv[s], wide[s], logs[s], returns[s], span)
        grads_back.append(trade(outs))
        for k in range(group):
            own_rows = lax.dynamic_index_in_dim(rows[s], me ^ k, 0, False)
            head_grads = head_grads + dot_of(outs[k], own_rows, 1, 0)
    pair = low(grad_pair).reshape(2, 4, 2, half, 4, piece)
    packed = jnp.concatenate([packed, jnp.transpose(pair, (4, 2, 1, 0, 3, 5))], 3)
    scattered = lax.psum_scatter(
        packed.reshape((32,) + packed.shape[3:]),
        ("fsdp", "ctx", "tp"),
        scatter_dimension=0,
        tiled=False,
    ).astype(jnp.float32)
    other_half = swap_cores(scattered)
    shards = jnp.concatenate(
        [
            jnp.where(ctx_index == 0, scattered, other_half),
            jnp.where(ctx_index == 0, other_half, scattered),
        ],
        1,
    )
    head_grads = head_grads.reshape(3 * HEAD_DIM, 4, piece)
    pieces = [lax.dynamic_index_in_dim(head_grads, fsdp_index ^ k, 1, False) for k in range(4)]
    head_shard = pieces[0] + sum(
        lax.ppermute(pieces[k], "fsdp", [(i, i ^ k) for i in range(4)]) for k in range(1, 4)
    )
    head_shard = jnp.transpose(head_shard.reshape(3, HEAD_DIM, piece), (0, 2, 1))
    other_shard = swap_cores(head_shard)
    grad_self = jnp.concatenate(
        [
            jnp.where(ctx_index == 0, head_shard, other_shard),
            jnp.where(ctx_index == 0, other_shard, head_shard),
        ],
        2,
    )
    input_grads, gains_one, shifts_one = [], 0.0, 0.0
    for s in range(batches):
        upstream = dot_of(jnp.concatenate(grads_back[s]), qkv_slots, 0, 0)
        start_sum = tokens[s].astype(jnp.float32) + embedded[s]
        unused, unit, inverse = norm_rows(start_sum, norm_gain[0], norm_bias[0])
        back, gain, shift = norm_back_rows(upstream, unit, inverse, norm_gain[0])
        input_grads.append(grad_after[s] + back)
        gains_one, shifts_one = gains_one + gain, shifts_one + shift
    gain_grad, bias_grad, square_totals = lax.psum(
        (
            jnp.stack([gains_one, stats[4], stats[6]]),
            jnp.stack([shifts_one, stats[5], stats[7]]),
            jnp.sum(stats[:4], -1),
        ),
        ("fsdp", "ctx", "tp"),
    )
    entries = (
        tokens.shape[0]
        * tokens.shape[1]
        * tokens.shape[2]
        * lax.axis_size("fsdp")
        * lax.axis_size("ctx")
        * lax.axis_size("tp")
    )
    return (
        final,
        jnp.stack(input_grads),
        encoder_grad,
        grad_self,
        shards[0].T,
        flip(shards[11:13]),
        shards[1],
        shards[2],
        shards[3:7].reshape(width, piece).T,
        shards[7:11].reshape(width, piece),
        gain_grad,
        bias_grad[:2],
        bias_grad[2],
        jnp.sqrt(square_totals / entries),
    )


def solution(mesh):
    placed = (
        P("fsdp", ("ctx", "tp"), None),
        P("fsdp"),
        P(),
        P("fsdp"),
        P("fsdp", None, None),
        P(None, "fsdp", "tp"),
        P("fsdp", "tp"),
        P(None, "fsdp", "tp"),
        P("tp", "fsdp"),
        P("tp", "fsdp"),
        P("fsdp", "tp"),
        P("tp", "fsdp"),
        P(),
        P(),
        P("fsdp", ("ctx", "tp"), None),
    )
    heads_fit = dict(mesh.shape) == {"fsdp": 4, "ctx": 2, "tp": 4}
    return jax.shard_map(
        local_heads if heads_fit else local,
        mesh=mesh,
        in_specs=placed,
        out_specs=(
            P("fsdp", ("ctx", "tp"), None),
            P("fsdp", ("ctx", "tp"), None),
            P("fsdp", ("ctx", "tp"), None),
            P(None, "fsdp", "tp"),
            P("fsdp", "tp"),
            P(None, "fsdp", "tp"),
            P("tp", "fsdp"),
            P("tp", "fsdp"),
            P("fsdp", "tp"),
            P("tp", "fsdp"),
            P(),
            P(),
            P(),
            P(),
        ),
        check_vma=False,
    )
```

```python
import functools
import math

import jax
import jax.numpy as jnp
from jax import lax
from jax.experimental import pallas as pl
from jax.experimental.pallas import tpu as pltpu
from jax.sharding import PartitionSpec as P

HEAD_DIM = 64


EPS = 1e-05
NEG = -1e30
ROOT_HALF = 1.0 / math.sqrt(2.0)
INV_ROOT_TWO_PI = 1.0 / math.sqrt(2.0 * math.pi)
VMEM_LIMIT = 60 * 2**20


def norm_rows(hidden, scaling, offsets):
    centre = hidden - jnp.mean(hidden, -1, keepdims=True)
    inverse = lax.rsqrt(jnp.mean(centre * centre, -1, keepdims=True) + EPS)
    unit_rows = centre * inverse
    return (unit_rows * scaling + offsets, unit_rows, inverse)


def norm_back(upstream, unit_rows, inverse, scaling):
    scaled = upstream * scaling
    result = inverse * (
        scaled
        - jnp.mean(scaled, -1, keepdims=True)
        - unit_rows * jnp.mean(scaled * unit_rows, -1, keepdims=True)
    )
    return (result, jnp.sum(upstream * unit_rows, (0, 1)), jnp.sum(upstream, (0, 1)))


def gelu_parts(inputs):
    normal_cdf = 0.5 * (1.0 + lax.erf(inputs * ROOT_HALF))
    return (
        inputs * normal_cdf,
        normal_cdf + inputs * jnp.exp(-0.5 * inputs * inputs) * INV_ROOT_TWO_PI,
    )


def spread_rows(rows):
    return lax.all_gather(rows, "tp", axis=1, tiled=True)


def spread_grads(grad_rows):
    return lax.all_gather(grad_rows, "tp", axis=1, tiled=True)


def finish_branch(local_in, local_weight):
    return lax.psum_scatter(
        jnp.einsum("scw,wd->scd", local_in, local_weight, preferred_element_type=jnp.float32),
        "tp",
        scatter_dimension=1,
        tiled=True,
    )


def finish_grad(local_grad, local_weight):
    return lax.psum_scatter(
        jnp.einsum("scw,dw->scd", local_grad, local_weight, preferred_element_type=jnp.float32),
        "tp",
        scatter_dimension=1,
        tiled=True,
    )


def block_scores(queries, key_block, query_pos, key_pos, lengths, factor):
    scores = (
        jnp.einsum("sqhe,skhe->sqhk", queries, key_block, preferred_element_type=jnp.float32)
        * factor
    )
    visible = (key_pos[None, None, :] <= query_pos[None, :, None]) | (
        key_pos[None, None, :] < lengths[:, None, None]
    )
    return jnp.where(visible[:, :, None, :], scores, NEG)


def attend_forward(queries, key_rows, value_rows, query_pos, lengths, key_span, factor):
    length = key_rows.shape[1]

    def attend_advance(running, offset):
        highest, totals, summed = running
        key_block = lax.dynamic_slice_in_dim(key_rows, offset, key_span, 1)
        value_block = lax.dynamic_slice_in_dim(value_rows, offset, key_span, 1)
        scores = block_scores(
            queries, key_block, query_pos, offset + lax.iota(jnp.int32, key_span), lengths, factor
        )
        new_high = jnp.maximum(highest, jnp.max(scores, -1))
        weights = jnp.exp(scores - new_high[..., None])
        fading = jnp.exp(highest - new_high)
        totals = totals * fading + jnp.sum(weights, -1)
        summed = summed * fading[..., None] + jnp.einsum(
            "sqhk,skhe->sqhe",
            weights.astype(jnp.bfloat16),
            value_block,
            preferred_element_type=jnp.float32,
        )
        return ((new_high, totals, summed), None)

    stat_shape = queries.shape[:3]
    initial = (
        jnp.full(stat_shape, NEG, jnp.float32),
        jnp.zeros(stat_shape, jnp.float32),
        jnp.zeros(queries.shape, jnp.float32),
    )
    offsets = jnp.arange(length // key_span, dtype=jnp.int32) * key_span
    (highest, totals, summed), unused = lax.scan(attend_advance, initial, offsets)
    return (summed / totals[..., None], highest + jnp.log(totals))


def attend_block(
    queries,
    grad_out,
    log_rows,
    delta_rows,
    key_block,
    value_block,
    query_pos,
    key_pos,
    lengths,
    factor,
):
    scores = block_scores(queries, key_block, query_pos, key_pos, lengths, factor)
    probs = jnp.exp(scores - log_rows[..., None])
    grad_probs = jnp.einsum(
        "sqhe,skhe->sqhk", grad_out, value_block, preferred_element_type=jnp.float32
    )
    grad_scores = (probs * (grad_probs - delta_rows[..., None])).astype(jnp.bfloat16)
    return (probs.astype(jnp.bfloat16), grad_scores)


def key_sweep(
    queries,
    grad_out,
    log_rows,
    delta_rows,
    key_rows,
    value_rows,
    query_pos,
    lengths,
    key_span,
    factor,
):
    batches, row_count, head_count, head_depth = queries.shape
    length = key_rows.shape[1]

    def key_advance(grad_query, offset):
        key_block = lax.dynamic_slice_in_dim(key_rows, offset, key_span, 1)
        value_block = lax.dynamic_slice_in_dim(value_rows, offset, key_span, 1)
        key_pos = offset + lax.iota(jnp.int32, key_span)
        probs_low, grad_scores = attend_block(
            queries,
            grad_out,
            log_rows,
            delta_rows,
            key_block,
            value_block,
            query_pos,
            key_pos,
            lengths,
            factor,
        )
        grad_query = (
            grad_query
            + jnp.einsum(
                "sqhk,skhe->sqhe", grad_scores, key_block, preferred_element_type=jnp.float32
            )
            * factor
        )
        grad_key = (
            jnp.einsum("sqhk,sqhe->kshe", grad_scores, queries, preferred_element_type=jnp.float32)
            * factor
        )
        grad_value = jnp.einsum(
            "sqhk,sqhe->kshe", probs_low, grad_out, preferred_element_type=jnp.float32
        )
        return (grad_query, (grad_key, grad_value))

    offsets = jnp.arange(length // key_span, dtype=jnp.int32) * key_span
    grad_query, stacked = lax.scan(key_advance, jnp.zeros(queries.shape, jnp.float32), offsets)
    flat_shape = (length, batches, head_count * head_depth)
    return (grad_query, stacked[0].reshape(flat_shape), stacked[1].reshape(flat_shape))


def local(
    tokens,
    timesteps,
    time_table,
    prefix,
    encoder,
    self_qkv,
    cross_q,
    cross_kv,
    self_out,
    cross_out,
    ffn_up,
    ffn_down,
    norm_gain,
    norm_bias,
    cotangent,
):
    proj_self, proj_query, proj_pair, back_self, back_cross, expand_full, shrink_full = (
        lax.all_gather(self_qkv, "fsdp", axis=1, tiled=True),
        lax.all_gather(cross_q, "fsdp", axis=0, tiled=True),
        lax.all_gather(cross_kv, "fsdp", axis=1, tiled=True),
        lax.all_gather(self_out, "fsdp", axis=1, tiled=True),
        lax.all_gather(cross_out, "fsdp", axis=1, tiled=True),
        lax.all_gather(ffn_up, "fsdp", axis=0, tiled=True),
        lax.all_gather(ffn_down, "fsdp", axis=1, tiled=True),
    )
    batches = tokens.shape[0]
    model_width = tokens.shape[2]
    local_width = proj_query.shape[1]
    head_count = local_width // HEAD_DIM
    factor = HEAD_DIM ** (-0.5)
    ctx_index = lax.axis_index("ctx")
    local_stack = jnp.transpose(proj_self, (1, 0, 2)).reshape(model_width, 3 * local_width)
    steps_onehot = (timesteps[:, None] == lax.iota(jnp.int32, time_table.shape[0])[None, :]).astype(
        jnp.bfloat16
    )
    embedded = jnp.dot(steps_onehot, time_table, preferred_element_type=jnp.float32)
    start_sum = tokens.astype(jnp.float32) + embedded[:, None, :]
    normed_one, unit_one, inverse_one = norm_rows(start_sum, norm_gain[0], norm_bias[0])
    rows_self = spread_rows(normed_one.astype(jnp.bfloat16))
    row_count = rows_self.shape[1]
    head_shape = (batches, row_count, head_count, HEAD_DIM)
    projected = jnp.einsum(
        "scd,kdw->kscw", rows_self, proj_self, preferred_element_type=jnp.float32
    ).astype(jnp.bfloat16)
    queries, key_local, value_local = (projected[0], projected[1], projected[2])
    key_all, value_all = (
        lax.all_gather(key_local, "ctx", axis=1, tiled=True),
        lax.all_gather(value_local, "ctx", axis=1, tiled=True),
    )
    length = key_all.shape[1]
    key_span = min(512, length)
    query_pos = ctx_index * row_count + lax.iota(jnp.int32, row_count)
    keys_four = key_all.reshape(batches, length, head_count, HEAD_DIM)
    values_four = value_all.reshape(batches, length, head_count, HEAD_DIM)
    queries_four = queries.reshape(head_shape)
    attended, log_total = attend_forward(
        queries_four, keys_four, values_four, query_pos, prefix, key_span, factor
    )
    context_one = attended.reshape(batches, row_count, local_width).astype(jnp.bfloat16)
    branch_one = finish_branch(context_one, back_self)
    after_one = start_sum + branch_one
    normed_two, unit_two, inverse_two = norm_rows(after_one, norm_gain[1], norm_bias[1])
    rows_cross = spread_rows(normed_two.astype(jnp.bfloat16))
    cross_queries = jnp.einsum(
        "scd,dw->scw", rows_cross, proj_query, preferred_element_type=jnp.float32
    ).astype(jnp.bfloat16)
    enc_pair = jnp.einsum(
        "sed,kdw->ksew", encoder, proj_pair, preferred_element_type=jnp.float32
    ).astype(jnp.bfloat16)
    enc_count = encoder.shape[1]
    cross_keys = enc_pair[0].reshape(batches, enc_count, head_count, HEAD_DIM)
    cross_values = enc_pair[1].reshape(batches, enc_count, head_count, HEAD_DIM)
    cross_four = cross_queries.reshape(head_shape)
    cross_probs = jax.nn.softmax(
        jnp.einsum("sqhe,skhe->sqhk", cross_four, cross_keys, preferred_element_type=jnp.float32)
        * factor,
        axis=-1,
    )
    cross_low = cross_probs.astype(jnp.bfloat16)
    context_two = (
        jnp.einsum("sqhk,skhe->sqhe", cross_low, cross_values, preferred_element_type=jnp.float32)
        .reshape(batches, row_count, local_width)
        .astype(jnp.bfloat16)
    )
    branch_two = finish_branch(context_two, back_cross)
    after_two = after_one + branch_two
    normed_three, unit_three, inverse_three = norm_rows(after_two, norm_gain[2], norm_bias[2])
    rows_ffn = spread_rows(normed_three.astype(jnp.bfloat16))
    pre_act = jnp.einsum("scd,df->scf", rows_ffn, expand_full, preferred_element_type=jnp.float32)
    activated, slopes = gelu_parts(pre_act)
    hidden_low = activated.astype(jnp.bfloat16)
    branch_three = finish_branch(hidden_low, shrink_full)
    final_sum = after_two + branch_three
    grad_three = spread_grads(cotangent)
    grad_shrink = jnp.einsum(
        "scf,scd->fd", hidden_low, grad_three, preferred_element_type=jnp.float32
    )
    grad_pre = (
        jnp.einsum("scd,fd->scf", grad_three, shrink_full, preferred_element_type=jnp.float32)
        * slopes
    ).astype(jnp.bfloat16)
    grad_expand = jnp.einsum("scd,scf->df", rows_ffn, grad_pre, preferred_element_type=jnp.float32)
    back_three, gain_three, shift_three = norm_back(
        finish_grad(grad_pre, expand_full), unit_three, inverse_three, norm_gain[2]
    )
    grad_after_two = cotangent.astype(jnp.float32) + back_three
    grad_two = spread_grads(grad_after_two.astype(jnp.bfloat16))
    grad_back_cross = jnp.einsum(
        "scw,scd->wd", context_two, grad_two, preferred_element_type=jnp.float32
    )
    grad_context_two = jnp.einsum(
        "scd,wd->scw", grad_two, back_cross, preferred_element_type=jnp.float32
    ).astype(jnp.bfloat16)
    grad_cross_four = grad_context_two.reshape(head_shape)
    grad_cross_probs = jnp.einsum(
        "sqhe,skhe->sqhk", grad_cross_four, cross_values, preferred_element_type=jnp.float32
    )
    grad_cross_scores = (
        cross_probs
        * (grad_cross_probs - jnp.sum(cross_probs * grad_cross_probs, -1, keepdims=True))
    ).astype(jnp.bfloat16)
    grad_cross_q = (
        (
            jnp.einsum(
                "sqhk,skhe->sqhe", grad_cross_scores, cross_keys, preferred_element_type=jnp.float32
            )
            * factor
        )
        .reshape(batches, row_count, local_width)
        .astype(jnp.bfloat16)
    )
    part_keys = (
        jnp.einsum(
            "sqhk,sqhe->skhe", grad_cross_scores, cross_four, preferred_element_type=jnp.float32
        )
        * factor
    ).reshape(batches, enc_count, local_width)
    part_values = jnp.einsum(
        "sqhk,sqhe->skhe", cross_low, grad_cross_four, preferred_element_type=jnp.float32
    ).reshape(batches, enc_count, local_width)
    enc_keys, enc_values = (
        lax.psum_scatter(part_keys, "ctx", scatter_dimension=1, tiled=True),
        lax.psum_scatter(part_values, "ctx", scatter_dimension=1, tiled=True),
    )
    enc_keys = enc_keys.astype(jnp.bfloat16)
    enc_values = enc_values.astype(jnp.bfloat16)
    enc_share = enc_keys.shape[1]
    enc_rows = lax.dynamic_slice_in_dim(encoder, ctx_index * enc_share, enc_share, 1)
    grad_pair = jnp.stack(
        [
            jnp.einsum("sed,sew->dw", enc_rows, enc_keys, preferred_element_type=jnp.float32),
            jnp.einsum("sed,sew->dw", enc_rows, enc_values, preferred_element_type=jnp.float32),
        ]
    )
    encoder_grad = lax.psum_scatter(
        jnp.einsum("sew,dw->sed", enc_keys, proj_pair[0], preferred_element_type=jnp.float32)
        + jnp.einsum("sew,dw->sed", enc_values, proj_pair[1], preferred_element_type=jnp.float32),
        "tp",
        scatter_dimension=1,
        tiled=True,
    )
    grad_query_proj = jnp.einsum(
        "scd,scw->dw", rows_cross, grad_cross_q, preferred_element_type=jnp.float32
    )
    back_two, gain_two, shift_two = norm_back(
        finish_grad(grad_cross_q, proj_query), unit_two, inverse_two, norm_gain[1]
    )
    grad_after_one = grad_after_two + back_two
    grad_one = spread_grads(grad_after_one.astype(jnp.bfloat16))
    grad_back_self = jnp.einsum(
        "scw,scd->wd", context_one, grad_one, preferred_element_type=jnp.float32
    )
    grad_context_one = jnp.einsum(
        "scd,wd->scw", grad_one, back_self, preferred_element_type=jnp.float32
    ).astype(jnp.bfloat16)
    grad_ctx_four = grad_context_one.reshape(head_shape)
    delta_rows = jnp.sum(grad_ctx_four.astype(jnp.float32) * attended, -1)
    grad_query, grad_key_all, grad_value_all = key_sweep(
        queries_four,
        grad_ctx_four,
        log_total,
        delta_rows,
        keys_four,
        values_four,
        query_pos,
        prefix,
        key_span,
        factor,
    )
    own_keys, own_values = (
        lax.psum_scatter(grad_key_all, "ctx", scatter_dimension=0, tiled=True),
        lax.psum_scatter(grad_value_all, "ctx", scatter_dimension=0, tiled=True),
    )
    own_keys = jnp.transpose(own_keys, (1, 0, 2))
    own_values = jnp.transpose(own_values, (1, 0, 2))
    grad_joined = jnp.concatenate(
        [grad_query.reshape(batches, row_count, local_width), own_keys, own_values], -1
    ).astype(jnp.bfloat16)
    grad_proj_self = jnp.transpose(
        jnp.einsum(
            "scd,scw->dw", rows_self, grad_joined, preferred_element_type=jnp.float32
        ).reshape(model_width, 3, local_width),
        (1, 0, 2),
    )
    back_one, gain_one, shift_one = norm_back(
        finish_grad(grad_joined, local_stack), unit_one, inverse_one, norm_gain[0]
    )
    input_grad = grad_after_one + back_one
    shard_grads = (
        lax.psum_scatter(grad_proj_self, "fsdp", scatter_dimension=1, tiled=True),
        lax.psum_scatter(grad_query_proj, "fsdp", scatter_dimension=0, tiled=True),
        lax.psum_scatter(grad_pair, "fsdp", scatter_dimension=1, tiled=True),
        lax.psum_scatter(grad_back_self, "fsdp", scatter_dimension=1, tiled=True),
        lax.psum_scatter(grad_back_cross, "fsdp", scatter_dimension=1, tiled=True),
        lax.psum_scatter(grad_expand, "fsdp", scatter_dimension=0, tiled=True),
        lax.psum_scatter(grad_shrink, "fsdp", scatter_dimension=1, tiled=True),
    )
    full_grads = lax.psum(
        (
            shard_grads[0],
            shard_grads[1],
            shard_grads[2],
            shard_grads[3],
            shard_grads[4],
            shard_grads[5],
            shard_grads[6],
        ),
        "ctx",
    )
    squares = jnp.stack(
        [
            jnp.sum(final_sum * final_sum),
            jnp.sum(branch_one * branch_one),
            jnp.sum(branch_two * branch_two),
            jnp.sum(branch_three * branch_three),
        ]
    )
    gain_grad, bias_grad, square_totals = lax.psum(
        (
            jnp.stack([gain_one, gain_two, gain_three]),
            jnp.stack([shift_one, shift_two, shift_three]),
            squares,
        ),
        ("fsdp", "ctx", "tp"),
    )
    entries = (
        tokens.shape[0]
        * tokens.shape[1]
        * tokens.shape[2]
        * lax.axis_size("fsdp")
        * lax.axis_size("ctx")
        * lax.axis_size("tp")
    )
    norms = jnp.sqrt(square_totals / entries)
    return (
        final_sum,
        input_grad,
        encoder_grad,
        full_grads[0],
        full_grads[1],
        full_grads[2],
        full_grads[3],
        full_grads[4],
        full_grads[5],
        full_grads[6],
        gain_grad,
        bias_grad[:2],
        bias_grad[2],
        norms,
    )


def dot_of(left, right, left_dim, right_dim):
    return lax.dot_general(
        left, right, (((left_dim,), (right_dim,)), ((), ())), preferred_element_type=jnp.float32
    )


def bounds(prefix, start, query_span, key_span):
    whole = jnp.maximum(prefix, start + 1) // key_span
    every = (jnp.maximum(prefix, start + query_span) + key_span - 1) // key_span
    return whole, every


def hide(scores, limit, offset):
    return jnp.where(lax.broadcasted_iota(jnp.int32, scores.shape, 0) < limit - offset, scores, NEG)


def low(value):
    return value.astype(jnp.bfloat16)


def rows_norm(hidden, scaling, offsets):
    centre = hidden - jnp.mean(hidden, -1, keepdims=True)
    inverse = lax.rsqrt(jnp.mean(centre * centre, -1, keepdims=True) + EPS)
    unit_rows = centre * inverse
    return low(unit_rows * scaling + offsets), unit_rows, inverse


def rows_back(upstream, unit_rows, inverse, scaling):
    scaled = upstream * scaling
    result = inverse * (
        scaled
        - jnp.mean(scaled, -1, keepdims=True)
        - unit_rows * jnp.mean(scaled * unit_rows, -1, keepdims=True)
    )
    return (
        result,
        jnp.sum(upstream * unit_rows, 0, keepdims=True),
        jnp.sum(upstream, 0, keepdims=True),
    )


MESH = pl.DeviceIdType.MESH


def meet(group, tp, fsdp):
    here, core, chip = lax.axis_index("fsdp"), lax.axis_index("ctx"), lax.axis_index("tp")
    me = core * tp + chip
    barrier = pltpu.get_barrier_semaphore()
    for k in range(1, group):
        other = me ^ k
        pl.semaphore_signal(
            barrier, inc=1, device_id={"ctx": other // tp, "tp": other % tp}, device_id_type=MESH
        )
    for k in range(1, fsdp):
        pl.semaphore_signal(barrier, inc=1, device_id={"fsdp": here ^ k}, device_id_type=MESH)
    pl.semaphore_wait(barrier, group - 1 + fsdp - 1)


def forward_kernel(
    prefix_ref,
    tokens_ref,
    step_ref,
    gain_ref,
    bias_ref,
    mine_ref,
    rows_out,
    qkv_ref,
    wide_ref,
    log_ref,
    ctx_ref,
    weight_ref,
    rows_ref,
    columns,
    weight,
    keys_ref,
    values_ref,
    low_ref,
    landing,
    w_send,
    w_recv,
    x_send,
    x_recv,
    c_send,
    c_recv,
    keep_sem,
    *,
    span,
    tp,
    fsdp,
):
    batches, chunk, width = tokens_ref.shape
    group = rows_ref.shape[1]
    length = group * chunk
    blocks, ratio = length // span, span // chunk
    wide_blocks = max(1, length // 2 // span)
    factor = HEAD_DIM**-0.5
    here, core, chip = lax.axis_index("fsdp"), lax.axis_index("ctx"), lax.axis_index("tp")
    me = core * tp + chip
    meet(group, tp, fsdp)

    def w_copy(k):
        return pltpu.make_async_remote_copy(
            src_ref=mine_ref,
            dst_ref=columns.at[k],
            send_sem=w_send.at[k],
            recv_sem=w_recv.at[k],
            device_id={"fsdp": here ^ k},
            device_id_type=MESH,
        )

    for k in range(1, fsdp):
        w_copy(k).start()

    def x_copy(seq, origin, kind):
        target = ({"tp": chip + 1}, {"tp": chip - 1}, {"ctx": 1 - core})[kind]
        block = rows_ref.at[seq, core * tp + origin]
        return pltpu.make_async_remote_copy(
            src_ref=block,
            dst_ref=block,
            send_sem=x_send.at[seq, origin, kind],
            recv_sem=x_recv.at[seq, core * tp + origin],
            device_id=target,
            device_id_type=MESH,
        )

    def x_wait(seq, place):
        pltpu.make_async_remote_copy(
            src_ref=rows_ref.at[seq, place],
            dst_ref=rows_ref.at[seq, place],
            send_sem=x_send.at[seq, 0, 0],
            recv_sem=x_recv.at[seq, place],
            device_id={"ctx": 1 - core},
            device_id_type=MESH,
        ).wait_recv()

    def own_sends(seq):
        @pl.when(chip < tp - 1)
        def upward():
            x_copy(seq, chip, 0).start()

        @pl.when(chip > 0)
        def downward():
            x_copy(seq, chip, 1).start()

        x_copy(seq, chip, 2).start()

    def normalise(seq):
        start_sum = tokens_ref[seq].astype(jnp.float32) + step_ref[seq]
        normed, unused, unused_too = rows_norm(start_sum, gain_ref[...], bias_ref[...])
        rows_ref[seq, me] = normed

    normalise(0)
    own_sends(0)
    normalise(1)
    values_ref[:, HEAD_DIM:, :] = jnp.ones_like(values_ref[:, HEAD_DIM:, :])
    piece = mine_ref.shape[1]
    for k in range(fsdp):
        if k:
            w_copy(k).wait_recv()
        part = columns[k] if k else mine_ref[...]
        for f in range(fsdp):

            @pl.when((here ^ k) == f)
            def place(f=f, part=part):
                weight[:, f * piece : (f + 1) * piece] = part

    weight_ref[...] = weight[...]

    def project(seq, place):
        rows = rows_ref[seq, place]
        joined = low(dot_of(weight[...], rows, 1, 1))
        at = pl.ds(pl.multiple_of(place * chunk, chunk), chunk)
        qkv_ref[seq, :HEAD_DIM, at] = joined[:HEAD_DIM] * jnp.bfloat16(factor)
        qkv_ref[seq, HEAD_DIM:, at] = joined[HEAD_DIM:]
        values_ref[seq, :HEAD_DIM, at] = joined[2 * HEAD_DIM :]
        keys_ref[seq, at, :] = low(dot_of(rows, weight[HEAD_DIM : 2 * HEAD_DIM, :], 1, 1))

    def stage(seq, hop):
        @pl.when(chip >= hop)
        def from_below():
            x_wait(seq, core * tp + chip - hop)

            @pl.when(chip < tp - 1)
            def onward():
                x_copy(seq, chip - hop, 0).start()

            x_copy(seq, chip - hop, 2).start()

        @pl.when(chip + hop < tp)
        def from_above():
            x_wait(seq, core * tp + chip + hop)

            @pl.when(chip > 0)
            def onward():
                x_copy(seq, chip + hop, 1).start()

            x_copy(seq, chip + hop, 2).start()

    def project_some(seq, first, count):
        def one(k, unused):
            project(seq, first + k)
            return unused

        lax.fori_loop(0, count, one, 0)

    def complete(seq):
        def one(k, unused):
            x_wait(seq, (1 - core) * tp + k)
            return unused

        project_some(seq, core * tp, tp)
        lax.fori_loop(0, tp, one, 0)
        project_some(seq, (1 - core) * tp, tp)

    for hop in range(1, tp):
        stage(0, hop)
        if hop == tp - 2:
            own_sends(1)
    complete(0)

    def c_copy(seq, place):
        return pltpu.make_async_remote_copy(
            src_ref=low_ref.at[seq, place],
            dst_ref=landing.at[seq, me],
            send_sem=c_send.at[seq, place],
            recv_sem=c_recv.at[seq, me],
            device_id={"ctx": place // tp, "tp": place % tp},
            device_id_type=MESH,
        )

    def c_wait(seq, place):
        pltpu.make_async_remote_copy(
            src_ref=low_ref.at[seq, place],
            dst_ref=landing.at[seq, place],
            send_sem=c_send.at[seq, place],
            recv_sem=c_recv.at[seq, place],
            device_id={"ctx": place // tp, "tp": place % tp},
            device_id_type=MESH,
        ).wait_recv()

    def attend(index, unused):
        seq, block = index // blocks, index % blocks

        @pl.when(index == blocks - 1)
        def pass_on():
            stage(1, 1)

        @pl.when(index == blocks)
        def receive():
            for hop in range(3, tp):
                stage(1, hop)
            complete(1)

        start = pl.multiple_of(block * span, span)
        queries = qkv_ref[seq, :HEAD_DIM, pl.ds(start, span)]
        limit = jnp.maximum(
            prefix_ref[seq], start + 1 + lax.broadcasted_iota(jnp.int32, (1, span), 1)
        )

        def advance(other, carry, masked):
            highest, total = carry
            offset = pl.multiple_of(other * span, span)
            scores = dot_of(keys_ref[seq, pl.ds(offset, span), :], queries, 1, 0)
            if masked:
                scores = hide(scores, limit, offset)
            higher = jnp.maximum(highest, jnp.max(scores, axis=0, keepdims=True))
            weights = low(jnp.exp(scores - higher))
            fading = jnp.exp(highest - higher)
            total = total * fading + dot_of(values_ref[seq, :, pl.ds(offset, span)], weights, 1, 0)
            return higher, total

        carry = (
            jnp.full((1, span), NEG, jnp.float32),
            jnp.zeros((values_ref.shape[1], span), jnp.float32),
        )
        carry = lax.fori_loop(0, block, lambda j, c: advance(j, c, False), carry)
        highest, total = lax.fori_loop(
            block, jnp.maximum(block + 1, wide_blocks), lambda j, c: advance(j, c, True), carry
        )
        weight_sum = total[HEAD_DIM : HEAD_DIM + 1, :]
        attended = total[:HEAD_DIM, :] / weight_sum
        wide_ref[seq, :, pl.ds(start, span)] = attended
        log_ref[seq, :, pl.ds(start, span)] = highest + jnp.log(weight_sum)
        attended = low(attended)
        for part in range(ratio):
            place = block * ratio + part
            low_ref[seq, place] = attended[:, part * chunk : (part + 1) * chunk]

            @pl.when(place != me)
            def send(place=place):
                c_copy(seq, place).start()

        @pl.when(index == blocks - 1)
        def pass_on_two():
            stage(1, 2)

        return unused

    lax.fori_loop(0, batches * blocks, attend, 0)
    keep = pltpu.make_async_copy(rows_ref, rows_out, keep_sem)
    keep.start()
    for seq in range(batches):

        def collect(k, unused, seq=seq):
            c_wait(seq, me ^ k)
            ctx_ref[seq, me ^ k] = landing[seq, me ^ k]
            return unused

        lax.fori_loop(1, group, collect, 0)
        ctx_ref[seq, me] = low_ref[seq, me]
    for k in range(1, fsdp):
        w_copy(k).wait_send()
    for seq in range(batches):
        for hop in range(tp):

            @pl.when(chip >= hop)
            def sent_up(seq=seq, hop=hop):
                @pl.when(chip < tp - 1)
                def onward():
                    x_copy(seq, chip - hop, 0).wait_send()

                x_copy(seq, chip - hop, 2).wait_send()

            @pl.when(chip + hop < tp)
            def sent_down(seq=seq, hop=hop):
                @pl.when(chip > 0)
                def onward():
                    x_copy(seq, chip + hop, 1).wait_send()

                if hop:
                    x_copy(seq, chip + hop, 2).wait_send()

        def sent(k, unused, seq=seq):
            c_copy(seq, me ^ k).wait_send()
            return unused

        lax.fori_loop(1, group, sent, 0)
    keep.wait()


def forward_group(prefix, tokens, steps, gain, bias, mine, span, group, tp, fsdp):
    batches, chunk, width = tokens.shape
    length = group * chunk
    bf16, f32 = jnp.bfloat16, jnp.float32
    struct = jax.ShapeDtypeStruct
    inside = pl.BlockSpec(memory_space=pltpu.VMEM)
    dma = pltpu.SemaphoreType.DMA
    return pl.pallas_call(
        functools.partial(forward_kernel, span=span, tp=tp, fsdp=fsdp),
        in_specs=[pl.BlockSpec(memory_space=pltpu.SMEM)] + [inside] * 5,
        out_specs=[pl.BlockSpec(memory_space=pl.ANY)] + [inside] * 5,
        out_shape=[
            struct((batches, group, chunk, width), bf16),
            struct((batches, 3 * HEAD_DIM, length), bf16),
            struct((batches, HEAD_DIM, length), f32),
            struct((batches, 1, length), f32),
            struct((batches, group, HEAD_DIM, chunk), bf16),
            struct((3 * HEAD_DIM, width), bf16),
        ],
        scratch_shapes=[
            pltpu.VMEM((batches, group, chunk, width), bf16),
            pltpu.VMEM((fsdp,) + mine.shape, bf16),
            pltpu.VMEM((3 * HEAD_DIM, width), bf16),
            pltpu.VMEM((batches, length, HEAD_DIM), bf16),
            pltpu.VMEM((batches, HEAD_DIM + 16, length), bf16),
            pltpu.VMEM((batches, group, HEAD_DIM, chunk), bf16),
            pltpu.VMEM((batches, group, HEAD_DIM, chunk), bf16),
            dma((fsdp,)),
            dma((fsdp,)),
            dma((batches, tp, 3)),
            dma((batches, group)),
            dma((batches, group)),
            dma((batches, group)),
            dma,
        ],
        compiler_params=pltpu.CompilerParams(
            vmem_limit_bytes=VMEM_LIMIT, collective_id=1, has_side_effects=True
        ),
        cost_estimate=pl.CostEstimate(
            flops=60_000_000_000, bytes_accessed=30_000_000, transcendentals=20_000_000
        ),
        name="forward_group",
    )(prefix, tokens, steps, gain, bias, mine)


QUERY, KEY, VALUE, SELF_OUT, CROSS_OUT, UP, DOWN = 0, 1, 2, 3, 4, 5, 9


def middle_kernel(
    gathered,
    tokens_ref,
    step_ref,
    enc_ref,
    cot_ref,
    gain_ref,
    bias_ref,
    ctx_ref,
    final_ref,
    after_ref,
    back_ref,
    enc_grad_ref,
    stats_ref,
    packed_ref,
    weights,
    totals,
    context,
    queries,
    keys,
    values,
    probs,
    context_two,
    grad_heads,
    grad_queries,
    grad_keys,
    grad_values,
    sem,
    *,
    tp,
    group,
):
    seq = pl.program_id(0)
    chunk, width = tokens_ref.shape[1:]
    piece = gathered.shape[-1]
    factor = HEAD_DIM**-0.5
    heads = width // HEAD_DIM

    @pl.when(seq == 0)
    def assemble():
        copies = []
        for f in range(width // piece):
            for c in range(group // tp):
                for t in range(tp):
                    head = t * (group // tp) + c
                    copies.append(
                        pltpu.make_async_copy(
                            gathered.at[f, c, t, pl.ds(3, weights.shape[0])],
                            weights.at[
                                :, pl.ds(head * HEAD_DIM, HEAD_DIM), pl.ds(f * piece, piece)
                            ],
                            sem.at[(f * group // tp + c) * tp + t],
                        )
                    )
        for copy in copies:
            copy.start()
        totals[...] = jnp.zeros_like(totals)
        stats_ref[...] = jnp.zeros_like(stats_ref)
        for copy in copies:
            copy.wait()

    for other in range(group):
        head = (other % tp) * (group // tp) + other // tp
        context[head * HEAD_DIM : (head + 1) * HEAD_DIM, :] = ctx_ref[0, other]
    start_sum = tokens_ref[0].astype(jnp.float32) + step_ref[0]
    branch_one = dot_of(context[...], weights[SELF_OUT], 0, 0)
    after_one = start_sum + branch_one
    stats_ref[1:2, :] += jnp.sum(branch_one * branch_one, 0, keepdims=True)
    normed_two, unit_two, inverse_two = rows_norm(after_one, gain_ref[1:2], bias_ref[1:2])
    queries[...] = low(dot_of(weights[QUERY], normed_two, 1, 1))
    keys[...] = low(dot_of(weights[KEY], enc_ref[0], 1, 1))
    values[...] = low(dot_of(weights[VALUE], enc_ref[0], 1, 1))

    def attend(head, unused):
        rows = pl.ds(pl.multiple_of(head * HEAD_DIM, HEAD_DIM), HEAD_DIM)
        scores = dot_of(keys[rows, :].T, queries[rows, :], 1, 0) * factor
        powers = jnp.exp(scores - jnp.max(scores, 0, keepdims=True))
        attn = powers / jnp.sum(powers, 0, keepdims=True)
        probs[head] = attn
        context_two[rows, :] = low(dot_of(values[rows, :], low(attn), 1, 0))
        return unused

    lax.fori_loop(0, heads, attend, 0, unroll=2)
    branch_two = dot_of(context_two[...], weights[CROSS_OUT], 0, 0)
    after_two = after_one + branch_two
    stats_ref[2:3, :] += jnp.sum(branch_two * branch_two, 0, keepdims=True)
    normed_three, unit_three, inverse_three = rows_norm(after_two, gain_ref[2:3], bias_ref[2:3])
    grad_three = cot_ref[0]

    def feed(part, carry):
        branch, grad = carry
        up, down = weights[UP + part], weights[DOWN + part]
        inputs = dot_of(up, normed_three, 1, 1)
        activated, slopes = gelu_parts(inputs)
        hidden = low(activated)
        branch = branch + dot_of(hidden, down, 0, 0)
        totals[DOWN - 2 + part] += dot_of(hidden, grad_three, 1, 0)
        grad_pre = low(dot_of(down, grad_three, 1, 1) * slopes)
        totals[UP - 2 + part] += dot_of(grad_pre, normed_three, 1, 0)
        return branch, grad + dot_of(grad_pre, up, 0, 0)

    blank = jnp.zeros((chunk, width), jnp.float32)
    branch_three, grad_norm = lax.fori_loop(0, DOWN - UP, feed, (blank, blank))
    final_sum = after_two + branch_three
    final_ref[0] = final_sum
    stats_ref[0:1, :] += jnp.sum(final_sum * final_sum, 0, keepdims=True)
    stats_ref[3:4, :] += jnp.sum(branch_three * branch_three, 0, keepdims=True)
    back, gain_sum, bias_sum = rows_back(grad_norm, unit_three, inverse_three, gain_ref[2:3])
    stats_ref[6:7, :] += gain_sum
    stats_ref[7:8, :] += bias_sum
    grad_after_two = grad_three.astype(jnp.float32) + back
    grad_two = low(grad_after_two)
    totals[2] += dot_of(context_two[...], grad_two, 1, 0)
    grad_heads[...] = low(dot_of(weights[CROSS_OUT], grad_two, 1, 1))

    def attend_back(head, unused):
        rows = pl.ds(pl.multiple_of(head * HEAD_DIM, HEAD_DIM), HEAD_DIM)
        grads = grad_heads[rows, :]
        attn = probs[head]
        grad_probs = dot_of(values[rows, :].T, grads, 1, 0)
        grad_scores = low(
            attn * (grad_probs - jnp.sum(attn * grad_probs, 0, keepdims=True))
        )
        grad_queries[rows, :] = low(dot_of(keys[rows, :], grad_scores, 1, 0) * factor)
        grad_keys[rows, :] = dot_of(queries[rows, :], grad_scores, 1, 1) * factor
        grad_values[rows, :] = dot_of(grads, low(attn), 1, 1)
        return unused

    lax.fori_loop(0, heads, attend_back, 0, unroll=2)
    enc_grad_ref[0, :, :width] = low(grad_keys[...].T)
    enc_grad_ref[0, :, width:] = low(grad_values[...].T)
    totals[0] += dot_of(grad_queries[...], normed_two, 1, 0)
    upstream = dot_of(grad_queries[...], weights[QUERY], 0, 0)
    back, gain_sum, bias_sum = rows_back(upstream, unit_two, inverse_two, gain_ref[1:2])
    stats_ref[4:5, :] += gain_sum
    stats_ref[5:6, :] += bias_sum
    grad_after_one = grad_after_two + back
    after_ref[0] = grad_after_one
    grad_one = low(grad_after_one)
    totals[1] += dot_of(context[...], grad_one, 1, 0)
    context[...] = low(dot_of(weights[SELF_OUT], grad_one, 1, 1))
    for other in range(group):
        head = (other % tp) * (group // tp) + other // tp
        back_ref[0, other] = context[head * HEAD_DIM : (head + 1) * HEAD_DIM, :]

    @pl.when(seq == pl.num_programs(0) - 1)
    def pack():
        for f in range(width // piece):
            for c in range(group // tp):
                for t in range(tp):
                    head = t * (group // tp) + c
                    packed_ref[c, f, t] = low(
                        totals[
                            :,
                            head * HEAD_DIM : (head + 1) * HEAD_DIM,
                            f * piece : (f + 1) * piece,
                        ]
                    )


def middle(gathered, tokens, steps, encoder, cotangent, gains, biases, contexts, tp):
    batches, chunk, width = tokens.shape
    group = contexts.shape[1]
    enc_count = encoder.shape[1]
    heads = width // HEAD_DIM
    bf16, f32 = jnp.bfloat16, jnp.float32
    struct = jax.ShapeDtypeStruct
    each = lambda *shape: pl.BlockSpec((1,) + shape, lambda i: (i,) + (0,) * len(shape))
    once = lambda *shape: pl.BlockSpec(
        shape, lambda i: (0,) * len(shape), pipeline_mode=pl.Buffered(1)
    )
    count = gathered.shape[3] - 3
    packed = (group // tp, gathered.shape[0], tp, count - 2) + gathered.shape[4:]
    return pl.pallas_call(
        functools.partial(middle_kernel, tp=tp, group=group),
            grid=(batches,),
            in_specs=[
                pl.BlockSpec(memory_space=pl.ANY),
                each(chunk, width),
                each(1, width),
                each(enc_count, width),
                each(chunk, width),
                once(3, width),
                once(3, width),
                each(group, HEAD_DIM, chunk),
            ],
            out_specs=[
                each(chunk, width),
                each(chunk, width),
                each(group, HEAD_DIM, chunk),
                each(enc_count, 2 * width),
                once(8, width),
                once(*packed),
            ],
            scratch_shapes=[
                pltpu.VMEM((count, width, width), bf16),
                pltpu.VMEM((count - 2, width, width), f32),
                pltpu.VMEM((width, chunk), bf16),
                pltpu.VMEM((width, chunk), bf16),
                pltpu.VMEM((width, enc_count), bf16),
                pltpu.VMEM((width, enc_count), bf16),
                pltpu.VMEM((heads, enc_count, chunk), f32),
                pltpu.VMEM((width, chunk), bf16),
                pltpu.VMEM((width, chunk), bf16),
                pltpu.VMEM((width, chunk), bf16),
                pltpu.VMEM((width, enc_count), f32),
                pltpu.VMEM((width, enc_count), f32),
                pltpu.SemaphoreType.DMA((32,)),
            ],
        out_shape=[
            struct((batches, chunk, width), f32),
            struct((batches, chunk, width), f32),
            struct((batches, group, HEAD_DIM, chunk), bf16),
            struct((batches, enc_count, 2 * width), bf16),
            struct((8, width), f32),
            struct(packed, bf16),
        ],
        compiler_params=pltpu.CompilerParams(vmem_limit_bytes=VMEM_LIMIT),
        cost_estimate=pl.CostEstimate(
            flops=30_000_000_000, bytes_accessed=30_000_000, transcendentals=10_000_000
        ),
        name="middle",
    )(gathered, tokens, steps, encoder, cotangent, gains, biases, contexts)


def backward_kernel(
    prefix_ref,
    returned,
    enc_parts,
    packed,
    gathered,
    rows_in,
    qkv_ref,
    wide_ref,
    log_ref,
    tokens_ref,
    step_ref,
    gain_ref,
    after_ref,
    enc_ref,
    stats_ref,
    input_ref,
    enc_out,
    self_out,
    query_out,
    pair_out,
    back_out,
    cross_out,
    up_out,
    down_out,
    sums_out,
    landing,
    outgoing,
    incoming,
    queries_ref,
    keys_ref,
    values_ref,
    grad_ref,
    gradt_ref,
    delta_ref,
    grad_keys_ref,
    grad_values_ref,
    rows_ref,
    heads_ref,
    pair_weights,
    enc_landing,
    pair_ref,
    pair_landing,
    core_landing,
    partial_ref,
    fsdp_landing,
    line_ref,
    line_landing,
    shard_ref,
    head_ref,
    head_landing,
    head_shard,
    sums_ref,
    sums_landing,
    sums_two,
    d_send,
    d_recv,
    e_send,
    e_recv,
    g_send,
    g_recv,
    r_send,
    r_recv,
    f_send,
    f_recv,
    t_send,
    t_recv,
    h_send,
    h_recv,
    s_send,
    s_recv,
    local_sem,
    rows_sem,
    *,
    span,
    tp,
    fsdp,
):
    batches, chunk, width = tokens_ref.shape
    group = landing.shape[1]
    length = group * chunk
    blocks, ratio = length // span, span // chunk
    wide_blocks = max(1, length // 2 // span)
    factor = HEAD_DIM**-0.5
    here, core, chip = lax.axis_index("fsdp"), lax.axis_index("ctx"), lax.axis_index("tp")
    me = core * tp + chip
    cores = group // tp
    share = enc_landing.shape[2]
    piece = width // fsdp
    early = packed.shape[3]
    meet(group, tp, fsdp)

    def send_to(source, target, send, recv, **place):
        return pltpu.make_async_remote_copy(
            src_ref=source,
            dst_ref=target,
            send_sem=send,
            recv_sem=recv,
            device_id=place,
            device_id_type=MESH,
        )

    def member(place):
        return {"ctx": place // tp, "tp": place % tp}

    local = [
        pltpu.make_async_copy(
            packed.at[core], partial_ref.at[:, :, pl.ds(0, early)], local_sem.at[0]
        )
    ]
    for seq in range(batches):
        local.append(
            pltpu.make_async_copy(
                returned.at[seq, me], landing.at[seq, me], local_sem.at[1 + seq]
            )
        )
    local.append(
        pltpu.make_async_copy(
            enc_parts.at[:, pl.ds(pl.multiple_of(me * share, share), share)],
            enc_landing.at[me],
            local_sem.at[1 + batches],
        )
    )
    first = 2 + batches
    for f in range(fsdp):
        for c in range(cores):
            for t in range(tp):
                head = t * cores + c
                number = (f * cores + c) * tp + t
                local.append(
                    pltpu.make_async_copy(
                        gathered.at[f, c, t, pl.ds(0, 3)],
                        heads_ref.at[c * tp + t, :, :, pl.ds(f * piece, piece)],
                        local_sem.at[first + 2 * number],
                    )
                )
                local.append(
                    pltpu.make_async_copy(
                        gathered.at[f, c, t, pl.ds(3 + KEY, 2)],
                        pair_weights.at[
                            :, pl.ds(head * HEAD_DIM, HEAD_DIM), pl.ds(f * piece, piece)
                        ],
                        local_sem.at[first + 2 * number + 1],
                    )
                )

    def d_copy(seq, place):
        return send_to(
            returned.at[seq, place],
            landing.at[seq, me],
            d_send.at[seq, place],
            d_recv.at[seq, me],
            **member(place),
        )

    def d_wait(seq, place):
        send_to(
            returned.at[seq, place],
            landing.at[seq, place],
            d_send.at[seq, place],
            d_recv.at[seq, place],
            **member(place),
        ).wait_recv()

    def e_copy(place):
        return send_to(
            enc_parts.at[:, pl.ds(pl.multiple_of(place * share, share), share)],
            enc_landing.at[me],
            e_send.at[place],
            e_recv.at[me],
            **member(place),
        )

    def e_wait(place):
        send_to(
            enc_landing.at[place],
            enc_landing.at[place],
            e_send.at[place],
            e_recv.at[place],
            **member(place),
        ).wait_recv()

    core_copy = send_to(
        packed.at[1 - core], core_landing, r_send.at[0], r_recv.at[0], ctx=1 - core
    )
    pair_copy = send_to(
        pair_ref.at[1 - core], pair_landing, r_send.at[1], r_recv.at[1], ctx=1 - core
    )
    shard_copy = send_to(
        shard_ref.at[core], shard_ref.at[core], r_send.at[2], r_recv.at[2], ctx=1 - core
    )
    shard_wait = send_to(
        shard_ref.at[1 - core], shard_ref.at[1 - core], r_send.at[2], r_recv.at[2], ctx=1 - core
    )
    head_copy = send_to(
        head_shard.at[core], head_shard.at[core], r_send.at[3], r_recv.at[3], ctx=1 - core
    )
    head_wait = send_to(
        head_shard.at[1 - core], head_shard.at[1 - core], r_send.at[3], r_recv.at[3], ctx=1 - core
    )
    f_copies = [
        send_to(
            partial_ref.at[here ^ k], fsdp_landing.at[k - 1], f_send.at[k], f_recv.at[k], fsdp=here ^ k
        )
        for k in range(1, fsdp)
    ]
    t_copies = [
        send_to(line_ref.at[chip ^ k], line_landing.at[k - 1], t_send.at[k], t_recv.at[k], tp=chip ^ k)
        for k in range(1, tp)
    ]
    h_copies = [
        send_to(
            head_ref.at[here ^ k], head_landing.at[k - 1], h_send.at[k], h_recv.at[k], fsdp=here ^ k
        )
        for k in range(1, fsdp)
    ]

    def s_copy(k):
        return send_to(
            sums_ref, sums_landing.at[k], s_send.at[k], s_recv.at[k], **member(me ^ k)
        )

    s_fsdp = [
        send_to(
            sums_two, sums_landing.at[group + k], s_send.at[group + k], s_recv.at[group + k], fsdp=here ^ k
        )
        for k in range(1, fsdp)
    ]

    for seq in range(batches):
        local[1 + seq].start()

    def start_grads(seq):
        def one(k, unused):
            d_copy(seq, me ^ k).start()
            return unused

        lax.fori_loop(1, group, one, 0)

    start_grads(0)
    core_copy.start()
    for copy in [local[0]] + local[1 + batches :]:
        copy.start()
    start_grads(1)

    def start_enc(k, unused):
        e_copy(me ^ k).start()
        return unused

    lax.fori_loop(1, group, start_enc, 0)

    def g_copy(seq, place, part):
        lines = pl.ds(0, HEAD_DIM) if part == 0 else pl.ds(HEAD_DIM, 2 * HEAD_DIM)
        return send_to(
            outgoing.at[seq, place, lines],
            incoming.at[seq, me, lines],
            g_send.at[seq, place, part],
            g_recv.at[seq, me, part],
            **member(place),
        )

    def g_wait(seq, place, part):
        lines = pl.ds(0, HEAD_DIM) if part == 0 else pl.ds(HEAD_DIM, 2 * HEAD_DIM)
        send_to(
            outgoing.at[seq, place, lines],
            incoming.at[seq, place, lines],
            g_send.at[seq, place, part],
            g_recv.at[seq, place, part],
            **member(place),
        ).wait_recv()

    def prepare(seq):
        pltpu.make_async_copy(
            returned.at[seq, me], landing.at[seq, me], local_sem.at[1 + seq]
        ).wait()

        def arrive(k, unused):
            d_wait(seq, me ^ k)
            return unused

        lax.fori_loop(1, group, arrive, 0)

        def lay(place, unused):
            at = pl.ds(pl.multiple_of(place * chunk, chunk), chunk)
            grads = landing[seq, place]
            gradt_ref[:, at] = grads
            grad_ref[at, :] = grads.T
            delta_ref[:, at] = jnp.sum(
                grads.astype(jnp.float32) * wide_ref[seq, :, at], axis=0, keepdims=True
            )
            queries_ref[at, :] = qkv_ref[seq, :HEAD_DIM, at].T
            keys_ref[at, :] = qkv_ref[seq, HEAD_DIM : 2 * HEAD_DIM, at].T
            values_ref[at, :] = qkv_ref[seq, 2 * HEAD_DIM :, at].T
            return unused

        lax.fori_loop(0, group, lay, 0)
        grad_keys_ref[...] = jnp.zeros_like(grad_keys_ref)
        grad_values_ref[...] = jnp.zeros_like(grad_values_ref)

    def encoder_part():
        local[1 + batches].wait()

        def arrive(k, unused):
            e_wait(me ^ k)
            return unused

        lax.fori_loop(1, group, arrive, 0)
        total = enc_landing[0].astype(jnp.float32)
        for place in range(1, group):
            total = total + enc_landing[place].astype(jnp.float32)
        for copy in local[first:]:
            copy.wait()
        grads = low(total)
        enc_rows = enc_ref[:, pl.ds(pl.multiple_of(me * share, share), share), :]
        flat, enc_flat = grads.reshape(batches * share, 2 * width), enc_rows.reshape(
            batches * share, width
        )
        result = dot_of(flat[:, :width], pair_weights[0], 1, 0) + dot_of(
            flat[:, width:], pair_weights[1], 1, 0
        )
        enc_out[...] = result.reshape(batches, share, width)
        for which in range(2):
            grad = low(dot_of(flat[:, which * width : (which + 1) * width], enc_flat, 0, 0))
            for f in range(fsdp):
                for c in range(cores):
                    for t in range(tp):
                        head = t * cores + c
                        pair_ref[c, f, t, which] = grad[
                            head * HEAD_DIM : (head + 1) * HEAD_DIM, f * piece : (f + 1) * piece
                        ]
        pair_copy.start()

    def sum_cores():
        local[0].wait()
        core_copy.wait_recv()
        pair_copy.wait_recv()

        def one(f, unused):
            def two(t, unused):
                partial_ref[f, t, :early] = low(
                    partial_ref[f, t, :early].astype(jnp.float32)
                    + core_landing[f, t].astype(jnp.float32)
                )
                partial_ref[f, t, early:] = low(
                    pair_ref[core, f, t].astype(jnp.float32)
                    + pair_landing[f, t].astype(jnp.float32)
                )
                return unused

            return lax.fori_loop(0, tp, two, unused)

        lax.fori_loop(0, fsdp, one, 0)
        for copy in f_copies:
            copy.start()

    def sum_fsdp():
        for copy in f_copies:
            copy.wait_recv()

        def one(t, unused):
            total = partial_ref[here, t].astype(jnp.float32)
            for k in range(fsdp - 1):
                total = total + fsdp_landing[k, t].astype(jnp.float32)
            line_ref[t] = low(total)
            return unused

        lax.fori_loop(0, tp, one, 0)
        for copy in t_copies:
            copy.start()

    def sum_line():
        for copy in t_copies:
            copy.wait_recv()
        total = line_ref[chip].astype(jnp.float32)
        for k in range(tp - 1):
            total = total + line_landing[k].astype(jnp.float32)
        shard_ref[core] = total
        shard_copy.start()

    prepare(0)

    def attend(index, unused):
        seq, block = index // blocks, blocks - 1 - index % blocks

        @pl.when(index == 2)
        def encoder_hook():
            encoder_part()

        @pl.when(index == blocks - 1)
        def core_hook():
            sum_cores()

        @pl.when(index == blocks)
        def next_sequence():
            prepare(1)

        @pl.when(index == blocks + 1)
        def fsdp_hook():
            sum_fsdp()

        @pl.when(index == blocks + 2)
        def line_hook():
            sum_line()

        start = pl.multiple_of(block * span, span)
        at = pl.ds(start, span)
        queries_t, queries = qkv_ref[seq, :HEAD_DIM, at], queries_ref[at, :]
        grads_t, grads = gradt_ref[:, at], grad_ref[at, :]
        logs, deltas = log_ref[seq, :, at], delta_ref[:, at]
        limit = jnp.maximum(
            prefix_ref[seq], start + 1 + lax.broadcasted_iota(jnp.int32, (1, span), 1)
        )

        def advance(other, grad_queries, masked):
            offset = pl.multiple_of(other * span, span)
            there = pl.ds(offset, span)
            scores = dot_of(keys_ref[there, :], queries_t, 1, 0)
            if masked:
                scores = hide(scores, limit, offset)
            probs = jnp.exp(scores - logs)
            grad_probs = dot_of(values_ref[there, :], grads_t, 1, 0)
            grad_scores = low(probs * (grad_probs - deltas))
            grad_values_ref[there, :] += dot_of(low(probs), grads, 1, 0)
            grad_keys_ref[there, :] += dot_of(grad_scores, queries, 1, 0)
            return grad_queries + dot_of(
                qkv_ref[seq, HEAD_DIM : 2 * HEAD_DIM, there], grad_scores, 1, 0
            )

        grad_queries = jnp.zeros((HEAD_DIM, span), jnp.float32)
        grad_queries = lax.fori_loop(0, block, lambda j, c: advance(j, c, False), grad_queries)
        grad_queries = lax.fori_loop(
            block, jnp.maximum(block + 1, wide_blocks), lambda j, c: advance(j, c, True), grad_queries
        )
        done = low(grad_queries * factor)
        for part in range(ratio):
            place = block * ratio + part
            outgoing[seq, place, :HEAD_DIM, :] = done[:, part * chunk : (part + 1) * chunk]

            @pl.when(place != me)
            def send(place=place):
                g_copy(seq, place, 0).start()

        lowest = jnp.where(block == 0, 0, block)
        highest = jnp.where(
            block == 0, wide_blocks, jnp.where(block >= wide_blocks, block + 1, block)
        )

        def give(place, unused):
            at = pl.ds(pl.multiple_of(place * chunk, chunk), chunk)
            outgoing[seq, place, HEAD_DIM : 2 * HEAD_DIM, :] = low(grad_keys_ref[at, :].T)
            outgoing[seq, place, 2 * HEAD_DIM :, :] = low(grad_values_ref[at, :].T)

            @pl.when(place != me)
            def send():
                g_copy(seq, place, 1).start()

            return unused

        lax.fori_loop(lowest * ratio, highest * ratio, give, 0)
        return unused

    lax.fori_loop(0, batches * blocks, attend, 0)
    sums_ref[...] = jnp.zeros_like(sums_ref)
    sums_ref[:8, :] = stats_ref[...]

    def rows_copy(number):
        return pltpu.make_async_copy(
            rows_in.at[number // group, number % group],
            rows_ref.at[number % rows_ref.shape[0]],
            rows_sem.at[number % rows_ref.shape[0]],
        )

    depth = rows_ref.shape[0]
    for number in range(depth):
        rows_copy(number).start()

    def weigh(number, total):
        rows_copy(number).wait()
        total = total + dot_of(
            outgoing[number // group, number % group], rows_ref[number % depth], 1, 0
        )

        @pl.when(number + depth < batches * group)
        def more():
            rows_copy(number + depth).start()

        return total

    total = lax.fori_loop(
        0, batches * group, weigh, jnp.zeros((3 * HEAD_DIM, width), jnp.float32)
    )
    for f in range(fsdp):
        head_ref[f] = total[:, f * piece : (f + 1) * piece]
    for copy in h_copies:
        copy.start()

    def finish(seq, unused):
        def arrive(k, unused):
            g_wait(seq, me ^ k, 0)
            g_wait(seq, me ^ k, 1)
            return unused

        lax.fori_loop(1, group, arrive, 0)
        incoming[seq, me] = outgoing[seq, me]
        upstream = dot_of(
            incoming[seq].reshape(group * 3 * HEAD_DIM, chunk),
            heads_ref[...].reshape(group * 3 * HEAD_DIM, width),
            0,
            0,
        )
        start_sum = tokens_ref[seq].astype(jnp.float32) + step_ref[seq]
        centre = start_sum - jnp.mean(start_sum, -1, keepdims=True)
        inverse = lax.rsqrt(jnp.mean(centre * centre, -1, keepdims=True) + EPS)
        back, gain_sum, bias_sum = rows_back(upstream, centre * inverse, inverse, gain_ref[...])
        input_ref[seq] = after_ref[seq] + back
        sums_ref[8:9, :] += gain_sum
        sums_ref[9:10, :] += bias_sum
        return unused

    lax.fori_loop(0, batches, finish, 0)

    def start_sums(k, unused):
        s_copy(k).start()
        return unused

    lax.fori_loop(1, group, start_sums, 0)
    for copy in h_copies:
        copy.wait_recv()
    total = head_ref[here]
    for k in range(fsdp - 1):
        total = total + head_landing[k]
    head_shard[core] = total
    head_copy.start()

    def arrive_sums(k, total):
        s_copy(k).wait_recv()
        return total + sums_landing[k]

    sums_two[...] = lax.fori_loop(1, group, arrive_sums, sums_ref[...])
    for copy in s_fsdp:
        copy.start()
    shard_wait.wait_recv()

    def whole(block):
        return jnp.concatenate([shard_ref[0, block], shard_ref[1, block]], 0)

    query_out[...] = whole(0).T
    back_out[...] = whole(1)
    cross_out[...] = whole(2)
    for part in range(4):
        up_out[:, part * piece : (part + 1) * piece] = whole(3 + part).T
        down_out[part * piece : (part + 1) * piece, :] = whole(7 + part)
    pair_out[0] = whole(11).T
    pair_out[1] = whole(12).T
    head_wait.wait_recv()
    for which in range(3):
        lines = slice(which * HEAD_DIM, (which + 1) * HEAD_DIM)
        self_out[which] = jnp.concatenate([head_shard[0, lines], head_shard[1, lines]], 0).T
    total = sums_two[...]
    for k, copy in enumerate(s_fsdp):
        copy.wait_recv()
        total = total + sums_landing[group + 1 + k]
    sums_out[...] = total
    core_copy.wait_send()
    pair_copy.wait_send()
    shard_copy.wait_send()
    head_copy.wait_send()
    for copy in f_copies + t_copies + h_copies + s_fsdp:
        copy.wait_send()

    def sent(k, unused):
        e_copy(me ^ k).wait_send()
        s_copy(k).wait_send()
        for seq in range(batches):
            d_copy(seq, me ^ k).wait_send()
            g_copy(seq, me ^ k, 0).wait_send()
            g_copy(seq, me ^ k, 1).wait_send()
        return unused

    lax.fori_loop(1, group, sent, 0)


def backward_group(
    prefix,
    returned,
    enc_parts,
    packed,
    gathered,
    rows,
    qkv,
    wide,
    logs,
    tokens,
    steps,
    gain,
    after,
    encoder,
    stats,
    span,
    tp,
    fsdp,
):
    batches, chunk, width = tokens.shape
    group = returned.shape[1]
    length = group * chunk
    share = encoder.shape[1] // group
    piece = width // fsdp
    count = packed.shape[3]
    tail = packed.shape[4:]
    bf16, f32 = jnp.bfloat16, jnp.float32
    struct = jax.ShapeDtypeStruct
    inside = pl.BlockSpec(memory_space=pltpu.VMEM)
    outside = pl.BlockSpec(memory_space=pl.ANY)
    dma = pltpu.SemaphoreType.DMA
    vmem = pltpu.VMEM
    parts = group * fsdp
    return pl.pallas_call(
        functools.partial(backward_kernel, span=span, tp=tp, fsdp=fsdp),
        in_specs=[pl.BlockSpec(memory_space=pltpu.SMEM)] + [outside] * 5 + [inside] * 9,
        out_specs=[inside] * 10,
        out_shape=[
            struct((batches, chunk, width), f32),
            struct((batches, share, width), f32),
            struct((3, piece, piece), f32),
            struct((piece, piece), f32),
            struct((2, piece, piece), f32),
            struct((piece, piece), f32),
            struct((piece, piece), f32),
            struct((piece, width), f32),
            struct((width, piece), f32),
            struct((16, width), f32),
        ],
        scratch_shapes=[
            vmem((batches, group, HEAD_DIM, chunk), bf16),
            vmem((batches, group, 3 * HEAD_DIM, chunk), bf16),
            vmem((batches, group, 3 * HEAD_DIM, chunk), bf16),
            vmem((length, HEAD_DIM), bf16),
            vmem((length, HEAD_DIM), bf16),
            vmem((length, HEAD_DIM), bf16),
            vmem((length, HEAD_DIM), bf16),
            vmem((HEAD_DIM, length), bf16),
            vmem((1, length), f32),
            vmem((length, HEAD_DIM), f32),
            vmem((length, HEAD_DIM), f32),
            vmem((4, chunk, width), bf16),
            vmem((group, 3, HEAD_DIM, width), bf16),
            vmem((2, width, width), bf16),
            vmem((group, batches, share, 2 * width), bf16),
            vmem((group // tp, fsdp, tp, 2) + tail, bf16),
            vmem((fsdp, tp, 2) + tail, bf16),
            vmem((fsdp, tp, count) + tail, bf16),
            vmem((fsdp, tp, count + 2) + tail, bf16),
            vmem((fsdp - 1, tp, count + 2) + tail, bf16),
            vmem((tp, count + 2) + tail, bf16),
            vmem((tp - 1, count + 2) + tail, bf16),
            vmem((2, count + 2) + tail, f32),
            vmem((fsdp, 3 * HEAD_DIM, piece), f32),
            vmem((fsdp - 1, 3 * HEAD_DIM, piece), f32),
            vmem((2, 3 * HEAD_DIM, piece), f32),
            vmem((16, width), f32),
            vmem((group + fsdp, 16, width), f32),
            vmem((16, width), f32),
            dma((batches, group)),
            dma((batches, group)),
            dma((group,)),
            dma((group,)),
            dma((batches, group, 2)),
            dma((batches, group, 2)),
            dma((4,)),
            dma((4,)),
            dma((fsdp,)),
            dma((fsdp,)),
            dma((tp,)),
            dma((tp,)),
            dma((fsdp,)),
            dma((fsdp,)),
            dma((group + fsdp,)),
            dma((group + fsdp,)),
            dma((2 + batches + 2 * parts,)),
            dma((4,)),
        ],
        compiler_params=pltpu.CompilerParams(
            vmem_limit_bytes=VMEM_LIMIT, collective_id=2, has_side_effects=True
        ),
        cost_estimate=pl.CostEstimate(
            flops=100_000_000_000, bytes_accessed=40_000_000, transcendentals=20_000_000
        ),
        name="backward_group",
    )(
        prefix,
        returned,
        enc_parts,
        packed,
        gathered,
        rows,
        qkv,
        wide,
        logs,
        tokens,
        steps,
        gain,
        after,
        encoder,
        stats,
    )


def local_heads(
    tokens,
    timesteps,
    time_table,
    prefix,
    encoder,
    self_qkv,
    cross_q,
    cross_kv,
    self_out,
    cross_out,
    ffn_up,
    ffn_down,
    norm_gain,
    norm_bias,
    cotangent,
):
    batches, chunk, width = tokens.shape
    group = 8
    length = group * chunk
    enc_count = encoder.shape[1]
    factor = HEAD_DIM ** (-0.5)
    ctx_index, tp_index = lax.axis_index("ctx"), lax.axis_index("tp")
    me = ctx_index * 4 + tp_index
    span = 1024
    piece = width // 4
    flip = lambda w: jnp.swapaxes(w, -1, -2)
    blocks = jnp.concatenate(
        [
            flip(self_qkv),
            flip(cross_q)[None],
            flip(cross_kv),
            self_out[None],
            cross_out[None],
            flip(ffn_up).reshape(4, piece, piece),
            ffn_down.reshape(4, piece, piece),
        ]
    )
    count = blocks.shape[0]
    half = piece // 2
    own_half = lax.dynamic_slice_in_dim(blocks, ctx_index * half, half, 1)
    gathered = lax.all_gather(own_half, ("fsdp", "ctx", "tp"), axis=0, tiled=False)
    gathered = gathered.reshape(4, 2, 4, count, half, piece)
    mine = own_half[:3].reshape(3 * HEAD_DIM, piece)
    fsdp_index = lax.axis_index("fsdp")
    steps_onehot = (timesteps[:, None] == lax.iota(jnp.int32, time_table.shape[0])[None, :]).astype(
        jnp.bfloat16
    )
    embedded = jnp.dot(steps_onehot, time_table, preferred_element_type=jnp.float32)[:, None, :]
    rows, qkv, wide, logs, contexts, head_weight = forward_group(
        prefix, tokens, embedded, norm_gain[:1], norm_bias[:1], mine, span, group, 4, 4
    )
    final, grad_after, returned, enc_parts, stats, packed = middle(
        gathered,
        tokens,
        embedded,
        encoder,
        cotangent,
        norm_gain,
        norm_bias,
        contexts,
        4,
    )
    outs = backward_group(
        prefix,
        returned,
        enc_parts,
        packed,
        gathered,
        rows,
        qkv,
        wide,
        logs,
        tokens,
        embedded,
        norm_gain[:1],
        grad_after,
        encoder,
        stats,
        span,
        4,
        4,
    )
    sums = outs[9]
    entries = (
        tokens.shape[0]
        * tokens.shape[1]
        * tokens.shape[2]
        * lax.axis_size("fsdp")
        * lax.axis_size("ctx")
        * lax.axis_size("tp")
    )
    return (
        final,
        *outs[:9],
        jnp.stack([sums[8], sums[4], sums[6]]),
        jnp.stack([sums[9], sums[5]]),
        sums[7],
        jnp.sqrt(jnp.sum(sums[:4], -1) / entries),
    )


def solution(mesh):
    placed = (
        P("fsdp", ("ctx", "tp"), None),
        P("fsdp"),
        P(),
        P("fsdp"),
        P("fsdp", None, None),
        P(None, "fsdp", "tp"),
        P("fsdp", "tp"),
        P(None, "fsdp", "tp"),
        P("tp", "fsdp"),
        P("tp", "fsdp"),
        P("fsdp", "tp"),
        P("tp", "fsdp"),
        P(),
        P(),
        P("fsdp", ("ctx", "tp"), None),
    )
    heads_fit = dict(mesh.shape) == {"fsdp": 4, "ctx": 2, "tp": 4}
    return jax.shard_map(
        local_heads if heads_fit else local,
        mesh=mesh,
        in_specs=placed,
        out_specs=(
            P("fsdp", ("ctx", "tp"), None),
            P("fsdp", ("ctx", "tp"), None),
            P("fsdp", ("ctx", "tp"), None),
            P(None, "fsdp", "tp"),
            P("fsdp", "tp"),
            P(None, "fsdp", "tp"),
            P("tp", "fsdp"),
            P("tp", "fsdp"),
            P("fsdp", "tp"),
            P("tp", "fsdp"),
            P(),
            P(),
            P(),
            P(),
        ),
        check_vma=False,
    )
```

```python
import functools
import math

import jax
import jax.numpy as jnp
from jax import lax
from jax.experimental import pallas as pl
from jax.experimental.pallas import tpu as pltpu
from jax.sharding import PartitionSpec as P

HEAD_DIM = 64


EPS = 1e-05
NEG = -1e30
ROOT_HALF = 1.0 / math.sqrt(2.0)
INV_ROOT_TWO_PI = 1.0 / math.sqrt(2.0 * math.pi)
VMEM_LIMIT = 62 * 2**20


def norm_rows(hidden, scaling, offsets):
    centre = hidden - jnp.mean(hidden, -1, keepdims=True)
    inverse = lax.rsqrt(jnp.mean(centre * centre, -1, keepdims=True) + EPS)
    unit_rows = centre * inverse
    return (unit_rows * scaling + offsets, unit_rows, inverse)


def norm_back(upstream, unit_rows, inverse, scaling):
    scaled = upstream * scaling
    result = inverse * (
        scaled
        - jnp.mean(scaled, -1, keepdims=True)
        - unit_rows * jnp.mean(scaled * unit_rows, -1, keepdims=True)
    )
    return (result, jnp.sum(upstream * unit_rows, (0, 1)), jnp.sum(upstream, (0, 1)))


def gelu_parts(inputs):
    normal_cdf = 0.5 * (1.0 + lax.erf(inputs * ROOT_HALF))
    return (
        inputs * normal_cdf,
        normal_cdf + inputs * jnp.exp(-0.5 * inputs * inputs) * INV_ROOT_TWO_PI,
    )


def spread_rows(rows):
    return lax.all_gather(rows, "tp", axis=1, tiled=True)


def spread_grads(grad_rows):
    return lax.all_gather(grad_rows, "tp", axis=1, tiled=True)


def finish_branch(local_in, local_weight):
    return lax.psum_scatter(
        jnp.einsum("scw,wd->scd", local_in, local_weight, preferred_element_type=jnp.float32),
        "tp",
        scatter_dimension=1,
        tiled=True,
    )


def finish_grad(local_grad, local_weight):
    return lax.psum_scatter(
        jnp.einsum("scw,dw->scd", local_grad, local_weight, preferred_element_type=jnp.float32),
        "tp",
        scatter_dimension=1,
        tiled=True,
    )


def block_scores(queries, key_block, query_pos, key_pos, lengths, factor):
    scores = (
        jnp.einsum("sqhe,skhe->sqhk", queries, key_block, preferred_element_type=jnp.float32)
        * factor
    )
    visible = (key_pos[None, None, :] <= query_pos[None, :, None]) | (
        key_pos[None, None, :] < lengths[:, None, None]
    )
    return jnp.where(visible[:, :, None, :], scores, NEG)


def attend_forward(queries, key_rows, value_rows, query_pos, lengths, key_span, factor):
    length = key_rows.shape[1]

    def attend_advance(running, offset):
        highest, totals, summed = running
        key_block = lax.dynamic_slice_in_dim(key_rows, offset, key_span, 1)
        value_block = lax.dynamic_slice_in_dim(value_rows, offset, key_span, 1)
        scores = block_scores(
            queries, key_block, query_pos, offset + lax.iota(jnp.int32, key_span), lengths, factor
        )
        new_high = jnp.maximum(highest, jnp.max(scores, -1))
        weights = jnp.exp(scores - new_high[..., None])
        fading = jnp.exp(highest - new_high)
        totals = totals * fading + jnp.sum(weights, -1)
        summed = summed * fading[..., None] + jnp.einsum(
            "sqhk,skhe->sqhe",
            weights.astype(jnp.bfloat16),
            value_block,
            preferred_element_type=jnp.float32,
        )
        return ((new_high, totals, summed), None)

    stat_shape = queries.shape[:3]
    initial = (
        jnp.full(stat_shape, NEG, jnp.float32),
        jnp.zeros(stat_shape, jnp.float32),
        jnp.zeros(queries.shape, jnp.float32),
    )
    offsets = jnp.arange(length // key_span, dtype=jnp.int32) * key_span
    (highest, totals, summed), unused = lax.scan(attend_advance, initial, offsets)
    return (summed / totals[..., None], highest + jnp.log(totals))


def attend_block(
    queries,
    grad_out,
    log_rows,
    delta_rows,
    key_block,
    value_block,
    query_pos,
    key_pos,
    lengths,
    factor,
):
    scores = block_scores(queries, key_block, query_pos, key_pos, lengths, factor)
    probs = jnp.exp(scores - log_rows[..., None])
    grad_probs = jnp.einsum(
        "sqhe,skhe->sqhk", grad_out, value_block, preferred_element_type=jnp.float32
    )
    grad_scores = (probs * (grad_probs - delta_rows[..., None])).astype(jnp.bfloat16)
    return (probs.astype(jnp.bfloat16), grad_scores)


def key_sweep(
    queries,
    grad_out,
    log_rows,
    delta_rows,
    key_rows,
    value_rows,
    query_pos,
    lengths,
    key_span,
    factor,
):
    batches, row_count, head_count, head_depth = queries.shape
    length = key_rows.shape[1]

    def key_advance(grad_query, offset):
        key_block = lax.dynamic_slice_in_dim(key_rows, offset, key_span, 1)
        value_block = lax.dynamic_slice_in_dim(value_rows, offset, key_span, 1)
        key_pos = offset + lax.iota(jnp.int32, key_span)
        probs_low, grad_scores = attend_block(
            queries,
            grad_out,
            log_rows,
            delta_rows,
            key_block,
            value_block,
            query_pos,
            key_pos,
            lengths,
            factor,
        )
        grad_query = (
            grad_query
            + jnp.einsum(
                "sqhk,skhe->sqhe", grad_scores, key_block, preferred_element_type=jnp.float32
            )
            * factor
        )
        grad_key = (
            jnp.einsum("sqhk,sqhe->kshe", grad_scores, queries, preferred_element_type=jnp.float32)
            * factor
        )
        grad_value = jnp.einsum(
            "sqhk,sqhe->kshe", probs_low, grad_out, preferred_element_type=jnp.float32
        )
        return (grad_query, (grad_key, grad_value))

    offsets = jnp.arange(length // key_span, dtype=jnp.int32) * key_span
    grad_query, stacked = lax.scan(key_advance, jnp.zeros(queries.shape, jnp.float32), offsets)
    flat_shape = (length, batches, head_count * head_depth)
    return (grad_query, stacked[0].reshape(flat_shape), stacked[1].reshape(flat_shape))


def local(
    tokens,
    timesteps,
    time_table,
    prefix,
    encoder,
    self_qkv,
    cross_q,
    cross_kv,
    self_out,
    cross_out,
    ffn_up,
    ffn_down,
    norm_gain,
    norm_bias,
    cotangent,
):
    proj_self, proj_query, proj_pair, back_self, back_cross, expand_full, shrink_full = (
        lax.all_gather(self_qkv, "fsdp", axis=1, tiled=True),
        lax.all_gather(cross_q, "fsdp", axis=0, tiled=True),
        lax.all_gather(cross_kv, "fsdp", axis=1, tiled=True),
        lax.all_gather(self_out, "fsdp", axis=1, tiled=True),
        lax.all_gather(cross_out, "fsdp", axis=1, tiled=True),
        lax.all_gather(ffn_up, "fsdp", axis=0, tiled=True),
        lax.all_gather(ffn_down, "fsdp", axis=1, tiled=True),
    )
    batches = tokens.shape[0]
    model_width = tokens.shape[2]
    local_width = proj_query.shape[1]
    head_count = local_width // HEAD_DIM
    factor = HEAD_DIM ** (-0.5)
    ctx_index = lax.axis_index("ctx")
    local_stack = jnp.transpose(proj_self, (1, 0, 2)).reshape(model_width, 3 * local_width)
    steps_onehot = (timesteps[:, None] == lax.iota(jnp.int32, time_table.shape[0])[None, :]).astype(
        jnp.bfloat16
    )
    embedded = jnp.dot(steps_onehot, time_table, preferred_element_type=jnp.float32)
    start_sum = tokens.astype(jnp.float32) + embedded[:, None, :]
    normed_one, unit_one, inverse_one = norm_rows(start_sum, norm_gain[0], norm_bias[0])
    rows_self = spread_rows(normed_one.astype(jnp.bfloat16))
    row_count = rows_self.shape[1]
    head_shape = (batches, row_count, head_count, HEAD_DIM)
    projected = jnp.einsum(
        "scd,kdw->kscw", rows_self, proj_self, preferred_element_type=jnp.float32
    ).astype(jnp.bfloat16)
    queries, key_local, value_local = (projected[0], projected[1], projected[2])
    key_all, value_all = (
        lax.all_gather(key_local, "ctx", axis=1, tiled=True),
        lax.all_gather(value_local, "ctx", axis=1, tiled=True),
    )
    length = key_all.shape[1]
    key_span = min(512, length)
    query_pos = ctx_index * row_count + lax.iota(jnp.int32, row_count)
    keys_four = key_all.reshape(batches, length, head_count, HEAD_DIM)
    values_four = value_all.reshape(batches, length, head_count, HEAD_DIM)
    queries_four = queries.reshape(head_shape)
    attended, log_total = attend_forward(
        queries_four, keys_four, values_four, query_pos, prefix, key_span, factor
    )
    context_one = attended.reshape(batches, row_count, local_width).astype(jnp.bfloat16)
    branch_one = finish_branch(context_one, back_self)
    after_one = start_sum + branch_one
    normed_two, unit_two, inverse_two = norm_rows(after_one, norm_gain[1], norm_bias[1])
    rows_cross = spread_rows(normed_two.astype(jnp.bfloat16))
    cross_queries = jnp.einsum(
        "scd,dw->scw", rows_cross, proj_query, preferred_element_type=jnp.float32
    ).astype(jnp.bfloat16)
    enc_pair = jnp.einsum(
        "sed,kdw->ksew", encoder, proj_pair, preferred_element_type=jnp.float32
    ).astype(jnp.bfloat16)
    enc_count = encoder.shape[1]
    cross_keys = enc_pair[0].reshape(batches, enc_count, head_count, HEAD_DIM)
    cross_values = enc_pair[1].reshape(batches, enc_count, head_count, HEAD_DIM)
    cross_four = cross_queries.reshape(head_shape)
    cross_probs = jax.nn.softmax(
        jnp.einsum("sqhe,skhe->sqhk", cross_four, cross_keys, preferred_element_type=jnp.float32)
        * factor,
        axis=-1,
    )
    cross_low = cross_probs.astype(jnp.bfloat16)
    context_two = (
        jnp.einsum("sqhk,skhe->sqhe", cross_low, cross_values, preferred_element_type=jnp.float32)
        .reshape(batches, row_count, local_width)
        .astype(jnp.bfloat16)
    )
    branch_two = finish_branch(context_two, back_cross)
    after_two = after_one + branch_two
    normed_three, unit_three, inverse_three = norm_rows(after_two, norm_gain[2], norm_bias[2])
    rows_ffn = spread_rows(normed_three.astype(jnp.bfloat16))
    pre_act = jnp.einsum("scd,df->scf", rows_ffn, expand_full, preferred_element_type=jnp.float32)
    activated, slopes = gelu_parts(pre_act)
    hidden_low = activated.astype(jnp.bfloat16)
    branch_three = finish_branch(hidden_low, shrink_full)
    final_sum = after_two + branch_three
    grad_three = spread_grads(cotangent)
    grad_shrink = jnp.einsum(
        "scf,scd->fd", hidden_low, grad_three, preferred_element_type=jnp.float32
    )
    grad_pre = (
        jnp.einsum("scd,fd->scf", grad_three, shrink_full, preferred_element_type=jnp.float32)
        * slopes
    ).astype(jnp.bfloat16)
    grad_expand = jnp.einsum("scd,scf->df", rows_ffn, grad_pre, preferred_element_type=jnp.float32)
    back_three, gain_three, shift_three = norm_back(
        finish_grad(grad_pre, expand_full), unit_three, inverse_three, norm_gain[2]
    )
    grad_after_two = cotangent.astype(jnp.float32) + back_three
    grad_two = spread_grads(grad_after_two.astype(jnp.bfloat16))
    grad_back_cross = jnp.einsum(
        "scw,scd->wd", context_two, grad_two, preferred_element_type=jnp.float32
    )
    grad_context_two = jnp.einsum(
        "scd,wd->scw", grad_two, back_cross, preferred_element_type=jnp.float32
    ).astype(jnp.bfloat16)
    grad_cross_four = grad_context_two.reshape(head_shape)
    grad_cross_probs = jnp.einsum(
        "sqhe,skhe->sqhk", grad_cross_four, cross_values, preferred_element_type=jnp.float32
    )
    grad_cross_scores = (
        cross_probs
        * (grad_cross_probs - jnp.sum(cross_probs * grad_cross_probs, -1, keepdims=True))
    ).astype(jnp.bfloat16)
    grad_cross_q = (
        (
            jnp.einsum(
                "sqhk,skhe->sqhe", grad_cross_scores, cross_keys, preferred_element_type=jnp.float32
            )
            * factor
        )
        .reshape(batches, row_count, local_width)
        .astype(jnp.bfloat16)
    )
    part_keys = (
        jnp.einsum(
            "sqhk,sqhe->skhe", grad_cross_scores, cross_four, preferred_element_type=jnp.float32
        )
        * factor
    ).reshape(batches, enc_count, local_width)
    part_values = jnp.einsum(
        "sqhk,sqhe->skhe", cross_low, grad_cross_four, preferred_element_type=jnp.float32
    ).reshape(batches, enc_count, local_width)
    enc_keys, enc_values = (
        lax.psum_scatter(part_keys, "ctx", scatter_dimension=1, tiled=True),
        lax.psum_scatter(part_values, "ctx", scatter_dimension=1, tiled=True),
    )
    enc_keys = enc_keys.astype(jnp.bfloat16)
    enc_values = enc_values.astype(jnp.bfloat16)
    enc_share = enc_keys.shape[1]
    enc_rows = lax.dynamic_slice_in_dim(encoder, ctx_index * enc_share, enc_share, 1)
    grad_pair = jnp.stack(
        [
            jnp.einsum("sed,sew->dw", enc_rows, enc_keys, preferred_element_type=jnp.float32),
            jnp.einsum("sed,sew->dw", enc_rows, enc_values, preferred_element_type=jnp.float32),
        ]
    )
    encoder_grad = lax.psum_scatter(
        jnp.einsum("sew,dw->sed", enc_keys, proj_pair[0], preferred_element_type=jnp.float32)
        + jnp.einsum("sew,dw->sed", enc_values, proj_pair[1], preferred_element_type=jnp.float32),
        "tp",
        scatter_dimension=1,
        tiled=True,
    )
    grad_query_proj = jnp.einsum(
        "scd,scw->dw", rows_cross, grad_cross_q, preferred_element_type=jnp.float32
    )
    back_two, gain_two, shift_two = norm_back(
        finish_grad(grad_cross_q, proj_query), unit_two, inverse_two, norm_gain[1]
    )
    grad_after_one = grad_after_two + back_two
    grad_one = spread_grads(grad_after_one.astype(jnp.bfloat16))
    grad_back_self = jnp.einsum(
        "scw,scd->wd", context_one, grad_one, preferred_element_type=jnp.float32
    )
    grad_context_one = jnp.einsum(
        "scd,wd->scw", grad_one, back_self, preferred_element_type=jnp.float32
    ).astype(jnp.bfloat16)
    grad_ctx_four = grad_context_one.reshape(head_shape)
    delta_rows = jnp.sum(grad_ctx_four.astype(jnp.float32) * attended, -1)
    grad_query, grad_key_all, grad_value_all = key_sweep(
        queries_four,
        grad_ctx_four,
        log_total,
        delta_rows,
        keys_four,
        values_four,
        query_pos,
        prefix,
        key_span,
        factor,
    )
    own_keys, own_values = (
        lax.psum_scatter(grad_key_all, "ctx", scatter_dimension=0, tiled=True),
        lax.psum_scatter(grad_value_all, "ctx", scatter_dimension=0, tiled=True),
    )
    own_keys = jnp.transpose(own_keys, (1, 0, 2))
    own_values = jnp.transpose(own_values, (1, 0, 2))
    grad_joined = jnp.concatenate(
        [grad_query.reshape(batches, row_count, local_width), own_keys, own_values], -1
    ).astype(jnp.bfloat16)
    grad_proj_self = jnp.transpose(
        jnp.einsum(
            "scd,scw->dw", rows_self, grad_joined, preferred_element_type=jnp.float32
        ).reshape(model_width, 3, local_width),
        (1, 0, 2),
    )
    back_one, gain_one, shift_one = norm_back(
        finish_grad(grad_joined, local_stack), unit_one, inverse_one, norm_gain[0]
    )
    input_grad = grad_after_one + back_one
    shard_grads = (
        lax.psum_scatter(grad_proj_self, "fsdp", scatter_dimension=1, tiled=True),
        lax.psum_scatter(grad_query_proj, "fsdp", scatter_dimension=0, tiled=True),
        lax.psum_scatter(grad_pair, "fsdp", scatter_dimension=1, tiled=True),
        lax.psum_scatter(grad_back_self, "fsdp", scatter_dimension=1, tiled=True),
        lax.psum_scatter(grad_back_cross, "fsdp", scatter_dimension=1, tiled=True),
        lax.psum_scatter(grad_expand, "fsdp", scatter_dimension=0, tiled=True),
        lax.psum_scatter(grad_shrink, "fsdp", scatter_dimension=1, tiled=True),
    )
    full_grads = lax.psum(
        (
            shard_grads[0],
            shard_grads[1],
            shard_grads[2],
            shard_grads[3],
            shard_grads[4],
            shard_grads[5],
            shard_grads[6],
        ),
        "ctx",
    )
    squares = jnp.stack(
        [
            jnp.sum(final_sum * final_sum),
            jnp.sum(branch_one * branch_one),
            jnp.sum(branch_two * branch_two),
            jnp.sum(branch_three * branch_three),
        ]
    )
    gain_grad, bias_grad, square_totals = lax.psum(
        (
            jnp.stack([gain_one, gain_two, gain_three]),
            jnp.stack([shift_one, shift_two, shift_three]),
            squares,
        ),
        ("fsdp", "ctx", "tp"),
    )
    entries = (
        tokens.shape[0]
        * tokens.shape[1]
        * tokens.shape[2]
        * lax.axis_size("fsdp")
        * lax.axis_size("ctx")
        * lax.axis_size("tp")
    )
    norms = jnp.sqrt(square_totals / entries)
    return (
        final_sum,
        input_grad,
        encoder_grad,
        full_grads[0],
        full_grads[1],
        full_grads[2],
        full_grads[3],
        full_grads[4],
        full_grads[5],
        full_grads[6],
        gain_grad,
        bias_grad[:2],
        bias_grad[2],
        norms,
    )


def dot_of(left, right, left_dim, right_dim):
    return lax.dot_general(
        left, right, (((left_dim,), (right_dim,)), ((), ())), preferred_element_type=jnp.float32
    )


def bounds(prefix, start, query_span, key_span):
    whole = jnp.maximum(prefix, start + 1) // key_span
    every = (jnp.maximum(prefix, start + query_span) + key_span - 1) // key_span
    return whole, every


def hide(scores, limit, offset):
    return jnp.where(lax.broadcasted_iota(jnp.int32, scores.shape, 0) < limit - offset, scores, NEG)


def low(value):
    return value.astype(jnp.bfloat16)


STRIP = 64


def in_strips(work, *values, strip=STRIP, axis=0):
    count = values[0].shape[axis] // strip
    cut = lambda v, n: lax.slice_in_dim(v, n * strip, (n + 1) * strip, axis=axis)
    parts = [work(*[cut(v, n) for v in values]) for n in range(count)]
    return tuple(jnp.concatenate(p, axis) for p in zip(*parts))


def gelu_strip(inputs):
    activated, slopes = gelu_parts(inputs)
    return low(activated), slopes


def rows_unit(hidden):
    centre = hidden - jnp.mean(hidden, -1, keepdims=True)
    inverse = lax.rsqrt(jnp.mean(centre * centre, -1, keepdims=True) + EPS)
    return centre * inverse, inverse


def rows_norm(hidden, scaling, offsets):
    def strip(rows):
        unit_rows, inverse = rows_unit(rows)
        return low(unit_rows * scaling + offsets), unit_rows, inverse

    return in_strips(strip, hidden)


def rows_back(upstream, unit_rows, inverse, scaling):
    sums = [jnp.zeros((8, upstream.shape[1]), jnp.float32)] * 2

    def strip(rows, units, inverses):
        scaled = rows * scaling
        for n, term in enumerate((rows * units, rows)):
            sums[n] = sums[n] + jnp.sum(term.reshape(-1, 8, term.shape[1]), 0)
        return (
            inverses
            * (
                scaled
                - jnp.mean(scaled, -1, keepdims=True)
                - units * jnp.mean(scaled * units, -1, keepdims=True)
            ),
        )

    (result,) = in_strips(strip, upstream, unit_rows, inverse)
    return result, jnp.sum(sums[0], 0, keepdims=True), jnp.sum(sums[1], 0, keepdims=True)


MESH = pl.DeviceIdType.MESH


def meet(group, tp, fsdp):
    here, core, chip = lax.axis_index("fsdp"), lax.axis_index("ctx"), lax.axis_index("tp")
    me = core * tp + chip
    barrier = pltpu.get_barrier_semaphore()
    for k in range(1, group):
        other = me ^ k
        pl.semaphore_signal(
            barrier, inc=1, device_id={"ctx": other // tp, "tp": other % tp}, device_id_type=MESH
        )
    for k in range(1, fsdp):
        pl.semaphore_signal(barrier, inc=1, device_id={"fsdp": here ^ k}, device_id_type=MESH)
    pl.semaphore_wait(barrier, group - 1 + fsdp - 1)


def forward_kernel(
    prefix_ref,
    tokens_ref,
    step_ref,
    gain_ref,
    bias_ref,
    mine_ref,
    rows_out,
    qkv_ref,
    wide_ref,
    log_ref,
    ctx_ref,
    weight,
    rows_ref,
    other_ref,
    columns,
    pair_ref,
    keys_ref,
    values_ref,
    low_ref,
    landing,
    w_send,
    w_recv,
    v_send,
    v_recv,
    x_send,
    x_recv,
    c_send,
    c_recv,
    keep_sem,
    *,
    span,
    tp,
    fsdp,
):
    batches, chunk, width = tokens_ref.shape
    group = rows_ref.shape[0]
    length = group * chunk
    blocks, ratio = length // span, span // chunk
    wide_blocks = max(1, length // 2 // span)
    factor = HEAD_DIM**-0.5
    here, core, chip = lax.axis_index("fsdp"), lax.axis_index("ctx"), lax.axis_index("tp")
    me = core * tp + chip
    mine = chip // 2
    inner = (chip == 1) | (chip == 2)
    other_inner, other_outer = 2 - mine, 3 - 3 * mine
    meet(group, tp, fsdp)

    def send_to(source, target, send, recv, **place):
        return pltpu.make_async_remote_copy(
            src_ref=source,
            dst_ref=target,
            send_sem=send,
            recv_sem=recv,
            device_id=place,
            device_id_type=MESH,
        )

    v_core, v_chip = chip % 2, chip // 2 + 2 * core
    v_own = (v_core == core) & (v_chip == chip)
    v_copy = send_to(mine_ref, pair_ref, v_send.at[0], v_recv.at[0], ctx=v_core, tp=v_chip)

    @pl.when(v_own)
    def keep_pair():
        pair_ref[...] = mine_ref[...]

    @pl.when(jnp.logical_not(v_own))
    def send_pair():
        v_copy.start()

    comes = (chip // 2 != core) | (2 * (chip % 2) + core != chip)

    def w_copy(k):
        return send_to(pair_ref, columns.at[k], w_send.at[k], w_recv.at[k], fsdp=here ^ k)

    def normalise(seq, target, at):
        start_sum = tokens_ref[seq].astype(jnp.float32) + step_ref[seq]
        target[at] = rows_norm(start_sum, gain_ref[...], bias_ref[...])[0]

    def x_copy(kind):
        block = rows_ref.at[me]
        near = rows_ref.at[core * tp + (chip ^ 1)]
        second = rows_ref.at[core * tp + other_inner]
        third = rows_ref.at[core * tp + other_outer]
        source, place, target = (
            (block, me, {"tp": chip ^ 1}),
            (other_ref.at[0], me, {"tp": other_inner}),
            (block, me, {"ctx": 1 - core}),
            (near, core * tp + (chip ^ 1), {"ctx": 1 - core}),
            (second, core * tp + other_inner, {"ctx": 1 - core}),
            (third, core * tp + other_outer, {"ctx": 1 - core}),
            (second, core * tp + other_inner, {"tp": chip ^ 1}),
            (third, core * tp + other_outer, {"tp": chip ^ 1}),
            (other_ref.at[0], me, {"tp": other_outer}),
        )[kind]
        return send_to(source, rows_ref.at[place], x_send.at[kind], x_recv.at[place], **target)

    def x_wait(place):
        send_to(
            rows_ref.at[place], rows_ref.at[place], x_send.at[0], x_recv.at[place], ctx=1 - core
        ).wait_recv()

    def arrive(number):
        x_wait(core * tp + (chip ^ 1, other_inner, other_outer)[number])
        if number:

            @pl.when(inner & (core == 0))
            def onward():
                x_copy(5 + number).start()

        x_copy(3 + number).start()

    normalise(mine, rows_ref, me)
    normalise(1 - mine, other_ref, 0)

    @pl.when(core == 0)
    def first_half():
        x_copy(2).start()

        @pl.when(inner)
        def from_inner():
            x_copy(1).start()
            x_copy(0).start()

        @pl.when(jnp.logical_not(inner))
        def from_outer():
            x_copy(0).start()

    @pl.when(comes)
    def pair_here():
        v_copy.wait_recv()

    for k in range(1, fsdp):
        w_copy(k).start()
    values_ref[:, HEAD_DIM:, :] = jnp.ones_like(values_ref[:, HEAD_DIM:, :])

    def project(place, unused):
        rows = rows_ref[place]
        joined = low(dot_of(weight[...], rows, 1, 1))
        at = pl.ds(pl.multiple_of(place * chunk, chunk), chunk)
        for head in range(2):
            queries, keys, values = (
                joined[(3 * head + n) * HEAD_DIM : (3 * head + n + 1) * HEAD_DIM] for n in range(3)
            )
            qkv_ref[head, :HEAD_DIM, at] = queries * jnp.bfloat16(factor)
            qkv_ref[head, HEAD_DIM : 2 * HEAD_DIM, at] = keys
            qkv_ref[head, 2 * HEAD_DIM :, at] = values
            values_ref[head, :HEAD_DIM, at] = values
            keys_ref[head, at, :] = keys.T
        return unused

    @pl.when(core == 0)
    def first_lines():
        @pl.when(jnp.logical_not(inner))
        def then_other():
            x_copy(0).wait_send()
            x_copy(1).start()

        for number in range(3):
            arrive(number)

    @pl.when(core == 1)
    def second_lines():
        for place in range(tp):
            x_wait(place)
        for kind in (2, 1, 8, 0):
            x_copy(kind).start()

    piece = mine_ref.shape[1]
    for k in range(fsdp):
        if k:
            w_copy(k).wait_recv()
        part = columns[k] if k else pair_ref[...]
        for f in range(fsdp):

            @pl.when((here ^ k) == f)
            def place(f=f, part=part):
                weight[:, f * piece : (f + 1) * piece] = part

    lax.fori_loop(0, tp, project, 0)

    def c_copy(head, place):
        return send_to(
            low_ref.at[head, place],
            landing.at[head, me],
            c_send.at[head, place],
            c_recv.at[head, me],
            ctx=place // tp,
            tp=place % tp,
        )

    def c_wait(head, place):
        send_to(
            low_ref.at[head, place],
            landing.at[head, place],
            c_send.at[head, place],
            c_recv.at[head, place],
            ctx=place // tp,
            tp=place % tp,
        ).wait_recv()

    def attend(index, unused):
        block, head = index // 2, index % 2

        @pl.when((core == 1) & (index == 3))
        def near_lines():
            arrive(0)

        @pl.when(index == 4)
        def second_half():
            @pl.when(core == 0)
            def wait_other():
                for place in range(tp, group):
                    x_wait(place)

            @pl.when(core == 1)
            def far_lines():
                arrive(1)
                arrive(2)

            lax.fori_loop(tp, group, project, 0)

        start = pl.multiple_of(block * span, span)
        queries = qkv_ref[head, :HEAD_DIM, pl.ds(start, span)]
        limit = jnp.maximum(
            prefix_ref[mine], start + 1 + lax.broadcasted_iota(jnp.int32, (1, span), 1)
        )

        def advance(other, carry, masked):
            highest, total = carry
            offset = pl.multiple_of(other * span, span)
            scores = dot_of(keys_ref[head, pl.ds(offset, span), :], queries, 1, 0)
            if masked:
                scores = hide(scores, limit, offset)
            higher = jnp.maximum(highest, jnp.max(scores, axis=0, keepdims=True))
            weights = low(jnp.exp(scores - higher))
            fading = jnp.exp(highest - higher)
            total = total * fading + dot_of(
                values_ref[head, :, pl.ds(offset, span)], weights, 1, 0
            )
            return higher, total

        carry = (
            jnp.full((1, span), NEG, jnp.float32),
            jnp.zeros((values_ref.shape[1], span), jnp.float32),
        )
        carry = lax.fori_loop(0, block, lambda j, c: advance(j, c, False), carry)
        highest, total = lax.fori_loop(
            block, jnp.maximum(block + 1, wide_blocks), lambda j, c: advance(j, c, True), carry
        )
        weight_sum = total[HEAD_DIM : HEAD_DIM + 1, :]
        attended = total[:HEAD_DIM, :] / weight_sum
        wide_ref[head, :, pl.ds(start, span)] = attended
        log_ref[head, :, pl.ds(start, span)] = highest + jnp.log(weight_sum)
        attended = low(attended)
        for part in range(ratio):
            place = block * ratio + part
            low_ref[head, place] = attended[:, part * chunk : (part + 1) * chunk]

            @pl.when(place != me)
            def send(place=place):
                c_copy(head, place).start()

        return unused

    lax.fori_loop(0, 2 * blocks, attend, 0)
    keep = pltpu.make_async_copy(rows_ref, rows_out, keep_sem)
    keep.start()
    for head in range(2):

        def collect(k, unused, head=head):
            c_wait(head, me ^ k)
            ctx_ref[head, me ^ k] = landing[head, me ^ k]
            return unused

        lax.fori_loop(1, group, collect, 0)
        ctx_ref[head, me] = low_ref[head, me]
    for k in range(1, fsdp):
        w_copy(k).wait_send()

    @pl.when(jnp.logical_not(v_own))
    def pair_sent():
        v_copy.wait_send()

    for kind in range(1, 6):
        x_copy(kind).wait_send()

    @pl.when(inner | (core == 1))
    def own_sent():
        x_copy(0).wait_send()

    @pl.when(inner & (core == 0))
    def lines_sent():
        x_copy(6).wait_send()
        x_copy(7).wait_send()

    @pl.when(core == 1)
    def direct_sent():
        x_copy(8).wait_send()

    for head in range(2):

        def sent(k, unused, head=head):
            c_copy(head, me ^ k).wait_send()
            return unused

        lax.fori_loop(1, group, sent, 0)
    keep.wait()


def forward_group(prefix, tokens, steps, gain, bias, mine, span, group, tp, fsdp):
    batches, chunk, width = tokens.shape
    length = group * chunk
    bf16, f32 = jnp.bfloat16, jnp.float32
    struct = jax.ShapeDtypeStruct
    inside = pl.BlockSpec(memory_space=pltpu.VMEM)
    dma = pltpu.SemaphoreType.DMA
    return pl.pallas_call(
        functools.partial(forward_kernel, span=span, tp=tp, fsdp=fsdp),
        in_specs=[pl.BlockSpec(memory_space=pltpu.SMEM)] + [inside] * 5,
        out_specs=[pl.BlockSpec(memory_space=pl.ANY)] + [inside] * 5,
        out_shape=[
            struct((group, chunk, width), bf16),
            struct((2, 3 * HEAD_DIM, length), bf16),
            struct((2, HEAD_DIM, length), f32),
            struct((2, 1, length), f32),
            struct((2, group, HEAD_DIM, chunk), bf16),
            struct((6 * HEAD_DIM, width), bf16),
        ],
        scratch_shapes=[
            pltpu.VMEM((group, chunk, width), bf16),
            pltpu.VMEM((1, chunk, width), bf16),
            pltpu.VMEM((fsdp,) + mine.shape, bf16),
            pltpu.VMEM(mine.shape, bf16),
            pltpu.VMEM((2, length, HEAD_DIM), bf16),
            pltpu.VMEM((2, HEAD_DIM + 16, length), bf16),
            pltpu.VMEM((2, group, HEAD_DIM, chunk), bf16),
            pltpu.VMEM((2, group, HEAD_DIM, chunk), bf16),
            dma((fsdp,)),
            dma((fsdp,)),
            dma((1,)),
            dma((1,)),
            dma((9,)),
            dma((group,)),
            dma((2, group)),
            dma((2, group)),
            dma,
        ],
        compiler_params=pltpu.CompilerParams(
            vmem_limit_bytes=VMEM_LIMIT, collective_id=1, has_side_effects=True
        ),
        cost_estimate=pl.CostEstimate(
            flops=60_000_000_000, bytes_accessed=30_000_000, transcendentals=20_000_000
        ),
        name="forward_group",
    )(prefix, tokens, steps, gain, bias, mine)


QUERY, KEY, VALUE, SELF_OUT, CROSS_OUT, UP, DOWN = 0, 1, 2, 3, 4, 5, 9


def middle_kernel(
    gathered,
    tokens_ref,
    step_ref,
    enc_ref,
    cot_ref,
    gain_ref,
    bias_ref,
    ctx_ref,
    final_ref,
    after_ref,
    back_ref,
    enc_grad_ref,
    stats_ref,
    packed_ref,
    weights,
    totals,
    context,
    queries,
    keys,
    values,
    probs,
    context_two,
    grad_heads,
    grad_queries,
    grad_keys,
    grad_values,
    back_rows,
    landing,
    d_send,
    d_recv,
    sem,
    *,
    tp,
    fsdp,
):
    batches, chunk, width = tokens_ref.shape
    group = landing.shape[1]
    core, chip = lax.axis_index("ctx"), lax.axis_index("tp")
    me = core * tp + chip
    mine = chip // 2
    meet(group, tp, fsdp)
    piece = gathered.shape[-1]
    factor = HEAD_DIM**-0.5
    heads = width // HEAD_DIM

    copies = []
    for f in range(width // piece):
        for c in range(group // tp):
            for t in range(tp):
                head = t * (group // tp) + c
                copies.append(
                    pltpu.make_async_copy(
                        gathered.at[f, c, t, pl.ds(3, weights.shape[0])],
                        weights.at[:, pl.ds(head * HEAD_DIM, HEAD_DIM), pl.ds(f * piece, piece)],
                        sem.at[(f * group // tp + c) * tp + t],
                    )
                )
    for copy in copies:
        copy.start()
    totals[...] = jnp.zeros_like(totals)
    stats_ref[...] = jnp.zeros_like(stats_ref)
    for copy in copies:
        copy.wait()

    owners = [(2 * (2 * z + c) + n, n, c * tp + z) for z in (0, 1) for c in (0, 1) for n in (0, 1)]

    def d_copy(turn, seq, head, number, owner):
        return pltpu.make_async_remote_copy(
            src_ref=back_rows.at[turn, pl.ds(head * HEAD_DIM, HEAD_DIM)],
            dst_ref=landing.at[number, me],
            send_sem=d_send.at[turn, head],
            recv_sem=d_recv.at[number, me],
            device_id={"ctx": owner // tp, "tp": owner % tp + 2 * seq},
            device_id_type=MESH,
        )

    def one_sequence(turn, unused):
        seq = jnp.where(turn == 0, 1 - mine, mine)
        for head, number, owner in owners:
            context[head * HEAD_DIM : (head + 1) * HEAD_DIM, :] = ctx_ref[number, owner + 2 * seq]
        start_sum = tokens_ref[seq].astype(jnp.float32) + step_ref[seq]
        branch_one = dot_of(context[...], weights[SELF_OUT], 0, 0)
        after_one = start_sum + branch_one
        stats_ref[1:2, :] += jnp.sum(branch_one * branch_one, 0, keepdims=True)
        normed_two, unit_two, inverse_two = rows_norm(after_one, gain_ref[1:2], bias_ref[1:2])
        queries[...] = low(dot_of(weights[QUERY], normed_two, 1, 1))
        keys[...] = low(dot_of(weights[KEY], enc_ref[seq], 1, 1))
        values[...] = low(dot_of(weights[VALUE], enc_ref[seq], 1, 1))

        def attend(head, unused):
            rows = pl.ds(pl.multiple_of(head * HEAD_DIM, HEAD_DIM), HEAD_DIM)
            scores = dot_of(keys[rows, :].T, queries[rows, :], 1, 0) * factor

            def strip(columns):
                powers = jnp.exp(columns - jnp.max(columns, 0, keepdims=True))
                return (powers / jnp.sum(powers, 0, keepdims=True),)

            (attn,) = in_strips(strip, scores, strip=128, axis=1)
            probs[head] = attn
            context_two[rows, :] = low(dot_of(values[rows, :], low(attn), 1, 0))
            return unused

        lax.fori_loop(0, heads, attend, 0, unroll=8)
        branch_two = dot_of(context_two[...], weights[CROSS_OUT], 0, 0)
        after_two = after_one + branch_two
        stats_ref[2:3, :] += jnp.sum(branch_two * branch_two, 0, keepdims=True)
        normed_three, unit_three, inverse_three = rows_norm(after_two, gain_ref[2:3], bias_ref[2:3])
        grad_three = cot_ref[seq]

        def feed(part, carry):
            branch, grad = carry
            up, down = weights[UP + part], weights[DOWN + part]
            inputs = dot_of(up, normed_three, 1, 1)
            hidden, slopes = in_strips(gelu_strip, inputs, strip=32)
            branch = branch + dot_of(hidden, down, 0, 0)
            totals[DOWN - 2 + part] += dot_of(hidden, grad_three, 1, 0)
            grad_pre = low(dot_of(down, grad_three, 1, 1) * slopes)
            totals[UP - 2 + part] += dot_of(grad_pre, normed_three, 1, 0)
            return branch, grad + dot_of(grad_pre, up, 0, 0)

        blank = jnp.zeros((chunk, width), jnp.float32)
        branch_three, grad_norm = lax.fori_loop(0, DOWN - UP, feed, (blank, blank), unroll=4)
        final_sum = after_two + branch_three
        final_ref[seq] = final_sum
        stats_ref[0:1, :] += jnp.sum(final_sum * final_sum, 0, keepdims=True)
        stats_ref[3:4, :] += jnp.sum(branch_three * branch_three, 0, keepdims=True)
        back, gain_sum, bias_sum = rows_back(grad_norm, unit_three, inverse_three, gain_ref[2:3])
        stats_ref[6:7, :] += gain_sum
        stats_ref[7:8, :] += bias_sum
        grad_after_two = grad_three.astype(jnp.float32) + back
        grad_two = low(grad_after_two)
        totals[2] += dot_of(context_two[...], grad_two, 1, 0)
        grad_heads[...] = low(dot_of(weights[CROSS_OUT], grad_two, 1, 1))

        def attend_back(head, unused):
            rows = pl.ds(pl.multiple_of(head * HEAD_DIM, HEAD_DIM), HEAD_DIM)
            grads = grad_heads[rows, :]
            attn = probs[head]
            grad_probs = dot_of(values[rows, :].T, grads, 1, 0)

            def strip(ones, others):
                return (low(ones * (others - jnp.sum(ones * others, 0, keepdims=True))),)

            (grad_scores,) = in_strips(strip, attn, grad_probs, strip=128, axis=1)
            grad_queries[rows, :] = low(dot_of(keys[rows, :], grad_scores, 1, 0) * factor)
            grad_keys[rows, :] = dot_of(queries[rows, :], grad_scores, 1, 1) * factor
            grad_values[rows, :] = dot_of(grads, low(attn), 1, 1)
            return unused

        lax.fori_loop(0, heads, attend_back, 0, unroll=8)
        enc_grad_ref[seq, :, :width] = low(grad_keys[...].T)
        enc_grad_ref[seq, :, width:] = low(grad_values[...].T)
        totals[0] += dot_of(grad_queries[...], normed_two, 1, 0)
        upstream = dot_of(grad_queries[...], weights[QUERY], 0, 0)
        back, gain_sum, bias_sum = rows_back(upstream, unit_two, inverse_two, gain_ref[1:2])
        stats_ref[4:5, :] += gain_sum
        stats_ref[5:6, :] += bias_sum
        grad_after_one = grad_after_two + back
        after_ref[seq] = grad_after_one
        grad_one = low(grad_after_one)
        totals[1] += dot_of(context[...], grad_one, 1, 0)
        context[...] = low(dot_of(weights[SELF_OUT], grad_one, 1, 1))
        back_rows[turn] = context[...]
        for head, number, owner in owners:

            @pl.when(owner + 2 * seq != me)
            def give(head=head, number=number, owner=owner):
                d_copy(turn, seq, head, number, owner).start()

            @pl.when(owner + 2 * seq == me)
            def keep(head=head, number=number):
                back_ref[number, me] = context[head * HEAD_DIM : (head + 1) * HEAD_DIM, :]

        return unused


    lax.fori_loop(0, batches, one_sequence, 0)
    for f in range(width // piece):
        for c in range(group // tp):
            for t in range(tp):
                head = t * (group // tp) + c
                packed_ref[c, f, t] = low(
                    totals[
                        :,
                        head * HEAD_DIM : (head + 1) * HEAD_DIM,
                        f * piece : (f + 1) * piece,
                    ]
                )

    def collect(k, unused):
        place = me ^ k
        for number in range(2):
            pltpu.make_async_remote_copy(
                src_ref=landing.at[number, place],
                dst_ref=landing.at[number, place],
                send_sem=d_send.at[0, 0],
                recv_sem=d_recv.at[number, place],
                device_id={"ctx": place // tp, "tp": place % tp},
                device_id_type=MESH,
            ).wait_recv()
            back_ref[number, place] = landing[number, place]
        return unused

    lax.fori_loop(1, group, collect, 0)
    for turn in range(batches):
        seq = 1 - mine if turn == 0 else mine
        for head, number, owner in owners:

            @pl.when(owner + 2 * seq != me)
            def given(turn=turn, seq=seq, head=head, number=number, owner=owner):
                d_copy(turn, seq, head, number, owner).wait_send()


def middle(
    gathered, tokens, steps, encoder, cotangent, gains, biases, contexts, tp, fsdp
):
    batches, chunk, width = tokens.shape
    group = contexts.shape[1]
    enc_count = encoder.shape[1]
    heads = width // HEAD_DIM
    bf16, f32 = jnp.bfloat16, jnp.float32
    struct = jax.ShapeDtypeStruct
    inside = pl.BlockSpec(memory_space=pltpu.VMEM)
    dma = pltpu.SemaphoreType.DMA
    count = gathered.shape[3] - 3
    packed = (group // tp, gathered.shape[0], tp, count - 2) + gathered.shape[4:]
    return pl.pallas_call(
        functools.partial(middle_kernel, tp=tp, fsdp=fsdp),
        in_specs=[pl.BlockSpec(memory_space=pl.ANY)] + [inside] * 7,
        out_specs=[inside] * 6,
        out_shape=[
            struct((batches, chunk, width), f32),
            struct((batches, chunk, width), f32),
            struct((2, group, HEAD_DIM, chunk), bf16),
            struct((batches, enc_count, 2 * width), bf16),
            struct((8, width), f32),
            struct(packed, bf16),
        ],
        scratch_shapes=[
            pltpu.VMEM((count, width, width), bf16),
            pltpu.VMEM((count - 2, width, width), f32),
            pltpu.VMEM((width, chunk), bf16),
            pltpu.VMEM((width, chunk), bf16),
            pltpu.VMEM((width, enc_count), bf16),
            pltpu.VMEM((width, enc_count), bf16),
            pltpu.VMEM((heads, enc_count, chunk), f32),
            pltpu.VMEM((width, chunk), bf16),
            pltpu.VMEM((width, chunk), bf16),
            pltpu.VMEM((width, chunk), bf16),
            pltpu.VMEM((width, enc_count), f32),
            pltpu.VMEM((width, enc_count), f32),
            pltpu.VMEM((batches, width, chunk), bf16),
            pltpu.VMEM((2, group, HEAD_DIM, chunk), bf16),
            dma((batches, heads)),
            dma((2, group)),
            dma((32,)),
        ],
        compiler_params=pltpu.CompilerParams(
            vmem_limit_bytes=VMEM_LIMIT, collective_id=3, has_side_effects=True
        ),
        cost_estimate=pl.CostEstimate(
            flops=30_000_000_000, bytes_accessed=30_000_000, transcendentals=10_000_000
        ),
        name="middle",
    )(gathered, tokens, steps, encoder, cotangent, gains, biases, contexts)


def backward_kernel(
    prefix_ref,
    enc_parts,
    packed,
    gathered,
    rows_in,
    landing,
    weight,
    qkv_ref,
    wide_ref,
    log_ref,
    tokens_ref,
    step_ref,
    gain_ref,
    after_ref,
    enc_ref,
    stats_ref,
    input_ref,
    enc_out,
    self_out,
    query_out,
    pair_out,
    back_out,
    cross_out,
    up_out,
    down_out,
    sums_out,
    outgoing,
    core_rows,
    core_rows_landing,
    sum_rows,
    incoming,
    queries_ref,
    pairs_ref,
    grad_ref,
    delta_ref,
    grad_pairs_ref,
    rows_ref,
    pair_weights,
    enc_own,
    enc_core,
    enc_sum,
    enc_landing,
    pair_ref,
    pair_landing,
    core_landing,
    partial_ref,
    fsdp_landing,
    line_ref,
    line_landing,
    shard_ref,
    head_ref,
    head_landing,
    head_pair,
    head_two,
    sums_ref,
    sums_landing,
    sums_two,
    e_send,
    e_recv,
    x_send,
    x_recv,
    i_send,
    i_recv,
    r_send,
    r_recv,
    f_send,
    f_recv,
    t_send,
    t_recv,
    h_send,
    h_recv,
    p_send,
    p_recv,
    s_send,
    s_recv,
    local_sem,
    rows_sem,
    *,
    span,
    tp,
    fsdp,
):
    batches, chunk, width = tokens_ref.shape
    group = landing.shape[1]
    length = group * chunk
    blocks, ratio = length // span, span // chunk
    wide_blocks = max(1, length // 2 // span)
    factor = HEAD_DIM**-0.5
    here, core, chip = lax.axis_index("fsdp"), lax.axis_index("ctx"), lax.axis_index("tp")
    me = core * tp + chip
    mine = chip // 2
    cores = group // tp
    share = enc_landing.shape[2]
    piece = width // fsdp
    early = packed.shape[3]
    meet(group, tp, fsdp)

    def send_to(source, target, send, recv, **place):
        return pltpu.make_async_remote_copy(
            src_ref=source,
            dst_ref=target,
            send_sem=send,
            recv_sem=recv,
            device_id=place,
            device_id_type=MESH,
        )

    def member(place):
        return {"ctx": place // tp, "tp": place % tp}

    local = [
        pltpu.make_async_copy(
            packed.at[core], partial_ref.at[:, :, pl.ds(0, early)], local_sem.at[0]
        ),
        pltpu.make_async_copy(
            enc_parts.at[:, pl.ds(pl.multiple_of(core * tp * share, share), tp * share)],
            enc_own,
            local_sem.at[1],
        ),
    ]
    first = len(local)
    for f in range(fsdp):
        for c in range(cores):
            for t in range(tp):
                head = t * cores + c
                local.append(
                    pltpu.make_async_copy(
                        gathered.at[f, c, t, pl.ds(3 + KEY, 2)],
                        pair_weights.at[
                            :, pl.ds(head * HEAD_DIM, HEAD_DIM), pl.ds(f * piece, piece)
                        ],
                        local_sem.at[first + (f * cores + c) * tp + t],
                    )
                )
    enc_copy = send_to(
        enc_parts.at[:, pl.ds(pl.multiple_of((1 - core) * tp * share, share), tp * share)],
        enc_core,
        e_send.at[0],
        e_recv.at[0],
        ctx=1 - core,
    )
    enc_line = [
        send_to(
            enc_sum.at[chip ^ n], enc_landing.at[n - 1], e_send.at[n], e_recv.at[n], tp=chip ^ n
        )
        for n in range(1, tp)
    ]

    core_copy = send_to(
        packed.at[1 - core], core_landing, r_send.at[0], r_recv.at[0], ctx=1 - core
    )
    pair_copy = send_to(
        pair_ref.at[1 - core], pair_landing, r_send.at[1], r_recv.at[1], ctx=1 - core
    )
    shard_copy = send_to(
        shard_ref.at[core], shard_ref.at[core], r_send.at[2], r_recv.at[2], ctx=1 - core
    )
    shard_wait = send_to(
        shard_ref.at[1 - core], shard_ref.at[1 - core], r_send.at[2], r_recv.at[2], ctx=1 - core
    )
    f_copies = [
        send_to(
            partial_ref.at[here ^ n, :, pl.ds(0, early)],
            fsdp_landing.at[n - 1, :, pl.ds(0, early)],
            f_send.at[n],
            f_recv.at[n],
            fsdp=here ^ n,
        )
        for n in range(1, fsdp)
    ]
    f_pairs = [
        send_to(
            partial_ref.at[here ^ n, :, pl.ds(early, 2)],
            fsdp_landing.at[n - 1, :, pl.ds(early, 2)],
            f_send.at[fsdp + n],
            f_recv.at[fsdp + n],
            fsdp=here ^ n,
        )
        for n in range(1, fsdp)
    ]
    t_copies = [
        send_to(line_ref.at[chip ^ k], line_landing.at[k - 1], t_send.at[k], t_recv.at[k], tp=chip ^ k)
        for k in range(1, tp)
    ]
    h_copies = [
        send_to(
            head_ref.at[here ^ k], head_landing.at[k - 1], h_send.at[k], h_recv.at[k], fsdp=here ^ k
        )
        for k in range(1, fsdp)
    ]

    pair_chip = 2 * (chip % 2) + core
    p_copies = [
        send_to(head_pair, head_two.at[mine], p_send.at[c], p_recv.at[mine], ctx=c, tp=pair_chip)
        for c in range(2)
    ]
    p_waits = [
        send_to(head_pair, head_two.at[n], p_send.at[0], p_recv.at[n], ctx=c, tp=t)
        for n, c, t in ((0, chip % 2, chip // 2), (1, chip % 2, chip // 2 + 2))
    ]
    p_here = [
        (core == chip % 2) & (chip == chip // 2 + 2 * n) for n in range(2)
    ]

    def s_copy(k):
        return send_to(
            sums_ref, sums_landing.at[k], s_send.at[k], s_recv.at[k], **member(me ^ k)
        )

    s_fsdp = [
        send_to(
            sums_two, sums_landing.at[group + k], s_send.at[group + k], s_recv.at[group + k], fsdp=here ^ k
        )
        for k in range(1, fsdp)
    ]

    enc_copy.start()
    core_copy.start()
    for copy in local:
        copy.start()

    def core_rows_copy(place):
        slot = place % tp
        return send_to(
            core_rows.at[slot], core_rows_landing.at[slot], x_send.at[slot], x_recv.at[slot], ctx=1 - core
        )

    def owner_copy(place):
        slot = place % tp
        return send_to(
            sum_rows.at[slot],
            incoming.at[mine, chip % 2],
            i_send.at[slot],
            i_recv.at[mine, chip % 2],
            tp=slot,
        )

    def spread(place):
        upstream = dot_of(outgoing[place].reshape(6 * HEAD_DIM, chunk), weight[...], 0, 0)
        slot = place % tp

        @pl.when(place // tp != core)
        def hand_over():
            core_rows[slot] = low(upstream)
            core_rows_copy(place).start()

        @pl.when(place // tp == core)
        def collect():
            core_rows_copy(place).wait_recv()
            total = low(upstream + core_rows_landing[slot].astype(jnp.float32))

            @pl.when(place == me)
            def own():
                incoming[mine, chip % 2] = total

            @pl.when(place != me)
            def send():
                sum_rows[slot] = total
                owner_copy(place).start()

    def prepare(seq):
        def lay(place, unused):
            at = pl.ds(pl.multiple_of(place * chunk, chunk), chunk)
            grads = landing[seq, place]
            blank = jnp.zeros_like(grads)
            grad_ref[seq, at, :] = jnp.concatenate([blank, grads], 0).T
            delta_ref[seq, :, at] = jnp.sum(
                grads.astype(jnp.float32) * wide_ref[seq, :, at], axis=0, keepdims=True
            )
            queries_ref[seq, at, :] = jnp.concatenate([qkv_ref[seq, :HEAD_DIM, at], blank], 0).T
            pairs_ref[seq, at, :] = qkv_ref[seq, HEAD_DIM:, at].T
            return unused

        lax.fori_loop(0, group, lay, 0)
        grad_pairs_ref[seq] = jnp.zeros(grad_pairs_ref.shape[1:], jnp.float32)

    def encoder_cores():
        local[1].wait()
        enc_copy.wait_recv()
        for t in range(tp):
            lines = slice(t * share, (t + 1) * share)
            enc_sum[t] = low(
                enc_own[:, lines].astype(jnp.float32) + enc_core[:, lines].astype(jnp.float32)
            )
        for copy in enc_line:
            copy.start()

    def encoder_part():
        total = enc_sum[chip].astype(jnp.float32)
        for n, copy in enumerate(enc_line):
            copy.wait_recv()
            total = total + enc_landing[n].astype(jnp.float32)
        for copy in local[first:]:
            copy.wait()
        grads = low(total)
        enc_rows = enc_ref[:, pl.ds(pl.multiple_of(me * share, share), share), :]
        flat, enc_flat = grads.reshape(batches * share, 2 * width), enc_rows.reshape(
            batches * share, width
        )
        result = dot_of(flat[:, :width], pair_weights[0], 1, 0) + dot_of(
            flat[:, width:], pair_weights[1], 1, 0
        )
        enc_out[...] = result.reshape(batches, share, width)
        for which in range(2):
            grad = low(dot_of(flat[:, which * width : (which + 1) * width], enc_flat, 0, 0))
            for f in range(fsdp):
                for c in range(cores):
                    for t in range(tp):
                        head = t * cores + c
                        pair_ref[c, f, t, which] = grad[
                            head * HEAD_DIM : (head + 1) * HEAD_DIM, f * piece : (f + 1) * piece
                        ]
        pair_copy.start()

    def sum_cores():
        local[0].wait()
        core_copy.wait_recv()

        def one(f, unused):
            def two(t, unused):
                partial_ref[f, t, :early] = low(
                    partial_ref[f, t, :early].astype(jnp.float32)
                    + core_landing[f, t].astype(jnp.float32)
                )
                return unused

            return lax.fori_loop(0, tp, two, unused)

        lax.fori_loop(0, fsdp, one, 0)
        for copy in f_copies:
            copy.start()

    def sum_pairs():
        pair_copy.wait_recv()
        for f in range(fsdp):
            for t in range(tp):
                partial_ref[f, t, early:] = low(
                    pair_ref[core, f, t].astype(jnp.float32)
                    + pair_landing[f, t].astype(jnp.float32)
                )
        for copy in f_pairs:
            copy.start()

    def sum_fsdp():
        for copy in f_copies + f_pairs:
            copy.wait_recv()

        def one(t, unused):
            total = partial_ref[here, t].astype(jnp.float32)
            for k in range(fsdp - 1):
                total = total + fsdp_landing[k, t].astype(jnp.float32)
            line_ref[t] = low(total)
            return unused

        lax.fori_loop(0, tp, one, 0)
        for copy in t_copies:
            copy.start()

    def sum_line():
        for copy in t_copies:
            copy.wait_recv()
        total = line_ref[chip].astype(jnp.float32)
        for k in range(tp - 1):
            total = total + line_landing[k].astype(jnp.float32)
        shard_ref[core] = total
        shard_copy.start()

    for head in range(2):
        prepare(head)

    def attend(index, unused):
        block, seq = blocks - 1 - index // 2, index % 2

        def hook(at, work):
            @pl.when(index == at)
            def run():
                work()

        hook(1, encoder_cores)
        hook(1, sum_cores)
        hook(2, encoder_part)
        hook(3, sum_pairs)
        hook(5, sum_fsdp)
        start = pl.multiple_of(block * span, span)
        at = pl.ds(start, span)
        blank = jnp.zeros((HEAD_DIM, span), jnp.bfloat16)
        queries_t = jnp.concatenate([qkv_ref[seq, :HEAD_DIM, at], blank], 0)
        queries = queries_ref[seq, at, :]
        grads = grad_ref[seq, at, :]
        grads_t = jnp.concatenate(
            [landing[seq, block * ratio + part] for part in range(ratio)], 1
        )
        grads_t = jnp.concatenate([blank, grads_t], 0)
        logs, deltas = log_ref[seq, :, at], delta_ref[seq, :, at]
        limit = jnp.maximum(
            prefix_ref[mine], start + 1 + lax.broadcasted_iota(jnp.int32, (1, span), 1)
        )

        def advance(other, grad_queries, masked):
            offset = pl.multiple_of(other * span, span)
            there = pl.ds(offset, span)
            pairs = pairs_ref[seq, there, :]
            scores = dot_of(pairs, queries_t, 1, 0)
            if masked:
                scores = hide(scores, limit, offset)
            probs = jnp.exp(scores - logs)
            grad_probs = dot_of(pairs, grads_t, 1, 0)
            grad_scores = low(probs * (grad_probs - deltas))
            grad_pairs_ref[seq, there, :] += dot_of(low(probs), grads, 1, 0) + dot_of(
                grad_scores, queries, 1, 0
            )
            return grad_queries + dot_of(
                qkv_ref[seq, HEAD_DIM : 2 * HEAD_DIM, there], grad_scores, 1, 0
            )

        grad_queries = jnp.zeros((HEAD_DIM, span), jnp.float32)
        grad_queries = lax.fori_loop(0, block, lambda j, c: advance(j, c, False), grad_queries)
        grad_queries = lax.fori_loop(
            block, jnp.maximum(block + 1, wide_blocks), lambda j, c: advance(j, c, True), grad_queries
        )
        done = low(grad_queries * factor)
        for part in range(ratio):
            place = block * ratio + part
            outgoing[place, seq, :HEAD_DIM, :] = done[:, part * chunk : (part + 1) * chunk]

        lowest = jnp.where(block == 0, 0, block)
        highest = jnp.where(
            block == 0, wide_blocks, jnp.where(block >= wide_blocks, block + 1, block)
        )

        def give(place, unused):
            at = pl.ds(pl.multiple_of(place * chunk, chunk), chunk)
            outgoing[place, seq, HEAD_DIM:, :] = low(grad_pairs_ref[seq, at, :].T)
            return unused

        lax.fori_loop(lowest * ratio, highest * ratio, give, 0)

        @pl.when(seq == 1)
        def both_heads():
            def one(place, unused):
                spread(place)
                return unused

            lax.fori_loop(lowest * ratio, highest * ratio, one, 0)

        return unused

    lax.fori_loop(0, 2 * blocks, attend, 0)
    sums_ref[...] = jnp.zeros_like(sums_ref)
    sums_ref[:8, :] = stats_ref[...]

    def rows_copy(number):
        return pltpu.make_async_copy(
            rows_in.at[number],
            rows_ref.at[number % rows_ref.shape[0]],
            rows_sem.at[number % rows_ref.shape[0]],
        )

    depth = rows_ref.shape[0]
    for number in range(depth):
        rows_copy(number).start()

    def weigh(number, total):
        rows_copy(number).wait()
        total = total + dot_of(
            outgoing[number].reshape(6 * HEAD_DIM, chunk), rows_ref[number % depth], 1, 0
        )

        @pl.when(number + depth < group)
        def more():
            rows_copy(number + depth).start()

        return total

    total = lax.fori_loop(
        0, group, weigh, jnp.zeros((6 * HEAD_DIM, width), jnp.float32)
    )
    for f in range(fsdp):
        head_ref[f] = total[:, f * piece : (f + 1) * piece]
    for copy in h_copies:
        copy.start()
    sum_line()

    for copy in h_copies:
        copy.wait_recv()
    total = head_ref[here]
    for k in range(fsdp - 1):
        total = total + head_landing[k]
    head_pair[...] = low(total)
    for c in range(2):
        there = (core == c) & (pair_chip == chip)

        @pl.when(there)
        def stay():
            head_two[mine] = head_pair[...]

        @pl.when(jnp.logical_not(there))
        def leave(c=c):
            p_copies[c].start()

    def finish(seq, unused):
        for number in range(2):
            source = 2 * seq + number

            @pl.when(source != chip)
            def come(number=number, source=source):
                send_to(
                    incoming.at[seq, number],
                    incoming.at[seq, number],
                    i_send.at[0],
                    i_recv.at[seq, number],
                    tp=source,
                ).wait_recv()

        upstream = incoming[seq, 0].astype(jnp.float32) + incoming[seq, 1].astype(jnp.float32)
        start_sum = tokens_ref[seq].astype(jnp.float32) + step_ref[seq]
        unit_rows, inverse = in_strips(rows_unit, start_sum)
        back, gain_sum, bias_sum = rows_back(upstream, unit_rows, inverse, gain_ref[...])
        input_ref[seq] = after_ref[seq] + back
        sums_ref[8:9, :] += gain_sum
        sums_ref[9:10, :] += bias_sum
        return unused

    lax.fori_loop(0, batches, finish, 0)

    def start_sums(k, unused):
        s_copy(k).start()
        return unused

    lax.fori_loop(1, group, start_sums, 0)
    def arrive_sums(k, total):
        s_copy(k).wait_recv()
        return total + sums_landing[k]

    sums_two[...] = lax.fori_loop(1, group, arrive_sums, sums_ref[...])
    for copy in s_fsdp:
        copy.start()
    shard_wait.wait_recv()

    def whole(block):
        return jnp.concatenate([shard_ref[0, block], shard_ref[1, block]], 0)

    query_out[...] = whole(0).T
    back_out[...] = whole(1)
    cross_out[...] = whole(2)
    for part in range(4):
        up_out[:, part * piece : (part + 1) * piece] = whole(3 + part).T
        down_out[part * piece : (part + 1) * piece, :] = whole(7 + part)
    pair_out[0] = whole(11).T
    pair_out[1] = whole(12).T
    for n in range(2):

        @pl.when(jnp.logical_not(p_here[n]))
        def pair_come(n=n):
            p_waits[n].wait_recv()

    total = head_two[0].astype(jnp.float32) + head_two[1].astype(jnp.float32)
    for which in range(3):
        self_out[which] = jnp.concatenate(
            [
                total[(3 * n + which) * HEAD_DIM : (3 * n + which + 1) * HEAD_DIM]
                for n in range(2)
            ],
            0,
        ).T
    total = sums_two[...]
    for k, copy in enumerate(s_fsdp):
        copy.wait_recv()
        total = total + sums_landing[group + 1 + k]
    sums_out[...] = total
    core_copy.wait_send()
    pair_copy.wait_send()
    shard_copy.wait_send()
    for c in range(2):

        @pl.when(jnp.logical_not((core == c) & (pair_chip == chip)))
        def pair_sent(c=c):
            p_copies[c].wait_send()

    enc_copy.wait_send()
    for copy in enc_line + f_copies + f_pairs + t_copies + h_copies + s_fsdp:
        copy.wait_send()

    def sent(k, unused):
        s_copy(k).wait_send()
        return unused

    lax.fori_loop(1, group, sent, 0)

    def rows_sent(slot, unused):
        core_rows_copy((1 - core) * tp + slot).wait_send()

        @pl.when(slot != chip)
        def left():
            owner_copy(core * tp + slot).wait_send()

        return unused

    lax.fori_loop(0, tp, rows_sent, 0)


def backward_group(
    prefix,
    enc_parts,
    packed,
    gathered,
    rows,
    returned,
    weight,
    qkv,
    wide,
    logs,
    tokens,
    steps,
    gain,
    after,
    encoder,
    stats,
    span,
    tp,
    fsdp,
):
    batches, chunk, width = tokens.shape
    group = returned.shape[1]
    length = group * chunk
    share = encoder.shape[1] // group
    piece = width // fsdp
    count = packed.shape[3]
    tail = packed.shape[4:]
    bf16, f32 = jnp.bfloat16, jnp.float32
    struct = jax.ShapeDtypeStruct
    inside = pl.BlockSpec(memory_space=pltpu.VMEM)
    outside = pl.BlockSpec(memory_space=pl.ANY)
    dma = pltpu.SemaphoreType.DMA
    vmem = pltpu.VMEM
    parts = group * fsdp
    return pl.pallas_call(
        functools.partial(backward_kernel, span=span, tp=tp, fsdp=fsdp),
        in_specs=[pl.BlockSpec(memory_space=pltpu.SMEM)] + [outside] * 4 + [inside] * 11,
        out_specs=[inside] * 10,
        out_shape=[
            struct((batches, chunk, width), f32),
            struct((batches, share, width), f32),
            struct((3, piece, piece), f32),
            struct((piece, piece), f32),
            struct((2, piece, piece), f32),
            struct((piece, piece), f32),
            struct((piece, piece), f32),
            struct((piece, width), f32),
            struct((width, piece), f32),
            struct((16, width), f32),
        ],
        scratch_shapes=[
            vmem((group, 2, 3 * HEAD_DIM, chunk), bf16),
            vmem((tp, chunk, width), bf16),
            vmem((tp, chunk, width), bf16),
            vmem((tp, chunk, width), bf16),
            vmem((batches, 2, chunk, width), bf16),
            vmem((2, length, 2 * HEAD_DIM), bf16),
            vmem((2, length, 2 * HEAD_DIM), bf16),
            vmem((2, length, 2 * HEAD_DIM), bf16),
            vmem((2, 1, length), f32),
            vmem((2, length, 2 * HEAD_DIM), f32),
            vmem((2, chunk, width), bf16),
            vmem((2, width, width), bf16),
            vmem((batches, tp * share, 2 * width), bf16),
            vmem((batches, tp * share, 2 * width), bf16),
            vmem((tp, batches, share, 2 * width), bf16),
            vmem((tp - 1, batches, share, 2 * width), bf16),
            vmem((group // tp, fsdp, tp, 2) + tail, bf16),
            vmem((fsdp, tp, 2) + tail, bf16),
            vmem((fsdp, tp, count) + tail, bf16),
            vmem((fsdp, tp, count + 2) + tail, bf16),
            vmem((fsdp - 1, tp, count + 2) + tail, bf16),
            vmem((tp, count + 2) + tail, bf16),
            vmem((tp - 1, count + 2) + tail, bf16),
            vmem((2, count + 2) + tail, f32),
            vmem((fsdp, 6 * HEAD_DIM, piece), f32),
            vmem((fsdp - 1, 6 * HEAD_DIM, piece), f32),
            vmem((6 * HEAD_DIM, piece), bf16),
            vmem((2, 6 * HEAD_DIM, piece), bf16),
            vmem((16, width), f32),
            vmem((group + fsdp, 16, width), f32),
            vmem((16, width), f32),
            dma((tp,)),
            dma((tp,)),
            dma((tp,)),
            dma((tp,)),
            dma((tp,)),
            dma((batches, 2)),
            dma((4,)),
            dma((4,)),
            dma((2 * fsdp,)),
            dma((2 * fsdp,)),
            dma((tp,)),
            dma((tp,)),
            dma((fsdp,)),
            dma((fsdp,)),
            dma((2,)),
            dma((2,)),
            dma((group + fsdp,)),
            dma((group + fsdp,)),
            dma((2 + parts,)),
            dma((2,)),
        ],
        compiler_params=pltpu.CompilerParams(
            vmem_limit_bytes=VMEM_LIMIT, collective_id=2, has_side_effects=True
        ),
        cost_estimate=pl.CostEstimate(
            flops=100_000_000_000, bytes_accessed=40_000_000, transcendentals=20_000_000
        ),
        name="backward_group",
    )(
        prefix,
        enc_parts,
        packed,
        gathered,
        rows,
        returned,
        weight,
        qkv,
        wide,
        logs,
        tokens,
        steps,
        gain,
        after,
        encoder,
        stats,
    )


def local_heads(
    tokens,
    timesteps,
    time_table,
    prefix,
    encoder,
    self_qkv,
    cross_q,
    cross_kv,
    self_out,
    cross_out,
    ffn_up,
    ffn_down,
    norm_gain,
    norm_bias,
    cotangent,
):
    batches, chunk, width = tokens.shape
    group = 8
    length = group * chunk
    ctx_index = lax.axis_index("ctx")
    span = 1024
    piece = width // 4
    flip = lambda w: jnp.swapaxes(w, -1, -2)
    blocks = jnp.concatenate(
        [
            flip(self_qkv),
            flip(cross_q)[None],
            flip(cross_kv),
            self_out[None],
            cross_out[None],
            flip(ffn_up).reshape(4, piece, piece),
            ffn_down.reshape(4, piece, piece),
        ]
    )
    count = blocks.shape[0]
    half = piece // 2
    own_half = lax.dynamic_slice_in_dim(blocks, ctx_index * half, half, 1)
    gathered = lax.all_gather(own_half, ("fsdp", "ctx", "tp"), axis=0, tiled=False)
    gathered = gathered.reshape(4, 2, 4, count, half, piece)
    mine = blocks[:3].reshape(3, 2, HEAD_DIM, piece)
    mine = jnp.transpose(mine, (1, 0, 2, 3)).reshape(6 * HEAD_DIM, piece)
    steps_onehot = (timesteps[:, None] == lax.iota(jnp.int32, time_table.shape[0])[None, :]).astype(
        jnp.bfloat16
    )
    embedded = jnp.dot(steps_onehot, time_table, preferred_element_type=jnp.float32)[:, None, :]
    rows, qkv, wide, logs, contexts, weight = forward_group(
        prefix, tokens, embedded, norm_gain[:1], norm_bias[:1], mine, span, group, 4, 4
    )
    final, grad_after, returned, enc_parts, stats, packed = middle(
        gathered,
        tokens,
        embedded,
        encoder,
        cotangent,
        norm_gain,
        norm_bias,
        contexts,
        4,
        4,
    )
    outs = backward_group(
        prefix,
        enc_parts,
        packed,
        gathered,
        rows,
        returned,
        weight,
        qkv,
        wide,
        logs,
        tokens,
        embedded,
        norm_gain[:1],
        grad_after,
        encoder,
        stats,
        span,
        4,
        4,
    )
    sums = outs[9]
    entries = (
        tokens.shape[0]
        * tokens.shape[1]
        * tokens.shape[2]
        * lax.axis_size("fsdp")
        * lax.axis_size("ctx")
        * lax.axis_size("tp")
    )
    return (
        final,
        *outs[:9],
        jnp.stack([sums[8], sums[4], sums[6]]),
        jnp.stack([sums[9], sums[5]]),
        sums[7],
        jnp.sqrt(jnp.sum(sums[:4], -1) / entries),
    )


def solution(mesh):
    placed = (
        P("fsdp", ("ctx", "tp"), None),
        P("fsdp"),
        P(),
        P("fsdp"),
        P("fsdp", None, None),
        P(None, "fsdp", "tp"),
        P("fsdp", "tp"),
        P(None, "fsdp", "tp"),
        P("tp", "fsdp"),
        P("tp", "fsdp"),
        P("fsdp", "tp"),
        P("tp", "fsdp"),
        P(),
        P(),
        P("fsdp", ("ctx", "tp"), None),
    )
    heads_fit = dict(mesh.shape) == {"fsdp": 4, "ctx": 2, "tp": 4}
    return jax.shard_map(
        local_heads if heads_fit else local,
        mesh=mesh,
        in_specs=placed,
        out_specs=(
            P("fsdp", ("ctx", "tp"), None),
            P("fsdp", ("ctx", "tp"), None),
            P("fsdp", ("ctx", "tp"), None),
            P(None, "fsdp", "tp"),
            P("fsdp", "tp"),
            P(None, "fsdp", "tp"),
            P("tp", "fsdp"),
            P("tp", "fsdp"),
            P("fsdp", "tp"),
            P("tp", "fsdp"),
            P(),
            P(),
            P(),
            P(),
        ),
        check_vma=False,
    )
```

```python
import functools
import math

import jax
import jax.numpy as jnp
from jax import lax
from jax.experimental import pallas as pl
from jax.experimental.pallas import tpu as pltpu
from jax.sharding import PartitionSpec as P

HEAD_DIM = 64


EPS = 1e-05
NEG = -1e30
ROOT_HALF = 1.0 / math.sqrt(2.0)
INV_ROOT_TWO_PI = 1.0 / math.sqrt(2.0 * math.pi)
VMEM_LIMIT = 62 * 2**20


def norm_rows(hidden, scaling, offsets):
    centre = hidden - jnp.mean(hidden, -1, keepdims=True)
    inverse = lax.rsqrt(jnp.mean(centre * centre, -1, keepdims=True) + EPS)
    unit_rows = centre * inverse
    return (unit_rows * scaling + offsets, unit_rows, inverse)


def norm_back(upstream, unit_rows, inverse, scaling):
    scaled = upstream * scaling
    result = inverse * (
        scaled
        - jnp.mean(scaled, -1, keepdims=True)
        - unit_rows * jnp.mean(scaled * unit_rows, -1, keepdims=True)
    )
    return (result, jnp.sum(upstream * unit_rows, (0, 1)), jnp.sum(upstream, (0, 1)))


def gelu_parts(inputs):
    normal_cdf = 0.5 * (1.0 + lax.erf(inputs * ROOT_HALF))
    return (
        inputs * normal_cdf,
        normal_cdf + inputs * jnp.exp(-0.5 * inputs * inputs) * INV_ROOT_TWO_PI,
    )


def spread_rows(rows):
    return lax.all_gather(rows, "tp", axis=1, tiled=True)


def spread_grads(grad_rows):
    return lax.all_gather(grad_rows, "tp", axis=1, tiled=True)


def finish_branch(local_in, local_weight):
    return lax.psum_scatter(
        jnp.einsum("scw,wd->scd", local_in, local_weight, preferred_element_type=jnp.float32),
        "tp",
        scatter_dimension=1,
        tiled=True,
    )


def finish_grad(local_grad, local_weight):
    return lax.psum_scatter(
        jnp.einsum("scw,dw->scd", local_grad, local_weight, preferred_element_type=jnp.float32),
        "tp",
        scatter_dimension=1,
        tiled=True,
    )


def block_scores(queries, key_block, query_pos, key_pos, lengths, factor):
    scores = (
        jnp.einsum("sqhe,skhe->sqhk", queries, key_block, preferred_element_type=jnp.float32)
        * factor
    )
    visible = (key_pos[None, None, :] <= query_pos[None, :, None]) | (
        key_pos[None, None, :] < lengths[:, None, None]
    )
    return jnp.where(visible[:, :, None, :], scores, NEG)


def attend_forward(queries, key_rows, value_rows, query_pos, lengths, key_span, factor):
    length = key_rows.shape[1]

    def attend_advance(running, offset):
        highest, totals, summed = running
        key_block = lax.dynamic_slice_in_dim(key_rows, offset, key_span, 1)
        value_block = lax.dynamic_slice_in_dim(value_rows, offset, key_span, 1)
        scores = block_scores(
            queries, key_block, query_pos, offset + lax.iota(jnp.int32, key_span), lengths, factor
        )
        new_high = jnp.maximum(highest, jnp.max(scores, -1))
        weights = jnp.exp(scores - new_high[..., None])
        fading = jnp.exp(highest - new_high)
        totals = totals * fading + jnp.sum(weights, -1)
        summed = summed * fading[..., None] + jnp.einsum(
            "sqhk,skhe->sqhe",
            weights.astype(jnp.bfloat16),
            value_block,
            preferred_element_type=jnp.float32,
        )
        return ((new_high, totals, summed), None)

    stat_shape = queries.shape[:3]
    initial = (
        jnp.full(stat_shape, NEG, jnp.float32),
        jnp.zeros(stat_shape, jnp.float32),
        jnp.zeros(queries.shape, jnp.float32),
    )
    offsets = jnp.arange(length // key_span, dtype=jnp.int32) * key_span
    (highest, totals, summed), unused = lax.scan(attend_advance, initial, offsets)
    return (summed / totals[..., None], highest + jnp.log(totals))


def attend_block(
    queries,
    grad_out,
    log_rows,
    delta_rows,
    key_block,
    value_block,
    query_pos,
    key_pos,
    lengths,
    factor,
):
    scores = block_scores(queries, key_block, query_pos, key_pos, lengths, factor)
    probs = jnp.exp(scores - log_rows[..., None])
    grad_probs = jnp.einsum(
        "sqhe,skhe->sqhk", grad_out, value_block, preferred_element_type=jnp.float32
    )
    grad_scores = (probs * (grad_probs - delta_rows[..., None])).astype(jnp.bfloat16)
    return (probs.astype(jnp.bfloat16), grad_scores)


def key_sweep(
    queries,
    grad_out,
    log_rows,
    delta_rows,
    key_rows,
    value_rows,
    query_pos,
    lengths,
    key_span,
    factor,
):
    batches, row_count, head_count, head_depth = queries.shape
    length = key_rows.shape[1]

    def key_advance(grad_query, offset):
        key_block = lax.dynamic_slice_in_dim(key_rows, offset, key_span, 1)
        value_block = lax.dynamic_slice_in_dim(value_rows, offset, key_span, 1)
        key_pos = offset + lax.iota(jnp.int32, key_span)
        probs_low, grad_scores = attend_block(
            queries,
            grad_out,
            log_rows,
            delta_rows,
            key_block,
            value_block,
            query_pos,
            key_pos,
            lengths,
            factor,
        )
        grad_query = (
            grad_query
            + jnp.einsum(
                "sqhk,skhe->sqhe", grad_scores, key_block, preferred_element_type=jnp.float32
            )
            * factor
        )
        grad_key = (
            jnp.einsum("sqhk,sqhe->kshe", grad_scores, queries, preferred_element_type=jnp.float32)
            * factor
        )
        grad_value = jnp.einsum(
            "sqhk,sqhe->kshe", probs_low, grad_out, preferred_element_type=jnp.float32
        )
        return (grad_query, (grad_key, grad_value))

    offsets = jnp.arange(length // key_span, dtype=jnp.int32) * key_span
    grad_query, stacked = lax.scan(key_advance, jnp.zeros(queries.shape, jnp.float32), offsets)
    flat_shape = (length, batches, head_count * head_depth)
    return (grad_query, stacked[0].reshape(flat_shape), stacked[1].reshape(flat_shape))


def local(
    tokens,
    timesteps,
    time_table,
    prefix,
    encoder,
    self_qkv,
    cross_q,
    cross_kv,
    self_out,
    cross_out,
    ffn_up,
    ffn_down,
    norm_gain,
    norm_bias,
    cotangent,
):
    proj_self, proj_query, proj_pair, back_self, back_cross, expand_full, shrink_full = (
        lax.all_gather(self_qkv, "fsdp", axis=1, tiled=True),
        lax.all_gather(cross_q, "fsdp", axis=0, tiled=True),
        lax.all_gather(cross_kv, "fsdp", axis=1, tiled=True),
        lax.all_gather(self_out, "fsdp", axis=1, tiled=True),
        lax.all_gather(cross_out, "fsdp", axis=1, tiled=True),
        lax.all_gather(ffn_up, "fsdp", axis=0, tiled=True),
        lax.all_gather(ffn_down, "fsdp", axis=1, tiled=True),
    )
    batches = tokens.shape[0]
    model_width = tokens.shape[2]
    local_width = proj_query.shape[1]
    head_count = local_width // HEAD_DIM
    factor = HEAD_DIM ** (-0.5)
    ctx_index = lax.axis_index("ctx")
    local_stack = jnp.transpose(proj_self, (1, 0, 2)).reshape(model_width, 3 * local_width)
    steps_onehot = (timesteps[:, None] == lax.iota(jnp.int32, time_table.shape[0])[None, :]).astype(
        jnp.bfloat16
    )
    embedded = jnp.dot(steps_onehot, time_table, preferred_element_type=jnp.float32)
    start_sum = tokens.astype(jnp.float32) + embedded[:, None, :]
    normed_one, unit_one, inverse_one = norm_rows(start_sum, norm_gain[0], norm_bias[0])
    rows_self = spread_rows(normed_one.astype(jnp.bfloat16))
    row_count = rows_self.shape[1]
    head_shape = (batches, row_count, head_count, HEAD_DIM)
    projected = jnp.einsum(
        "scd,kdw->kscw", rows_self, proj_self, preferred_element_type=jnp.float32
    ).astype(jnp.bfloat16)
    queries, key_local, value_local = (projected[0], projected[1], projected[2])
    key_all, value_all = (
        lax.all_gather(key_local, "ctx", axis=1, tiled=True),
        lax.all_gather(value_local, "ctx", axis=1, tiled=True),
    )
    length = key_all.shape[1]
    key_span = min(512, length)
    query_pos = ctx_index * row_count + lax.iota(jnp.int32, row_count)
    keys_four = key_all.reshape(batches, length, head_count, HEAD_DIM)
    values_four = value_all.reshape(batches, length, head_count, HEAD_DIM)
    queries_four = queries.reshape(head_shape)
    attended, log_total = attend_forward(
        queries_four, keys_four, values_four, query_pos, prefix, key_span, factor
    )
    context_one = attended.reshape(batches, row_count, local_width).astype(jnp.bfloat16)
    branch_one = finish_branch(context_one, back_self)
    after_one = start_sum + branch_one
    normed_two, unit_two, inverse_two = norm_rows(after_one, norm_gain[1], norm_bias[1])
    rows_cross = spread_rows(normed_two.astype(jnp.bfloat16))
    cross_queries = jnp.einsum(
        "scd,dw->scw", rows_cross, proj_query, preferred_element_type=jnp.float32
    ).astype(jnp.bfloat16)
    enc_pair = jnp.einsum(
        "sed,kdw->ksew", encoder, proj_pair, preferred_element_type=jnp.float32
    ).astype(jnp.bfloat16)
    enc_count = encoder.shape[1]
    cross_keys = enc_pair[0].reshape(batches, enc_count, head_count, HEAD_DIM)
    cross_values = enc_pair[1].reshape(batches, enc_count, head_count, HEAD_DIM)
    cross_four = cross_queries.reshape(head_shape)
    cross_probs = jax.nn.softmax(
        jnp.einsum("sqhe,skhe->sqhk", cross_four, cross_keys, preferred_element_type=jnp.float32)
        * factor,
        axis=-1,
    )
    cross_low = cross_probs.astype(jnp.bfloat16)
    context_two = (
        jnp.einsum("sqhk,skhe->sqhe", cross_low, cross_values, preferred_element_type=jnp.float32)
        .reshape(batches, row_count, local_width)
        .astype(jnp.bfloat16)
    )
    branch_two = finish_branch(context_two, back_cross)
    after_two = after_one + branch_two
    normed_three, unit_three, inverse_three = norm_rows(after_two, norm_gain[2], norm_bias[2])
    rows_ffn = spread_rows(normed_three.astype(jnp.bfloat16))
    pre_act = jnp.einsum("scd,df->scf", rows_ffn, expand_full, preferred_element_type=jnp.float32)
    activated, slopes = gelu_parts(pre_act)
    hidden_low = activated.astype(jnp.bfloat16)
    branch_three = finish_branch(hidden_low, shrink_full)
    final_sum = after_two + branch_three
    grad_three = spread_grads(cotangent)
    grad_shrink = jnp.einsum(
        "scf,scd->fd", hidden_low, grad_three, preferred_element_type=jnp.float32
    )
    grad_pre = (
        jnp.einsum("scd,fd->scf", grad_three, shrink_full, preferred_element_type=jnp.float32)
        * slopes
    ).astype(jnp.bfloat16)
    grad_expand = jnp.einsum("scd,scf->df", rows_ffn, grad_pre, preferred_element_type=jnp.float32)
    back_three, gain_three, shift_three = norm_back(
        finish_grad(grad_pre, expand_full), unit_three, inverse_three, norm_gain[2]
    )
    grad_after_two = cotangent.astype(jnp.float32) + back_three
    grad_two = spread_grads(grad_after_two.astype(jnp.bfloat16))
    grad_back_cross = jnp.einsum(
        "scw,scd->wd", context_two, grad_two, preferred_element_type=jnp.float32
    )
    grad_context_two = jnp.einsum(
        "scd,wd->scw", grad_two, back_cross, preferred_element_type=jnp.float32
    ).astype(jnp.bfloat16)
    grad_cross_four = grad_context_two.reshape(head_shape)
    grad_cross_probs = jnp.einsum(
        "sqhe,skhe->sqhk", grad_cross_four, cross_values, preferred_element_type=jnp.float32
    )
    grad_cross_scores = (
        cross_probs
        * (grad_cross_probs - jnp.sum(cross_probs * grad_cross_probs, -1, keepdims=True))
    ).astype(jnp.bfloat16)
    grad_cross_q = (
        (
            jnp.einsum(
                "sqhk,skhe->sqhe", grad_cross_scores, cross_keys, preferred_element_type=jnp.float32
            )
            * factor
        )
        .reshape(batches, row_count, local_width)
        .astype(jnp.bfloat16)
    )
    part_keys = (
        jnp.einsum(
            "sqhk,sqhe->skhe", grad_cross_scores, cross_four, preferred_element_type=jnp.float32
        )
        * factor
    ).reshape(batches, enc_count, local_width)
    part_values = jnp.einsum(
        "sqhk,sqhe->skhe", cross_low, grad_cross_four, preferred_element_type=jnp.float32
    ).reshape(batches, enc_count, local_width)
    enc_keys, enc_values = (
        lax.psum_scatter(part_keys, "ctx", scatter_dimension=1, tiled=True),
        lax.psum_scatter(part_values, "ctx", scatter_dimension=1, tiled=True),
    )
    enc_keys = enc_keys.astype(jnp.bfloat16)
    enc_values = enc_values.astype(jnp.bfloat16)
    enc_share = enc_keys.shape[1]
    enc_rows = lax.dynamic_slice_in_dim(encoder, ctx_index * enc_share, enc_share, 1)
    grad_pair = jnp.stack(
        [
            jnp.einsum("sed,sew->dw", enc_rows, enc_keys, preferred_element_type=jnp.float32),
            jnp.einsum("sed,sew->dw", enc_rows, enc_values, preferred_element_type=jnp.float32),
        ]
    )
    encoder_grad = lax.psum_scatter(
        jnp.einsum("sew,dw->sed", enc_keys, proj_pair[0], preferred_element_type=jnp.float32)
        + jnp.einsum("sew,dw->sed", enc_values, proj_pair[1], preferred_element_type=jnp.float32),
        "tp",
        scatter_dimension=1,
        tiled=True,
    )
    grad_query_proj = jnp.einsum(
        "scd,scw->dw", rows_cross, grad_cross_q, preferred_element_type=jnp.float32
    )
    back_two, gain_two, shift_two = norm_back(
        finish_grad(grad_cross_q, proj_query), unit_two, inverse_two, norm_gain[1]
    )
    grad_after_one = grad_after_two + back_two
    grad_one = spread_grads(grad_after_one.astype(jnp.bfloat16))
    grad_back_self = jnp.einsum(
        "scw,scd->wd", context_one, grad_one, preferred_element_type=jnp.float32
    )
    grad_context_one = jnp.einsum(
        "scd,wd->scw", grad_one, back_self, preferred_element_type=jnp.float32
    ).astype(jnp.bfloat16)
    grad_ctx_four = grad_context_one.reshape(head_shape)
    delta_rows = jnp.sum(grad_ctx_four.astype(jnp.float32) * attended, -1)
    grad_query, grad_key_all, grad_value_all = key_sweep(
        queries_four,
        grad_ctx_four,
        log_total,
        delta_rows,
        keys_four,
        values_four,
        query_pos,
        prefix,
        key_span,
        factor,
    )
    own_keys, own_values = (
        lax.psum_scatter(grad_key_all, "ctx", scatter_dimension=0, tiled=True),
        lax.psum_scatter(grad_value_all, "ctx", scatter_dimension=0, tiled=True),
    )
    own_keys = jnp.transpose(own_keys, (1, 0, 2))
    own_values = jnp.transpose(own_values, (1, 0, 2))
    grad_joined = jnp.concatenate(
        [grad_query.reshape(batches, row_count, local_width), own_keys, own_values], -1
    ).astype(jnp.bfloat16)
    grad_proj_self = jnp.transpose(
        jnp.einsum(
            "scd,scw->dw", rows_self, grad_joined, preferred_element_type=jnp.float32
        ).reshape(model_width, 3, local_width),
        (1, 0, 2),
    )
    back_one, gain_one, shift_one = norm_back(
        finish_grad(grad_joined, local_stack), unit_one, inverse_one, norm_gain[0]
    )
    input_grad = grad_after_one + back_one
    shard_grads = (
        lax.psum_scatter(grad_proj_self, "fsdp", scatter_dimension=1, tiled=True),
        lax.psum_scatter(grad_query_proj, "fsdp", scatter_dimension=0, tiled=True),
        lax.psum_scatter(grad_pair, "fsdp", scatter_dimension=1, tiled=True),
        lax.psum_scatter(grad_back_self, "fsdp", scatter_dimension=1, tiled=True),
        lax.psum_scatter(grad_back_cross, "fsdp", scatter_dimension=1, tiled=True),
        lax.psum_scatter(grad_expand, "fsdp", scatter_dimension=0, tiled=True),
        lax.psum_scatter(grad_shrink, "fsdp", scatter_dimension=1, tiled=True),
    )
    full_grads = lax.psum(
        (
            shard_grads[0],
            shard_grads[1],
            shard_grads[2],
            shard_grads[3],
            shard_grads[4],
            shard_grads[5],
            shard_grads[6],
        ),
        "ctx",
    )
    squares = jnp.stack(
        [
            jnp.sum(final_sum * final_sum),
            jnp.sum(branch_one * branch_one),
            jnp.sum(branch_two * branch_two),
            jnp.sum(branch_three * branch_three),
        ]
    )
    gain_grad, bias_grad, square_totals = lax.psum(
        (
            jnp.stack([gain_one, gain_two, gain_three]),
            jnp.stack([shift_one, shift_two, shift_three]),
            squares,
        ),
        ("fsdp", "ctx", "tp"),
    )
    entries = (
        tokens.shape[0]
        * tokens.shape[1]
        * tokens.shape[2]
        * lax.axis_size("fsdp")
        * lax.axis_size("ctx")
        * lax.axis_size("tp")
    )
    norms = jnp.sqrt(square_totals / entries)
    return (
        final_sum,
        input_grad,
        encoder_grad,
        full_grads[0],
        full_grads[1],
        full_grads[2],
        full_grads[3],
        full_grads[4],
        full_grads[5],
        full_grads[6],
        gain_grad,
        bias_grad[:2],
        bias_grad[2],
        norms,
    )


def dot_of(left, right, left_dim, right_dim):
    return lax.dot_general(
        left, right, (((left_dim,), (right_dim,)), ((), ())), preferred_element_type=jnp.float32
    )


def bounds(prefix, start, query_span, key_span):
    whole = jnp.maximum(prefix, start + 1) // key_span
    every = (jnp.maximum(prefix, start + query_span) + key_span - 1) // key_span
    return whole, every


def hide(scores, limit, offset):
    return jnp.where(lax.broadcasted_iota(jnp.int32, scores.shape, 0) < limit - offset, scores, NEG)


def low(value):
    return value.astype(jnp.bfloat16)


STRIP = 64


def in_strips(work, *values, strip=STRIP, axis=0):
    count = values[0].shape[axis] // strip
    cut = lambda v, n: lax.slice_in_dim(v, n * strip, (n + 1) * strip, axis=axis)
    parts = [work(*[cut(v, n) for v in values]) for n in range(count)]
    return tuple(jnp.concatenate(p, axis) for p in zip(*parts))


def gelu_strip(inputs):
    activated, slopes = gelu_parts(inputs)
    return low(activated), slopes


def rows_unit(hidden):
    centre = hidden - jnp.mean(hidden, -1, keepdims=True)
    inverse = lax.rsqrt(jnp.mean(centre * centre, -1, keepdims=True) + EPS)
    return centre * inverse, inverse


def rows_norm(hidden, scaling, offsets):
    def strip(rows):
        unit_rows, inverse = rows_unit(rows)
        return low(unit_rows * scaling + offsets), unit_rows, inverse

    return in_strips(strip, hidden)


def rows_back(upstream, unit_rows, inverse, scaling):
    sums = [jnp.zeros((8, upstream.shape[1]), jnp.float32)] * 2

    def strip(rows, units, inverses):
        scaled = rows * scaling
        for n, term in enumerate((rows * units, rows)):
            sums[n] = sums[n] + jnp.sum(term.reshape(-1, 8, term.shape[1]), 0)
        return (
            inverses
            * (
                scaled
                - jnp.mean(scaled, -1, keepdims=True)
                - units * jnp.mean(scaled * units, -1, keepdims=True)
            ),
        )

    (result,) = in_strips(strip, upstream, unit_rows, inverse)
    return result, jnp.sum(sums[0], 0, keepdims=True), jnp.sum(sums[1], 0, keepdims=True)


MESH = pl.DeviceIdType.MESH


def meet(group, tp, fsdp):
    here, core, chip = lax.axis_index("fsdp"), lax.axis_index("ctx"), lax.axis_index("tp")
    me = core * tp + chip
    barrier = pltpu.get_barrier_semaphore()
    for k in range(1, group):
        other = me ^ k
        pl.semaphore_signal(
            barrier, inc=1, device_id={"ctx": other // tp, "tp": other % tp}, device_id_type=MESH
        )
    for k in range(1, fsdp):
        pl.semaphore_signal(barrier, inc=1, device_id={"fsdp": here ^ k}, device_id_type=MESH)
    pl.semaphore_wait(barrier, group - 1 + fsdp - 1)


def forward_kernel(
    prefix_ref,
    tokens_ref,
    step_ref,
    gain_ref,
    bias_ref,
    mine_ref,
    rows_out,
    qkv_ref,
    wide_ref,
    log_ref,
    ctx_ref,
    weight,
    rows_ref,
    other_ref,
    columns,
    pair_ref,
    keys_ref,
    values_ref,
    low_ref,
    landing,
    w_send,
    w_recv,
    v_send,
    v_recv,
    x_send,
    x_recv,
    c_send,
    c_recv,
    keep_sem,
    *,
    span,
    tp,
    fsdp,
):
    batches, chunk, width = tokens_ref.shape
    group = rows_ref.shape[0]
    length = group * chunk
    blocks, ratio = length // span, span // chunk
    wide_blocks = max(1, length // 2 // span)
    factor = HEAD_DIM**-0.5
    here, core, chip = lax.axis_index("fsdp"), lax.axis_index("ctx"), lax.axis_index("tp")
    me = core * tp + chip
    mine = chip // 2
    inner = (chip == 1) | (chip == 2)
    other_inner, other_outer = 2 - mine, 3 - 3 * mine
    meet(group, tp, fsdp)

    def send_to(source, target, send, recv, **place):
        return pltpu.make_async_remote_copy(
            src_ref=source,
            dst_ref=target,
            send_sem=send,
            recv_sem=recv,
            device_id=place,
            device_id_type=MESH,
        )

    v_core, v_chip = chip % 2, chip // 2 + 2 * core
    v_own = (v_core == core) & (v_chip == chip)
    v_copy = send_to(mine_ref, pair_ref, v_send.at[0], v_recv.at[0], ctx=v_core, tp=v_chip)

    @pl.when(v_own)
    def keep_pair():
        pair_ref[...] = mine_ref[...]

    @pl.when(jnp.logical_not(v_own))
    def send_pair():
        v_copy.start()

    comes = (chip // 2 != core) | (2 * (chip % 2) + core != chip)

    def w_copy(k):
        return send_to(pair_ref, columns.at[k], w_send.at[k], w_recv.at[k], fsdp=here ^ k)

    def normalise(seq, target, at):
        start_sum = tokens_ref[seq].astype(jnp.float32) + step_ref[seq]
        target[at] = rows_norm(start_sum, gain_ref[0:1], bias_ref[0:1])[0]

    def x_copy(kind):
        block = rows_ref.at[me]
        near = rows_ref.at[core * tp + (chip ^ 1)]
        second = rows_ref.at[core * tp + other_inner]
        third = rows_ref.at[core * tp + other_outer]
        source, place, target = (
            (block, me, {"tp": chip ^ 1}),
            (other_ref.at[0], me, {"tp": other_inner}),
            (block, me, {"ctx": 1 - core}),
            (near, core * tp + (chip ^ 1), {"ctx": 1 - core}),
            (second, core * tp + other_inner, {"ctx": 1 - core}),
            (third, core * tp + other_outer, {"ctx": 1 - core}),
            (second, core * tp + other_inner, {"tp": chip ^ 1}),
            (third, core * tp + other_outer, {"tp": chip ^ 1}),
            (other_ref.at[0], me, {"tp": other_outer}),
        )[kind]
        return send_to(source, rows_ref.at[place], x_send.at[kind], x_recv.at[place], **target)

    def x_wait(place):
        send_to(
            rows_ref.at[place], rows_ref.at[place], x_send.at[0], x_recv.at[place], ctx=1 - core
        ).wait_recv()

    def arrive(number):
        x_wait(core * tp + (chip ^ 1, other_inner, other_outer)[number])
        if number:

            @pl.when(inner & (core == 0))
            def onward():
                x_copy(5 + number).start()

        x_copy(3 + number).start()

    normalise(mine, rows_ref, me)
    normalise(1 - mine, other_ref, 0)

    @pl.when(core == 0)
    def first_half():
        x_copy(2).start()

        @pl.when(inner)
        def from_inner():
            x_copy(1).start()
            x_copy(0).start()

        @pl.when(jnp.logical_not(inner))
        def from_outer():
            x_copy(0).start()

    @pl.when(comes)
    def pair_here():
        v_copy.wait_recv()

    for k in range(1, fsdp):
        w_copy(k).start()
    values_ref[:, HEAD_DIM:, :] = jnp.ones_like(values_ref[:, HEAD_DIM:, :])

    def project(place, unused):
        rows = rows_ref[place]
        joined = low(dot_of(weight[...], rows, 1, 1))
        at = pl.ds(pl.multiple_of(place * chunk, chunk), chunk)
        for head in range(2):
            queries, keys, values = (
                joined[(3 * head + n) * HEAD_DIM : (3 * head + n + 1) * HEAD_DIM] for n in range(3)
            )
            qkv_ref[head, :HEAD_DIM, at] = queries * jnp.bfloat16(factor)
            qkv_ref[head, HEAD_DIM : 2 * HEAD_DIM, at] = keys
            qkv_ref[head, 2 * HEAD_DIM :, at] = values
            values_ref[head, :HEAD_DIM, at] = values
            keys_ref[head, at, :] = keys.T
        return unused

    @pl.when(core == 0)
    def first_lines():
        @pl.when(jnp.logical_not(inner))
        def then_other():
            x_copy(0).wait_send()
            x_copy(1).start()

        for number in range(3):
            arrive(number)

    @pl.when(core == 1)
    def second_lines():
        for place in range(tp):
            x_wait(place)
        for kind in (2, 1, 8, 0):
            x_copy(kind).start()

    piece = mine_ref.shape[1]
    for k in range(fsdp):
        if k:
            w_copy(k).wait_recv()
        part = columns[k] if k else pair_ref[...]
        for f in range(fsdp):

            @pl.when((here ^ k) == f)
            def place(f=f, part=part):
                weight[:, f * piece : (f + 1) * piece] = part

    lax.fori_loop(0, tp, project, 0)

    def c_copy(head, place):
        return send_to(
            low_ref.at[head, place],
            landing.at[head, me],
            c_send.at[head, place],
            c_recv.at[head, me],
            ctx=place // tp,
            tp=place % tp,
        )

    def c_wait(head, place):
        send_to(
            low_ref.at[head, place],
            landing.at[head, place],
            c_send.at[head, place],
            c_recv.at[head, place],
            ctx=place // tp,
            tp=place % tp,
        ).wait_recv()

    def attend(index, unused):
        block, head = index // 2, index % 2

        @pl.when((core == 1) & (index == 3))
        def near_lines():
            arrive(0)

        @pl.when(index == 4)
        def second_half():
            @pl.when(core == 0)
            def wait_other():
                for place in range(tp, group):
                    x_wait(place)

            @pl.when(core == 1)
            def far_lines():
                arrive(1)
                arrive(2)

            lax.fori_loop(tp, group, project, 0)

        start = pl.multiple_of(block * span, span)
        queries = qkv_ref[head, :HEAD_DIM, pl.ds(start, span)]
        limit = jnp.maximum(
            prefix_ref[mine], start + 1 + lax.broadcasted_iota(jnp.int32, (1, span), 1)
        )

        def advance(other, carry, masked):
            highest, total = carry
            offset = pl.multiple_of(other * span, span)
            scores = dot_of(keys_ref[head, pl.ds(offset, span), :], queries, 1, 0)
            if masked:
                scores = hide(scores, limit, offset)
            higher = jnp.maximum(highest, jnp.max(scores, axis=0, keepdims=True))
            weights = low(jnp.exp(scores - higher))
            fading = jnp.exp(highest - higher)
            total = total * fading + dot_of(
                values_ref[head, :, pl.ds(offset, span)], weights, 1, 0
            )
            return higher, total

        carry = (
            jnp.full((1, span), NEG, jnp.float32),
            jnp.zeros((values_ref.shape[1], span), jnp.float32),
        )
        carry = lax.fori_loop(0, block, lambda j, c: advance(j, c, False), carry)
        highest, total = lax.fori_loop(
            block, jnp.maximum(block + 1, wide_blocks), lambda j, c: advance(j, c, True), carry
        )
        weight_sum = total[HEAD_DIM : HEAD_DIM + 1, :]
        attended = total[:HEAD_DIM, :] / weight_sum
        wide_ref[head, :, pl.ds(start, span)] = attended
        log_ref[head, :, pl.ds(start, span)] = highest + jnp.log(weight_sum)
        attended = low(attended)
        for part in range(ratio):
            place = block * ratio + part
            low_ref[head, place] = attended[:, part * chunk : (part + 1) * chunk]

            @pl.when(place != me)
            def send(place=place):
                c_copy(head, place).start()

        return unused

    lax.fori_loop(0, 2 * blocks, attend, 0)
    keep = pltpu.make_async_copy(rows_ref, rows_out, keep_sem)
    keep.start()
    for head in range(2):

        def collect(k, unused, head=head):
            c_wait(head, me ^ k)
            ctx_ref[head, me ^ k] = landing[head, me ^ k]
            return unused

        lax.fori_loop(1, group, collect, 0)
        ctx_ref[head, me] = low_ref[head, me]
    for k in range(1, fsdp):
        w_copy(k).wait_send()

    @pl.when(jnp.logical_not(v_own))
    def pair_sent():
        v_copy.wait_send()

    for kind in range(1, 6):
        x_copy(kind).wait_send()

    @pl.when(inner | (core == 1))
    def own_sent():
        x_copy(0).wait_send()

    @pl.when(inner & (core == 0))
    def lines_sent():
        x_copy(6).wait_send()
        x_copy(7).wait_send()

    @pl.when(core == 1)
    def direct_sent():
        x_copy(8).wait_send()

    for head in range(2):

        def sent(k, unused, head=head):
            c_copy(head, me ^ k).wait_send()
            return unused

        lax.fori_loop(1, group, sent, 0)
    keep.wait()


def forward_group(prefix, tokens, steps, gain, bias, mine, span, group, tp, fsdp):
    batches, chunk, width = tokens.shape
    length = group * chunk
    bf16, f32 = jnp.bfloat16, jnp.float32
    struct = jax.ShapeDtypeStruct
    inside = pl.BlockSpec(memory_space=pltpu.VMEM)
    dma = pltpu.SemaphoreType.DMA
    return pl.pallas_call(
        functools.partial(forward_kernel, span=span, tp=tp, fsdp=fsdp),
        in_specs=[pl.BlockSpec(memory_space=pltpu.SMEM)] + [inside] * 5,
        out_specs=[pl.BlockSpec(memory_space=pl.ANY)] + [inside] * 5,
        out_shape=[
            struct((group, chunk, width), bf16),
            struct((2, 3 * HEAD_DIM, length), bf16),
            struct((2, HEAD_DIM, length), f32),
            struct((2, 1, length), f32),
            struct((2, group, HEAD_DIM, chunk), bf16),
            struct((6 * HEAD_DIM, width), bf16),
        ],
        scratch_shapes=[
            pltpu.VMEM((group, chunk, width), bf16),
            pltpu.VMEM((1, chunk, width), bf16),
            pltpu.VMEM((fsdp,) + mine.shape, bf16),
            pltpu.VMEM(mine.shape, bf16),
            pltpu.VMEM((2, length, HEAD_DIM), bf16),
            pltpu.VMEM((2, HEAD_DIM + 16, length), bf16),
            pltpu.VMEM((2, group, HEAD_DIM, chunk), bf16),
            pltpu.VMEM((2, group, HEAD_DIM, chunk), bf16),
            dma((fsdp,)),
            dma((fsdp,)),
            dma((1,)),
            dma((1,)),
            dma((9,)),
            dma((group,)),
            dma((2, group)),
            dma((2, group)),
            dma,
        ],
        compiler_params=pltpu.CompilerParams(
            vmem_limit_bytes=VMEM_LIMIT, collective_id=1, has_side_effects=True
        ),
        cost_estimate=pl.CostEstimate(
            flops=60_000_000_000, bytes_accessed=30_000_000, transcendentals=20_000_000
        ),
        name="forward_group",
    )(prefix, tokens, steps, gain, bias, mine)


QUERY, KEY, VALUE, SELF_OUT, CROSS_OUT, UP, DOWN = 0, 1, 2, 3, 4, 5, 9


def middle_kernel(
    gathered,
    tokens_ref,
    step_ref,
    enc_ref,
    cot_ref,
    gain_ref,
    bias_ref,
    ctx_ref,
    final_ref,
    after_ref,
    back_ref,
    enc_grad_ref,
    stats_ref,
    packed_ref,
    weights,
    hidden_all,
    pre_all,
    three_all,
    two_all,
    grad_two_all,
    grad_one_all,
    cross_all,
    query_all,
    context_all,
    queries,
    keys,
    values,
    probs,
    grad_heads,
    grad_keys,
    grad_values,
    back_rows,
    landing,
    d_send,
    d_recv,
    sem,
    *,
    tp,
    fsdp,
):
    batches, chunk, width = tokens_ref.shape
    group = landing.shape[1]
    core, chip = lax.axis_index("ctx"), lax.axis_index("tp")
    me = core * tp + chip
    mine = chip // 2
    meet(group, tp, fsdp)
    piece = gathered.shape[-1]
    factor = HEAD_DIM**-0.5
    heads = width // HEAD_DIM

    copies = []
    for f in range(width // piece):
        for c in range(group // tp):
            for t in range(tp):
                head = t * (group // tp) + c
                copies.append(
                    pltpu.make_async_copy(
                        gathered.at[f, c, t],
                        weights.at[:, pl.ds(head * HEAD_DIM, HEAD_DIM), pl.ds(f * piece, piece)],
                        sem.at[(f * group // tp + c) * tp + t],
                    )
                )
    for copy in copies:
        copy.start()
    stats_ref[...] = jnp.zeros_like(stats_ref)
    for copy in copies:
        copy.wait()

    owners = [(2 * (2 * z + c) + n, n, c * tp + z) for z in (0, 1) for c in (0, 1) for n in (0, 1)]

    def d_copy(turn, seq, head, number, owner):
        return pltpu.make_async_remote_copy(
            src_ref=back_rows.at[turn, pl.ds(head * HEAD_DIM, HEAD_DIM)],
            dst_ref=landing.at[number, me],
            send_sem=d_send.at[turn, head],
            recv_sem=d_recv.at[number, me],
            device_id={"ctx": owner // tp, "tp": owner % tp + 2 * seq},
            device_id_type=MESH,
        )

    def one_sequence(turn, unused):
        seq = jnp.where(turn == 0, 1 - mine, mine)
        at = pl.ds(pl.multiple_of(seq * chunk, chunk), chunk)
        for head, number, owner in owners:
            context_all[head * HEAD_DIM : (head + 1) * HEAD_DIM, at] = ctx_ref[number, owner + 2 * seq]
        start_sum = tokens_ref[seq].astype(jnp.float32) + step_ref[seq]
        branch_one = dot_of(context_all[:, at], weights[SELF_OUT], 0, 0)
        after_one = start_sum + branch_one
        stats_ref[1:2, :] += jnp.sum(branch_one * branch_one, 0, keepdims=True)
        normed_two, unit_two, inverse_two = rows_norm(after_one, gain_ref[1:2], bias_ref[1:2])
        two_all[at, :] = normed_two
        queries[...] = low(dot_of(weights[QUERY], normed_two, 1, 1))
        keys[...] = low(dot_of(weights[KEY], enc_ref[seq], 1, 1))
        values[...] = low(dot_of(weights[VALUE], enc_ref[seq], 1, 1))

        def attend(head, unused):
            rows = pl.ds(pl.multiple_of(head * HEAD_DIM, HEAD_DIM), HEAD_DIM)
            scores = dot_of(keys[rows, :].T, queries[rows, :], 1, 0) * factor

            def strip(columns):
                powers = jnp.exp(columns - jnp.max(columns, 0, keepdims=True))
                return (powers / jnp.sum(powers, 0, keepdims=True),)

            (attn,) = in_strips(strip, scores, strip=128, axis=1)
            probs[head] = attn
            cross_all[rows, at] = low(dot_of(values[rows, :], low(attn), 1, 0))
            return unused

        lax.fori_loop(0, heads, attend, 0, unroll=8)
        branch_two = dot_of(cross_all[:, at], weights[CROSS_OUT], 0, 0)
        after_two = after_one + branch_two
        stats_ref[2:3, :] += jnp.sum(branch_two * branch_two, 0, keepdims=True)
        normed_three, unit_three, inverse_three = rows_norm(after_two, gain_ref[2:3], bias_ref[2:3])
        three_all[at, :] = normed_three
        grad_three = cot_ref[seq]

        def feed(part, carry):
            branch, grad = carry
            up, down = weights[UP + part], weights[DOWN + part]
            inputs = dot_of(up, normed_three, 1, 1)
            hidden, slopes = in_strips(gelu_strip, inputs, strip=32)
            branch = branch + dot_of(hidden, down, 0, 0)
            hidden_all[part, :, at] = hidden
            grad_pre = low(dot_of(down, grad_three, 1, 1) * slopes)
            pre_all[part, :, at] = grad_pre
            return branch, grad + dot_of(grad_pre, up, 0, 0)

        blank = jnp.zeros((chunk, width), jnp.float32)
        branch_three, grad_norm = lax.fori_loop(0, DOWN - UP, feed, (blank, blank), unroll=4)
        final_sum = after_two + branch_three
        final_ref[seq] = final_sum
        stats_ref[0:1, :] += jnp.sum(final_sum * final_sum, 0, keepdims=True)
        stats_ref[3:4, :] += jnp.sum(branch_three * branch_three, 0, keepdims=True)
        back, gain_sum, bias_sum = rows_back(grad_norm, unit_three, inverse_three, gain_ref[2:3])
        stats_ref[6:7, :] += gain_sum
        stats_ref[7:8, :] += bias_sum
        grad_after_two = grad_three.astype(jnp.float32) + back
        grad_two = low(grad_after_two)
        grad_two_all[at, :] = grad_two
        grad_heads[...] = low(dot_of(weights[CROSS_OUT], grad_two, 1, 1))

        def attend_back(head, unused):
            rows = pl.ds(pl.multiple_of(head * HEAD_DIM, HEAD_DIM), HEAD_DIM)
            grads = grad_heads[rows, :]
            attn = probs[head]
            grad_probs = dot_of(values[rows, :].T, grads, 1, 0)

            def strip(ones, others):
                return (low(ones * (others - jnp.sum(ones * others, 0, keepdims=True))),)

            (grad_scores,) = in_strips(strip, attn, grad_probs, strip=128, axis=1)
            query_all[rows, at] = low(dot_of(keys[rows, :], grad_scores, 1, 0) * factor)
            grad_keys[rows, :] = dot_of(queries[rows, :], grad_scores, 1, 1) * factor
            grad_values[rows, :] = dot_of(grads, low(attn), 1, 1)
            return unused

        lax.fori_loop(0, heads, attend_back, 0, unroll=8)
        enc_grad_ref[seq, :, :width] = low(grad_keys[...].T)
        enc_grad_ref[seq, :, width:] = low(grad_values[...].T)
        upstream = dot_of(query_all[:, at], weights[QUERY], 0, 0)
        back, gain_sum, bias_sum = rows_back(upstream, unit_two, inverse_two, gain_ref[1:2])
        stats_ref[4:5, :] += gain_sum
        stats_ref[5:6, :] += bias_sum
        grad_after_one = grad_after_two + back
        after_ref[seq] = grad_after_one
        grad_one = low(grad_after_one)
        grad_one_all[at, :] = grad_one
        back_rows[turn] = low(dot_of(weights[SELF_OUT], grad_one, 1, 1))
        for head, number, owner in owners:

            @pl.when(owner + 2 * seq != me)
            def give(head=head, number=number, owner=owner):
                d_copy(turn, seq, head, number, owner).start()

            @pl.when(owner + 2 * seq == me)
            def keep(head=head, number=number):
                back_ref[number, me] = back_rows[turn, head * HEAD_DIM : (head + 1) * HEAD_DIM, :]

        return unused


    lax.fori_loop(0, batches, one_sequence, 0)
    def pack(block, left, right):
        total = low(dot_of(left, right, 1, 0))
        for f in range(width // piece):
            for c in range(group // tp):
                for t in range(tp):
                    head = t * (group // tp) + c
                    packed_ref[c, f, t, block] = total[
                        head * HEAD_DIM : (head + 1) * HEAD_DIM, f * piece : (f + 1) * piece
                    ]

    grad_three_all = cot_ref[...].reshape(batches * chunk, width)
    pack(0, query_all[...], two_all[...])
    pack(1, context_all[...], grad_one_all[...])
    pack(2, cross_all[...], grad_two_all[...])

    def pack_feed(part, unused):
        pack(UP - 2 + part, pre_all[part], three_all[...])
        pack(DOWN - 2 + part, hidden_all[part], grad_three_all)
        return unused

    lax.fori_loop(0, DOWN - UP, pack_feed, 0)

    def collect(k, unused):
        place = me ^ k
        for number in range(2):
            pltpu.make_async_remote_copy(
                src_ref=landing.at[number, place],
                dst_ref=landing.at[number, place],
                send_sem=d_send.at[0, 0],
                recv_sem=d_recv.at[number, place],
                device_id={"ctx": place // tp, "tp": place % tp},
                device_id_type=MESH,
            ).wait_recv()
            back_ref[number, place] = landing[number, place]
        return unused

    lax.fori_loop(1, group, collect, 0)
    for turn in range(batches):
        seq = 1 - mine if turn == 0 else mine
        for head, number, owner in owners:

            @pl.when(owner + 2 * seq != me)
            def given(turn=turn, seq=seq, head=head, number=number, owner=owner):
                d_copy(turn, seq, head, number, owner).wait_send()


def middle(
    gathered, tokens, steps, encoder, cotangent, gains, biases, contexts, tp, fsdp
):
    batches, chunk, width = tokens.shape
    group = contexts.shape[1]
    enc_count = encoder.shape[1]
    heads = width // HEAD_DIM
    bf16, f32 = jnp.bfloat16, jnp.float32
    struct = jax.ShapeDtypeStruct
    inside = pl.BlockSpec(memory_space=pltpu.VMEM)
    dma = pltpu.SemaphoreType.DMA
    count = gathered.shape[3]
    packed = (group // tp, gathered.shape[0], tp, count - 2) + gathered.shape[4:]
    return pl.pallas_call(
        functools.partial(middle_kernel, tp=tp, fsdp=fsdp),
        in_specs=[pl.BlockSpec(memory_space=pl.ANY)] + [inside] * 7,
        out_specs=[inside] * 6,
        out_shape=[
            struct((batches, chunk, width), f32),
            struct((batches, chunk, width), f32),
            struct((2, group, HEAD_DIM, chunk), bf16),
            struct((batches, enc_count, 2 * width), bf16),
            struct((8, width), f32),
            struct(packed, bf16),
        ],
        scratch_shapes=[
            pltpu.VMEM((count, width, width), bf16),
            pltpu.VMEM((DOWN - UP, width, batches * chunk), bf16),
            pltpu.VMEM((DOWN - UP, width, batches * chunk), bf16),
            pltpu.VMEM((batches * chunk, width), bf16),
            pltpu.VMEM((batches * chunk, width), bf16),
            pltpu.VMEM((batches * chunk, width), bf16),
            pltpu.VMEM((batches * chunk, width), bf16),
            pltpu.VMEM((width, batches * chunk), bf16),
            pltpu.VMEM((width, batches * chunk), bf16),
            pltpu.VMEM((width, batches * chunk), bf16),
            pltpu.VMEM((width, chunk), bf16),
            pltpu.VMEM((width, enc_count), bf16),
            pltpu.VMEM((width, enc_count), bf16),
            pltpu.VMEM((heads, enc_count, chunk), f32),
            pltpu.VMEM((width, chunk), bf16),
            pltpu.VMEM((width, enc_count), f32),
            pltpu.VMEM((width, enc_count), f32),
            pltpu.VMEM((batches, width, chunk), bf16),
            pltpu.VMEM((2, group, HEAD_DIM, chunk), bf16),
            dma((batches, heads)),
            dma((2, group)),
            dma((32,)),
        ],
        compiler_params=pltpu.CompilerParams(
            vmem_limit_bytes=VMEM_LIMIT, collective_id=3, has_side_effects=True
        ),
        cost_estimate=pl.CostEstimate(
            flops=30_000_000_000, bytes_accessed=30_000_000, transcendentals=10_000_000
        ),
        name="middle",
    )(gathered, tokens, steps, encoder, cotangent, gains, biases, contexts)


def backward_kernel(
    prefix_ref,
    enc_parts,
    packed,
    gathered,
    rows_in,
    landing,
    weight,
    qkv_ref,
    wide_ref,
    log_ref,
    tokens_ref,
    step_ref,
    gain_ref,
    bias_ref,
    after_ref,
    enc_ref,
    stats_ref,
    input_ref,
    enc_out,
    self_out,
    query_out,
    pair_out,
    back_out,
    cross_out,
    up_out,
    down_out,
    sums_out,
    outgoing,
    core_rows,
    core_rows_landing,
    sum_rows,
    incoming,
    queries_ref,
    pairs_ref,
    grad_ref,
    delta_ref,
    grad_pairs_ref,
    rows_ref,
    pair_weights,
    enc_own,
    enc_core,
    enc_sum,
    enc_landing,
    pair_ref,
    pair_landing,
    core_landing,
    partial_ref,
    fsdp_landing,
    line_ref,
    line_landing,
    shard_ref,
    head_ref,
    head_landing,
    head_pair,
    head_two,
    sums_ref,
    sums_landing,
    sums_two,
    e_send,
    e_recv,
    x_send,
    x_recv,
    i_send,
    i_recv,
    r_send,
    r_recv,
    f_send,
    f_recv,
    t_send,
    t_recv,
    h_send,
    h_recv,
    p_send,
    p_recv,
    s_send,
    s_recv,
    local_sem,
    rows_sem,
    *,
    span,
    tp,
    fsdp,
):
    batches, chunk, width = tokens_ref.shape
    group = landing.shape[1]
    length = group * chunk
    blocks, ratio = length // span, span // chunk
    wide_blocks = max(1, length // 2 // span)
    factor = HEAD_DIM**-0.5
    here, core, chip = lax.axis_index("fsdp"), lax.axis_index("ctx"), lax.axis_index("tp")
    me = core * tp + chip
    mine = chip // 2
    cores = group // tp
    share = enc_landing.shape[2]
    piece = width // fsdp
    early = packed.shape[3]
    meet(group, tp, fsdp)

    def send_to(source, target, send, recv, **place):
        return pltpu.make_async_remote_copy(
            src_ref=source,
            dst_ref=target,
            send_sem=send,
            recv_sem=recv,
            device_id=place,
            device_id_type=MESH,
        )

    def member(place):
        return {"ctx": place // tp, "tp": place % tp}

    local = [
        pltpu.make_async_copy(
            packed.at[core], partial_ref.at[:, :, pl.ds(0, early)], local_sem.at[0]
        ),
        pltpu.make_async_copy(
            enc_parts.at[:, pl.ds(pl.multiple_of(core * tp * share, share), tp * share)],
            enc_own,
            local_sem.at[1],
        ),
    ]
    first = len(local)
    for f in range(fsdp):
        for c in range(cores):
            for t in range(tp):
                head = t * cores + c
                local.append(
                    pltpu.make_async_copy(
                        gathered.at[f, c, t, pl.ds(KEY, 2)],
                        pair_weights.at[
                            :, pl.ds(head * HEAD_DIM, HEAD_DIM), pl.ds(f * piece, piece)
                        ],
                        local_sem.at[first + (f * cores + c) * tp + t],
                    )
                )
    enc_copy = send_to(
        enc_parts.at[:, pl.ds(pl.multiple_of((1 - core) * tp * share, share), tp * share)],
        enc_core,
        e_send.at[0],
        e_recv.at[0],
        ctx=1 - core,
    )
    enc_line = [
        send_to(
            enc_sum.at[chip ^ n], enc_landing.at[n - 1], e_send.at[n], e_recv.at[n], tp=chip ^ n
        )
        for n in range(1, tp)
    ]

    core_copy = send_to(
        packed.at[1 - core], core_landing, r_send.at[0], r_recv.at[0], ctx=1 - core
    )
    pair_copy = send_to(
        pair_ref.at[1 - core], pair_landing, r_send.at[1], r_recv.at[1], ctx=1 - core
    )
    shard_copy = send_to(
        shard_ref.at[core], shard_ref.at[core], r_send.at[2], r_recv.at[2], ctx=1 - core
    )
    shard_wait = send_to(
        shard_ref.at[1 - core], shard_ref.at[1 - core], r_send.at[2], r_recv.at[2], ctx=1 - core
    )
    f_copies = [
        send_to(
            partial_ref.at[here ^ n, :, pl.ds(0, early)],
            fsdp_landing.at[n - 1, :, pl.ds(0, early)],
            f_send.at[n],
            f_recv.at[n],
            fsdp=here ^ n,
        )
        for n in range(1, fsdp)
    ]
    f_pairs = [
        send_to(
            partial_ref.at[here ^ n, :, pl.ds(early, 2)],
            fsdp_landing.at[n - 1, :, pl.ds(early, 2)],
            f_send.at[fsdp + n],
            f_recv.at[fsdp + n],
            fsdp=here ^ n,
        )
        for n in range(1, fsdp)
    ]
    t_copies = [
        send_to(line_ref.at[chip ^ k], line_landing.at[k - 1], t_send.at[k], t_recv.at[k], tp=chip ^ k)
        for k in range(1, tp)
    ]
    h_copies = [
        send_to(
            head_ref.at[here ^ k], head_landing.at[k - 1], h_send.at[k], h_recv.at[k], fsdp=here ^ k
        )
        for k in range(1, fsdp)
    ]

    pair_chip = 2 * (chip % 2) + core
    p_copies = [
        send_to(head_pair, head_two.at[mine], p_send.at[c], p_recv.at[mine], ctx=c, tp=pair_chip)
        for c in range(2)
    ]
    p_waits = [
        send_to(head_pair, head_two.at[n], p_send.at[0], p_recv.at[n], ctx=c, tp=t)
        for n, c, t in ((0, chip % 2, chip // 2), (1, chip % 2, chip // 2 + 2))
    ]
    p_here = [
        (core == chip % 2) & (chip == chip // 2 + 2 * n) for n in range(2)
    ]

    def s_copy(k):
        return send_to(
            sums_ref, sums_landing.at[k], s_send.at[k], s_recv.at[k], **member(me ^ k)
        )

    s_fsdp = [
        send_to(
            sums_two, sums_landing.at[group + k], s_send.at[group + k], s_recv.at[group + k], fsdp=here ^ k
        )
        for k in range(1, fsdp)
    ]

    enc_copy.start()
    core_copy.start()
    for copy in local:
        copy.start()

    def core_rows_copy(place):
        slot = place % tp
        return send_to(
            core_rows.at[slot], core_rows_landing.at[slot], x_send.at[slot], x_recv.at[slot], ctx=1 - core
        )

    def owner_copy(place):
        slot = place % tp
        return send_to(
            sum_rows.at[slot],
            incoming.at[mine, chip % 2],
            i_send.at[slot],
            i_recv.at[mine, chip % 2],
            tp=slot,
        )

    def spread(place):
        upstream = dot_of(outgoing[place].reshape(6 * HEAD_DIM, chunk), weight[...], 0, 0)
        slot = place % tp

        @pl.when(place // tp != core)
        def hand_over():
            core_rows[slot] = low(upstream)
            core_rows_copy(place).start()

        @pl.when(place // tp == core)
        def collect():
            core_rows_copy(place).wait_recv()
            total = low(upstream + core_rows_landing[slot].astype(jnp.float32))

            @pl.when(place == me)
            def own():
                incoming[mine, chip % 2] = total

            @pl.when(place != me)
            def send():
                sum_rows[slot] = total
                owner_copy(place).start()

    def prepare(seq):
        def lay(place, unused):
            at = pl.ds(pl.multiple_of(place * chunk, chunk), chunk)
            grads = landing[seq, place]
            blank = jnp.zeros_like(grads)
            grad_ref[seq, at, :] = jnp.concatenate([blank, grads], 0).T
            delta_ref[seq, :, at] = jnp.sum(
                grads.astype(jnp.float32) * wide_ref[seq, :, at], axis=0, keepdims=True
            )
            queries_ref[seq, at, :] = jnp.concatenate([qkv_ref[seq, :HEAD_DIM, at], blank], 0).T
            pairs_ref[seq, at, :] = qkv_ref[seq, HEAD_DIM:, at].T
            return unused

        lax.fori_loop(0, group, lay, 0)
        grad_pairs_ref[seq] = jnp.zeros(grad_pairs_ref.shape[1:], jnp.float32)

    def encoder_cores():
        local[1].wait()
        enc_copy.wait_recv()
        for t in range(tp):
            lines = slice(t * share, (t + 1) * share)
            enc_sum[t] = low(
                enc_own[:, lines].astype(jnp.float32) + enc_core[:, lines].astype(jnp.float32)
            )
        for copy in enc_line:
            copy.start()

    def encoder_part():
        total = enc_sum[chip].astype(jnp.float32)
        for n, copy in enumerate(enc_line):
            copy.wait_recv()
            total = total + enc_landing[n].astype(jnp.float32)
        for copy in local[first:]:
            copy.wait()
        grads = low(total)
        enc_rows = enc_ref[:, pl.ds(pl.multiple_of(me * share, share), share), :]
        flat, enc_flat = grads.reshape(batches * share, 2 * width), enc_rows.reshape(
            batches * share, width
        )
        result = dot_of(flat[:, :width], pair_weights[0], 1, 0) + dot_of(
            flat[:, width:], pair_weights[1], 1, 0
        )
        enc_out[...] = result.reshape(batches, share, width)
        for which in range(2):
            grad = low(dot_of(flat[:, which * width : (which + 1) * width], enc_flat, 0, 0))
            for f in range(fsdp):
                for c in range(cores):
                    for t in range(tp):
                        head = t * cores + c
                        pair_ref[c, f, t, which] = grad[
                            head * HEAD_DIM : (head + 1) * HEAD_DIM, f * piece : (f + 1) * piece
                        ]
        pair_copy.start()

    def sum_cores():
        local[0].wait()
        core_copy.wait_recv()

        def one(f, unused):
            def two(t, unused):
                partial_ref[f, t, :early] = low(
                    partial_ref[f, t, :early].astype(jnp.float32)
                    + core_landing[f, t].astype(jnp.float32)
                )
                return unused

            return lax.fori_loop(0, tp, two, unused)

        lax.fori_loop(0, fsdp, one, 0)
        for copy in f_copies:
            copy.start()

    def sum_pairs():
        pair_copy.wait_recv()
        for f in range(fsdp):
            for t in range(tp):
                partial_ref[f, t, early:] = low(
                    pair_ref[core, f, t].astype(jnp.float32)
                    + pair_landing[f, t].astype(jnp.float32)
                )
        for copy in f_pairs:
            copy.start()

    def sum_fsdp():
        for copy in f_copies + f_pairs:
            copy.wait_recv()

        def one(t, unused):
            total = partial_ref[here, t].astype(jnp.float32)
            for k in range(fsdp - 1):
                total = total + fsdp_landing[k, t].astype(jnp.float32)
            line_ref[t] = low(total)
            return unused

        lax.fori_loop(0, tp, one, 0)
        for copy in t_copies:
            copy.start()

    def sum_line():
        for copy in t_copies:
            copy.wait_recv()
        total = line_ref[chip].astype(jnp.float32)
        for k in range(tp - 1):
            total = total + line_landing[k].astype(jnp.float32)
        shard_ref[core] = total
        shard_copy.start()

    for head in range(2):
        prepare(head)

    def attend(index, unused):
        block, seq = blocks - 1 - index // 2, index % 2

        def hook(at, work):
            @pl.when(index == at)
            def run():
                work()

        hook(1, encoder_cores)
        hook(1, sum_cores)
        hook(2, encoder_part)
        hook(3, sum_pairs)
        hook(5, sum_fsdp)
        start = pl.multiple_of(block * span, span)
        at = pl.ds(start, span)
        blank = jnp.zeros((HEAD_DIM, span), jnp.bfloat16)
        queries_t = jnp.concatenate([qkv_ref[seq, :HEAD_DIM, at], blank], 0)
        queries = queries_ref[seq, at, :]
        grads = grad_ref[seq, at, :]
        grads_t = jnp.concatenate(
            [landing[seq, block * ratio + part] for part in range(ratio)], 1
        )
        grads_t = jnp.concatenate([blank, grads_t], 0)
        logs, deltas = log_ref[seq, :, at], delta_ref[seq, :, at]
        limit = jnp.maximum(
            prefix_ref[mine], start + 1 + lax.broadcasted_iota(jnp.int32, (1, span), 1)
        )

        def advance(other, grad_queries, masked):
            offset = pl.multiple_of(other * span, span)
            there = pl.ds(offset, span)
            pairs = pairs_ref[seq, there, :]
            scores = dot_of(pairs, queries_t, 1, 0)
            if masked:
                scores = hide(scores, limit, offset)
            probs = jnp.exp(scores - logs)
            grad_probs = dot_of(pairs, grads_t, 1, 0)
            grad_scores = low(probs * (grad_probs - deltas))
            grad_pairs_ref[seq, there, :] += dot_of(low(probs), grads, 1, 0) + dot_of(
                grad_scores, queries, 1, 0
            )
            return grad_queries + dot_of(
                qkv_ref[seq, HEAD_DIM : 2 * HEAD_DIM, there], grad_scores, 1, 0
            )

        grad_queries = jnp.zeros((HEAD_DIM, span), jnp.float32)
        grad_queries = lax.fori_loop(0, block, lambda j, c: advance(j, c, False), grad_queries)
        grad_queries = lax.fori_loop(
            block, jnp.maximum(block + 1, wide_blocks), lambda j, c: advance(j, c, True), grad_queries
        )
        done = low(grad_queries * factor)
        for part in range(ratio):
            place = block * ratio + part
            outgoing[place, seq, :HEAD_DIM, :] = done[:, part * chunk : (part + 1) * chunk]

        lowest = jnp.where(block == 0, 0, block)
        highest = jnp.where(
            block == 0, wide_blocks, jnp.where(block >= wide_blocks, block + 1, block)
        )

        def give(place, unused):
            at = pl.ds(pl.multiple_of(place * chunk, chunk), chunk)
            outgoing[place, seq, HEAD_DIM:, :] = low(grad_pairs_ref[seq, at, :].T)
            return unused

        lax.fori_loop(lowest * ratio, highest * ratio, give, 0)

        @pl.when(seq == 1)
        def both_heads():
            def one(place, unused):
                spread(place)
                return unused

            lax.fori_loop(lowest * ratio, highest * ratio, one, 0)

        return unused

    lax.fori_loop(0, 2 * blocks, attend, 0)
    sums_ref[...] = jnp.zeros_like(sums_ref)
    sums_ref[:8, :] = stats_ref[...]

    def rows_copy(number):
        return pltpu.make_async_copy(
            rows_in.at[number],
            rows_ref.at[number % rows_ref.shape[0]],
            rows_sem.at[number % rows_ref.shape[0]],
        )

    depth = rows_ref.shape[0]
    for number in range(depth):
        rows_copy(number).start()

    ones = jnp.ones((chunk, piece), jnp.bfloat16)

    def weigh(number, totals):
        rows_copy(number).wait()
        grads = outgoing[number].reshape(6 * HEAD_DIM, chunk)
        total = totals[0] + dot_of(grads, rows_ref[number % depth], 1, 0)

        @pl.when(number + depth < group)
        def more():
            rows_copy(number + depth).start()

        return total, totals[1] + dot_of(grads, ones, 1, 0)

    total, plain = lax.fori_loop(
        0,
        group,
        weigh,
        (
            jnp.zeros((6 * HEAD_DIM, width), jnp.float32),
            jnp.zeros((6 * HEAD_DIM, piece), jnp.float32),
        ),
    )
    weights = weight[...].astype(jnp.float32)
    bias_sum = jnp.sum(weights * jnp.concatenate([plain] * (width // piece), 1), 0, keepdims=True)
    gain_sum = jnp.sum(weights * total, 0, keepdims=True) - bias_ref[0:1] * bias_sum
    sums_ref[8:9, :] = gain_sum / gain_ref[0:1]
    sums_ref[9:10, :] = bias_sum

    def start_sums(k, unused):
        s_copy(k).start()
        return unused

    lax.fori_loop(1, group, start_sums, 0)
    for f in range(fsdp):
        head_ref[f] = total[:, f * piece : (f + 1) * piece]
    for copy in h_copies:
        copy.start()
    sum_line()

    for copy in h_copies:
        copy.wait_recv()
    total = head_ref[here]
    for k in range(fsdp - 1):
        total = total + head_landing[k]
    head_pair[...] = low(total)
    for c in range(2):
        there = (core == c) & (pair_chip == chip)

        @pl.when(there)
        def stay():
            head_two[mine] = head_pair[...]

        @pl.when(jnp.logical_not(there))
        def leave(c=c):
            p_copies[c].start()

    def arrive_sums(k, total):
        s_copy(k).wait_recv()
        return total + sums_landing[k]

    sums_two[...] = lax.fori_loop(1, group, arrive_sums, sums_ref[...])
    for copy in s_fsdp:
        copy.start()

    def finish(seq, unused):
        for number in range(2):
            source = 2 * seq + number

            @pl.when(source != chip)
            def come(number=number, source=source):
                send_to(
                    incoming.at[seq, number],
                    incoming.at[seq, number],
                    i_send.at[0],
                    i_recv.at[seq, number],
                    tp=source,
                ).wait_recv()

        upstream = incoming[seq, 0].astype(jnp.float32) + incoming[seq, 1].astype(jnp.float32)
        start_sum = tokens_ref[seq].astype(jnp.float32) + step_ref[seq]
        unit_rows, inverse = in_strips(rows_unit, start_sum)
        input_ref[seq] = after_ref[seq] + rows_back(
            upstream, unit_rows, inverse, gain_ref[0:1]
        )[0]
        return unused

    lax.fori_loop(0, batches, finish, 0)

    shard_wait.wait_recv()

    def whole(block):
        return jnp.concatenate([shard_ref[0, block], shard_ref[1, block]], 0)

    query_out[...] = whole(0).T
    back_out[...] = whole(1)
    cross_out[...] = whole(2)
    for part in range(4):
        up_out[:, part * piece : (part + 1) * piece] = whole(3 + part).T
        down_out[part * piece : (part + 1) * piece, :] = whole(7 + part)
    pair_out[0] = whole(11).T
    pair_out[1] = whole(12).T
    for n in range(2):

        @pl.when(jnp.logical_not(p_here[n]))
        def pair_come(n=n):
            p_waits[n].wait_recv()

    total = head_two[0].astype(jnp.float32) + head_two[1].astype(jnp.float32)
    for which in range(3):
        self_out[which] = jnp.concatenate(
            [
                total[(3 * n + which) * HEAD_DIM : (3 * n + which + 1) * HEAD_DIM]
                for n in range(2)
            ],
            0,
        ).T
    total = sums_two[...]
    for k, copy in enumerate(s_fsdp):
        copy.wait_recv()
        total = total + sums_landing[group + 1 + k]
    sums_out[...] = total
    core_copy.wait_send()
    pair_copy.wait_send()
    shard_copy.wait_send()
    for c in range(2):

        @pl.when(jnp.logical_not((core == c) & (pair_chip == chip)))
        def pair_sent(c=c):
            p_copies[c].wait_send()

    enc_copy.wait_send()
    for copy in enc_line + f_copies + f_pairs + t_copies + h_copies + s_fsdp:
        copy.wait_send()

    def sent(k, unused):
        s_copy(k).wait_send()
        return unused

    lax.fori_loop(1, group, sent, 0)

    def rows_sent(slot, unused):
        core_rows_copy((1 - core) * tp + slot).wait_send()

        @pl.when(slot != chip)
        def left():
            owner_copy(core * tp + slot).wait_send()

        return unused

    lax.fori_loop(0, tp, rows_sent, 0)


def backward_group(
    prefix,
    enc_parts,
    packed,
    gathered,
    rows,
    returned,
    weight,
    qkv,
    wide,
    logs,
    tokens,
    steps,
    gain,
    bias,
    after,
    encoder,
    stats,
    span,
    tp,
    fsdp,
):
    batches, chunk, width = tokens.shape
    group = returned.shape[1]
    length = group * chunk
    share = encoder.shape[1] // group
    piece = width // fsdp
    count = packed.shape[3]
    tail = packed.shape[4:]
    bf16, f32 = jnp.bfloat16, jnp.float32
    struct = jax.ShapeDtypeStruct
    inside = pl.BlockSpec(memory_space=pltpu.VMEM)
    outside = pl.BlockSpec(memory_space=pl.ANY)
    dma = pltpu.SemaphoreType.DMA
    vmem = pltpu.VMEM
    parts = group * fsdp
    return pl.pallas_call(
        functools.partial(backward_kernel, span=span, tp=tp, fsdp=fsdp),
        in_specs=[pl.BlockSpec(memory_space=pltpu.SMEM)] + [outside] * 4 + [inside] * 12,
        out_specs=[inside] * 10,
        out_shape=[
            struct((batches, chunk, width), f32),
            struct((batches, share, width), f32),
            struct((3, piece, piece), f32),
            struct((piece, piece), f32),
            struct((2, piece, piece), f32),
            struct((piece, piece), f32),
            struct((piece, piece), f32),
            struct((piece, width), f32),
            struct((width, piece), f32),
            struct((16, width), f32),
        ],
        scratch_shapes=[
            vmem((group, 2, 3 * HEAD_DIM, chunk), bf16),
            vmem((tp, chunk, width), bf16),
            vmem((tp, chunk, width), bf16),
            vmem((tp, chunk, width), bf16),
            vmem((batches, 2, chunk, width), bf16),
            vmem((2, length, 2 * HEAD_DIM), bf16),
            vmem((2, length, 2 * HEAD_DIM), bf16),
            vmem((2, length, 2 * HEAD_DIM), bf16),
            vmem((2, 1, length), f32),
            vmem((2, length, 2 * HEAD_DIM), f32),
            vmem((2, chunk, width), bf16),
            vmem((2, width, width), bf16),
            vmem((batches, tp * share, 2 * width), bf16),
            vmem((batches, tp * share, 2 * width), bf16),
            vmem((tp, batches, share, 2 * width), bf16),
            vmem((tp - 1, batches, share, 2 * width), bf16),
            vmem((group // tp, fsdp, tp, 2) + tail, bf16),
            vmem((fsdp, tp, 2) + tail, bf16),
            vmem((fsdp, tp, count) + tail, bf16),
            vmem((fsdp, tp, count + 2) + tail, bf16),
            vmem((fsdp - 1, tp, count + 2) + tail, bf16),
            vmem((tp, count + 2) + tail, bf16),
            vmem((tp - 1, count + 2) + tail, bf16),
            vmem((2, count + 2) + tail, f32),
            vmem((fsdp, 6 * HEAD_DIM, piece), f32),
            vmem((fsdp - 1, 6 * HEAD_DIM, piece), f32),
            vmem((6 * HEAD_DIM, piece), bf16),
            vmem((2, 6 * HEAD_DIM, piece), bf16),
            vmem((16, width), f32),
            vmem((group + fsdp, 16, width), f32),
            vmem((16, width), f32),
            dma((tp,)),
            dma((tp,)),
            dma((tp,)),
            dma((tp,)),
            dma((tp,)),
            dma((batches, 2)),
            dma((4,)),
            dma((4,)),
            dma((2 * fsdp,)),
            dma((2 * fsdp,)),
            dma((tp,)),
            dma((tp,)),
            dma((fsdp,)),
            dma((fsdp,)),
            dma((2,)),
            dma((2,)),
            dma((group + fsdp,)),
            dma((group + fsdp,)),
            dma((2 + parts,)),
            dma((2,)),
        ],
        compiler_params=pltpu.CompilerParams(
            vmem_limit_bytes=VMEM_LIMIT, collective_id=2, has_side_effects=True
        ),
        cost_estimate=pl.CostEstimate(
            flops=100_000_000_000, bytes_accessed=40_000_000, transcendentals=20_000_000
        ),
        name="backward_group",
    )(
        prefix,
        enc_parts,
        packed,
        gathered,
        rows,
        returned,
        weight,
        qkv,
        wide,
        logs,
        tokens,
        steps,
        gain,
        bias,
        after,
        encoder,
        stats,
    )


def pack_kernel(
    scalars,
    table_ref,
    qkv_ref,
    query_ref,
    pair_ref,
    self_ref,
    cross_ref,
    up_ref,
    down_ref,
    half_ref,
    mine_ref,
    steps_ref,
    blocks,
):
    piece = query_ref.shape[0]
    blocks[0] = query_ref[...].T
    for n in range(2):
        blocks[1 + n] = pair_ref[n].T
    blocks[3] = self_ref[...]
    blocks[4] = cross_ref[...]
    for n in range(4):
        blocks[5 + n] = up_ref[:, n * piece : (n + 1) * piece].T
        blocks[9 + n] = down_ref[n * piece : (n + 1) * piece, :]
    half = piece // 2
    half_ref[...] = blocks[:, pl.ds(pl.multiple_of(scalars[0] * half, half), half), :]
    for which in range(3):
        flipped = qkv_ref[which].T
        for head in range(2):
            mine_ref[(3 * head + which) * HEAD_DIM : (3 * head + which + 1) * HEAD_DIM, :] = (
                flipped[head * HEAD_DIM : (head + 1) * HEAD_DIM]
            )
    table = table_ref[...].astype(jnp.float32)
    rows = lax.broadcasted_iota(jnp.int32, table.shape, 0)
    for seq in range(steps_ref.shape[0]):
        chosen = jnp.where(rows == scalars[1 + seq], table, 0.0)
        steps_ref[seq] = jnp.sum(chosen, 0, keepdims=True)


def pack_weights(scalars, table, self_qkv, cross_q, cross_kv, self_out, cross_out, up, down):
    piece = cross_q.shape[0]
    width = table.shape[1]
    batches = scalars.shape[0] - 1
    bf16 = jnp.bfloat16
    struct = jax.ShapeDtypeStruct
    inside = pl.BlockSpec(memory_space=pltpu.VMEM)
    return pl.pallas_call(
        pack_kernel,
        in_specs=[pl.BlockSpec(memory_space=pltpu.SMEM)] + [inside] * 8,
        out_specs=[inside] * 3,
        out_shape=[
            struct((13, piece // 2, piece), bf16),
            struct((3 * piece, piece), bf16),
            struct((batches, 1, width), jnp.float32),
        ],
        scratch_shapes=[pltpu.VMEM((13, piece, piece), bf16)],
        name="pack_weights",
    )(scalars, table, self_qkv, cross_q, cross_kv, self_out, cross_out, up, down)


def collect_kernel(*refs, large, small, entries):
    ins, outs = refs[: large + small + 1], refs[large + small + 1 :]
    for n in range(large):
        outs[n][...] = ins[n][...]

    @pl.when(pl.program_id(0) == 0)
    def once():
        for n in range(large, large + small):
            outs[n][...] = ins[n][...]
        sums = ins[large + small]
        gain_ref, bias_ref, feed_ref, norms_ref = outs[large + small :]
        for n, row in enumerate((8, 4, 6)):
            gain_ref[n : n + 1, :] = sums[row : row + 1, :]
        for n, row in enumerate((9, 5)):
            bias_ref[n : n + 1, :] = sums[row : row + 1, :]
        feed_ref[...] = sums[7:8, :]
        norms_ref[...] = jnp.sqrt(jnp.sum(sums[0:4, :], 1, keepdims=True) * (1.0 / entries))


def collect(large, small, sums, entries):
    width = sums.shape[1]
    f32 = jnp.float32
    struct = jax.ShapeDtypeStruct
    rest = [struct(v.shape, v.dtype) for v in small]
    extra = [struct((3, width), f32), struct((2, width), f32), struct((1, width), f32)]
    extra = extra + [struct((4, 1), f32)]
    still = lambda v: pl.BlockSpec(v.shape, lambda i, rank=len(v.shape): (0,) * rank)
    steps = 4
    moving = lambda v: pl.BlockSpec(
        (1, v.shape[0] * v.shape[1] // steps, v.shape[2]),
        lambda i, per=steps // v.shape[0]: (i // per, i % per, 0),
    )
    return pl.pallas_call(
        functools.partial(collect_kernel, large=len(large), small=len(small), entries=entries),
        grid=(steps,),
        in_specs=[moving(v) for v in large] + [still(v) for v in small] + [still(sums)],
        out_specs=[moving(v) for v in large] + [still(v) for v in rest + extra],
        out_shape=[struct(v.shape, v.dtype) for v in large] + rest + extra,
        name="collect",
    )(*large, *small, sums)


def local_heads(
    tokens,
    timesteps,
    time_table,
    prefix,
    encoder,
    self_qkv,
    cross_q,
    cross_kv,
    self_out,
    cross_out,
    ffn_up,
    ffn_down,
    norm_gain,
    norm_bias,
    cotangent,
):
    batches, chunk, width = tokens.shape
    group = 8
    length = group * chunk
    ctx_index = lax.axis_index("ctx")
    span = 1024
    own_half, mine, embedded = pack_weights(
        jnp.concatenate([ctx_index[None].astype(jnp.int32), timesteps]),
        time_table,
        self_qkv,
        cross_q,
        cross_kv,
        self_out,
        cross_out,
        ffn_up,
        ffn_down,
    )
    gathered = lax.all_gather(own_half, ("fsdp", "ctx", "tp"), axis=0, tiled=False)
    gathered = gathered.reshape((4, 2, 4) + own_half.shape)
    rows, qkv, wide, logs, contexts, weight = forward_group(
        prefix, tokens, embedded, norm_gain, norm_bias, mine, span, group, 4, 4
    )
    final, grad_after, returned, enc_parts, stats, packed = middle(
        gathered,
        tokens,
        embedded,
        encoder,
        cotangent,
        norm_gain,
        norm_bias,
        contexts,
        4,
        4,
    )
    outs = backward_group(
        prefix,
        enc_parts,
        packed,
        gathered,
        rows,
        returned,
        weight,
        qkv,
        wide,
        logs,
        tokens,
        embedded,
        norm_gain,
        norm_bias,
        grad_after,
        encoder,
        stats,
        span,
        4,
        4,
    )
    sums = outs[9]
    entries = (
        tokens.shape[0]
        * tokens.shape[1]
        * tokens.shape[2]
        * lax.axis_size("fsdp")
        * lax.axis_size("ctx")
        * lax.axis_size("tp")
    )
    results = collect((final, *outs[:2]), outs[2:9], sums, entries)
    return (*results[:12], results[12].reshape(width), results[13].reshape(4))


def solution(mesh):
    placed = (
        P("fsdp", ("ctx", "tp"), None),
        P("fsdp"),
        P(),
        P("fsdp"),
        P("fsdp", None, None),
        P(None, "fsdp", "tp"),
        P("fsdp", "tp"),
        P(None, "fsdp", "tp"),
        P("tp", "fsdp"),
        P("tp", "fsdp"),
        P("fsdp", "tp"),
        P("tp", "fsdp"),
        P(),
        P(),
        P("fsdp", ("ctx", "tp"), None),
    )
    heads_fit = dict(mesh.shape) == {"fsdp": 4, "ctx": 2, "tp": 4}
    return jax.shard_map(
        local_heads if heads_fit else local,
        mesh=mesh,
        in_specs=placed,
        out_specs=(
            P("fsdp", ("ctx", "tp"), None),
            P("fsdp", ("ctx", "tp"), None),
            P("fsdp", ("ctx", "tp"), None),
            P(None, "fsdp", "tp"),
            P("fsdp", "tp"),
            P(None, "fsdp", "tp"),
            P("tp", "fsdp"),
            P("tp", "fsdp"),
            P("fsdp", "tp"),
            P("tp", "fsdp"),
            P(),
            P(),
            P(),
            P(),
        ),
        check_vma=False,
    )
```

```python
import functools
import math

import jax
import jax.numpy as jnp
from jax import lax
from jax.experimental import pallas as pl
from jax.experimental.pallas import tpu as pltpu
from jax.sharding import PartitionSpec as P

HEAD_DIM = 64


EPS = 1e-05
NEG = -1e30
ROOT_HALF = 1.0 / math.sqrt(2.0)
INV_ROOT_TWO_PI = 1.0 / math.sqrt(2.0 * math.pi)
VMEM_LIMIT = 63 * 2**20


def norm_rows(hidden, scaling, offsets):
    centre = hidden - jnp.mean(hidden, -1, keepdims=True)
    inverse = lax.rsqrt(jnp.mean(centre * centre, -1, keepdims=True) + EPS)
    unit_rows = centre * inverse
    return (unit_rows * scaling + offsets, unit_rows, inverse)


def norm_back(upstream, unit_rows, inverse, scaling):
    scaled = upstream * scaling
    result = inverse * (
        scaled
        - jnp.mean(scaled, -1, keepdims=True)
        - unit_rows * jnp.mean(scaled * unit_rows, -1, keepdims=True)
    )
    return (result, jnp.sum(upstream * unit_rows, (0, 1)), jnp.sum(upstream, (0, 1)))


def gelu_parts(inputs):
    normal_cdf = 0.5 * (1.0 + lax.erf(inputs * ROOT_HALF))
    return (
        inputs * normal_cdf,
        normal_cdf + inputs * jnp.exp(-0.5 * inputs * inputs) * INV_ROOT_TWO_PI,
    )


def spread_rows(rows):
    return lax.all_gather(rows, "tp", axis=1, tiled=True)


def spread_grads(grad_rows):
    return lax.all_gather(grad_rows, "tp", axis=1, tiled=True)


def finish_branch(local_in, local_weight):
    return lax.psum_scatter(
        jnp.einsum("scw,wd->scd", local_in, local_weight, preferred_element_type=jnp.float32),
        "tp",
        scatter_dimension=1,
        tiled=True,
    )


def finish_grad(local_grad, local_weight):
    return lax.psum_scatter(
        jnp.einsum("scw,dw->scd", local_grad, local_weight, preferred_element_type=jnp.float32),
        "tp",
        scatter_dimension=1,
        tiled=True,
    )


def block_scores(queries, key_block, query_pos, key_pos, lengths, factor):
    scores = (
        jnp.einsum("sqhe,skhe->sqhk", queries, key_block, preferred_element_type=jnp.float32)
        * factor
    )
    visible = (key_pos[None, None, :] <= query_pos[None, :, None]) | (
        key_pos[None, None, :] < lengths[:, None, None]
    )
    return jnp.where(visible[:, :, None, :], scores, NEG)


def attend_forward(queries, key_rows, value_rows, query_pos, lengths, key_span, factor):
    length = key_rows.shape[1]

    def attend_advance(running, offset):
        highest, totals, summed = running
        key_block = lax.dynamic_slice_in_dim(key_rows, offset, key_span, 1)
        value_block = lax.dynamic_slice_in_dim(value_rows, offset, key_span, 1)
        scores = block_scores(
            queries, key_block, query_pos, offset + lax.iota(jnp.int32, key_span), lengths, factor
        )
        new_high = jnp.maximum(highest, jnp.max(scores, -1))
        weights = jnp.exp(scores - new_high[..., None])
        fading = jnp.exp(highest - new_high)
        totals = totals * fading + jnp.sum(weights, -1)
        summed = summed * fading[..., None] + jnp.einsum(
            "sqhk,skhe->sqhe",
            weights.astype(jnp.bfloat16),
            value_block,
            preferred_element_type=jnp.float32,
        )
        return ((new_high, totals, summed), None)

    stat_shape = queries.shape[:3]
    initial = (
        jnp.full(stat_shape, NEG, jnp.float32),
        jnp.zeros(stat_shape, jnp.float32),
        jnp.zeros(queries.shape, jnp.float32),
    )
    offsets = jnp.arange(length // key_span, dtype=jnp.int32) * key_span
    (highest, totals, summed), unused = lax.scan(attend_advance, initial, offsets)
    return (summed / totals[..., None], highest + jnp.log(totals))


def attend_block(
    queries,
    grad_out,
    log_rows,
    delta_rows,
    key_block,
    value_block,
    query_pos,
    key_pos,
    lengths,
    factor,
):
    scores = block_scores(queries, key_block, query_pos, key_pos, lengths, factor)
    probs = jnp.exp(scores - log_rows[..., None])
    grad_probs = jnp.einsum(
        "sqhe,skhe->sqhk", grad_out, value_block, preferred_element_type=jnp.float32
    )
    grad_scores = (probs * (grad_probs - delta_rows[..., None])).astype(jnp.bfloat16)
    return (probs.astype(jnp.bfloat16), grad_scores)


def key_sweep(
    queries,
    grad_out,
    log_rows,
    delta_rows,
    key_rows,
    value_rows,
    query_pos,
    lengths,
    key_span,
    factor,
):
    batches, row_count, head_count, head_depth = queries.shape
    length = key_rows.shape[1]

    def key_advance(grad_query, offset):
        key_block = lax.dynamic_slice_in_dim(key_rows, offset, key_span, 1)
        value_block = lax.dynamic_slice_in_dim(value_rows, offset, key_span, 1)
        key_pos = offset + lax.iota(jnp.int32, key_span)
        probs_low, grad_scores = attend_block(
            queries,
            grad_out,
            log_rows,
            delta_rows,
            key_block,
            value_block,
            query_pos,
            key_pos,
            lengths,
            factor,
        )
        grad_query = (
            grad_query
            + jnp.einsum(
                "sqhk,skhe->sqhe", grad_scores, key_block, preferred_element_type=jnp.float32
            )
            * factor
        )
        grad_key = (
            jnp.einsum("sqhk,sqhe->kshe", grad_scores, queries, preferred_element_type=jnp.float32)
            * factor
        )
        grad_value = jnp.einsum(
            "sqhk,sqhe->kshe", probs_low, grad_out, preferred_element_type=jnp.float32
        )
        return (grad_query, (grad_key, grad_value))

    offsets = jnp.arange(length // key_span, dtype=jnp.int32) * key_span
    grad_query, stacked = lax.scan(key_advance, jnp.zeros(queries.shape, jnp.float32), offsets)
    flat_shape = (length, batches, head_count * head_depth)
    return (grad_query, stacked[0].reshape(flat_shape), stacked[1].reshape(flat_shape))


def local(
    tokens,
    timesteps,
    time_table,
    prefix,
    encoder,
    self_qkv,
    cross_q,
    cross_kv,
    self_out,
    cross_out,
    ffn_up,
    ffn_down,
    norm_gain,
    norm_bias,
    cotangent,
):
    proj_self, proj_query, proj_pair, back_self, back_cross, expand_full, shrink_full = (
        lax.all_gather(self_qkv, "fsdp", axis=1, tiled=True),
        lax.all_gather(cross_q, "fsdp", axis=0, tiled=True),
        lax.all_gather(cross_kv, "fsdp", axis=1, tiled=True),
        lax.all_gather(self_out, "fsdp", axis=1, tiled=True),
        lax.all_gather(cross_out, "fsdp", axis=1, tiled=True),
        lax.all_gather(ffn_up, "fsdp", axis=0, tiled=True),
        lax.all_gather(ffn_down, "fsdp", axis=1, tiled=True),
    )
    batches = tokens.shape[0]
    model_width = tokens.shape[2]
    local_width = proj_query.shape[1]
    head_count = local_width // HEAD_DIM
    factor = HEAD_DIM ** (-0.5)
    ctx_index = lax.axis_index("ctx")
    local_stack = jnp.transpose(proj_self, (1, 0, 2)).reshape(model_width, 3 * local_width)
    steps_onehot = (timesteps[:, None] == lax.iota(jnp.int32, time_table.shape[0])[None, :]).astype(
        jnp.bfloat16
    )
    embedded = jnp.dot(steps_onehot, time_table, preferred_element_type=jnp.float32)
    start_sum = tokens.astype(jnp.float32) + embedded[:, None, :]
    normed_one, unit_one, inverse_one = norm_rows(start_sum, norm_gain[0], norm_bias[0])
    rows_self = spread_rows(normed_one.astype(jnp.bfloat16))
    row_count = rows_self.shape[1]
    head_shape = (batches, row_count, head_count, HEAD_DIM)
    projected = jnp.einsum(
        "scd,kdw->kscw", rows_self, proj_self, preferred_element_type=jnp.float32
    ).astype(jnp.bfloat16)
    queries, key_local, value_local = (projected[0], projected[1], projected[2])
    key_all, value_all = (
        lax.all_gather(key_local, "ctx", axis=1, tiled=True),
        lax.all_gather(value_local, "ctx", axis=1, tiled=True),
    )
    length = key_all.shape[1]
    key_span = min(512, length)
    query_pos = ctx_index * row_count + lax.iota(jnp.int32, row_count)
    keys_four = key_all.reshape(batches, length, head_count, HEAD_DIM)
    values_four = value_all.reshape(batches, length, head_count, HEAD_DIM)
    queries_four = queries.reshape(head_shape)
    attended, log_total = attend_forward(
        queries_four, keys_four, values_four, query_pos, prefix, key_span, factor
    )
    context_one = attended.reshape(batches, row_count, local_width).astype(jnp.bfloat16)
    branch_one = finish_branch(context_one, back_self)
    after_one = start_sum + branch_one
    normed_two, unit_two, inverse_two = norm_rows(after_one, norm_gain[1], norm_bias[1])
    rows_cross = spread_rows(normed_two.astype(jnp.bfloat16))
    cross_queries = jnp.einsum(
        "scd,dw->scw", rows_cross, proj_query, preferred_element_type=jnp.float32
    ).astype(jnp.bfloat16)
    enc_pair = jnp.einsum(
        "sed,kdw->ksew", encoder, proj_pair, preferred_element_type=jnp.float32
    ).astype(jnp.bfloat16)
    enc_count = encoder.shape[1]
    cross_keys = enc_pair[0].reshape(batches, enc_count, head_count, HEAD_DIM)
    cross_values = enc_pair[1].reshape(batches, enc_count, head_count, HEAD_DIM)
    cross_four = cross_queries.reshape(head_shape)
    cross_probs = jax.nn.softmax(
        jnp.einsum("sqhe,skhe->sqhk", cross_four, cross_keys, preferred_element_type=jnp.float32)
        * factor,
        axis=-1,
    )
    cross_low = cross_probs.astype(jnp.bfloat16)
    context_two = (
        jnp.einsum("sqhk,skhe->sqhe", cross_low, cross_values, preferred_element_type=jnp.float32)
        .reshape(batches, row_count, local_width)
        .astype(jnp.bfloat16)
    )
    branch_two = finish_branch(context_two, back_cross)
    after_two = after_one + branch_two
    normed_three, unit_three, inverse_three = norm_rows(after_two, norm_gain[2], norm_bias[2])
    rows_ffn = spread_rows(normed_three.astype(jnp.bfloat16))
    pre_act = jnp.einsum("scd,df->scf", rows_ffn, expand_full, preferred_element_type=jnp.float32)
    activated, slopes = gelu_parts(pre_act)
    hidden_low = activated.astype(jnp.bfloat16)
    branch_three = finish_branch(hidden_low, shrink_full)
    final_sum = after_two + branch_three
    grad_three = spread_grads(cotangent)
    grad_shrink = jnp.einsum(
        "scf,scd->fd", hidden_low, grad_three, preferred_element_type=jnp.float32
    )
    grad_pre = (
        jnp.einsum("scd,fd->scf", grad_three, shrink_full, preferred_element_type=jnp.float32)
        * slopes
    ).astype(jnp.bfloat16)
    grad_expand = jnp.einsum("scd,scf->df", rows_ffn, grad_pre, preferred_element_type=jnp.float32)
    back_three, gain_three, shift_three = norm_back(
        finish_grad(grad_pre, expand_full), unit_three, inverse_three, norm_gain[2]
    )
    grad_after_two = cotangent.astype(jnp.float32) + back_three
    grad_two = spread_grads(grad_after_two.astype(jnp.bfloat16))
    grad_back_cross = jnp.einsum(
        "scw,scd->wd", context_two, grad_two, preferred_element_type=jnp.float32
    )
    grad_context_two = jnp.einsum(
        "scd,wd->scw", grad_two, back_cross, preferred_element_type=jnp.float32
    ).astype(jnp.bfloat16)
    grad_cross_four = grad_context_two.reshape(head_shape)
    grad_cross_probs = jnp.einsum(
        "sqhe,skhe->sqhk", grad_cross_four, cross_values, preferred_element_type=jnp.float32
    )
    grad_cross_scores = (
        cross_probs
        * (grad_cross_probs - jnp.sum(cross_probs * grad_cross_probs, -1, keepdims=True))
    ).astype(jnp.bfloat16)
    grad_cross_q = (
        (
            jnp.einsum(
                "sqhk,skhe->sqhe", grad_cross_scores, cross_keys, preferred_element_type=jnp.float32
            )
            * factor
        )
        .reshape(batches, row_count, local_width)
        .astype(jnp.bfloat16)
    )
    part_keys = (
        jnp.einsum(
            "sqhk,sqhe->skhe", grad_cross_scores, cross_four, preferred_element_type=jnp.float32
        )
        * factor
    ).reshape(batches, enc_count, local_width)
    part_values = jnp.einsum(
        "sqhk,sqhe->skhe", cross_low, grad_cross_four, preferred_element_type=jnp.float32
    ).reshape(batches, enc_count, local_width)
    enc_keys, enc_values = (
        lax.psum_scatter(part_keys, "ctx", scatter_dimension=1, tiled=True),
        lax.psum_scatter(part_values, "ctx", scatter_dimension=1, tiled=True),
    )
    enc_keys = enc_keys.astype(jnp.bfloat16)
    enc_values = enc_values.astype(jnp.bfloat16)
    enc_share = enc_keys.shape[1]
    enc_rows = lax.dynamic_slice_in_dim(encoder, ctx_index * enc_share, enc_share, 1)
    grad_pair = jnp.stack(
        [
            jnp.einsum("sed,sew->dw", enc_rows, enc_keys, preferred_element_type=jnp.float32),
            jnp.einsum("sed,sew->dw", enc_rows, enc_values, preferred_element_type=jnp.float32),
        ]
    )
    encoder_grad = lax.psum_scatter(
        jnp.einsum("sew,dw->sed", enc_keys, proj_pair[0], preferred_element_type=jnp.float32)
        + jnp.einsum("sew,dw->sed", enc_values, proj_pair[1], preferred_element_type=jnp.float32),
        "tp",
        scatter_dimension=1,
        tiled=True,
    )
    grad_query_proj = jnp.einsum(
        "scd,scw->dw", rows_cross, grad_cross_q, preferred_element_type=jnp.float32
    )
    back_two, gain_two, shift_two = norm_back(
        finish_grad(grad_cross_q, proj_query), unit_two, inverse_two, norm_gain[1]
    )
    grad_after_one = grad_after_two + back_two
    grad_one = spread_grads(grad_after_one.astype(jnp.bfloat16))
    grad_back_self = jnp.einsum(
        "scw,scd->wd", context_one, grad_one, preferred_element_type=jnp.float32
    )
    grad_context_one = jnp.einsum(
        "scd,wd->scw", grad_one, back_self, preferred_element_type=jnp.float32
    ).astype(jnp.bfloat16)
    grad_ctx_four = grad_context_one.reshape(head_shape)
    delta_rows = jnp.sum(grad_ctx_four.astype(jnp.float32) * attended, -1)
    grad_query, grad_key_all, grad_value_all = key_sweep(
        queries_four,
        grad_ctx_four,
        log_total,
        delta_rows,
        keys_four,
        values_four,
        query_pos,
        prefix,
        key_span,
        factor,
    )
    own_keys, own_values = (
        lax.psum_scatter(grad_key_all, "ctx", scatter_dimension=0, tiled=True),
        lax.psum_scatter(grad_value_all, "ctx", scatter_dimension=0, tiled=True),
    )
    own_keys = jnp.transpose(own_keys, (1, 0, 2))
    own_values = jnp.transpose(own_values, (1, 0, 2))
    grad_joined = jnp.concatenate(
        [grad_query.reshape(batches, row_count, local_width), own_keys, own_values], -1
    ).astype(jnp.bfloat16)
    grad_proj_self = jnp.transpose(
        jnp.einsum(
            "scd,scw->dw", rows_self, grad_joined, preferred_element_type=jnp.float32
        ).reshape(model_width, 3, local_width),
        (1, 0, 2),
    )
    back_one, gain_one, shift_one = norm_back(
        finish_grad(grad_joined, local_stack), unit_one, inverse_one, norm_gain[0]
    )
    input_grad = grad_after_one + back_one
    shard_grads = (
        lax.psum_scatter(grad_proj_self, "fsdp", scatter_dimension=1, tiled=True),
        lax.psum_scatter(grad_query_proj, "fsdp", scatter_dimension=0, tiled=True),
        lax.psum_scatter(grad_pair, "fsdp", scatter_dimension=1, tiled=True),
        lax.psum_scatter(grad_back_self, "fsdp", scatter_dimension=1, tiled=True),
        lax.psum_scatter(grad_back_cross, "fsdp", scatter_dimension=1, tiled=True),
        lax.psum_scatter(grad_expand, "fsdp", scatter_dimension=0, tiled=True),
        lax.psum_scatter(grad_shrink, "fsdp", scatter_dimension=1, tiled=True),
    )
    full_grads = lax.psum(
        (
            shard_grads[0],
            shard_grads[1],
            shard_grads[2],
            shard_grads[3],
            shard_grads[4],
            shard_grads[5],
            shard_grads[6],
        ),
        "ctx",
    )
    squares = jnp.stack(
        [
            jnp.sum(final_sum * final_sum),
            jnp.sum(branch_one * branch_one),
            jnp.sum(branch_two * branch_two),
            jnp.sum(branch_three * branch_three),
        ]
    )
    gain_grad, bias_grad, square_totals = lax.psum(
        (
            jnp.stack([gain_one, gain_two, gain_three]),
            jnp.stack([shift_one, shift_two, shift_three]),
            squares,
        ),
        ("fsdp", "ctx", "tp"),
    )
    entries = (
        tokens.shape[0]
        * tokens.shape[1]
        * tokens.shape[2]
        * lax.axis_size("fsdp")
        * lax.axis_size("ctx")
        * lax.axis_size("tp")
    )
    norms = jnp.sqrt(square_totals / entries)
    return (
        final_sum,
        input_grad,
        encoder_grad,
        full_grads[0],
        full_grads[1],
        full_grads[2],
        full_grads[3],
        full_grads[4],
        full_grads[5],
        full_grads[6],
        gain_grad,
        bias_grad[:2],
        bias_grad[2],
        norms,
    )


def dot_of(left, right, left_dim, right_dim):
    return lax.dot_general(
        left, right, (((left_dim,), (right_dim,)), ((), ())), preferred_element_type=jnp.float32
    )


def bounds(prefix, start, query_span, key_span):
    whole = jnp.maximum(prefix, start + 1) // key_span
    every = (jnp.maximum(prefix, start + query_span) + key_span - 1) // key_span
    return whole, every


def hide(scores, limit, offset):
    return jnp.where(lax.broadcasted_iota(jnp.int32, scores.shape, 0) < limit - offset, scores, NEG)


def low(value):
    return value.astype(jnp.bfloat16)


STRIP = 64


def in_strips(work, *values, strip=STRIP, axis=0):
    count = values[0].shape[axis] // strip
    cut = lambda v, n: lax.slice_in_dim(v, n * strip, (n + 1) * strip, axis=axis)
    parts = [work(*[cut(v, n) for v in values]) for n in range(count)]
    return tuple(jnp.concatenate(p, axis) for p in zip(*parts))


def gelu_strip(inputs):
    activated, slopes = gelu_parts(inputs)
    return low(activated), slopes


def rows_unit(hidden):
    centre = hidden - jnp.mean(hidden, -1, keepdims=True)
    inverse = lax.rsqrt(jnp.mean(centre * centre, -1, keepdims=True) + EPS)
    return centre * inverse, inverse


def rows_norm(hidden, scaling, offsets):
    def strip(rows):
        unit_rows, inverse = rows_unit(rows)
        return low(unit_rows * scaling + offsets), unit_rows, inverse

    return in_strips(strip, hidden)


def rows_back(upstream, unit_rows, inverse, scaling):
    sums = [jnp.zeros((8, upstream.shape[1]), jnp.float32)] * 2

    def strip(rows, units, inverses):
        scaled = rows * scaling
        for n, term in enumerate((rows * units, rows)):
            sums[n] = sums[n] + jnp.sum(term.reshape(-1, 8, term.shape[1]), 0)
        return (
            inverses
            * (
                scaled
                - jnp.mean(scaled, -1, keepdims=True)
                - units * jnp.mean(scaled * units, -1, keepdims=True)
            ),
        )

    (result,) = in_strips(strip, upstream, unit_rows, inverse)
    return result, jnp.sum(sums[0], 0, keepdims=True), jnp.sum(sums[1], 0, keepdims=True)


MESH = pl.DeviceIdType.MESH


def meet(group, tp, fsdp):
    here, core, chip = lax.axis_index("fsdp"), lax.axis_index("ctx"), lax.axis_index("tp")
    me = core * tp + chip
    barrier = pltpu.get_barrier_semaphore()
    for k in range(1, group):
        other = me ^ k
        pl.semaphore_signal(
            barrier, inc=1, device_id={"ctx": other // tp, "tp": other % tp}, device_id_type=MESH
        )
    for k in range(1, fsdp):
        pl.semaphore_signal(barrier, inc=1, device_id={"fsdp": here ^ k}, device_id_type=MESH)
    pl.semaphore_wait(barrier, group - 1 + fsdp - 1)


def forward_kernel(
    prefix_ref,
    tokens_ref,
    step_ref,
    gain_ref,
    bias_ref,
    mine_ref,
    rows_out,
    qkv_ref,
    wide_ref,
    log_ref,
    ctx_ref,
    weight,
    rows_ref,
    other_ref,
    columns,
    pair_ref,
    keys_ref,
    values_ref,
    low_ref,
    landing,
    w_send,
    w_recv,
    v_send,
    v_recv,
    x_send,
    x_recv,
    c_send,
    c_recv,
    keep_sem,
    *,
    span,
    tp,
    fsdp,
):
    batches, chunk, width = tokens_ref.shape
    group = rows_ref.shape[0]
    length = group * chunk
    blocks, ratio = length // span, span // chunk
    wide_blocks = max(1, length // 2 // span)
    factor = HEAD_DIM**-0.5
    here, core, chip = lax.axis_index("fsdp"), lax.axis_index("ctx"), lax.axis_index("tp")
    me = core * tp + chip
    mine = chip // 2
    inner = (chip == 1) | (chip == 2)
    other_inner, other_outer = 2 - mine, 3 - 3 * mine
    meet(group, tp, fsdp)

    def send_to(source, target, send, recv, **place):
        return pltpu.make_async_remote_copy(
            src_ref=source,
            dst_ref=target,
            send_sem=send,
            recv_sem=recv,
            device_id=place,
            device_id_type=MESH,
        )

    v_core, v_chip = chip % 2, chip // 2 + 2 * core
    v_own = (v_core == core) & (v_chip == chip)
    v_copy = send_to(mine_ref, pair_ref, v_send.at[0], v_recv.at[0], ctx=v_core, tp=v_chip)

    @pl.when(v_own)
    def keep_pair():
        pair_ref[...] = mine_ref[...]

    @pl.when(jnp.logical_not(v_own))
    def send_pair():
        v_copy.start()

    comes = (chip // 2 != core) | (2 * (chip % 2) + core != chip)

    def w_copy(k):
        return send_to(pair_ref, columns.at[k], w_send.at[k], w_recv.at[k], fsdp=here ^ k)

    def normalise(seq, target, at):
        start_sum = tokens_ref[seq].astype(jnp.float32) + step_ref[seq]
        target[at] = rows_norm(start_sum, gain_ref[0:1], bias_ref[0:1])[0]

    def x_copy(kind):
        block = rows_ref.at[me]
        near = rows_ref.at[core * tp + (chip ^ 1)]
        second = rows_ref.at[core * tp + other_inner]
        third = rows_ref.at[core * tp + other_outer]
        source, place, target = (
            (block, me, {"tp": chip ^ 1}),
            (other_ref.at[0], me, {"tp": other_inner}),
            (block, me, {"ctx": 1 - core}),
            (near, core * tp + (chip ^ 1), {"ctx": 1 - core}),
            (second, core * tp + other_inner, {"ctx": 1 - core}),
            (third, core * tp + other_outer, {"ctx": 1 - core}),
            (second, core * tp + other_inner, {"tp": chip ^ 1}),
            (third, core * tp + other_outer, {"tp": chip ^ 1}),
            (other_ref.at[0], me, {"tp": other_outer}),
        )[kind]
        return send_to(source, rows_ref.at[place], x_send.at[kind], x_recv.at[place], **target)

    def x_wait(place):
        send_to(
            rows_ref.at[place], rows_ref.at[place], x_send.at[0], x_recv.at[place], ctx=1 - core
        ).wait_recv()

    def arrive(number):
        x_wait(core * tp + (chip ^ 1, other_inner, other_outer)[number])
        if number:

            @pl.when(inner & (core == 0))
            def onward():
                x_copy(5 + number).start()

        x_copy(3 + number).start()

    normalise(mine, rows_ref, me)
    normalise(1 - mine, other_ref, 0)

    @pl.when(core == 0)
    def first_half():
        x_copy(2).start()

        @pl.when(inner)
        def from_inner():
            x_copy(1).start()
            x_copy(0).start()

        @pl.when(jnp.logical_not(inner))
        def from_outer():
            x_copy(0).start()

    @pl.when(comes)
    def pair_here():
        v_copy.wait_recv()

    for k in range(1, fsdp):
        w_copy(k).start()
    values_ref[:, HEAD_DIM:, :] = jnp.ones_like(values_ref[:, HEAD_DIM:, :])

    def project(place, unused):
        rows = rows_ref[place]
        joined = low(dot_of(weight[...], rows, 1, 1))
        at = pl.ds(pl.multiple_of(place * chunk, chunk), chunk)
        for head in range(2):
            queries, keys, values = (
                joined[(3 * head + n) * HEAD_DIM : (3 * head + n + 1) * HEAD_DIM] for n in range(3)
            )
            qkv_ref[head, :HEAD_DIM, at] = queries * jnp.bfloat16(factor)
            qkv_ref[head, HEAD_DIM : 2 * HEAD_DIM, at] = keys
            qkv_ref[head, 2 * HEAD_DIM :, at] = values
            values_ref[head, :HEAD_DIM, at] = values
            keys_ref[head, at, :] = keys.T
        return unused

    @pl.when(core == 0)
    def first_lines():
        @pl.when(jnp.logical_not(inner))
        def then_other():
            x_copy(0).wait_send()
            x_copy(1).start()

        for number in range(3):
            arrive(number)

    @pl.when(core == 1)
    def second_lines():
        for place in range(tp):
            x_wait(place)
        for kind in (2, 1, 8, 0):
            x_copy(kind).start()

    piece = mine_ref.shape[1]
    for k in range(fsdp):
        if k:
            w_copy(k).wait_recv()
        part = columns[k] if k else pair_ref[...]
        for f in range(fsdp):

            @pl.when((here ^ k) == f)
            def place(f=f, part=part):
                weight[:, f * piece : (f + 1) * piece] = part

    lax.fori_loop(0, tp, project, 0)

    def c_copy(head, place):
        return send_to(
            low_ref.at[head, place],
            landing.at[head, me],
            c_send.at[head, place],
            c_recv.at[head, me],
            ctx=place // tp,
            tp=place % tp,
        )

    def c_wait(head, place):
        send_to(
            low_ref.at[head, place],
            landing.at[head, place],
            c_send.at[head, place],
            c_recv.at[head, place],
            ctx=place // tp,
            tp=place % tp,
        ).wait_recv()

    def attend(index, unused):
        block, head = (index // 2) ^ (1 - mine), index % 2

        @pl.when((core == 1) & (index == 3))
        def near_lines():
            arrive(0)

        @pl.when(index == 4)
        def second_half():
            @pl.when(core == 0)
            def wait_other():
                for place in range(tp, group):
                    x_wait(place)

            @pl.when(core == 1)
            def far_lines():
                arrive(1)
                arrive(2)

            lax.fori_loop(tp, group, project, 0)

        start = pl.multiple_of(block * span, span)
        queries = qkv_ref[head, :HEAD_DIM, pl.ds(start, span)]
        limit = jnp.maximum(
            prefix_ref[mine], start + 1 + lax.broadcasted_iota(jnp.int32, (1, span), 1)
        )

        def advance(offset, count, carry, columns=None):
            highest, total = carry
            first = 0 if columns is None else columns
            scores = dot_of(keys_ref[head, pl.ds(offset, count), :], queries[:, first:], 1, 0)
            if columns is not None:
                scores = hide(scores, limit[:, first:], offset)
            higher = jnp.maximum(highest, jnp.max(scores, axis=0, keepdims=True))
            weights = low(jnp.exp(scores - higher))
            fading = jnp.exp(highest - higher)
            total = total * fading + dot_of(
                values_ref[head, :, pl.ds(offset, count)], weights, 1, 0
            )
            return higher, total

        def whole_step(other, carry):
            return advance(pl.multiple_of(other * span, span), span, carry)

        def masked_step(other, carry):
            return advance(pl.multiple_of(other * span, span), span, carry, 0)

        def diagonal_step(other, carry):
            half = span // 2
            carry = advance(start, half, carry, 0)
            offset = pl.multiple_of(start + half, half)
            upper = advance(offset, half, tuple(v[:, half:] for v in carry), half)
            return tuple(jnp.concatenate([v[:, :half], u], 1) for v, u in zip(carry, upper))

        carry = (
            jnp.full((1, span), NEG, jnp.float32),
            jnp.zeros((values_ref.shape[1], span), jnp.float32),
        )
        carry = lax.fori_loop(0, block, whole_step, carry)
        carry = lax.fori_loop(block, wide_blocks, masked_step, carry)
        highest, total = lax.fori_loop(
            0, jnp.where(block >= wide_blocks, 1, 0), diagonal_step, carry
        )
        weight_sum = total[HEAD_DIM : HEAD_DIM + 1, :]
        attended = total[:HEAD_DIM, :] / weight_sum
        wide_ref[head, :, pl.ds(start, span)] = attended
        log_ref[head, :, pl.ds(start, span)] = highest + jnp.log(weight_sum)
        attended = low(attended)
        for part in range(ratio):
            place = block * ratio + part
            low_ref[head, place] = attended[:, part * chunk : (part + 1) * chunk]

            @pl.when(place != me)
            def send(place=place):
                c_copy(head, place).start()

        return unused

    lax.fori_loop(0, 2 * blocks, attend, 0)
    keep = pltpu.make_async_copy(rows_ref, rows_out, keep_sem)
    keep.start()
    for head in range(2):

        def collect(k, unused, head=head):
            c_wait(head, me ^ k)
            ctx_ref[head, me ^ k] = landing[head, me ^ k]
            return unused

        lax.fori_loop(1, group, collect, 0)
        ctx_ref[head, me] = low_ref[head, me]
    for k in range(1, fsdp):
        w_copy(k).wait_send()

    @pl.when(jnp.logical_not(v_own))
    def pair_sent():
        v_copy.wait_send()

    for kind in range(1, 6):
        x_copy(kind).wait_send()

    @pl.when(inner | (core == 1))
    def own_sent():
        x_copy(0).wait_send()

    @pl.when(inner & (core == 0))
    def lines_sent():
        x_copy(6).wait_send()
        x_copy(7).wait_send()

    @pl.when(core == 1)
    def direct_sent():
        x_copy(8).wait_send()

    for head in range(2):

        def sent(k, unused, head=head):
            c_copy(head, me ^ k).wait_send()
            return unused

        lax.fori_loop(1, group, sent, 0)
    keep.wait()


def forward_group(prefix, tokens, steps, gain, bias, mine, span, group, tp, fsdp):
    batches, chunk, width = tokens.shape
    length = group * chunk
    bf16, f32 = jnp.bfloat16, jnp.float32
    struct = jax.ShapeDtypeStruct
    inside = pl.BlockSpec(memory_space=pltpu.VMEM)
    dma = pltpu.SemaphoreType.DMA
    return pl.pallas_call(
        functools.partial(forward_kernel, span=span, tp=tp, fsdp=fsdp),
        in_specs=[pl.BlockSpec(memory_space=pltpu.SMEM)] + [inside] * 5,
        out_specs=[pl.BlockSpec(memory_space=pl.ANY)] + [inside] * 5,
        out_shape=[
            struct((group, chunk, width), bf16),
            struct((2, 3 * HEAD_DIM, length), bf16),
            struct((2, HEAD_DIM, length), f32),
            struct((2, 1, length), f32),
            struct((2, group, HEAD_DIM, chunk), bf16),
            struct((6 * HEAD_DIM, width), bf16),
        ],
        scratch_shapes=[
            pltpu.VMEM((group, chunk, width), bf16),
            pltpu.VMEM((1, chunk, width), bf16),
            pltpu.VMEM((fsdp,) + mine.shape, bf16),
            pltpu.VMEM(mine.shape, bf16),
            pltpu.VMEM((2, length, HEAD_DIM), bf16),
            pltpu.VMEM((2, HEAD_DIM + 16, length), bf16),
            pltpu.VMEM((2, group, HEAD_DIM, chunk), bf16),
            pltpu.VMEM((2, group, HEAD_DIM, chunk), bf16),
            dma((fsdp,)),
            dma((fsdp,)),
            dma((1,)),
            dma((1,)),
            dma((9,)),
            dma((group,)),
            dma((2, group)),
            dma((2, group)),
            dma,
        ],
        compiler_params=pltpu.CompilerParams(
            vmem_limit_bytes=VMEM_LIMIT, collective_id=1, has_side_effects=True
        ),
        cost_estimate=pl.CostEstimate(
            flops=60_000_000_000, bytes_accessed=30_000_000, transcendentals=20_000_000
        ),
        name="forward_group",
    )(prefix, tokens, steps, gain, bias, mine)


QUERY, KEY, VALUE, SELF_OUT, CROSS_OUT, UP, DOWN = 0, 1, 2, 3, 4, 5, 9


def middle_kernel(
    gathered,
    tokens_ref,
    step_ref,
    enc_ref,
    cot_ref,
    gain_ref,
    bias_ref,
    ctx_ref,
    final_ref,
    after_ref,
    back_ref,
    enc_grad_ref,
    stats_ref,
    packed_ref,
    weights,
    hidden_all,
    pre_all,
    three_all,
    two_all,
    grad_two_all,
    grad_one_all,
    cross_all,
    query_all,
    context_all,
    queries,
    keys,
    values,
    probs,
    grad_heads,
    grad_keys,
    grad_values,
    back_rows,
    landing,
    d_send,
    d_recv,
    sem,
    *,
    tp,
    fsdp,
):
    batches, chunk, width = tokens_ref.shape
    group = landing.shape[1]
    core, chip = lax.axis_index("ctx"), lax.axis_index("tp")
    me = core * tp + chip
    mine = chip // 2
    meet(group, tp, fsdp)
    piece = gathered.shape[-1]
    factor = HEAD_DIM**-0.5
    heads = width // HEAD_DIM

    copies = []
    for f in range(width // piece):
        for c in range(group // tp):
            for t in range(tp):
                head = t * (group // tp) + c
                copies.append(
                    pltpu.make_async_copy(
                        gathered.at[f, c, t],
                        weights.at[:, pl.ds(head * HEAD_DIM, HEAD_DIM), pl.ds(f * piece, piece)],
                        sem.at[(f * group // tp + c) * tp + t],
                    )
                )
    for copy in copies:
        copy.start()
    stats_ref[...] = jnp.zeros_like(stats_ref)
    for copy in copies:
        copy.wait()

    owners = [(2 * (2 * z + c) + n, n, c * tp + z) for z in (0, 1) for c in (0, 1) for n in (0, 1)]

    def d_copy(turn, seq, head, number, owner):
        return pltpu.make_async_remote_copy(
            src_ref=back_rows.at[turn, pl.ds(head * HEAD_DIM, HEAD_DIM)],
            dst_ref=landing.at[number, me],
            send_sem=d_send.at[turn, head],
            recv_sem=d_recv.at[number, me],
            device_id={"ctx": owner // tp, "tp": owner % tp + 2 * seq},
            device_id_type=MESH,
        )

    def one_sequence(turn, unused):
        seq = jnp.where(turn == 0, 1 - mine, mine)
        at = pl.ds(pl.multiple_of(seq * chunk, chunk), chunk)
        for head, number, owner in owners:
            context_all[head * HEAD_DIM : (head + 1) * HEAD_DIM, at] = ctx_ref[number, owner + 2 * seq]
        start_sum = tokens_ref[seq].astype(jnp.float32) + step_ref[seq]
        branch_one = dot_of(context_all[:, at], weights[SELF_OUT], 0, 0)
        after_one = start_sum + branch_one
        stats_ref[1:2, :] += jnp.sum(branch_one * branch_one, 0, keepdims=True)
        normed_two, unit_two, inverse_two = rows_norm(after_one, gain_ref[1:2], bias_ref[1:2])
        two_all[at, :] = normed_two
        queries[...] = low(dot_of(weights[QUERY], normed_two, 1, 1))
        keys[...] = low(dot_of(weights[KEY], enc_ref[seq], 1, 1))
        values[...] = low(dot_of(weights[VALUE], enc_ref[seq], 1, 1))

        def attend(head, unused):
            rows = pl.ds(pl.multiple_of(head * HEAD_DIM, HEAD_DIM), HEAD_DIM)
            scores = dot_of(keys[rows, :].T, queries[rows, :], 1, 0) * factor

            def strip(columns):
                powers = jnp.exp(columns - jnp.max(columns, 0, keepdims=True))
                return (powers / jnp.sum(powers, 0, keepdims=True),)

            (attn,) = in_strips(strip, scores, strip=128, axis=1)
            probs[head] = attn
            cross_all[rows, at] = low(dot_of(values[rows, :], low(attn), 1, 0))
            return unused

        lax.fori_loop(0, heads, attend, 0, unroll=8)
        branch_two = dot_of(cross_all[:, at], weights[CROSS_OUT], 0, 0)
        after_two = after_one + branch_two
        stats_ref[2:3, :] += jnp.sum(branch_two * branch_two, 0, keepdims=True)
        normed_three, unit_three, inverse_three = rows_norm(after_two, gain_ref[2:3], bias_ref[2:3])
        three_all[at, :] = normed_three
        grad_three = cot_ref[seq]

        def feed(part, carry):
            branch, grad = carry
            up, down = weights[UP + part], weights[DOWN + part]
            inputs = dot_of(up, normed_three, 1, 1)
            hidden, slopes = in_strips(gelu_strip, inputs, strip=32)
            branch = branch + dot_of(hidden, down, 0, 0)
            hidden_all[part, :, at] = hidden
            grad_pre = low(dot_of(down, grad_three, 1, 1) * slopes)
            pre_all[part, :, at] = grad_pre
            return branch, grad + dot_of(grad_pre, up, 0, 0)

        blank = jnp.zeros((chunk, width), jnp.float32)
        branch_three, grad_norm = lax.fori_loop(0, DOWN - UP, feed, (blank, blank), unroll=4)
        final_sum = after_two + branch_three
        final_ref[seq] = final_sum
        stats_ref[0:1, :] += jnp.sum(final_sum * final_sum, 0, keepdims=True)
        stats_ref[3:4, :] += jnp.sum(branch_three * branch_three, 0, keepdims=True)
        back, gain_sum, bias_sum = rows_back(grad_norm, unit_three, inverse_three, gain_ref[2:3])
        stats_ref[6:7, :] += gain_sum
        stats_ref[7:8, :] += bias_sum
        grad_after_two = grad_three.astype(jnp.float32) + back
        grad_two = low(grad_after_two)
        grad_two_all[at, :] = grad_two
        grad_heads[...] = low(dot_of(weights[CROSS_OUT], grad_two, 1, 1))

        def attend_back(head, unused):
            rows = pl.ds(pl.multiple_of(head * HEAD_DIM, HEAD_DIM), HEAD_DIM)
            grads = grad_heads[rows, :]
            attn = probs[head]
            grad_probs = dot_of(values[rows, :].T, grads, 1, 0)

            def strip(ones, others):
                return (low(ones * (others - jnp.sum(ones * others, 0, keepdims=True))),)

            (grad_scores,) = in_strips(strip, attn, grad_probs, strip=128, axis=1)
            query_all[rows, at] = low(dot_of(keys[rows, :], grad_scores, 1, 0) * factor)
            grad_keys[rows, :] = dot_of(queries[rows, :], grad_scores, 1, 1) * factor
            grad_values[rows, :] = dot_of(grads, low(attn), 1, 1)
            return unused

        lax.fori_loop(0, heads, attend_back, 0, unroll=8)
        enc_grad_ref[seq, :, :width] = low(grad_keys[...].T)
        enc_grad_ref[seq, :, width:] = low(grad_values[...].T)
        upstream = dot_of(query_all[:, at], weights[QUERY], 0, 0)
        back, gain_sum, bias_sum = rows_back(upstream, unit_two, inverse_two, gain_ref[1:2])
        stats_ref[4:5, :] += gain_sum
        stats_ref[5:6, :] += bias_sum
        grad_after_one = grad_after_two + back
        after_ref[seq] = grad_after_one
        grad_one = low(grad_after_one)
        grad_one_all[at, :] = grad_one
        back_rows[turn] = low(dot_of(weights[SELF_OUT], grad_one, 1, 1))
        for head, number, owner in owners:

            @pl.when(owner + 2 * seq != me)
            def give(head=head, number=number, owner=owner):
                d_copy(turn, seq, head, number, owner).start()

            @pl.when(owner + 2 * seq == me)
            def keep(head=head, number=number):
                back_ref[number, me] = back_rows[turn, head * HEAD_DIM : (head + 1) * HEAD_DIM, :]

        return unused


    lax.fori_loop(0, batches, one_sequence, 0)
    def pack(block, left, right):
        total = low(dot_of(left, right, 1, 0))
        for f in range(width // piece):
            for c in range(group // tp):
                for t in range(tp):
                    head = t * (group // tp) + c
                    packed_ref[c, f, t, block] = total[
                        head * HEAD_DIM : (head + 1) * HEAD_DIM, f * piece : (f + 1) * piece
                    ]

    grad_three_all = cot_ref[...].reshape(batches * chunk, width)
    pack(0, query_all[...], two_all[...])
    pack(1, context_all[...], grad_one_all[...])
    pack(2, cross_all[...], grad_two_all[...])

    def pack_feed(part, unused):
        pack(UP - 2 + part, pre_all[part], three_all[...])
        pack(DOWN - 2 + part, hidden_all[part], grad_three_all)
        return unused

    lax.fori_loop(0, DOWN - UP, pack_feed, 0)

    def collect(k, unused):
        place = me ^ k
        for number in range(2):
            pltpu.make_async_remote_copy(
                src_ref=landing.at[number, place],
                dst_ref=landing.at[number, place],
                send_sem=d_send.at[0, 0],
                recv_sem=d_recv.at[number, place],
                device_id={"ctx": place // tp, "tp": place % tp},
                device_id_type=MESH,
            ).wait_recv()
            back_ref[number, place] = landing[number, place]
        return unused

    lax.fori_loop(1, group, collect, 0)
    for turn in range(batches):
        seq = 1 - mine if turn == 0 else mine
        for head, number, owner in owners:

            @pl.when(owner + 2 * seq != me)
            def given(turn=turn, seq=seq, head=head, number=number, owner=owner):
                d_copy(turn, seq, head, number, owner).wait_send()


def middle(
    gathered, tokens, steps, encoder, cotangent, gains, biases, contexts, tp, fsdp
):
    batches, chunk, width = tokens.shape
    group = contexts.shape[1]
    enc_count = encoder.shape[1]
    heads = width // HEAD_DIM
    bf16, f32 = jnp.bfloat16, jnp.float32
    struct = jax.ShapeDtypeStruct
    inside = pl.BlockSpec(memory_space=pltpu.VMEM)
    dma = pltpu.SemaphoreType.DMA
    count = gathered.shape[3]
    packed = (group // tp, gathered.shape[0], tp, count - 2) + gathered.shape[4:]
    return pl.pallas_call(
        functools.partial(middle_kernel, tp=tp, fsdp=fsdp),
        in_specs=[pl.BlockSpec(memory_space=pl.ANY)] + [inside] * 7,
        out_specs=[inside] * 6,
        out_shape=[
            struct((batches, chunk, width), f32),
            struct((batches, chunk, width), f32),
            struct((2, group, HEAD_DIM, chunk), bf16),
            struct((batches, enc_count, 2 * width), bf16),
            struct((8, width), f32),
            struct(packed, bf16),
        ],
        scratch_shapes=[
            pltpu.VMEM((count, width, width), bf16),
            pltpu.VMEM((DOWN - UP, width, batches * chunk), bf16),
            pltpu.VMEM((DOWN - UP, width, batches * chunk), bf16),
            pltpu.VMEM((batches * chunk, width), bf16),
            pltpu.VMEM((batches * chunk, width), bf16),
            pltpu.VMEM((batches * chunk, width), bf16),
            pltpu.VMEM((batches * chunk, width), bf16),
            pltpu.VMEM((width, batches * chunk), bf16),
            pltpu.VMEM((width, batches * chunk), bf16),
            pltpu.VMEM((width, batches * chunk), bf16),
            pltpu.VMEM((width, chunk), bf16),
            pltpu.VMEM((width, enc_count), bf16),
            pltpu.VMEM((width, enc_count), bf16),
            pltpu.VMEM((heads, enc_count, chunk), f32),
            pltpu.VMEM((width, chunk), bf16),
            pltpu.VMEM((width, enc_count), f32),
            pltpu.VMEM((width, enc_count), f32),
            pltpu.VMEM((batches, width, chunk), bf16),
            pltpu.VMEM((2, group, HEAD_DIM, chunk), bf16),
            dma((batches, heads)),
            dma((2, group)),
            dma((32,)),
        ],
        compiler_params=pltpu.CompilerParams(
            vmem_limit_bytes=VMEM_LIMIT, collective_id=3, has_side_effects=True
        ),
        cost_estimate=pl.CostEstimate(
            flops=30_000_000_000, bytes_accessed=30_000_000, transcendentals=10_000_000
        ),
        name="middle",
    )(gathered, tokens, steps, encoder, cotangent, gains, biases, contexts)


def backward_kernel(
    prefix_ref,
    enc_parts,
    packed,
    gathered,
    rows_in,
    landing,
    weight,
    qkv_ref,
    wide_ref,
    log_ref,
    tokens_ref,
    step_ref,
    gain_ref,
    bias_ref,
    after_ref,
    enc_ref,
    stats_ref,
    input_ref,
    enc_out,
    self_out,
    query_out,
    pair_out,
    back_out,
    cross_out,
    up_out,
    down_out,
    sums_out,
    outgoing,
    core_rows,
    core_rows_landing,
    sum_rows,
    beside,
    incoming,
    queries_ref,
    pairs_ref,
    grad_ref,
    delta_ref,
    grad_pairs_ref,
    rows_ref,
    pair_weights,
    enc_own,
    enc_core,
    enc_sum,
    enc_landing,
    pair_ref,
    pair_landing,
    core_landing,
    partial_ref,
    fsdp_landing,
    line_ref,
    line_landing,
    shard_ref,
    head_ref,
    head_landing,
    head_pair,
    head_two,
    sums_ref,
    sums_landing,
    sums_two,
    e_send,
    e_recv,
    x_send,
    x_recv,
    i_send,
    i_recv,
    b_recv,
    r_send,
    r_recv,
    f_send,
    f_recv,
    t_send,
    t_recv,
    h_send,
    h_recv,
    p_send,
    p_recv,
    s_send,
    s_recv,
    local_sem,
    rows_sem,
    *,
    span,
    tp,
    fsdp,
):
    batches, chunk, width = tokens_ref.shape
    group = landing.shape[1]
    length = group * chunk
    blocks, ratio = length // span, span // chunk
    wide_blocks = max(1, length // 2 // span)
    factor = HEAD_DIM**-0.5
    here, core, chip = lax.axis_index("fsdp"), lax.axis_index("ctx"), lax.axis_index("tp")
    me = core * tp + chip
    mine = chip // 2
    inner = (chip == 1) | (chip == 2)
    cores = group // tp
    share = enc_landing.shape[2]
    piece = width // fsdp
    early = packed.shape[3]
    meet(group, tp, fsdp)

    def send_to(source, target, send, recv, **place):
        return pltpu.make_async_remote_copy(
            src_ref=source,
            dst_ref=target,
            send_sem=send,
            recv_sem=recv,
            device_id=place,
            device_id_type=MESH,
        )

    def member(place):
        return {"ctx": place // tp, "tp": place % tp}

    local = [
        pltpu.make_async_copy(
            packed.at[core], partial_ref.at[:, :, pl.ds(0, early)], local_sem.at[0]
        ),
        pltpu.make_async_copy(
            enc_parts.at[:, pl.ds(pl.multiple_of(core * tp * share, share), tp * share)],
            enc_own,
            local_sem.at[1],
        ),
    ]
    first = len(local)
    for f in range(fsdp):
        for c in range(cores):
            for t in range(tp):
                head = t * cores + c
                local.append(
                    pltpu.make_async_copy(
                        gathered.at[f, c, t, pl.ds(KEY, 2)],
                        pair_weights.at[
                            :, pl.ds(head * HEAD_DIM, HEAD_DIM), pl.ds(f * piece, piece)
                        ],
                        local_sem.at[first + (f * cores + c) * tp + t],
                    )
                )
    enc_copy = send_to(
        enc_parts.at[:, pl.ds(pl.multiple_of((1 - core) * tp * share, share), tp * share)],
        enc_core,
        e_send.at[0],
        e_recv.at[0],
        ctx=1 - core,
    )
    enc_line = [
        send_to(
            enc_sum.at[chip ^ n], enc_landing.at[n - 1], e_send.at[n], e_recv.at[n], tp=chip ^ n
        )
        for n in range(1, tp)
    ]

    core_copy = send_to(
        packed.at[1 - core], core_landing, r_send.at[0], r_recv.at[0], ctx=1 - core
    )
    pair_copy = send_to(
        pair_ref.at[1 - core], pair_landing, r_send.at[1], r_recv.at[1], ctx=1 - core
    )
    shard_copy = send_to(
        shard_ref.at[core], shard_ref.at[core], r_send.at[2], r_recv.at[2], ctx=1 - core
    )
    shard_wait = send_to(
        shard_ref.at[1 - core], shard_ref.at[1 - core], r_send.at[2], r_recv.at[2], ctx=1 - core
    )
    f_copies = [
        send_to(
            partial_ref.at[here ^ n, :, pl.ds(0, early)],
            fsdp_landing.at[n - 1, :, pl.ds(0, early)],
            f_send.at[n],
            f_recv.at[n],
            fsdp=here ^ n,
        )
        for n in range(1, fsdp)
    ]
    f_pairs = [
        send_to(
            partial_ref.at[here ^ n, :, pl.ds(early, 2)],
            fsdp_landing.at[n - 1, :, pl.ds(early, 2)],
            f_send.at[fsdp + n],
            f_recv.at[fsdp + n],
            fsdp=here ^ n,
        )
        for n in range(1, fsdp)
    ]
    t_copies = [
        send_to(line_ref.at[chip ^ k], line_landing.at[k - 1], t_send.at[k], t_recv.at[k], tp=chip ^ k)
        for k in range(1, tp)
    ]
    h_copies = [
        send_to(
            head_ref.at[here ^ k], head_landing.at[k - 1], h_send.at[k], h_recv.at[k], fsdp=here ^ k
        )
        for k in range(1, fsdp)
    ]

    pair_chip = 2 * (chip % 2) + core
    p_copies = [
        send_to(head_pair, head_two.at[mine], p_send.at[c], p_recv.at[mine], ctx=c, tp=pair_chip)
        for c in range(2)
    ]
    p_waits = [
        send_to(head_pair, head_two.at[n], p_send.at[0], p_recv.at[n], ctx=c, tp=t)
        for n, c, t in ((0, chip % 2, chip // 2), (1, chip % 2, chip // 2 + 2))
    ]
    p_here = [
        (core == chip % 2) & (chip == chip // 2 + 2 * n) for n in range(2)
    ]

    def s_copy(k):
        return send_to(
            sums_ref, sums_landing.at[k], s_send.at[k], s_recv.at[k], **member(me ^ k)
        )

    s_fsdp = [
        send_to(
            sums_two, sums_landing.at[group + k], s_send.at[group + k], s_recv.at[group + k], fsdp=here ^ k
        )
        for k in range(1, fsdp)
    ]

    enc_copy.start()
    core_copy.start()
    for copy in local:
        copy.start()

    def core_rows_copy(place):
        slot = place % tp
        return send_to(
            core_rows.at[slot], core_rows_landing.at[slot], x_send.at[slot], x_recv.at[slot], ctx=1 - core
        )

    def owner_copy(place):
        slot = place % tp
        return send_to(
            sum_rows.at[slot],
            incoming.at[mine, chip % 2],
            i_send.at[slot],
            i_recv.at[mine, chip % 2],
            tp=slot,
        )

    def spread(place):
        upstream = dot_of(outgoing[place].reshape(6 * HEAD_DIM, chunk), weight[...], 0, 0)
        slot = place % tp

        @pl.when(place // tp != core)
        def hand_over():
            core_rows[slot] = low(upstream)
            core_rows_copy(place).start()

        @pl.when(place // tp == core)
        def collect():
            core_rows_copy(place).wait_recv()
            total = low(upstream + core_rows_landing[slot].astype(jnp.float32))

            @pl.when(place == me)
            def own():
                incoming[mine, chip % 2] = total

            @pl.when(place != me)
            def send():
                sum_rows[slot] = total

                @pl.when((core == 0) & (slot // 2 != mine) & jnp.logical_not(inner))
                def to_inner():
                    beside_copy(slot).start()

                @pl.when((core == 1) | (slot // 2 == mine))
                def to_owner():
                    owner_copy(place).start()

    def beside_copy(slot):
        return send_to(
            sum_rows.at[slot], beside.at[slot % 2], i_send.at[slot], b_recv.at[slot % 2], tp=chip ^ 1
        )

    def pass_rows():
        for n in range(2):
            slot = 2 * (1 - mine) + n
            beside_copy(slot).wait_recv()
            sum_rows[slot] = low(
                sum_rows[slot].astype(jnp.float32) + beside[n].astype(jnp.float32)
            )
            owner_copy(slot).start()

    def prepare(seq):
        def lay(place, unused):
            at = pl.ds(pl.multiple_of(place * chunk, chunk), chunk)
            grads = landing[seq, place]
            blank = jnp.zeros_like(grads)
            grad_ref[seq, at, :] = jnp.concatenate([blank, grads], 0).T
            delta_ref[seq, :, at] = jnp.sum(
                grads.astype(jnp.float32) * wide_ref[seq, :, at], axis=0, keepdims=True
            )
            queries_ref[seq, at, :] = jnp.concatenate([qkv_ref[seq, :HEAD_DIM, at], blank], 0).T
            pairs_ref[seq, at, :] = qkv_ref[seq, HEAD_DIM:, at].T
            return unused

        lax.fori_loop(0, group, lay, 0)
        grad_pairs_ref[seq] = jnp.zeros(grad_pairs_ref.shape[1:], jnp.float32)

    def encoder_cores():
        local[1].wait()
        enc_copy.wait_recv()
        for t in range(tp):
            lines = slice(t * share, (t + 1) * share)
            enc_sum[t] = low(
                enc_own[:, lines].astype(jnp.float32) + enc_core[:, lines].astype(jnp.float32)
            )
        for copy in enc_line:
            copy.start()

    def encoder_part():
        total = enc_sum[chip].astype(jnp.float32)
        for n, copy in enumerate(enc_line):
            copy.wait_recv()
            total = total + enc_landing[n].astype(jnp.float32)
        for copy in local[first:]:
            copy.wait()
        grads = low(total)
        enc_rows = enc_ref[:, pl.ds(pl.multiple_of(me * share, share), share), :]
        flat, enc_flat = grads.reshape(batches * share, 2 * width), enc_rows.reshape(
            batches * share, width
        )
        result = dot_of(flat[:, :width], pair_weights[0], 1, 0) + dot_of(
            flat[:, width:], pair_weights[1], 1, 0
        )
        enc_out[...] = result.reshape(batches, share, width)
        for which in range(2):
            grad = low(dot_of(flat[:, which * width : (which + 1) * width], enc_flat, 0, 0))
            for f in range(fsdp):
                for c in range(cores):
                    for t in range(tp):
                        head = t * cores + c
                        pair_ref[c, f, t, which] = grad[
                            head * HEAD_DIM : (head + 1) * HEAD_DIM, f * piece : (f + 1) * piece
                        ]
        pair_copy.start()

    def sum_cores():
        local[0].wait()
        core_copy.wait_recv()

        def one(f, unused):
            def two(t, unused):
                partial_ref[f, t, :early] = low(
                    partial_ref[f, t, :early].astype(jnp.float32)
                    + core_landing[f, t].astype(jnp.float32)
                )
                return unused

            return lax.fori_loop(0, tp, two, unused)

        lax.fori_loop(0, fsdp, one, 0)
        for copy in f_copies:
            copy.start()

    def sum_pairs():
        pair_copy.wait_recv()
        for f in range(fsdp):
            for t in range(tp):
                partial_ref[f, t, early:] = low(
                    pair_ref[core, f, t].astype(jnp.float32)
                    + pair_landing[f, t].astype(jnp.float32)
                )
        for copy in f_pairs:
            copy.start()

    def sum_fsdp():
        for copy in f_copies + f_pairs:
            copy.wait_recv()

        def one(t, unused):
            total = partial_ref[here, t].astype(jnp.float32)
            for k in range(fsdp - 1):
                total = total + fsdp_landing[k, t].astype(jnp.float32)
            line_ref[t] = low(total)
            return unused

        lax.fori_loop(0, tp, one, 0)
        for copy in t_copies:
            copy.start()

    def sum_line():
        for copy in t_copies:
            copy.wait_recv()
        total = line_ref[chip].astype(jnp.float32)
        for k in range(tp - 1):
            total = total + line_landing[k].astype(jnp.float32)
        shard_ref[core] = total
        shard_copy.start()

    for head in range(2):
        prepare(head)

    def attend(index, unused):
        block, seq = blocks - 1 - index // 2, index % 2

        def hook(at, work):
            @pl.when(index == at)
            def run():
                work()

        hook(1, encoder_cores)
        hook(1, sum_cores)
        hook(2, encoder_part)
        hook(3, sum_pairs)
        hook(5, sum_fsdp)
        start = pl.multiple_of(block * span, span)
        at = pl.ds(start, span)
        blank = jnp.zeros((HEAD_DIM, span), jnp.bfloat16)
        queries_t = jnp.concatenate([qkv_ref[seq, :HEAD_DIM, at], blank], 0)
        queries = queries_ref[seq, at, :]
        grads = grad_ref[seq, at, :]
        grads_t = jnp.concatenate(
            [landing[seq, block * ratio + part] for part in range(ratio)], 1
        )
        grads_t = jnp.concatenate([blank, grads_t], 0)
        logs, deltas = log_ref[seq, :, at], delta_ref[seq, :, at]
        limit = jnp.maximum(
            prefix_ref[mine], start + 1 + lax.broadcasted_iota(jnp.int32, (1, span), 1)
        )

        def advance(offset, count, grad_queries, columns=None):
            first = 0 if columns is None else columns
            there = pl.ds(offset, count)
            pairs = pairs_ref[seq, there, :]
            scores = dot_of(pairs, queries_t[:, first:], 1, 0)
            if columns is not None:
                scores = hide(scores, limit[:, first:], offset)
            probs = jnp.exp(scores - logs[:, first:])
            grad_probs = dot_of(pairs, grads_t[:, first:], 1, 0)
            grad_scores = low(probs * (grad_probs - deltas[:, first:]))
            grad_pairs_ref[seq, there, :] += dot_of(low(probs), grads[first:], 1, 0) + dot_of(
                grad_scores, queries[first:], 1, 0
            )
            return grad_queries + dot_of(
                qkv_ref[seq, HEAD_DIM : 2 * HEAD_DIM, there], grad_scores, 1, 0
            )

        def whole_step(other, total):
            return advance(pl.multiple_of(other * span, span), span, total)

        def masked_step(other, total):
            return advance(pl.multiple_of(other * span, span), span, total, 0)

        def diagonal_step(other, total):
            half = span // 2
            total = advance(start, half, total, 0)
            offset = pl.multiple_of(start + half, half)
            upper = advance(offset, half, total[:, half:], half)
            return jnp.concatenate([total[:, :half], upper], 1)

        grad_queries = jnp.zeros((HEAD_DIM, span), jnp.float32)
        grad_queries = lax.fori_loop(0, block, whole_step, grad_queries)
        grad_queries = lax.fori_loop(block, wide_blocks, masked_step, grad_queries)
        grad_queries = lax.fori_loop(
            0, jnp.where(block >= wide_blocks, 1, 0), diagonal_step, grad_queries
        )
        done = low(grad_queries * factor)
        for part in range(ratio):
            place = block * ratio + part
            outgoing[place, seq, :HEAD_DIM, :] = done[:, part * chunk : (part + 1) * chunk]

        lowest = jnp.where(block == 0, 0, block)
        highest = jnp.where(
            block == 0, wide_blocks, jnp.where(block >= wide_blocks, block + 1, block)
        )

        def give(place, unused):
            at = pl.ds(pl.multiple_of(place * chunk, chunk), chunk)
            outgoing[place, seq, HEAD_DIM:, :] = low(grad_pairs_ref[seq, at, :].T)
            return unused

        lax.fori_loop(lowest * ratio, highest * ratio, give, 0)

        @pl.when(seq == 1)
        def both_heads():
            def one(place, unused):
                spread(place)
                return unused

            lax.fori_loop(lowest * ratio, highest * ratio, one, 0)

        return unused

    lax.fori_loop(0, 2 * blocks, attend, 0)

    @pl.when((core == 0) & inner)
    def last_rows():
        pass_rows()

    sums_ref[...] = jnp.zeros_like(sums_ref)
    sums_ref[:8, :] = stats_ref[...]

    def rows_copy(number):
        return pltpu.make_async_copy(
            rows_in.at[number],
            rows_ref.at[number % rows_ref.shape[0]],
            rows_sem.at[number % rows_ref.shape[0]],
        )

    depth = rows_ref.shape[0]
    for number in range(depth):
        rows_copy(number).start()

    ones = jnp.ones((chunk, piece), jnp.bfloat16)

    def weigh(number, totals):
        rows_copy(number).wait()
        grads = outgoing[number].reshape(6 * HEAD_DIM, chunk)
        total = totals[0] + dot_of(grads, rows_ref[number % depth], 1, 0)

        @pl.when(number + depth < group)
        def more():
            rows_copy(number + depth).start()

        return total, totals[1] + dot_of(grads, ones, 1, 0)

    total, plain = lax.fori_loop(
        0,
        group,
        weigh,
        (
            jnp.zeros((6 * HEAD_DIM, width), jnp.float32),
            jnp.zeros((6 * HEAD_DIM, piece), jnp.float32),
        ),
    )
    token_copies = [
        pltpu.make_async_copy(tokens_ref.at[n], rows_ref.at[n], rows_sem.at[n])
        for n in range(batches)
    ]
    for copy in token_copies:
        copy.start()
    weights = weight[...].astype(jnp.float32)
    bias_sum = jnp.sum(weights * jnp.concatenate([plain] * (width // piece), 1), 0, keepdims=True)
    gain_sum = jnp.sum(weights * total, 0, keepdims=True) - bias_ref[0:1] * bias_sum
    sums_ref[8:9, :] = gain_sum / gain_ref[0:1]
    sums_ref[9:10, :] = bias_sum

    def start_sums(k, unused):
        s_copy(k).start()
        return unused

    lax.fori_loop(1, group, start_sums, 0)
    for f in range(fsdp):
        head_ref[f] = total[:, f * piece : (f + 1) * piece]
    for copy in h_copies:
        copy.start()
    sum_line()

    for copy in h_copies:
        copy.wait_recv()
    total = head_ref[here]
    for k in range(fsdp - 1):
        total = total + head_landing[k]
    head_pair[...] = low(total)
    for c in range(2):
        there = (core == c) & (pair_chip == chip)

        @pl.when(there)
        def stay():
            head_two[mine] = head_pair[...]

        @pl.when(jnp.logical_not(there))
        def leave(c=c):
            p_copies[c].start()

    def arrive_sums(k, total):
        s_copy(k).wait_recv()
        return total + sums_landing[k]

    sums_two[...] = lax.fori_loop(1, group, arrive_sums, sums_ref[...])
    for copy in s_fsdp:
        copy.start()

    for copy in token_copies:
        copy.wait()

    def finish(seq, unused):
        for number in range(2):
            source = 2 * seq + number

            passed = (core == 0) & (seq != mine)

            @pl.when(passed & ((source == 0) | (source == 3)))
            def nothing(number=number):
                incoming[seq, number] = jnp.zeros((chunk, width), jnp.bfloat16)

            @pl.when((source != chip) & jnp.logical_not(passed & ((source == 0) | (source == 3))))
            def come(number=number, source=source):
                send_to(
                    incoming.at[seq, number],
                    incoming.at[seq, number],
                    i_send.at[0],
                    i_recv.at[seq, number],
                    tp=source,
                ).wait_recv()

        upstream = incoming[seq, 0].astype(jnp.float32) + incoming[seq, 1].astype(jnp.float32)
        start_sum = rows_ref[seq].astype(jnp.float32) + step_ref[seq]
        unit_rows, inverse = in_strips(rows_unit, start_sum)
        input_ref[seq] = after_ref[seq] + rows_back(
            upstream, unit_rows, inverse, gain_ref[0:1]
        )[0]
        return unused

    lax.fori_loop(0, batches, finish, 0)

    shard_wait.wait_recv()

    def whole(block):
        return jnp.concatenate([shard_ref[0, block], shard_ref[1, block]], 0)

    query_out[...] = whole(0).T
    back_out[...] = whole(1)
    cross_out[...] = whole(2)
    for part in range(4):
        up_out[:, part * piece : (part + 1) * piece] = whole(3 + part).T
        down_out[part * piece : (part + 1) * piece, :] = whole(7 + part)
    pair_out[0] = whole(11).T
    pair_out[1] = whole(12).T
    for n in range(2):

        @pl.when(jnp.logical_not(p_here[n]))
        def pair_come(n=n):
            p_waits[n].wait_recv()

    total = head_two[0].astype(jnp.float32) + head_two[1].astype(jnp.float32)
    for which in range(3):
        self_out[which] = jnp.concatenate(
            [
                total[(3 * n + which) * HEAD_DIM : (3 * n + which + 1) * HEAD_DIM]
                for n in range(2)
            ],
            0,
        ).T
    total = sums_two[...]
    for k, copy in enumerate(s_fsdp):
        copy.wait_recv()
        total = total + sums_landing[group + 1 + k]
    sums_out[...] = total
    core_copy.wait_send()
    pair_copy.wait_send()
    shard_copy.wait_send()
    for c in range(2):

        @pl.when(jnp.logical_not((core == c) & (pair_chip == chip)))
        def pair_sent(c=c):
            p_copies[c].wait_send()

    enc_copy.wait_send()
    for copy in enc_line + f_copies + f_pairs + t_copies + h_copies + s_fsdp:
        copy.wait_send()

    def sent(k, unused):
        s_copy(k).wait_send()
        return unused

    lax.fori_loop(1, group, sent, 0)

    def rows_sent(slot, unused):
        core_rows_copy((1 - core) * tp + slot).wait_send()

        @pl.when(slot != chip)
        def left():
            owner_copy(core * tp + slot).wait_send()

        return unused

    lax.fori_loop(0, tp, rows_sent, 0)


def backward_group(
    prefix,
    enc_parts,
    packed,
    gathered,
    rows,
    returned,
    weight,
    qkv,
    wide,
    logs,
    tokens,
    steps,
    gain,
    bias,
    after,
    encoder,
    stats,
    span,
    tp,
    fsdp,
):
    batches, chunk, width = tokens.shape
    group = returned.shape[1]
    length = group * chunk
    share = encoder.shape[1] // group
    piece = width // fsdp
    count = packed.shape[3]
    tail = packed.shape[4:]
    bf16, f32 = jnp.bfloat16, jnp.float32
    struct = jax.ShapeDtypeStruct
    inside = pl.BlockSpec(memory_space=pltpu.VMEM)
    outside = pl.BlockSpec(memory_space=pl.ANY)
    dma = pltpu.SemaphoreType.DMA
    vmem = pltpu.VMEM
    parts = group * fsdp
    return pl.pallas_call(
        functools.partial(backward_kernel, span=span, tp=tp, fsdp=fsdp),
        in_specs=[pl.BlockSpec(memory_space=pltpu.SMEM)] + [outside] * 4 + [inside] * 5 + [outside] + [inside] * 6,
        out_specs=[inside] * 10,
        out_shape=[
            struct((batches, chunk, width), f32),
            struct((batches, share, width), f32),
            struct((3, piece, piece), f32),
            struct((piece, piece), f32),
            struct((2, piece, piece), f32),
            struct((piece, piece), f32),
            struct((piece, piece), f32),
            struct((piece, width), f32),
            struct((width, piece), f32),
            struct((16, width), f32),
        ],
        scratch_shapes=[
            vmem((group, 2, 3 * HEAD_DIM, chunk), bf16),
            vmem((tp, chunk, width), bf16),
            vmem((tp, chunk, width), bf16),
            vmem((tp, chunk, width), bf16),
            vmem((2, chunk, width), bf16),
            vmem((batches, 2, chunk, width), bf16),
            vmem((2, length, 2 * HEAD_DIM), bf16),
            vmem((2, length, 2 * HEAD_DIM), bf16),
            vmem((2, length, 2 * HEAD_DIM), bf16),
            vmem((2, 1, length), f32),
            vmem((2, length, 2 * HEAD_DIM), f32),
            vmem((2, chunk, width), bf16),
            vmem((2, width, width), bf16),
            vmem((batches, tp * share, 2 * width), bf16),
            vmem((batches, tp * share, 2 * width), bf16),
            vmem((tp, batches, share, 2 * width), bf16),
            vmem((tp - 1, batches, share, 2 * width), bf16),
            vmem((group // tp, fsdp, tp, 2) + tail, bf16),
            vmem((fsdp, tp, 2) + tail, bf16),
            vmem((fsdp, tp, count) + tail, bf16),
            vmem((fsdp, tp, count + 2) + tail, bf16),
            vmem((fsdp - 1, tp, count + 2) + tail, bf16),
            vmem((tp, count + 2) + tail, bf16),
            vmem((tp - 1, count + 2) + tail, bf16),
            vmem((2, count + 2) + tail, f32),
            vmem((fsdp, 6 * HEAD_DIM, piece), f32),
            vmem((fsdp - 1, 6 * HEAD_DIM, piece), f32),
            vmem((6 * HEAD_DIM, piece), bf16),
            vmem((2, 6 * HEAD_DIM, piece), bf16),
            vmem((16, width), f32),
            vmem((group + fsdp, 16, width), f32),
            vmem((16, width), f32),
            dma((tp,)),
            dma((tp,)),
            dma((tp,)),
            dma((tp,)),
            dma((tp,)),
            dma((batches, 2)),
            dma((2,)),
            dma((4,)),
            dma((4,)),
            dma((2 * fsdp,)),
            dma((2 * fsdp,)),
            dma((tp,)),
            dma((tp,)),
            dma((fsdp,)),
            dma((fsdp,)),
            dma((2,)),
            dma((2,)),
            dma((group + fsdp,)),
            dma((group + fsdp,)),
            dma((2 + parts,)),
            dma((2,)),
        ],
        compiler_params=pltpu.CompilerParams(
            vmem_limit_bytes=VMEM_LIMIT, collective_id=2, has_side_effects=True
        ),
        cost_estimate=pl.CostEstimate(
            flops=100_000_000_000, bytes_accessed=40_000_000, transcendentals=20_000_000
        ),
        name="backward_group",
    )(
        prefix,
        enc_parts,
        packed,
        gathered,
        rows,
        returned,
        weight,
        qkv,
        wide,
        logs,
        tokens,
        steps,
        gain,
        bias,
        after,
        encoder,
        stats,
    )


def pack_kernel(
    scalars,
    table_ref,
    qkv_ref,
    query_ref,
    pair_ref,
    self_ref,
    cross_ref,
    up_ref,
    down_ref,
    half_ref,
    mine_ref,
    steps_ref,
    blocks,
):
    piece = query_ref.shape[0]
    blocks[0] = query_ref[...].T
    for n in range(2):
        blocks[1 + n] = pair_ref[n].T
    blocks[3] = self_ref[...]
    blocks[4] = cross_ref[...]
    for n in range(4):
        blocks[5 + n] = up_ref[:, n * piece : (n + 1) * piece].T
        blocks[9 + n] = down_ref[n * piece : (n + 1) * piece, :]
    half = piece // 2
    core = lax.axis_index("ctx")
    half_ref[...] = blocks[:, pl.ds(pl.multiple_of(core * half, half), half), :]
    for which in range(3):
        flipped = qkv_ref[which].T
        for head in range(2):
            mine_ref[(3 * head + which) * HEAD_DIM : (3 * head + which + 1) * HEAD_DIM, :] = (
                flipped[head * HEAD_DIM : (head + 1) * HEAD_DIM]
            )
    table = table_ref[...].astype(jnp.float32)
    rows = lax.broadcasted_iota(jnp.int32, table.shape, 0)
    for seq in range(steps_ref.shape[0]):
        chosen = jnp.where(rows == scalars[seq], table, 0.0)
        steps_ref[seq] = jnp.sum(chosen, 0, keepdims=True)


def pack_weights(scalars, table, self_qkv, cross_q, cross_kv, self_out, cross_out, up, down):
    piece = cross_q.shape[0]
    width = table.shape[1]
    batches = scalars.shape[0]
    bf16 = jnp.bfloat16
    struct = jax.ShapeDtypeStruct
    inside = pl.BlockSpec(memory_space=pltpu.VMEM)
    return pl.pallas_call(
        pack_kernel,
        in_specs=[pl.BlockSpec(memory_space=pltpu.SMEM)] + [inside] * 8,
        out_specs=[inside] * 3,
        out_shape=[
            struct((13, piece // 2, piece), bf16),
            struct((3 * piece, piece), bf16),
            struct((batches, 1, width), jnp.float32),
        ],
        scratch_shapes=[pltpu.VMEM((13, piece, piece), bf16)],
        name="pack_weights",
    )(scalars, table, self_qkv, cross_q, cross_kv, self_out, cross_out, up, down)


def collect_kernel(*refs, large, small, entries):
    ins, outs = refs[: large + small + 1], refs[large + small + 1 :]
    for n in range(large):
        outs[n][...] = ins[n][...]

    @pl.when(pl.program_id(0) == 0)
    def once():
        for n in range(large, large + small):
            outs[n][...] = ins[n][...]
        sums = ins[large + small]
        gain_ref, bias_ref, feed_ref, norms_ref = outs[large + small :]
        for n, row in enumerate((8, 4, 6)):
            gain_ref[n : n + 1, :] = sums[row : row + 1, :]
        for n, row in enumerate((9, 5)):
            bias_ref[n : n + 1, :] = sums[row : row + 1, :]
        feed_ref[...] = sums[7:8, :]
        totals = jnp.sum(sums[0:4, :], 1, keepdims=True) * (1.0 / entries)
        one = lax.broadcasted_iota(jnp.int32, (4, 128), 0) == lax.broadcasted_iota(
            jnp.int32, (4, 128), 1
        )
        norms_ref[...] = jnp.sqrt(jnp.sum(jnp.where(one, totals, 0.0), 0, keepdims=True))[:, :4]


def collect(large, small, sums, entries):
    width = sums.shape[1]
    f32 = jnp.float32
    struct = jax.ShapeDtypeStruct
    rest = [struct(v.shape, v.dtype) for v in small]
    extra = [struct((3, width), f32), struct((2, width), f32), struct((1, width), f32)]
    extra = extra + [struct((1, 4), f32)]
    still = lambda v: pl.BlockSpec(v.shape, lambda i, rank=len(v.shape): (0,) * rank)
    steps = 4
    moving = lambda v: pl.BlockSpec(
        (1, v.shape[0] * v.shape[1] // steps, v.shape[2]),
        lambda i, per=steps // v.shape[0]: (i // per, i % per, 0),
    )
    return pl.pallas_call(
        functools.partial(collect_kernel, large=len(large), small=len(small), entries=entries),
        grid=(steps,),
        in_specs=[moving(v) for v in large] + [still(v) for v in small] + [still(sums)],
        out_specs=[moving(v) for v in large] + [still(v) for v in rest + extra],
        out_shape=[struct(v.shape, v.dtype) for v in large] + rest + extra,
        name="collect",
    )(*large, *small, sums)


def local_heads(
    tokens,
    timesteps,
    time_table,
    prefix,
    encoder,
    self_qkv,
    cross_q,
    cross_kv,
    self_out,
    cross_out,
    ffn_up,
    ffn_down,
    norm_gain,
    norm_bias,
    cotangent,
):
    batches, chunk, width = tokens.shape
    group = 8
    length = group * chunk
    span = 1024
    own_half, mine, embedded = pack_weights(
        timesteps,
        time_table,
        self_qkv,
        cross_q,
        cross_kv,
        self_out,
        cross_out,
        ffn_up,
        ffn_down,
    )
    gathered = lax.all_gather(own_half, "tp", axis=0, tiled=False)
    gathered = lax.all_gather(gathered, ("fsdp", "ctx"), axis=0, tiled=False)
    gathered = gathered.reshape((4, 2, 4) + own_half.shape)
    rows, qkv, wide, logs, contexts, weight = forward_group(
        prefix, tokens, embedded, norm_gain, norm_bias, mine, span, group, 4, 4
    )
    final, grad_after, returned, enc_parts, stats, packed = middle(
        gathered,
        tokens,
        embedded,
        encoder,
        cotangent,
        norm_gain,
        norm_bias,
        contexts,
        4,
        4,
    )
    outs = backward_group(
        prefix,
        enc_parts,
        packed,
        gathered,
        rows,
        returned,
        weight,
        qkv,
        wide,
        logs,
        tokens,
        embedded,
        norm_gain,
        norm_bias,
        grad_after,
        encoder,
        stats,
        span,
        4,
        4,
    )
    sums = outs[9]
    entries = (
        tokens.shape[0]
        * tokens.shape[1]
        * tokens.shape[2]
        * lax.axis_size("fsdp")
        * lax.axis_size("ctx")
        * lax.axis_size("tp")
    )
    results = collect((final, *outs[:2]), outs[2:9], sums, entries)
    return (*results[:12], results[12].reshape(width), results[13].reshape(4))


def solution(mesh):
    placed = (
        P("fsdp", ("ctx", "tp"), None),
        P("fsdp"),
        P(),
        P("fsdp"),
        P("fsdp", None, None),
        P(None, "fsdp", "tp"),
        P("fsdp", "tp"),
        P(None, "fsdp", "tp"),
        P("tp", "fsdp"),
        P("tp", "fsdp"),
        P("fsdp", "tp"),
        P("tp", "fsdp"),
        P(),
        P(),
        P("fsdp", ("ctx", "tp"), None),
    )
    heads_fit = dict(mesh.shape) == {"fsdp": 4, "ctx": 2, "tp": 4}
    return jax.shard_map(
        local_heads if heads_fit else local,
        mesh=mesh,
        in_specs=placed,
        out_specs=(
            P("fsdp", ("ctx", "tp"), None),
            P("fsdp", ("ctx", "tp"), None),
            P("fsdp", ("ctx", "tp"), None),
            P(None, "fsdp", "tp"),
            P("fsdp", "tp"),
            P(None, "fsdp", "tp"),
            P("tp", "fsdp"),
            P("tp", "fsdp"),
            P("fsdp", "tp"),
            P("tp", "fsdp"),
            P(),
            P(),
            P(),
            P(),
        ),
        check_vma=False,
    )
```

```python
import functools
import math

import jax
import jax.numpy as jnp
from jax import lax
from jax.experimental import pallas as pl
from jax.experimental.pallas import tpu as pltpu
from jax.sharding import PartitionSpec as P

HEAD_DIM = 64


EPS = 1e-05
NEG = -1e30
ROOT_HALF = 1.0 / math.sqrt(2.0)
INV_ROOT_TWO_PI = 1.0 / math.sqrt(2.0 * math.pi)
VMEM_LIMIT = 63 * 2**20


def norm_rows(hidden, scaling, offsets):
    centre = hidden - jnp.mean(hidden, -1, keepdims=True)
    inverse = lax.rsqrt(jnp.mean(centre * centre, -1, keepdims=True) + EPS)
    unit_rows = centre * inverse
    return (unit_rows * scaling + offsets, unit_rows, inverse)


def norm_back(upstream, unit_rows, inverse, scaling):
    scaled = upstream * scaling
    result = inverse * (
        scaled
        - jnp.mean(scaled, -1, keepdims=True)
        - unit_rows * jnp.mean(scaled * unit_rows, -1, keepdims=True)
    )
    return (result, jnp.sum(upstream * unit_rows, (0, 1)), jnp.sum(upstream, (0, 1)))


def gelu_parts(inputs):
    normal_cdf = 0.5 * (1.0 + lax.erf(inputs * ROOT_HALF))
    return (
        inputs * normal_cdf,
        normal_cdf + inputs * jnp.exp(-0.5 * inputs * inputs) * INV_ROOT_TWO_PI,
    )


def spread_rows(rows):
    return lax.all_gather(rows, "tp", axis=1, tiled=True)


def spread_grads(grad_rows):
    return lax.all_gather(grad_rows, "tp", axis=1, tiled=True)


def finish_branch(local_in, local_weight):
    return lax.psum_scatter(
        jnp.einsum("scw,wd->scd", local_in, local_weight, preferred_element_type=jnp.float32),
        "tp",
        scatter_dimension=1,
        tiled=True,
    )


def finish_grad(local_grad, local_weight):
    return lax.psum_scatter(
        jnp.einsum("scw,dw->scd", local_grad, local_weight, preferred_element_type=jnp.float32),
        "tp",
        scatter_dimension=1,
        tiled=True,
    )


def block_scores(queries, key_block, query_pos, key_pos, lengths, factor):
    scores = (
        jnp.einsum("sqhe,skhe->sqhk", queries, key_block, preferred_element_type=jnp.float32)
        * factor
    )
    visible = (key_pos[None, None, :] <= query_pos[None, :, None]) | (
        key_pos[None, None, :] < lengths[:, None, None]
    )
    return jnp.where(visible[:, :, None, :], scores, NEG)


def attend_forward(queries, key_rows, value_rows, query_pos, lengths, key_span, factor):
    length = key_rows.shape[1]

    def attend_advance(running, offset):
        highest, totals, summed = running
        key_block = lax.dynamic_slice_in_dim(key_rows, offset, key_span, 1)
        value_block = lax.dynamic_slice_in_dim(value_rows, offset, key_span, 1)
        scores = block_scores(
            queries, key_block, query_pos, offset + lax.iota(jnp.int32, key_span), lengths, factor
        )
        new_high = jnp.maximum(highest, jnp.max(scores, -1))
        weights = jnp.exp(scores - new_high[..., None])
        fading = jnp.exp(highest - new_high)
        totals = totals * fading + jnp.sum(weights, -1)
        summed = summed * fading[..., None] + jnp.einsum(
            "sqhk,skhe->sqhe",
            weights.astype(jnp.bfloat16),
            value_block,
            preferred_element_type=jnp.float32,
        )
        return ((new_high, totals, summed), None)

    stat_shape = queries.shape[:3]
    initial = (
        jnp.full(stat_shape, NEG, jnp.float32),
        jnp.zeros(stat_shape, jnp.float32),
        jnp.zeros(queries.shape, jnp.float32),
    )
    offsets = jnp.arange(length // key_span, dtype=jnp.int32) * key_span
    (highest, totals, summed), unused = lax.scan(attend_advance, initial, offsets)
    return (summed / totals[..., None], highest + jnp.log(totals))


def attend_block(
    queries,
    grad_out,
    log_rows,
    delta_rows,
    key_block,
    value_block,
    query_pos,
    key_pos,
    lengths,
    factor,
):
    scores = block_scores(queries, key_block, query_pos, key_pos, lengths, factor)
    probs = jnp.exp(scores - log_rows[..., None])
    grad_probs = jnp.einsum(
        "sqhe,skhe->sqhk", grad_out, value_block, preferred_element_type=jnp.float32
    )
    grad_scores = (probs * (grad_probs - delta_rows[..., None])).astype(jnp.bfloat16)
    return (probs.astype(jnp.bfloat16), grad_scores)


def key_sweep(
    queries,
    grad_out,
    log_rows,
    delta_rows,
    key_rows,
    value_rows,
    query_pos,
    lengths,
    key_span,
    factor,
):
    batches, row_count, head_count, head_depth = queries.shape
    length = key_rows.shape[1]

    def key_advance(grad_query, offset):
        key_block = lax.dynamic_slice_in_dim(key_rows, offset, key_span, 1)
        value_block = lax.dynamic_slice_in_dim(value_rows, offset, key_span, 1)
        key_pos = offset + lax.iota(jnp.int32, key_span)
        probs_low, grad_scores = attend_block(
            queries,
            grad_out,
            log_rows,
            delta_rows,
            key_block,
            value_block,
            query_pos,
            key_pos,
            lengths,
            factor,
        )
        grad_query = (
            grad_query
            + jnp.einsum(
                "sqhk,skhe->sqhe", grad_scores, key_block, preferred_element_type=jnp.float32
            )
            * factor
        )
        grad_key = (
            jnp.einsum("sqhk,sqhe->kshe", grad_scores, queries, preferred_element_type=jnp.float32)
            * factor
        )
        grad_value = jnp.einsum(
            "sqhk,sqhe->kshe", probs_low, grad_out, preferred_element_type=jnp.float32
        )
        return (grad_query, (grad_key, grad_value))

    offsets = jnp.arange(length // key_span, dtype=jnp.int32) * key_span
    grad_query, stacked = lax.scan(key_advance, jnp.zeros(queries.shape, jnp.float32), offsets)
    flat_shape = (length, batches, head_count * head_depth)
    return (grad_query, stacked[0].reshape(flat_shape), stacked[1].reshape(flat_shape))


def local(
    tokens,
    timesteps,
    time_table,
    prefix,
    encoder,
    self_qkv,
    cross_q,
    cross_kv,
    self_out,
    cross_out,
    ffn_up,
    ffn_down,
    norm_gain,
    norm_bias,
    cotangent,
):
    proj_self, proj_query, proj_pair, back_self, back_cross, expand_full, shrink_full = (
        lax.all_gather(self_qkv, "fsdp", axis=1, tiled=True),
        lax.all_gather(cross_q, "fsdp", axis=0, tiled=True),
        lax.all_gather(cross_kv, "fsdp", axis=1, tiled=True),
        lax.all_gather(self_out, "fsdp", axis=1, tiled=True),
        lax.all_gather(cross_out, "fsdp", axis=1, tiled=True),
        lax.all_gather(ffn_up, "fsdp", axis=0, tiled=True),
        lax.all_gather(ffn_down, "fsdp", axis=1, tiled=True),
    )
    batches = tokens.shape[0]
    model_width = tokens.shape[2]
    local_width = proj_query.shape[1]
    head_count = local_width // HEAD_DIM
    factor = HEAD_DIM ** (-0.5)
    ctx_index = lax.axis_index("ctx")
    local_stack = jnp.transpose(proj_self, (1, 0, 2)).reshape(model_width, 3 * local_width)
    steps_onehot = (timesteps[:, None] == lax.iota(jnp.int32, time_table.shape[0])[None, :]).astype(
        jnp.bfloat16
    )
    embedded = jnp.dot(steps_onehot, time_table, preferred_element_type=jnp.float32)
    start_sum = tokens.astype(jnp.float32) + embedded[:, None, :]
    normed_one, unit_one, inverse_one = norm_rows(start_sum, norm_gain[0], norm_bias[0])
    rows_self = spread_rows(normed_one.astype(jnp.bfloat16))
    row_count = rows_self.shape[1]
    head_shape = (batches, row_count, head_count, HEAD_DIM)
    projected = jnp.einsum(
        "scd,kdw->kscw", rows_self, proj_self, preferred_element_type=jnp.float32
    ).astype(jnp.bfloat16)
    queries, key_local, value_local = (projected[0], projected[1], projected[2])
    key_all, value_all = (
        lax.all_gather(key_local, "ctx", axis=1, tiled=True),
        lax.all_gather(value_local, "ctx", axis=1, tiled=True),
    )
    length = key_all.shape[1]
    key_span = min(512, length)
    query_pos = ctx_index * row_count + lax.iota(jnp.int32, row_count)
    keys_four = key_all.reshape(batches, length, head_count, HEAD_DIM)
    values_four = value_all.reshape(batches, length, head_count, HEAD_DIM)
    queries_four = queries.reshape(head_shape)
    attended, log_total = attend_forward(
        queries_four, keys_four, values_four, query_pos, prefix, key_span, factor
    )
    context_one = attended.reshape(batches, row_count, local_width).astype(jnp.bfloat16)
    branch_one = finish_branch(context_one, back_self)
    after_one = start_sum + branch_one
    normed_two, unit_two, inverse_two = norm_rows(after_one, norm_gain[1], norm_bias[1])
    rows_cross = spread_rows(normed_two.astype(jnp.bfloat16))
    cross_queries = jnp.einsum(
        "scd,dw->scw", rows_cross, proj_query, preferred_element_type=jnp.float32
    ).astype(jnp.bfloat16)
    enc_pair = jnp.einsum(
        "sed,kdw->ksew", encoder, proj_pair, preferred_element_type=jnp.float32
    ).astype(jnp.bfloat16)
    enc_count = encoder.shape[1]
    cross_keys = enc_pair[0].reshape(batches, enc_count, head_count, HEAD_DIM)
    cross_values = enc_pair[1].reshape(batches, enc_count, head_count, HEAD_DIM)
    cross_four = cross_queries.reshape(head_shape)
    cross_probs = jax.nn.softmax(
        jnp.einsum("sqhe,skhe->sqhk", cross_four, cross_keys, preferred_element_type=jnp.float32)
        * factor,
        axis=-1,
    )
    cross_low = cross_probs.astype(jnp.bfloat16)
    context_two = (
        jnp.einsum("sqhk,skhe->sqhe", cross_low, cross_values, preferred_element_type=jnp.float32)
        .reshape(batches, row_count, local_width)
        .astype(jnp.bfloat16)
    )
    branch_two = finish_branch(context_two, back_cross)
    after_two = after_one + branch_two
    normed_three, unit_three, inverse_three = norm_rows(after_two, norm_gain[2], norm_bias[2])
    rows_ffn = spread_rows(normed_three.astype(jnp.bfloat16))
    pre_act = jnp.einsum("scd,df->scf", rows_ffn, expand_full, preferred_element_type=jnp.float32)
    activated, slopes = gelu_parts(pre_act)
    hidden_low = activated.astype(jnp.bfloat16)
    branch_three = finish_branch(hidden_low, shrink_full)
    final_sum = after_two + branch_three
    grad_three = spread_grads(cotangent)
    grad_shrink = jnp.einsum(
        "scf,scd->fd", hidden_low, grad_three, preferred_element_type=jnp.float32
    )
    grad_pre = (
        jnp.einsum("scd,fd->scf", grad_three, shrink_full, preferred_element_type=jnp.float32)
        * slopes
    ).astype(jnp.bfloat16)
    grad_expand = jnp.einsum("scd,scf->df", rows_ffn, grad_pre, preferred_element_type=jnp.float32)
    back_three, gain_three, shift_three = norm_back(
        finish_grad(grad_pre, expand_full), unit_three, inverse_three, norm_gain[2]
    )
    grad_after_two = cotangent.astype(jnp.float32) + back_three
    grad_two = spread_grads(grad_after_two.astype(jnp.bfloat16))
    grad_back_cross = jnp.einsum(
        "scw,scd->wd", context_two, grad_two, preferred_element_type=jnp.float32
    )
    grad_context_two = jnp.einsum(
        "scd,wd->scw", grad_two, back_cross, preferred_element_type=jnp.float32
    ).astype(jnp.bfloat16)
    grad_cross_four = grad_context_two.reshape(head_shape)
    grad_cross_probs = jnp.einsum(
        "sqhe,skhe->sqhk", grad_cross_four, cross_values, preferred_element_type=jnp.float32
    )
    grad_cross_scores = (
        cross_probs
        * (grad_cross_probs - jnp.sum(cross_probs * grad_cross_probs, -1, keepdims=True))
    ).astype(jnp.bfloat16)
    grad_cross_q = (
        (
            jnp.einsum(
                "sqhk,skhe->sqhe", grad_cross_scores, cross_keys, preferred_element_type=jnp.float32
            )
            * factor
        )
        .reshape(batches, row_count, local_width)
        .astype(jnp.bfloat16)
    )
    part_keys = (
        jnp.einsum(
            "sqhk,sqhe->skhe", grad_cross_scores, cross_four, preferred_element_type=jnp.float32
        )
        * factor
    ).reshape(batches, enc_count, local_width)
    part_values = jnp.einsum(
        "sqhk,sqhe->skhe", cross_low, grad_cross_four, preferred_element_type=jnp.float32
    ).reshape(batches, enc_count, local_width)
    enc_keys, enc_values = (
        lax.psum_scatter(part_keys, "ctx", scatter_dimension=1, tiled=True),
        lax.psum_scatter(part_values, "ctx", scatter_dimension=1, tiled=True),
    )
    enc_keys = enc_keys.astype(jnp.bfloat16)
    enc_values = enc_values.astype(jnp.bfloat16)
    enc_share = enc_keys.shape[1]
    enc_rows = lax.dynamic_slice_in_dim(encoder, ctx_index * enc_share, enc_share, 1)
    grad_pair = jnp.stack(
        [
            jnp.einsum("sed,sew->dw", enc_rows, enc_keys, preferred_element_type=jnp.float32),
            jnp.einsum("sed,sew->dw", enc_rows, enc_values, preferred_element_type=jnp.float32),
        ]
    )
    encoder_grad = lax.psum_scatter(
        jnp.einsum("sew,dw->sed", enc_keys, proj_pair[0], preferred_element_type=jnp.float32)
        + jnp.einsum("sew,dw->sed", enc_values, proj_pair[1], preferred_element_type=jnp.float32),
        "tp",
        scatter_dimension=1,
        tiled=True,
    )
    grad_query_proj = jnp.einsum(
        "scd,scw->dw", rows_cross, grad_cross_q, preferred_element_type=jnp.float32
    )
    back_two, gain_two, shift_two = norm_back(
        finish_grad(grad_cross_q, proj_query), unit_two, inverse_two, norm_gain[1]
    )
    grad_after_one = grad_after_two + back_two
    grad_one = spread_grads(grad_after_one.astype(jnp.bfloat16))
    grad_back_self = jnp.einsum(
        "scw,scd->wd", context_one, grad_one, preferred_element_type=jnp.float32
    )
    grad_context_one = jnp.einsum(
        "scd,wd->scw", grad_one, back_self, preferred_element_type=jnp.float32
    ).astype(jnp.bfloat16)
    grad_ctx_four = grad_context_one.reshape(head_shape)
    delta_rows = jnp.sum(grad_ctx_four.astype(jnp.float32) * attended, -1)
    grad_query, grad_key_all, grad_value_all = key_sweep(
        queries_four,
        grad_ctx_four,
        log_total,
        delta_rows,
        keys_four,
        values_four,
        query_pos,
        prefix,
        key_span,
        factor,
    )
    own_keys, own_values = (
        lax.psum_scatter(grad_key_all, "ctx", scatter_dimension=0, tiled=True),
        lax.psum_scatter(grad_value_all, "ctx", scatter_dimension=0, tiled=True),
    )
    own_keys = jnp.transpose(own_keys, (1, 0, 2))
    own_values = jnp.transpose(own_values, (1, 0, 2))
    grad_joined = jnp.concatenate(
        [grad_query.reshape(batches, row_count, local_width), own_keys, own_values], -1
    ).astype(jnp.bfloat16)
    grad_proj_self = jnp.transpose(
        jnp.einsum(
            "scd,scw->dw", rows_self, grad_joined, preferred_element_type=jnp.float32
        ).reshape(model_width, 3, local_width),
        (1, 0, 2),
    )
    back_one, gain_one, shift_one = norm_back(
        finish_grad(grad_joined, local_stack), unit_one, inverse_one, norm_gain[0]
    )
    input_grad = grad_after_one + back_one
    shard_grads = (
        lax.psum_scatter(grad_proj_self, "fsdp", scatter_dimension=1, tiled=True),
        lax.psum_scatter(grad_query_proj, "fsdp", scatter_dimension=0, tiled=True),
        lax.psum_scatter(grad_pair, "fsdp", scatter_dimension=1, tiled=True),
        lax.psum_scatter(grad_back_self, "fsdp", scatter_dimension=1, tiled=True),
        lax.psum_scatter(grad_back_cross, "fsdp", scatter_dimension=1, tiled=True),
        lax.psum_scatter(grad_expand, "fsdp", scatter_dimension=0, tiled=True),
        lax.psum_scatter(grad_shrink, "fsdp", scatter_dimension=1, tiled=True),
    )
    full_grads = lax.psum(
        (
            shard_grads[0],
            shard_grads[1],
            shard_grads[2],
            shard_grads[3],
            shard_grads[4],
            shard_grads[5],
            shard_grads[6],
        ),
        "ctx",
    )
    squares = jnp.stack(
        [
            jnp.sum(final_sum * final_sum),
            jnp.sum(branch_one * branch_one),
            jnp.sum(branch_two * branch_two),
            jnp.sum(branch_three * branch_three),
        ]
    )
    gain_grad, bias_grad, square_totals = lax.psum(
        (
            jnp.stack([gain_one, gain_two, gain_three]),
            jnp.stack([shift_one, shift_two, shift_three]),
            squares,
        ),
        ("fsdp", "ctx", "tp"),
    )
    entries = (
        tokens.shape[0]
        * tokens.shape[1]
        * tokens.shape[2]
        * lax.axis_size("fsdp")
        * lax.axis_size("ctx")
        * lax.axis_size("tp")
    )
    norms = jnp.sqrt(square_totals / entries)
    return (
        final_sum,
        input_grad,
        encoder_grad,
        full_grads[0],
        full_grads[1],
        full_grads[2],
        full_grads[3],
        full_grads[4],
        full_grads[5],
        full_grads[6],
        gain_grad,
        bias_grad[:2],
        bias_grad[2],
        norms,
    )


def dot_of(left, right, left_dim, right_dim):
    return lax.dot_general(
        left, right, (((left_dim,), (right_dim,)), ((), ())), preferred_element_type=jnp.float32
    )


def bounds(prefix, start, query_span, key_span):
    whole = jnp.maximum(prefix, start + 1) // key_span
    every = (jnp.maximum(prefix, start + query_span) + key_span - 1) // key_span
    return whole, every


def hide(scores, limit, offset):
    return jnp.where(lax.broadcasted_iota(jnp.int32, scores.shape, 0) < limit - offset, scores, NEG)


def low(value):
    return value.astype(jnp.bfloat16)


STRIP = 64


def in_strips(work, *values, strip=STRIP, axis=0):
    count = values[0].shape[axis] // strip
    cut = lambda v, n: lax.slice_in_dim(v, n * strip, (n + 1) * strip, axis=axis)
    parts = [work(*[cut(v, n) for v in values]) for n in range(count)]
    return tuple(jnp.concatenate(p, axis) for p in zip(*parts))


def gelu_strip(inputs):
    activated, slopes = gelu_parts(inputs)
    return low(activated), slopes


def rows_unit(hidden):
    centre = hidden - jnp.mean(hidden, -1, keepdims=True)
    inverse = lax.rsqrt(jnp.mean(centre * centre, -1, keepdims=True) + EPS)
    return centre * inverse, inverse


def rows_norm(hidden, scaling, offsets):
    def strip(rows):
        unit_rows, inverse = rows_unit(rows)
        return low(unit_rows * scaling + offsets), unit_rows, inverse

    return in_strips(strip, hidden)


def rows_back(upstream, unit_rows, inverse, scaling):
    sums = [jnp.zeros((8, upstream.shape[1]), jnp.float32)] * 2

    def strip(rows, units, inverses):
        scaled = rows * scaling
        for n, term in enumerate((rows * units, rows)):
            sums[n] = sums[n] + jnp.sum(term.reshape(-1, 8, term.shape[1]), 0)
        return (
            inverses
            * (
                scaled
                - jnp.mean(scaled, -1, keepdims=True)
                - units * jnp.mean(scaled * units, -1, keepdims=True)
            ),
        )

    (result,) = in_strips(strip, upstream, unit_rows, inverse)
    return result, jnp.sum(sums[0], 0, keepdims=True), jnp.sum(sums[1], 0, keepdims=True)


MESH = pl.DeviceIdType.MESH


def meet(group, tp, fsdp):
    here, core, chip = lax.axis_index("fsdp"), lax.axis_index("ctx"), lax.axis_index("tp")
    me = core * tp + chip
    barrier = pltpu.get_barrier_semaphore()
    for k in range(1, group):
        other = me ^ k
        pl.semaphore_signal(
            barrier, inc=1, device_id={"ctx": other // tp, "tp": other % tp}, device_id_type=MESH
        )
    for k in range(1, fsdp):
        pl.semaphore_signal(barrier, inc=1, device_id={"fsdp": here ^ k}, device_id_type=MESH)
    pl.semaphore_wait(barrier, group - 1 + fsdp - 1)


def forward_kernel(
    prefix_ref,
    tokens_ref,
    step_ref,
    gain_ref,
    bias_ref,
    mine_ref,
    rows_out,
    qkv_ref,
    wide_ref,
    log_ref,
    ctx_ref,
    weight,
    rows_ref,
    other_ref,
    columns,
    pair_ref,
    keys_ref,
    values_ref,
    low_ref,
    landing,
    w_send,
    w_recv,
    v_send,
    v_recv,
    x_send,
    x_recv,
    c_send,
    c_recv,
    keep_sem,
    *,
    span,
    tp,
    fsdp,
):
    batches, chunk, width = tokens_ref.shape
    group = rows_ref.shape[0]
    length = group * chunk
    blocks, ratio = length // span, span // chunk
    wide_blocks = max(1, length // 2 // span)
    factor = HEAD_DIM**-0.5
    here, core, chip = lax.axis_index("fsdp"), lax.axis_index("ctx"), lax.axis_index("tp")
    me = core * tp + chip
    mine = chip // 2
    inner = (chip == 1) | (chip == 2)
    other_inner, other_outer = 2 - mine, 3 - 3 * mine
    meet(group, tp, fsdp)

    def send_to(source, target, send, recv, **place):
        return pltpu.make_async_remote_copy(
            src_ref=source,
            dst_ref=target,
            send_sem=send,
            recv_sem=recv,
            device_id=place,
            device_id_type=MESH,
        )

    v_core, v_chip = chip % 2, chip // 2 + 2 * core
    v_own = (v_core == core) & (v_chip == chip)
    v_copy = send_to(mine_ref, pair_ref, v_send.at[0], v_recv.at[0], ctx=v_core, tp=v_chip)

    @pl.when(v_own)
    def keep_pair():
        pair_ref[...] = mine_ref[...]

    @pl.when(jnp.logical_not(v_own))
    def send_pair():
        v_copy.start()

    comes = (chip // 2 != core) | (2 * (chip % 2) + core != chip)

    def w_copy(k):
        return send_to(pair_ref, columns.at[k], w_send.at[k], w_recv.at[k], fsdp=here ^ k)

    def normalise(seq, target, at):
        start_sum = tokens_ref[seq].astype(jnp.float32) + step_ref[seq]
        target[at] = rows_norm(start_sum, gain_ref[0:1], bias_ref[0:1])[0]

    def x_copy(kind):
        block = rows_ref.at[me]
        near = rows_ref.at[core * tp + (chip ^ 1)]
        second = rows_ref.at[core * tp + other_inner]
        third = rows_ref.at[core * tp + other_outer]
        source, place, target = (
            (block, me, {"tp": chip ^ 1}),
            (other_ref.at[0], me, {"tp": other_inner}),
            (block, me, {"ctx": 1 - core}),
            (near, core * tp + (chip ^ 1), {"ctx": 1 - core}),
            (second, core * tp + other_inner, {"ctx": 1 - core}),
            (third, core * tp + other_outer, {"ctx": 1 - core}),
            (second, core * tp + other_inner, {"tp": chip ^ 1}),
            (third, core * tp + other_outer, {"tp": chip ^ 1}),
            (other_ref.at[0], me, {"tp": other_outer}),
        )[kind]
        return send_to(source, rows_ref.at[place], x_send.at[kind], x_recv.at[place], **target)

    def x_wait(place):
        send_to(
            rows_ref.at[place], rows_ref.at[place], x_send.at[0], x_recv.at[place], ctx=1 - core
        ).wait_recv()

    def arrive(number):
        x_wait(core * tp + (chip ^ 1, other_inner, other_outer)[number])
        if number:

            @pl.when(inner & (core == 0))
            def onward():
                x_copy(5 + number).start()

        x_copy(3 + number).start()

    normalise(mine, rows_ref, me)
    normalise(1 - mine, other_ref, 0)

    @pl.when(core == 0)
    def first_half():
        x_copy(2).start()

        @pl.when(inner)
        def from_inner():
            x_copy(1).start()
            x_copy(0).start()

        @pl.when(jnp.logical_not(inner))
        def from_outer():
            x_copy(0).start()

    @pl.when(comes)
    def pair_here():
        v_copy.wait_recv()

    for k in range(1, fsdp):
        w_copy(k).start()
    values_ref[:, HEAD_DIM:, :] = jnp.ones_like(values_ref[:, HEAD_DIM:, :])

    def project(place, unused):
        rows = rows_ref[place]
        joined = low(dot_of(weight[...], rows, 1, 1))
        at = pl.ds(pl.multiple_of(place * chunk, chunk), chunk)
        for head in range(2):
            queries, keys, values = (
                joined[(3 * head + n) * HEAD_DIM : (3 * head + n + 1) * HEAD_DIM] for n in range(3)
            )
            qkv_ref[head, :HEAD_DIM, at] = queries * jnp.bfloat16(factor)
            qkv_ref[head, HEAD_DIM : 2 * HEAD_DIM, at] = keys
            qkv_ref[head, 2 * HEAD_DIM :, at] = values
            values_ref[head, :HEAD_DIM, at] = values
            keys_ref[head, at, :] = keys.T
        return unused

    @pl.when(core == 0)
    def first_lines():
        @pl.when(jnp.logical_not(inner))
        def then_other():
            x_copy(0).wait_send()
            x_copy(1).start()

        for number in range(3):
            arrive(number)

    @pl.when(core == 1)
    def second_lines():
        for place in range(tp):
            x_wait(place)
        for kind in (2, 1, 8, 0):
            x_copy(kind).start()

    piece = mine_ref.shape[1]
    for k in range(fsdp):
        if k:
            w_copy(k).wait_recv()
        part = columns[k] if k else pair_ref[...]
        for f in range(fsdp):

            @pl.when((here ^ k) == f)
            def place(f=f, part=part):
                weight[:, f * piece : (f + 1) * piece] = part

    lax.fori_loop(0, tp, project, 0)

    def c_copy(head, place):
        return send_to(
            low_ref.at[head, place],
            landing.at[head, me],
            c_send.at[head, place],
            c_recv.at[head, me],
            ctx=place // tp,
            tp=place % tp,
        )

    def c_wait(head, place):
        send_to(
            low_ref.at[head, place],
            landing.at[head, place],
            c_send.at[head, place],
            c_recv.at[head, place],
            ctx=place // tp,
            tp=place % tp,
        ).wait_recv()

    def attend(index, unused):
        block, head = (index // 2) ^ (1 - mine), index % 2

        @pl.when((core == 1) & (index == 3))
        def near_lines():
            arrive(0)

        @pl.when(index == 4)
        def second_half():
            @pl.when(core == 0)
            def wait_other():
                for place in range(tp, group):
                    x_wait(place)

            @pl.when(core == 1)
            def far_lines():
                arrive(1)
                arrive(2)

            def first_results(place, unused):
                @pl.when(place != me)
                def send():
                    for number in range(2):
                        c_copy(number, place).start()

                return unused

            lax.fori_loop(0, tp, first_results, 0)
            lax.fori_loop(tp, group, project, 0)

        start = pl.multiple_of(block * span, span)
        queries = qkv_ref[head, :HEAD_DIM, pl.ds(start, span)]
        limit = jnp.maximum(
            prefix_ref[mine], start + 1 + lax.broadcasted_iota(jnp.int32, (1, span), 1)
        )

        def advance(offset, count, carry, columns=None):
            highest, total = carry
            first = 0 if columns is None else columns
            scores = dot_of(keys_ref[head, pl.ds(offset, count), :], queries[:, first:], 1, 0)
            if columns is not None:
                scores = hide(scores, limit[:, first:], offset)
            higher = jnp.maximum(highest, jnp.max(scores, axis=0, keepdims=True))
            weights = low(jnp.exp(scores - higher))
            fading = jnp.exp(highest - higher)
            total = total * fading + dot_of(
                values_ref[head, :, pl.ds(offset, count)], weights, 1, 0
            )
            return higher, total

        def whole_step(other, carry):
            return advance(pl.multiple_of(other * span, span), span, carry)

        def masked_step(other, carry):
            return advance(pl.multiple_of(other * span, span), span, carry, 0)

        def diagonal_step(other, carry):
            half = span // 2
            carry = advance(start, half, carry, 0)
            offset = pl.multiple_of(start + half, half)
            upper = advance(offset, half, tuple(v[:, half:] for v in carry), half)
            return tuple(jnp.concatenate([v[:, :half], u], 1) for v, u in zip(carry, upper))

        carry = (
            jnp.full((1, span), NEG, jnp.float32),
            jnp.zeros((values_ref.shape[1], span), jnp.float32),
        )
        carry = lax.fori_loop(0, block, whole_step, carry)
        carry = lax.fori_loop(block, wide_blocks, masked_step, carry)
        highest, total = lax.fori_loop(
            0, jnp.where(block >= wide_blocks, 1, 0), diagonal_step, carry
        )
        weight_sum = total[HEAD_DIM : HEAD_DIM + 1, :]
        attended = total[:HEAD_DIM, :] / weight_sum
        wide_ref[head, :, pl.ds(start, span)] = attended
        log_ref[head, :, pl.ds(start, span)] = highest + jnp.log(weight_sum)
        attended = low(attended)
        for part in range(ratio):
            place = block * ratio + part
            low_ref[head, place] = attended[:, part * chunk : (part + 1) * chunk]

            @pl.when((place != me) & (index >= 4))
            def send(place=place):
                c_copy(head, place).start()

        return unused

    lax.fori_loop(0, 2 * blocks, attend, 0)
    keep = pltpu.make_async_copy(rows_ref, rows_out, keep_sem)
    keep.start()
    for head in range(2):

        def collect(k, unused, head=head):
            c_wait(head, me ^ k)
            ctx_ref[head, me ^ k] = landing[head, me ^ k]
            return unused

        lax.fori_loop(1, group, collect, 0)
        ctx_ref[head, me] = low_ref[head, me]
    for k in range(1, fsdp):
        w_copy(k).wait_send()

    @pl.when(jnp.logical_not(v_own))
    def pair_sent():
        v_copy.wait_send()

    for kind in range(1, 6):
        x_copy(kind).wait_send()

    @pl.when(inner | (core == 1))
    def own_sent():
        x_copy(0).wait_send()

    @pl.when(inner & (core == 0))
    def lines_sent():
        x_copy(6).wait_send()
        x_copy(7).wait_send()

    @pl.when(core == 1)
    def direct_sent():
        x_copy(8).wait_send()

    for head in range(2):

        def sent(k, unused, head=head):
            c_copy(head, me ^ k).wait_send()
            return unused

        lax.fori_loop(1, group, sent, 0)
    keep.wait()


def forward_group(prefix, tokens, steps, gain, bias, mine, span, group, tp, fsdp):
    batches, chunk, width = tokens.shape
    length = group * chunk
    bf16, f32 = jnp.bfloat16, jnp.float32
    struct = jax.ShapeDtypeStruct
    inside = pl.BlockSpec(memory_space=pltpu.VMEM)
    dma = pltpu.SemaphoreType.DMA
    return pl.pallas_call(
        functools.partial(forward_kernel, span=span, tp=tp, fsdp=fsdp),
        in_specs=[pl.BlockSpec(memory_space=pltpu.SMEM)] + [inside] * 5,
        out_specs=[pl.BlockSpec(memory_space=pl.ANY)] + [inside] * 5,
        out_shape=[
            struct((group, chunk, width), bf16),
            struct((2, 3 * HEAD_DIM, length), bf16),
            struct((2, HEAD_DIM, length), f32),
            struct((2, 1, length), f32),
            struct((2, group, HEAD_DIM, chunk), bf16),
            struct((6 * HEAD_DIM, width), bf16),
        ],
        scratch_shapes=[
            pltpu.VMEM((group, chunk, width), bf16),
            pltpu.VMEM((1, chunk, width), bf16),
            pltpu.VMEM((fsdp,) + mine.shape, bf16),
            pltpu.VMEM(mine.shape, bf16),
            pltpu.VMEM((2, length, HEAD_DIM), bf16),
            pltpu.VMEM((2, HEAD_DIM + 16, length), bf16),
            pltpu.VMEM((2, group, HEAD_DIM, chunk), bf16),
            pltpu.VMEM((2, group, HEAD_DIM, chunk), bf16),
            dma((fsdp,)),
            dma((fsdp,)),
            dma((1,)),
            dma((1,)),
            dma((9,)),
            dma((group,)),
            dma((2, group)),
            dma((2, group)),
            dma,
        ],
        compiler_params=pltpu.CompilerParams(
            vmem_limit_bytes=VMEM_LIMIT, collective_id=1, has_side_effects=True
        ),
        cost_estimate=pl.CostEstimate(
            flops=60_000_000_000, bytes_accessed=30_000_000, transcendentals=20_000_000
        ),
        name="forward_group",
    )(prefix, tokens, steps, gain, bias, mine)


QUERY, KEY, VALUE, SELF_OUT, CROSS_OUT, UP, DOWN = 0, 1, 2, 3, 4, 5, 9


def middle_kernel(
    gathered,
    tokens_ref,
    step_ref,
    enc_ref,
    cot_ref,
    gain_ref,
    bias_ref,
    ctx_ref,
    final_ref,
    after_ref,
    back_ref,
    enc_grad_ref,
    stats_ref,
    packed_ref,
    weights,
    hidden_all,
    pre_all,
    three_all,
    two_all,
    grad_two_all,
    grad_one_all,
    cross_all,
    query_all,
    context_all,
    queries,
    keys,
    values,
    probs,
    grad_heads,
    grad_keys,
    grad_values,
    back_rows,
    landing,
    d_send,
    d_recv,
    sem,
    *,
    tp,
    fsdp,
):
    batches, chunk, width = tokens_ref.shape
    group = landing.shape[1]
    core, chip = lax.axis_index("ctx"), lax.axis_index("tp")
    me = core * tp + chip
    mine = chip // 2
    meet(group, tp, fsdp)
    piece = gathered.shape[-1]
    factor = HEAD_DIM**-0.5
    heads = width // HEAD_DIM

    copies = []
    for f in range(width // piece):
        for c in range(group // tp):
            for t in range(tp):
                head = t * (group // tp) + c
                copies.append(
                    pltpu.make_async_copy(
                        gathered.at[f, c, t],
                        weights.at[:, pl.ds(head * HEAD_DIM, HEAD_DIM), pl.ds(f * piece, piece)],
                        sem.at[(f * group // tp + c) * tp + t],
                    )
                )
    for copy in copies:
        copy.start()
    stats_ref[...] = jnp.zeros_like(stats_ref)
    for copy in copies:
        copy.wait()

    owners = [(2 * (2 * z + c) + n, n, c * tp + z) for z in (0, 1) for c in (0, 1) for n in (0, 1)]

    def d_copy(turn, seq, head, number, owner):
        return pltpu.make_async_remote_copy(
            src_ref=back_rows.at[turn, pl.ds(head * HEAD_DIM, HEAD_DIM)],
            dst_ref=landing.at[number, me],
            send_sem=d_send.at[turn, head],
            recv_sem=d_recv.at[number, me],
            device_id={"ctx": owner // tp, "tp": owner % tp + 2 * seq},
            device_id_type=MESH,
        )

    def one_sequence(turn, unused):
        seq = jnp.where(turn == 0, 1 - mine, mine)
        at = pl.ds(pl.multiple_of(seq * chunk, chunk), chunk)
        for head, number, owner in owners:
            context_all[head * HEAD_DIM : (head + 1) * HEAD_DIM, at] = ctx_ref[number, owner + 2 * seq]
        start_sum = tokens_ref[seq].astype(jnp.float32) + step_ref[seq]
        branch_one = dot_of(context_all[:, at], weights[SELF_OUT], 0, 0)
        after_one = start_sum + branch_one
        stats_ref[1:2, :] += jnp.sum(branch_one * branch_one, 0, keepdims=True)
        normed_two, unit_two, inverse_two = rows_norm(after_one, gain_ref[1:2], bias_ref[1:2])
        two_all[at, :] = normed_two
        queries[...] = low(dot_of(weights[QUERY], normed_two, 1, 1))
        keys[...] = low(dot_of(weights[KEY], enc_ref[seq], 1, 1))
        values[...] = low(dot_of(weights[VALUE], enc_ref[seq], 1, 1))

        def attend(head, unused):
            rows = pl.ds(pl.multiple_of(head * HEAD_DIM, HEAD_DIM), HEAD_DIM)
            scores = dot_of(keys[rows, :].T, queries[rows, :], 1, 0) * factor

            def strip(columns):
                powers = jnp.exp(columns - jnp.max(columns, 0, keepdims=True))
                return (powers / jnp.sum(powers, 0, keepdims=True),)

            (attn,) = in_strips(strip, scores, strip=128, axis=1)
            probs[head] = attn
            cross_all[rows, at] = low(dot_of(values[rows, :], low(attn), 1, 0))
            return unused

        lax.fori_loop(0, heads, attend, 0, unroll=8)
        branch_two = dot_of(cross_all[:, at], weights[CROSS_OUT], 0, 0)
        after_two = after_one + branch_two
        stats_ref[2:3, :] += jnp.sum(branch_two * branch_two, 0, keepdims=True)
        normed_three, unit_three, inverse_three = rows_norm(after_two, gain_ref[2:3], bias_ref[2:3])
        three_all[at, :] = normed_three
        grad_three = cot_ref[seq]

        def feed(part, carry):
            branch, grad = carry
            up, down = weights[UP + part], weights[DOWN + part]
            inputs = dot_of(up, normed_three, 1, 1)
            hidden, slopes = in_strips(gelu_strip, inputs, strip=32)
            branch = branch + dot_of(hidden, down, 0, 0)
            hidden_all[part, :, at] = hidden
            grad_pre = low(dot_of(down, grad_three, 1, 1) * slopes)
            pre_all[part, :, at] = grad_pre
            return branch, grad + dot_of(grad_pre, up, 0, 0)

        blank = jnp.zeros((chunk, width), jnp.float32)
        branch_three, grad_norm = lax.fori_loop(0, DOWN - UP, feed, (blank, blank), unroll=4)
        final_sum = after_two + branch_three
        final_ref[seq] = final_sum
        stats_ref[0:1, :] += jnp.sum(final_sum * final_sum, 0, keepdims=True)
        stats_ref[3:4, :] += jnp.sum(branch_three * branch_three, 0, keepdims=True)
        back, gain_sum, bias_sum = rows_back(grad_norm, unit_three, inverse_three, gain_ref[2:3])
        stats_ref[6:7, :] += gain_sum
        stats_ref[7:8, :] += bias_sum
        grad_after_two = grad_three.astype(jnp.float32) + back
        grad_two = low(grad_after_two)
        grad_two_all[at, :] = grad_two
        grad_heads[...] = low(dot_of(weights[CROSS_OUT], grad_two, 1, 1))

        def attend_back(head, unused):
            rows = pl.ds(pl.multiple_of(head * HEAD_DIM, HEAD_DIM), HEAD_DIM)
            grads = grad_heads[rows, :]
            attn = probs[head]
            grad_probs = dot_of(values[rows, :].T, grads, 1, 0)

            def strip(ones, others):
                return (low(ones * (others - jnp.sum(ones * others, 0, keepdims=True))),)

            (grad_scores,) = in_strips(strip, attn, grad_probs, strip=128, axis=1)
            query_all[rows, at] = low(dot_of(keys[rows, :], grad_scores, 1, 0) * factor)
            grad_keys[rows, :] = dot_of(queries[rows, :], grad_scores, 1, 1) * factor
            grad_values[rows, :] = dot_of(grads, low(attn), 1, 1)
            return unused

        lax.fori_loop(0, heads, attend_back, 0, unroll=8)
        enc_grad_ref[seq, :, :width] = low(grad_keys[...].T)
        enc_grad_ref[seq, :, width:] = low(grad_values[...].T)
        upstream = dot_of(query_all[:, at], weights[QUERY], 0, 0)
        back, gain_sum, bias_sum = rows_back(upstream, unit_two, inverse_two, gain_ref[1:2])
        stats_ref[4:5, :] += gain_sum
        stats_ref[5:6, :] += bias_sum
        grad_after_one = grad_after_two + back
        after_ref[seq] = grad_after_one
        grad_one = low(grad_after_one)
        grad_one_all[at, :] = grad_one
        back_rows[turn] = low(dot_of(weights[SELF_OUT], grad_one, 1, 1))
        for head, number, owner in owners:

            @pl.when(owner + 2 * seq != me)
            def give(head=head, number=number, owner=owner):
                d_copy(turn, seq, head, number, owner).start()

            @pl.when(owner + 2 * seq == me)
            def keep(head=head, number=number):
                back_ref[number, me] = back_rows[turn, head * HEAD_DIM : (head + 1) * HEAD_DIM, :]

        return unused


    lax.fori_loop(0, batches, one_sequence, 0)
    def pack(block, left, right):
        total = low(dot_of(left, right, 1, 0))
        for f in range(width // piece):
            for c in range(group // tp):
                for t in range(tp):
                    head = t * (group // tp) + c
                    packed_ref[c, f, t, block] = total[
                        head * HEAD_DIM : (head + 1) * HEAD_DIM, f * piece : (f + 1) * piece
                    ]

    grad_three_all = cot_ref[...].reshape(batches * chunk, width)
    pack(0, query_all[...], two_all[...])
    pack(1, context_all[...], grad_one_all[...])
    pack(2, cross_all[...], grad_two_all[...])

    def pack_feed(part, unused):
        pack(UP - 2 + part, pre_all[part], three_all[...])
        pack(DOWN - 2 + part, hidden_all[part], grad_three_all)
        return unused

    lax.fori_loop(0, DOWN - UP, pack_feed, 0)

    def collect(k, unused):
        place = me ^ k
        for number in range(2):
            pltpu.make_async_remote_copy(
                src_ref=landing.at[number, place],
                dst_ref=landing.at[number, place],
                send_sem=d_send.at[0, 0],
                recv_sem=d_recv.at[number, place],
                device_id={"ctx": place // tp, "tp": place % tp},
                device_id_type=MESH,
            ).wait_recv()
            back_ref[number, place] = landing[number, place]
        return unused

    lax.fori_loop(1, group, collect, 0)
    for turn in range(batches):
        seq = 1 - mine if turn == 0 else mine
        for head, number, owner in owners:

            @pl.when(owner + 2 * seq != me)
            def given(turn=turn, seq=seq, head=head, number=number, owner=owner):
                d_copy(turn, seq, head, number, owner).wait_send()


def middle(
    gathered, tokens, steps, encoder, cotangent, gains, biases, contexts, tp, fsdp
):
    batches, chunk, width = tokens.shape
    group = contexts.shape[1]
    enc_count = encoder.shape[1]
    heads = width // HEAD_DIM
    bf16, f32 = jnp.bfloat16, jnp.float32
    struct = jax.ShapeDtypeStruct
    inside = pl.BlockSpec(memory_space=pltpu.VMEM)
    dma = pltpu.SemaphoreType.DMA
    count = gathered.shape[3]
    packed = (group // tp, gathered.shape[0], tp, count - 2) + gathered.shape[4:]
    return pl.pallas_call(
        functools.partial(middle_kernel, tp=tp, fsdp=fsdp),
        in_specs=[pl.BlockSpec(memory_space=pl.ANY)] + [inside] * 7,
        out_specs=[inside] * 6,
        out_shape=[
            struct((batches, chunk, width), f32),
            struct((batches, chunk, width), f32),
            struct((2, group, HEAD_DIM, chunk), bf16),
            struct((batches, enc_count, 2 * width), bf16),
            struct((8, width), f32),
            struct(packed, bf16),
        ],
        scratch_shapes=[
            pltpu.VMEM((count, width, width), bf16),
            pltpu.VMEM((DOWN - UP, width, batches * chunk), bf16),
            pltpu.VMEM((DOWN - UP, width, batches * chunk), bf16),
            pltpu.VMEM((batches * chunk, width), bf16),
            pltpu.VMEM((batches * chunk, width), bf16),
            pltpu.VMEM((batches * chunk, width), bf16),
            pltpu.VMEM((batches * chunk, width), bf16),
            pltpu.VMEM((width, batches * chunk), bf16),
            pltpu.VMEM((width, batches * chunk), bf16),
            pltpu.VMEM((width, batches * chunk), bf16),
            pltpu.VMEM((width, chunk), bf16),
            pltpu.VMEM((width, enc_count), bf16),
            pltpu.VMEM((width, enc_count), bf16),
            pltpu.VMEM((heads, enc_count, chunk), f32),
            pltpu.VMEM((width, chunk), bf16),
            pltpu.VMEM((width, enc_count), f32),
            pltpu.VMEM((width, enc_count), f32),
            pltpu.VMEM((batches, width, chunk), bf16),
            pltpu.VMEM((2, group, HEAD_DIM, chunk), bf16),
            dma((batches, heads)),
            dma((2, group)),
            dma((32,)),
        ],
        compiler_params=pltpu.CompilerParams(
            vmem_limit_bytes=VMEM_LIMIT, collective_id=3, has_side_effects=True
        ),
        cost_estimate=pl.CostEstimate(
            flops=30_000_000_000, bytes_accessed=30_000_000, transcendentals=10_000_000
        ),
        name="middle",
    )(gathered, tokens, steps, encoder, cotangent, gains, biases, contexts)


def backward_kernel(
    prefix_ref,
    enc_parts,
    packed,
    gathered,
    rows_in,
    landing,
    weight,
    qkv_ref,
    wide_ref,
    log_ref,
    tokens_ref,
    step_ref,
    gain_ref,
    bias_ref,
    after_ref,
    enc_ref,
    stats_ref,
    input_ref,
    enc_out,
    self_out,
    query_out,
    pair_out,
    back_out,
    cross_out,
    up_out,
    down_out,
    sums_out,
    outgoing,
    core_rows,
    core_rows_landing,
    sum_rows,
    beside,
    incoming,
    queries_ref,
    pairs_ref,
    grad_ref,
    delta_ref,
    grad_pairs_ref,
    rows_ref,
    pair_weights,
    enc_own,
    enc_core,
    enc_sum,
    enc_landing,
    pair_ref,
    pair_landing,
    core_landing,
    partial_ref,
    fsdp_landing,
    line_ref,
    line_landing,
    shard_ref,
    head_ref,
    head_landing,
    head_pair,
    head_two,
    sums_ref,
    sums_landing,
    sums_two,
    e_send,
    e_recv,
    x_send,
    x_recv,
    i_send,
    i_recv,
    b_recv,
    r_send,
    r_recv,
    f_send,
    f_recv,
    t_send,
    t_recv,
    h_send,
    h_recv,
    p_send,
    p_recv,
    s_send,
    s_recv,
    local_sem,
    rows_sem,
    *,
    span,
    tp,
    fsdp,
):
    batches, chunk, width = tokens_ref.shape
    group = landing.shape[1]
    length = group * chunk
    blocks, ratio = length // span, span // chunk
    wide_blocks = max(1, length // 2 // span)
    factor = HEAD_DIM**-0.5
    here, core, chip = lax.axis_index("fsdp"), lax.axis_index("ctx"), lax.axis_index("tp")
    me = core * tp + chip
    mine = chip // 2
    inner = (chip == 1) | (chip == 2)
    cores = group // tp
    share = enc_landing.shape[2]
    piece = width // fsdp
    early = packed.shape[3]
    meet(group, tp, fsdp)

    def send_to(source, target, send, recv, **place):
        return pltpu.make_async_remote_copy(
            src_ref=source,
            dst_ref=target,
            send_sem=send,
            recv_sem=recv,
            device_id=place,
            device_id_type=MESH,
        )

    def member(place):
        return {"ctx": place // tp, "tp": place % tp}

    local = [
        pltpu.make_async_copy(
            packed.at[core], partial_ref.at[:, :, pl.ds(0, early)], local_sem.at[0]
        ),
        pltpu.make_async_copy(
            enc_parts.at[:, pl.ds(pl.multiple_of(core * tp * share, share), tp * share)],
            enc_own,
            local_sem.at[1],
        ),
    ]
    first = len(local)
    for f in range(fsdp):
        for c in range(cores):
            for t in range(tp):
                head = t * cores + c
                local.append(
                    pltpu.make_async_copy(
                        gathered.at[f, c, t, pl.ds(KEY, 2)],
                        pair_weights.at[
                            :, pl.ds(head * HEAD_DIM, HEAD_DIM), pl.ds(f * piece, piece)
                        ],
                        local_sem.at[first + (f * cores + c) * tp + t],
                    )
                )
    enc_copy = send_to(
        enc_parts.at[:, pl.ds(pl.multiple_of((1 - core) * tp * share, share), tp * share)],
        enc_core,
        e_send.at[0],
        e_recv.at[0],
        ctx=1 - core,
    )
    enc_line = [
        send_to(
            enc_sum.at[chip ^ n], enc_landing.at[n - 1], e_send.at[n], e_recv.at[n], tp=chip ^ n
        )
        for n in range(1, tp)
    ]

    core_copy = send_to(
        packed.at[1 - core], core_landing, r_send.at[0], r_recv.at[0], ctx=1 - core
    )
    pair_copy = send_to(
        pair_ref.at[1 - core], pair_landing, r_send.at[1], r_recv.at[1], ctx=1 - core
    )
    shard_copy = send_to(
        shard_ref.at[core], shard_ref.at[core], r_send.at[2], r_recv.at[2], ctx=1 - core
    )
    shard_wait = send_to(
        shard_ref.at[1 - core], shard_ref.at[1 - core], r_send.at[2], r_recv.at[2], ctx=1 - core
    )
    f_copies = [
        send_to(
            partial_ref.at[here ^ n, :, pl.ds(0, early)],
            fsdp_landing.at[n - 1, :, pl.ds(0, early)],
            f_send.at[n],
            f_recv.at[n],
            fsdp=here ^ n,
        )
        for n in range(1, fsdp)
    ]
    f_pairs = [
        send_to(
            partial_ref.at[here ^ n, :, pl.ds(early, 2)],
            fsdp_landing.at[n - 1, :, pl.ds(early, 2)],
            f_send.at[fsdp + n],
            f_recv.at[fsdp + n],
            fsdp=here ^ n,
        )
        for n in range(1, fsdp)
    ]
    t_copies = [
        send_to(line_ref.at[chip ^ k], line_landing.at[k - 1], t_send.at[k], t_recv.at[k], tp=chip ^ k)
        for k in range(1, tp)
    ]
    h_copies = [
        send_to(
            head_ref.at[here ^ k], head_landing.at[k - 1], h_send.at[k], h_recv.at[k], fsdp=here ^ k
        )
        for k in range(1, fsdp)
    ]

    pair_chip = 2 * (chip % 2) + core
    p_copies = [
        send_to(head_pair, head_two.at[mine], p_send.at[c], p_recv.at[mine], ctx=c, tp=pair_chip)
        for c in range(2)
    ]
    p_waits = [
        send_to(head_pair, head_two.at[n], p_send.at[0], p_recv.at[n], ctx=c, tp=t)
        for n, c, t in ((0, chip % 2, chip // 2), (1, chip % 2, chip // 2 + 2))
    ]
    p_here = [
        (core == chip % 2) & (chip == chip // 2 + 2 * n) for n in range(2)
    ]

    def s_copy(k):
        return send_to(
            sums_ref, sums_landing.at[k], s_send.at[k], s_recv.at[k], **member(me ^ k)
        )

    s_fsdp = [
        send_to(
            sums_two, sums_landing.at[group + k], s_send.at[group + k], s_recv.at[group + k], fsdp=here ^ k
        )
        for k in range(1, fsdp)
    ]

    enc_copy.start()
    core_copy.start()
    for copy in local:
        copy.start()

    def core_rows_copy(place):
        slot = place % tp
        return send_to(
            core_rows.at[slot], core_rows_landing.at[slot], x_send.at[slot], x_recv.at[slot], ctx=1 - core
        )

    def owner_copy(place):
        slot = place % tp
        return send_to(
            sum_rows.at[slot],
            incoming.at[mine, chip % 2],
            i_send.at[slot],
            i_recv.at[mine, chip % 2],
            tp=slot,
        )

    def spread(place):
        upstream = dot_of(outgoing[place].reshape(6 * HEAD_DIM, chunk), weight[...], 0, 0)
        slot = place % tp

        @pl.when(place // tp != core)
        def hand_over():
            core_rows[slot] = low(upstream)
            core_rows_copy(place).start()

        @pl.when(place // tp == core)
        def collect():
            core_rows_copy(place).wait_recv()
            total = low(upstream + core_rows_landing[slot].astype(jnp.float32))

            @pl.when(place == me)
            def own():
                incoming[mine, chip % 2] = total

            @pl.when(place != me)
            def send():
                sum_rows[slot] = total

                @pl.when((core == 0) & (slot // 2 != mine) & jnp.logical_not(inner))
                def to_inner():
                    beside_copy(slot).start()

                @pl.when((core == 1) | (slot // 2 == mine))
                def to_owner():
                    owner_copy(place).start()

    def beside_copy(slot):
        return send_to(
            sum_rows.at[slot], beside.at[slot % 2], i_send.at[slot], b_recv.at[slot % 2], tp=chip ^ 1
        )

    def pass_rows():
        for n in range(2):
            slot = 2 * (1 - mine) + n
            beside_copy(slot).wait_recv()
            sum_rows[slot] = low(
                sum_rows[slot].astype(jnp.float32) + beside[n].astype(jnp.float32)
            )
            owner_copy(slot).start()

    def prepare(seq):
        def lay(place, unused):
            at = pl.ds(pl.multiple_of(place * chunk, chunk), chunk)
            grads = landing[seq, place]
            blank = jnp.zeros_like(grads)
            grad_ref[seq, at, :] = jnp.concatenate([blank, grads], 0).T
            delta_ref[seq, :, at] = jnp.sum(
                grads.astype(jnp.float32) * wide_ref[seq, :, at], axis=0, keepdims=True
            )
            queries_ref[seq, at, :] = jnp.concatenate([qkv_ref[seq, :HEAD_DIM, at], blank], 0).T
            pairs_ref[seq, at, :] = qkv_ref[seq, HEAD_DIM:, at].T
            return unused

        lax.fori_loop(0, group, lay, 0)
        grad_pairs_ref[seq] = jnp.zeros(grad_pairs_ref.shape[1:], jnp.float32)

    def encoder_cores():
        local[1].wait()
        enc_copy.wait_recv()
        for t in range(tp):
            lines = slice(t * share, (t + 1) * share)
            enc_sum[t] = low(
                enc_own[:, lines].astype(jnp.float32) + enc_core[:, lines].astype(jnp.float32)
            )
        for copy in enc_line:
            copy.start()

    def encoder_part():
        total = enc_sum[chip].astype(jnp.float32)
        for n, copy in enumerate(enc_line):
            copy.wait_recv()
            total = total + enc_landing[n].astype(jnp.float32)
        for copy in local[first:]:
            copy.wait()
        grads = low(total)
        enc_rows = enc_ref[:, pl.ds(pl.multiple_of(me * share, share), share), :]
        flat, enc_flat = grads.reshape(batches * share, 2 * width), enc_rows.reshape(
            batches * share, width
        )
        result = dot_of(flat[:, :width], pair_weights[0], 1, 0) + dot_of(
            flat[:, width:], pair_weights[1], 1, 0
        )
        enc_out[...] = result.reshape(batches, share, width)
        for which in range(2):
            grad = low(dot_of(flat[:, which * width : (which + 1) * width], enc_flat, 0, 0))
            for f in range(fsdp):
                for c in range(cores):
                    for t in range(tp):
                        head = t * cores + c
                        pair_ref[c, f, t, which] = grad[
                            head * HEAD_DIM : (head + 1) * HEAD_DIM, f * piece : (f + 1) * piece
                        ]
        pair_copy.start()

    def sum_cores():
        local[0].wait()
        core_copy.wait_recv()

        def one(f, unused):
            def two(t, unused):
                partial_ref[f, t, :early] = low(
                    partial_ref[f, t, :early].astype(jnp.float32)
                    + core_landing[f, t].astype(jnp.float32)
                )
                return unused

            return lax.fori_loop(0, tp, two, unused)

        lax.fori_loop(0, fsdp, one, 0)
        for copy in f_copies:
            copy.start()

    def sum_pairs():
        pair_copy.wait_recv()
        for f in range(fsdp):
            for t in range(tp):
                partial_ref[f, t, early:] = low(
                    pair_ref[core, f, t].astype(jnp.float32)
                    + pair_landing[f, t].astype(jnp.float32)
                )
        for copy in f_pairs:
            copy.start()

    def sum_fsdp():
        for copy in f_copies + f_pairs:
            copy.wait_recv()

        def one(t, unused):
            total = partial_ref[here, t].astype(jnp.float32)
            for k in range(fsdp - 1):
                total = total + fsdp_landing[k, t].astype(jnp.float32)
            line_ref[t] = low(total)
            return unused

        lax.fori_loop(0, tp, one, 0)
        for copy in t_copies:
            copy.start()

    def sum_line():
        for copy in t_copies:
            copy.wait_recv()
        total = line_ref[chip].astype(jnp.float32)
        for k in range(tp - 1):
            total = total + line_landing[k].astype(jnp.float32)
        shard_ref[core] = total
        shard_copy.start()

    for head in range(2):
        prepare(head)

    def attend(index, unused):
        block, seq = blocks - 1 - index // 2, index % 2

        def hook(at, work):
            @pl.when(index == at)
            def run():
                work()

        hook(1, encoder_cores)
        hook(1, sum_cores)
        hook(2, encoder_part)
        hook(3, sum_pairs)
        hook(4, sum_fsdp)
        start = pl.multiple_of(block * span, span)
        at = pl.ds(start, span)
        blank = jnp.zeros((HEAD_DIM, span), jnp.bfloat16)
        queries_t = jnp.concatenate([qkv_ref[seq, :HEAD_DIM, at], blank], 0)
        queries = queries_ref[seq, at, :]
        grads = grad_ref[seq, at, :]
        grads_t = jnp.concatenate(
            [landing[seq, block * ratio + part] for part in range(ratio)], 1
        )
        grads_t = jnp.concatenate([blank, grads_t], 0)
        logs, deltas = log_ref[seq, :, at], delta_ref[seq, :, at]
        limit = jnp.maximum(
            prefix_ref[mine], start + 1 + lax.broadcasted_iota(jnp.int32, (1, span), 1)
        )

        def advance(offset, count, grad_queries, columns=None):
            first = 0 if columns is None else columns
            there = pl.ds(offset, count)
            pairs = pairs_ref[seq, there, :]
            scores = dot_of(pairs, queries_t[:, first:], 1, 0)
            if columns is not None:
                scores = hide(scores, limit[:, first:], offset)
            probs = jnp.exp(scores - logs[:, first:])
            grad_probs = dot_of(pairs, grads_t[:, first:], 1, 0)
            grad_scores = low(probs * (grad_probs - deltas[:, first:]))
            grad_pairs_ref[seq, there, :] += dot_of(low(probs), grads[first:], 1, 0) + dot_of(
                grad_scores, queries[first:], 1, 0
            )
            return grad_queries + dot_of(
                qkv_ref[seq, HEAD_DIM : 2 * HEAD_DIM, there], grad_scores, 1, 0
            )

        def whole_step(other, total):
            return advance(pl.multiple_of(other * span, span), span, total)

        def masked_step(other, total):
            return advance(pl.multiple_of(other * span, span), span, total, 0)

        def diagonal_step(other, total):
            half = span // 2
            total = advance(start, half, total, 0)
            offset = pl.multiple_of(start + half, half)
            upper = advance(offset, half, total[:, half:], half)
            return jnp.concatenate([total[:, :half], upper], 1)

        grad_queries = jnp.zeros((HEAD_DIM, span), jnp.float32)
        grad_queries = lax.fori_loop(0, block, whole_step, grad_queries)
        grad_queries = lax.fori_loop(block, wide_blocks, masked_step, grad_queries)
        grad_queries = lax.fori_loop(
            0, jnp.where(block >= wide_blocks, 1, 0), diagonal_step, grad_queries
        )
        done = low(grad_queries * factor)
        for part in range(ratio):
            place = block * ratio + part
            outgoing[place, seq, :HEAD_DIM, :] = done[:, part * chunk : (part + 1) * chunk]

        lowest = jnp.where(block == 0, 0, block)
        highest = jnp.where(
            block == 0, wide_blocks, jnp.where(block >= wide_blocks, block + 1, block)
        )

        def give(place, unused):
            at = pl.ds(pl.multiple_of(place * chunk, chunk), chunk)
            outgoing[place, seq, HEAD_DIM:, :] = low(grad_pairs_ref[seq, at, :].T)
            return unused

        lax.fori_loop(lowest * ratio, highest * ratio, give, 0)

        @pl.when(seq == 1)
        def both_heads():
            def one(place, unused):
                spread(place)
                return unused

            lax.fori_loop(lowest * ratio, highest * ratio, one, 0)

        return unused

    lax.fori_loop(0, 2 * blocks, attend, 0)

    sums_ref[...] = jnp.zeros_like(sums_ref)
    sums_ref[:8, :] = stats_ref[...]

    def rows_copy(number):
        return pltpu.make_async_copy(
            rows_in.at[number],
            rows_ref.at[number % rows_ref.shape[0]],
            rows_sem.at[number % rows_ref.shape[0]],
        )

    depth = rows_ref.shape[0]
    for number in range(depth):
        rows_copy(number).start()

    ones = jnp.ones((chunk, piece), jnp.bfloat16)

    def weigh(number, totals):
        rows_copy(number).wait()
        grads = outgoing[number].reshape(6 * HEAD_DIM, chunk)
        total = totals[0] + dot_of(grads, rows_ref[number % depth], 1, 0)

        @pl.when(number + depth < group)
        def more():
            rows_copy(number + depth).start()

        return total, totals[1] + dot_of(grads, ones, 1, 0)

    total, plain = lax.fori_loop(
        0,
        group,
        weigh,
        (
            jnp.zeros((6 * HEAD_DIM, width), jnp.float32),
            jnp.zeros((6 * HEAD_DIM, piece), jnp.float32),
        ),
    )
    token_copies = [
        pltpu.make_async_copy(tokens_ref.at[n], rows_ref.at[n], rows_sem.at[n])
        for n in range(batches)
    ]
    for copy in token_copies:
        copy.start()
    weights = weight[...].astype(jnp.float32)
    bias_sum = jnp.sum(weights * jnp.concatenate([plain] * (width // piece), 1), 0, keepdims=True)
    gain_sum = jnp.sum(weights * total, 0, keepdims=True) - bias_ref[0:1] * bias_sum
    sums_ref[8:9, :] = gain_sum / gain_ref[0:1]
    sums_ref[9:10, :] = bias_sum

    def start_sums(k, unused):
        s_copy(k).start()
        return unused

    lax.fori_loop(1, group, start_sums, 0)
    for f in range(fsdp):
        head_ref[f] = total[:, f * piece : (f + 1) * piece]
    for copy in h_copies:
        copy.start()

    @pl.when((core == 0) & inner)
    def last_rows():
        pass_rows()

    sum_line()

    for copy in h_copies:
        copy.wait_recv()
    total = head_ref[here]
    for k in range(fsdp - 1):
        total = total + head_landing[k]
    head_pair[...] = low(total)
    for c in range(2):
        there = (core == c) & (pair_chip == chip)

        @pl.when(there)
        def stay():
            head_two[mine] = head_pair[...]

        @pl.when(jnp.logical_not(there))
        def leave(c=c):
            p_copies[c].start()

    def arrive_sums(k, total):
        s_copy(k).wait_recv()
        return total + sums_landing[k]

    sums_two[...] = lax.fori_loop(1, group, arrive_sums, sums_ref[...])
    for copy in s_fsdp:
        copy.start()

    for copy in token_copies:
        copy.wait()

    def finish(seq, unused):
        for number in range(2):
            source = 2 * seq + number

            passed = (core == 0) & (seq != mine)

            @pl.when(passed & ((source == 0) | (source == 3)))
            def nothing(number=number):
                incoming[seq, number] = jnp.zeros((chunk, width), jnp.bfloat16)

            @pl.when((source != chip) & jnp.logical_not(passed & ((source == 0) | (source == 3))))
            def come(number=number, source=source):
                send_to(
                    incoming.at[seq, number],
                    incoming.at[seq, number],
                    i_send.at[0],
                    i_recv.at[seq, number],
                    tp=source,
                ).wait_recv()

        upstream = incoming[seq, 0].astype(jnp.float32) + incoming[seq, 1].astype(jnp.float32)
        start_sum = rows_ref[seq].astype(jnp.float32) + step_ref[seq]
        unit_rows, inverse = in_strips(rows_unit, start_sum)
        input_ref[seq] = after_ref[seq] + rows_back(
            upstream, unit_rows, inverse, gain_ref[0:1]
        )[0]
        return unused

    lax.fori_loop(0, batches, finish, 0)

    shard_wait.wait_recv()

    def whole(block):
        return jnp.concatenate([shard_ref[0, block], shard_ref[1, block]], 0)

    query_out[...] = whole(0).T
    back_out[...] = whole(1)
    cross_out[...] = whole(2)
    for part in range(4):
        up_out[:, part * piece : (part + 1) * piece] = whole(3 + part).T
        down_out[part * piece : (part + 1) * piece, :] = whole(7 + part)
    pair_out[0] = whole(11).T
    pair_out[1] = whole(12).T
    for n in range(2):

        @pl.when(jnp.logical_not(p_here[n]))
        def pair_come(n=n):
            p_waits[n].wait_recv()

    total = head_two[0].astype(jnp.float32) + head_two[1].astype(jnp.float32)
    for which in range(3):
        self_out[which] = jnp.concatenate(
            [
                total[(3 * n + which) * HEAD_DIM : (3 * n + which + 1) * HEAD_DIM]
                for n in range(2)
            ],
            0,
        ).T
    total = sums_two[...]
    for k, copy in enumerate(s_fsdp):
        copy.wait_recv()
        total = total + sums_landing[group + 1 + k]
    sums_out[...] = total
    core_copy.wait_send()
    pair_copy.wait_send()
    shard_copy.wait_send()
    for c in range(2):

        @pl.when(jnp.logical_not((core == c) & (pair_chip == chip)))
        def pair_sent(c=c):
            p_copies[c].wait_send()

    enc_copy.wait_send()
    for copy in enc_line + f_copies + f_pairs + t_copies + h_copies + s_fsdp:
        copy.wait_send()

    def sent(k, unused):
        s_copy(k).wait_send()
        return unused

    lax.fori_loop(1, group, sent, 0)

    def rows_sent(slot, unused):
        core_rows_copy((1 - core) * tp + slot).wait_send()

        @pl.when(slot != chip)
        def left():
            owner_copy(core * tp + slot).wait_send()

        return unused

    lax.fori_loop(0, tp, rows_sent, 0)


def backward_group(
    prefix,
    enc_parts,
    packed,
    gathered,
    rows,
    returned,
    weight,
    qkv,
    wide,
    logs,
    tokens,
    steps,
    gain,
    bias,
    after,
    encoder,
    stats,
    span,
    tp,
    fsdp,
):
    batches, chunk, width = tokens.shape
    group = returned.shape[1]
    length = group * chunk
    share = encoder.shape[1] // group
    piece = width // fsdp
    count = packed.shape[3]
    tail = packed.shape[4:]
    bf16, f32 = jnp.bfloat16, jnp.float32
    struct = jax.ShapeDtypeStruct
    inside = pl.BlockSpec(memory_space=pltpu.VMEM)
    outside = pl.BlockSpec(memory_space=pl.ANY)
    dma = pltpu.SemaphoreType.DMA
    vmem = pltpu.VMEM
    parts = group * fsdp
    return pl.pallas_call(
        functools.partial(backward_kernel, span=span, tp=tp, fsdp=fsdp),
        in_specs=[pl.BlockSpec(memory_space=pltpu.SMEM)] + [outside] * 4 + [inside] * 5 + [outside] + [inside] * 6,
        out_specs=[inside] * 10,
        out_shape=[
            struct((batches, chunk, width), f32),
            struct((batches, share, width), f32),
            struct((3, piece, piece), f32),
            struct((piece, piece), f32),
            struct((2, piece, piece), f32),
            struct((piece, piece), f32),
            struct((piece, piece), f32),
            struct((piece, width), f32),
            struct((width, piece), f32),
            struct((16, width), f32),
        ],
        scratch_shapes=[
            vmem((group, 2, 3 * HEAD_DIM, chunk), bf16),
            vmem((tp, chunk, width), bf16),
            vmem((tp, chunk, width), bf16),
            vmem((tp, chunk, width), bf16),
            vmem((2, chunk, width), bf16),
            vmem((batches, 2, chunk, width), bf16),
            vmem((2, length, 2 * HEAD_DIM), bf16),
            vmem((2, length, 2 * HEAD_DIM), bf16),
            vmem((2, length, 2 * HEAD_DIM), bf16),
            vmem((2, 1, length), f32),
            vmem((2, length, 2 * HEAD_DIM), f32),
            vmem((2, chunk, width), bf16),
            vmem((2, width, width), bf16),
            vmem((batches, tp * share, 2 * width), bf16),
            vmem((batches, tp * share, 2 * width), bf16),
            vmem((tp, batches, share, 2 * width), bf16),
            vmem((tp - 1, batches, share, 2 * width), bf16),
            vmem((group // tp, fsdp, tp, 2) + tail, bf16),
            vmem((fsdp, tp, 2) + tail, bf16),
            vmem((fsdp, tp, count) + tail, bf16),
            vmem((fsdp, tp, count + 2) + tail, bf16),
            vmem((fsdp - 1, tp, count + 2) + tail, bf16),
            vmem((tp, count + 2) + tail, bf16),
            vmem((tp - 1, count + 2) + tail, bf16),
            vmem((2, count + 2) + tail, f32),
            vmem((fsdp, 6 * HEAD_DIM, piece), f32),
            vmem((fsdp - 1, 6 * HEAD_DIM, piece), f32),
            vmem((6 * HEAD_DIM, piece), bf16),
            vmem((2, 6 * HEAD_DIM, piece), bf16),
            vmem((16, width), f32),
            vmem((group + fsdp, 16, width), f32),
            vmem((16, width), f32),
            dma((tp,)),
            dma((tp,)),
            dma((tp,)),
            dma((tp,)),
            dma((tp,)),
            dma((batches, 2)),
            dma((2,)),
            dma((4,)),
            dma((4,)),
            dma((2 * fsdp,)),
            dma((2 * fsdp,)),
            dma((tp,)),
            dma((tp,)),
            dma((fsdp,)),
            dma((fsdp,)),
            dma((2,)),
            dma((2,)),
            dma((group + fsdp,)),
            dma((group + fsdp,)),
            dma((2 + parts,)),
            dma((2,)),
        ],
        compiler_params=pltpu.CompilerParams(
            vmem_limit_bytes=VMEM_LIMIT, collective_id=2, has_side_effects=True
        ),
        cost_estimate=pl.CostEstimate(
            flops=100_000_000_000, bytes_accessed=40_000_000, transcendentals=20_000_000
        ),
        name="backward_group",
    )(
        prefix,
        enc_parts,
        packed,
        gathered,
        rows,
        returned,
        weight,
        qkv,
        wide,
        logs,
        tokens,
        steps,
        gain,
        bias,
        after,
        encoder,
        stats,
    )


def pack_kernel(
    scalars,
    table_ref,
    qkv_ref,
    query_ref,
    pair_ref,
    self_ref,
    cross_ref,
    up_ref,
    down_ref,
    half_ref,
    mine_ref,
    steps_ref,
    blocks,
):
    piece = query_ref.shape[0]
    blocks[0] = query_ref[...].T
    for n in range(2):
        blocks[1 + n] = pair_ref[n].T
    blocks[3] = self_ref[...]
    blocks[4] = cross_ref[...]
    for n in range(4):
        blocks[5 + n] = up_ref[:, n * piece : (n + 1) * piece].T
        blocks[9 + n] = down_ref[n * piece : (n + 1) * piece, :]
    half = piece // 2
    core = lax.axis_index("ctx")
    half_ref[...] = blocks[:, pl.ds(pl.multiple_of(core * half, half), half), :]
    for which in range(3):
        flipped = qkv_ref[which].T
        for head in range(2):
            mine_ref[(3 * head + which) * HEAD_DIM : (3 * head + which + 1) * HEAD_DIM, :] = (
                flipped[head * HEAD_DIM : (head + 1) * HEAD_DIM]
            )
    table = table_ref[...].astype(jnp.float32)
    rows = lax.broadcasted_iota(jnp.int32, table.shape, 0)
    for seq in range(steps_ref.shape[0]):
        chosen = jnp.where(rows == scalars[seq], table, 0.0)
        steps_ref[seq] = jnp.sum(chosen, 0, keepdims=True)


def pack_weights(scalars, table, self_qkv, cross_q, cross_kv, self_out, cross_out, up, down):
    piece = cross_q.shape[0]
    width = table.shape[1]
    batches = scalars.shape[0]
    bf16 = jnp.bfloat16
    struct = jax.ShapeDtypeStruct
    inside = pl.BlockSpec(memory_space=pltpu.VMEM)
    return pl.pallas_call(
        pack_kernel,
        in_specs=[pl.BlockSpec(memory_space=pltpu.SMEM)] + [inside] * 8,
        out_specs=[inside] * 3,
        out_shape=[
            struct((13, piece // 2, piece), bf16),
            struct((3 * piece, piece), bf16),
            struct((batches, 1, width), jnp.float32),
        ],
        scratch_shapes=[pltpu.VMEM((13, piece, piece), bf16)],
        name="pack_weights",
    )(scalars, table, self_qkv, cross_q, cross_kv, self_out, cross_out, up, down)


def collect_kernel(*refs, large, small, entries):
    ins, outs = refs[: large + small + 1], refs[large + small + 1 :]
    for n in range(large):
        outs[n][...] = ins[n][...]

    @pl.when(pl.program_id(0) == 0)
    def once():
        for n in range(large, large + small):
            outs[n][...] = ins[n][...]
        sums = ins[large + small]
        gain_ref, bias_ref, feed_ref, norms_ref = outs[large + small :]
        for n, row in enumerate((8, 4, 6)):
            gain_ref[n : n + 1, :] = sums[row : row + 1, :]
        for n, row in enumerate((9, 5)):
            bias_ref[n : n + 1, :] = sums[row : row + 1, :]
        feed_ref[...] = sums[7:8, :]
        totals = jnp.sum(sums[0:4, :], 1, keepdims=True) * (1.0 / entries)
        one = lax.broadcasted_iota(jnp.int32, (4, 128), 0) == lax.broadcasted_iota(
            jnp.int32, (4, 128), 1
        )
        norms_ref[...] = jnp.sqrt(jnp.sum(jnp.where(one, totals, 0.0), 0, keepdims=True))[:, :4]


def collect(large, small, sums, entries):
    width = sums.shape[1]
    f32 = jnp.float32
    struct = jax.ShapeDtypeStruct
    rest = [struct(v.shape, v.dtype) for v in small]
    extra = [struct((3, width), f32), struct((2, width), f32), struct((1, width), f32)]
    extra = extra + [struct((1, 4), f32)]
    still = lambda v: pl.BlockSpec(v.shape, lambda i, rank=len(v.shape): (0,) * rank)
    steps = 2
    moving = lambda v: pl.BlockSpec(
        (1, v.shape[0] * v.shape[1] // steps, v.shape[2]),
        lambda i, per=steps // v.shape[0]: (i // per, i % per, 0),
    )
    return pl.pallas_call(
        functools.partial(collect_kernel, large=len(large), small=len(small), entries=entries),
        grid=(steps,),
        in_specs=[moving(v) for v in large] + [still(v) for v in small] + [still(sums)],
        out_specs=[moving(v) for v in large] + [still(v) for v in rest + extra],
        out_shape=[struct(v.shape, v.dtype) for v in large] + rest + extra,
        name="collect",
    )(*large, *small, sums)


def local_heads(
    tokens,
    timesteps,
    time_table,
    prefix,
    encoder,
    self_qkv,
    cross_q,
    cross_kv,
    self_out,
    cross_out,
    ffn_up,
    ffn_down,
    norm_gain,
    norm_bias,
    cotangent,
):
    batches, chunk, width = tokens.shape
    group = 8
    length = group * chunk
    span = 1024
    own_half, mine, embedded = pack_weights(
        timesteps,
        time_table,
        self_qkv,
        cross_q,
        cross_kv,
        self_out,
        cross_out,
        ffn_up,
        ffn_down,
    )
    gathered = lax.all_gather(own_half, "tp", axis=0, tiled=False)
    gathered = lax.all_gather(gathered, ("fsdp", "ctx"), axis=0, tiled=False)
    gathered = gathered.reshape((4, 2, 4) + own_half.shape)
    rows, qkv, wide, logs, contexts, weight = forward_group(
        prefix, tokens, embedded, norm_gain, norm_bias, mine, span, group, 4, 4
    )
    final, grad_after, returned, enc_parts, stats, packed = middle(
        gathered,
        tokens,
        embedded,
        encoder,
        cotangent,
        norm_gain,
        norm_bias,
        contexts,
        4,
        4,
    )
    outs = backward_group(
        prefix,
        enc_parts,
        packed,
        gathered,
        rows,
        returned,
        weight,
        qkv,
        wide,
        logs,
        tokens,
        embedded,
        norm_gain,
        norm_bias,
        grad_after,
        encoder,
        stats,
        span,
        4,
        4,
    )
    sums = outs[9]
    entries = (
        tokens.shape[0]
        * tokens.shape[1]
        * tokens.shape[2]
        * lax.axis_size("fsdp")
        * lax.axis_size("ctx")
        * lax.axis_size("tp")
    )
    results = collect((final, *outs[:2]), outs[2:9], sums, entries)
    return (*results[:12], results[12].reshape(width), results[13].reshape(4))


def solution(mesh):
    placed = (
        P("fsdp", ("ctx", "tp"), None),
        P("fsdp"),
        P(),
        P("fsdp"),
        P("fsdp", None, None),
        P(None, "fsdp", "tp"),
        P("fsdp", "tp"),
        P(None, "fsdp", "tp"),
        P("tp", "fsdp"),
        P("tp", "fsdp"),
        P("fsdp", "tp"),
        P("tp", "fsdp"),
        P(),
        P(),
        P("fsdp", ("ctx", "tp"), None),
    )
    heads_fit = dict(mesh.shape) == {"fsdp": 4, "ctx": 2, "tp": 4}
    return jax.shard_map(
        local_heads if heads_fit else local,
        mesh=mesh,
        in_specs=placed,
        out_specs=(
            P("fsdp", ("ctx", "tp"), None),
            P("fsdp", ("ctx", "tp"), None),
            P("fsdp", ("ctx", "tp"), None),
            P(None, "fsdp", "tp"),
            P("fsdp", "tp"),
            P(None, "fsdp", "tp"),
            P("tp", "fsdp"),
            P("tp", "fsdp"),
            P("fsdp", "tp"),
            P("tp", "fsdp"),
            P(),
            P(),
            P(),
            P(),
        ),
        check_vma=False,
    )
```

```python
import functools
import math

import jax
import jax.numpy as jnp
from jax import lax
from jax.experimental import pallas as pl
from jax.experimental.pallas import tpu as pltpu
from jax.sharding import PartitionSpec as P

HEAD_DIM = 64


EPS = 1e-05
NEG = -1e30
ROOT_HALF = 1.0 / math.sqrt(2.0)
INV_ROOT_TWO_PI = 1.0 / math.sqrt(2.0 * math.pi)
VMEM_LIMIT = 63 * 2**20


def norm_rows(hidden, scaling, offsets):
    centre = hidden - jnp.mean(hidden, -1, keepdims=True)
    inverse = lax.rsqrt(jnp.mean(centre * centre, -1, keepdims=True) + EPS)
    unit_rows = centre * inverse
    return (unit_rows * scaling + offsets, unit_rows, inverse)


def norm_back(upstream, unit_rows, inverse, scaling):
    scaled = upstream * scaling
    result = inverse * (
        scaled
        - jnp.mean(scaled, -1, keepdims=True)
        - unit_rows * jnp.mean(scaled * unit_rows, -1, keepdims=True)
    )
    return (result, jnp.sum(upstream * unit_rows, (0, 1)), jnp.sum(upstream, (0, 1)))


def gelu_parts(inputs):
    normal_cdf = 0.5 * (1.0 + lax.erf(inputs * ROOT_HALF))
    return (
        inputs * normal_cdf,
        normal_cdf + inputs * jnp.exp(-0.5 * inputs * inputs) * INV_ROOT_TWO_PI,
    )


def spread_rows(rows):
    return lax.all_gather(rows, "tp", axis=1, tiled=True)


def spread_grads(grad_rows):
    return lax.all_gather(grad_rows, "tp", axis=1, tiled=True)


def finish_branch(local_in, local_weight):
    return lax.psum_scatter(
        jnp.einsum("scw,wd->scd", local_in, local_weight, preferred_element_type=jnp.float32),
        "tp",
        scatter_dimension=1,
        tiled=True,
    )


def finish_grad(local_grad, local_weight):
    return lax.psum_scatter(
        jnp.einsum("scw,dw->scd", local_grad, local_weight, preferred_element_type=jnp.float32),
        "tp",
        scatter_dimension=1,
        tiled=True,
    )


def block_scores(queries, key_block, query_pos, key_pos, lengths, factor):
    scores = (
        jnp.einsum("sqhe,skhe->sqhk", queries, key_block, preferred_element_type=jnp.float32)
        * factor
    )
    visible = (key_pos[None, None, :] <= query_pos[None, :, None]) | (
        key_pos[None, None, :] < lengths[:, None, None]
    )
    return jnp.where(visible[:, :, None, :], scores, NEG)


def attend_forward(queries, key_rows, value_rows, query_pos, lengths, key_span, factor):
    length = key_rows.shape[1]

    def attend_advance(running, offset):
        highest, totals, summed = running
        key_block = lax.dynamic_slice_in_dim(key_rows, offset, key_span, 1)
        value_block = lax.dynamic_slice_in_dim(value_rows, offset, key_span, 1)
        scores = block_scores(
            queries, key_block, query_pos, offset + lax.iota(jnp.int32, key_span), lengths, factor
        )
        new_high = jnp.maximum(highest, jnp.max(scores, -1))
        weights = jnp.exp(scores - new_high[..., None])
        fading = jnp.exp(highest - new_high)
        totals = totals * fading + jnp.sum(weights, -1)
        summed = summed * fading[..., None] + jnp.einsum(
            "sqhk,skhe->sqhe",
            weights.astype(jnp.bfloat16),
            value_block,
            preferred_element_type=jnp.float32,
        )
        return ((new_high, totals, summed), None)

    stat_shape = queries.shape[:3]
    initial = (
        jnp.full(stat_shape, NEG, jnp.float32),
        jnp.zeros(stat_shape, jnp.float32),
        jnp.zeros(queries.shape, jnp.float32),
    )
    offsets = jnp.arange(length // key_span, dtype=jnp.int32) * key_span
    (highest, totals, summed), unused = lax.scan(attend_advance, initial, offsets)
    return (summed / totals[..., None], highest + jnp.log(totals))


def attend_block(
    queries,
    grad_out,
    log_rows,
    delta_rows,
    key_block,
    value_block,
    query_pos,
    key_pos,
    lengths,
    factor,
):
    scores = block_scores(queries, key_block, query_pos, key_pos, lengths, factor)
    probs = jnp.exp(scores - log_rows[..., None])
    grad_probs = jnp.einsum(
        "sqhe,skhe->sqhk", grad_out, value_block, preferred_element_type=jnp.float32
    )
    grad_scores = (probs * (grad_probs - delta_rows[..., None])).astype(jnp.bfloat16)
    return (probs.astype(jnp.bfloat16), grad_scores)


def key_sweep(
    queries,
    grad_out,
    log_rows,
    delta_rows,
    key_rows,
    value_rows,
    query_pos,
    lengths,
    key_span,
    factor,
):
    batches, row_count, head_count, head_depth = queries.shape
    length = key_rows.shape[1]

    def key_advance(grad_query, offset):
        key_block = lax.dynamic_slice_in_dim(key_rows, offset, key_span, 1)
        value_block = lax.dynamic_slice_in_dim(value_rows, offset, key_span, 1)
        key_pos = offset + lax.iota(jnp.int32, key_span)
        probs_low, grad_scores = attend_block(
            queries,
            grad_out,
            log_rows,
            delta_rows,
            key_block,
            value_block,
            query_pos,
            key_pos,
            lengths,
            factor,
        )
        grad_query = (
            grad_query
            + jnp.einsum(
                "sqhk,skhe->sqhe", grad_scores, key_block, preferred_element_type=jnp.float32
            )
            * factor
        )
        grad_key = (
            jnp.einsum("sqhk,sqhe->kshe", grad_scores, queries, preferred_element_type=jnp.float32)
            * factor
        )
        grad_value = jnp.einsum(
            "sqhk,sqhe->kshe", probs_low, grad_out, preferred_element_type=jnp.float32
        )
        return (grad_query, (grad_key, grad_value))

    offsets = jnp.arange(length // key_span, dtype=jnp.int32) * key_span
    grad_query, stacked = lax.scan(key_advance, jnp.zeros(queries.shape, jnp.float32), offsets)
    flat_shape = (length, batches, head_count * head_depth)
    return (grad_query, stacked[0].reshape(flat_shape), stacked[1].reshape(flat_shape))


def local(
    tokens,
    timesteps,
    time_table,
    prefix,
    encoder,
    self_qkv,
    cross_q,
    cross_kv,
    self_out,
    cross_out,
    ffn_up,
    ffn_down,
    norm_gain,
    norm_bias,
    cotangent,
):
    proj_self, proj_query, proj_pair, back_self, back_cross, expand_full, shrink_full = (
        lax.all_gather(self_qkv, "fsdp", axis=1, tiled=True),
        lax.all_gather(cross_q, "fsdp", axis=0, tiled=True),
        lax.all_gather(cross_kv, "fsdp", axis=1, tiled=True),
        lax.all_gather(self_out, "fsdp", axis=1, tiled=True),
        lax.all_gather(cross_out, "fsdp", axis=1, tiled=True),
        lax.all_gather(ffn_up, "fsdp", axis=0, tiled=True),
        lax.all_gather(ffn_down, "fsdp", axis=1, tiled=True),
    )
    batches = tokens.shape[0]
    model_width = tokens.shape[2]
    local_width = proj_query.shape[1]
    head_count = local_width // HEAD_DIM
    factor = HEAD_DIM ** (-0.5)
    ctx_index = lax.axis_index("ctx")
    local_stack = jnp.transpose(proj_self, (1, 0, 2)).reshape(model_width, 3 * local_width)
    steps_onehot = (timesteps[:, None] == lax.iota(jnp.int32, time_table.shape[0])[None, :]).astype(
        jnp.bfloat16
    )
    embedded = jnp.dot(steps_onehot, time_table, preferred_element_type=jnp.float32)
    start_sum = tokens.astype(jnp.float32) + embedded[:, None, :]
    normed_one, unit_one, inverse_one = norm_rows(start_sum, norm_gain[0], norm_bias[0])
    rows_self = spread_rows(normed_one.astype(jnp.bfloat16))
    row_count = rows_self.shape[1]
    head_shape = (batches, row_count, head_count, HEAD_DIM)
    projected = jnp.einsum(
        "scd,kdw->kscw", rows_self, proj_self, preferred_element_type=jnp.float32
    ).astype(jnp.bfloat16)
    queries, key_local, value_local = (projected[0], projected[1], projected[2])
    key_all, value_all = (
        lax.all_gather(key_local, "ctx", axis=1, tiled=True),
        lax.all_gather(value_local, "ctx", axis=1, tiled=True),
    )
    length = key_all.shape[1]
    key_span = min(512, length)
    query_pos = ctx_index * row_count + lax.iota(jnp.int32, row_count)
    keys_four = key_all.reshape(batches, length, head_count, HEAD_DIM)
    values_four = value_all.reshape(batches, length, head_count, HEAD_DIM)
    queries_four = queries.reshape(head_shape)
    attended, log_total = attend_forward(
        queries_four, keys_four, values_four, query_pos, prefix, key_span, factor
    )
    context_one = attended.reshape(batches, row_count, local_width).astype(jnp.bfloat16)
    branch_one = finish_branch(context_one, back_self)
    after_one = start_sum + branch_one
    normed_two, unit_two, inverse_two = norm_rows(after_one, norm_gain[1], norm_bias[1])
    rows_cross = spread_rows(normed_two.astype(jnp.bfloat16))
    cross_queries = jnp.einsum(
        "scd,dw->scw", rows_cross, proj_query, preferred_element_type=jnp.float32
    ).astype(jnp.bfloat16)
    enc_pair = jnp.einsum(
        "sed,kdw->ksew", encoder, proj_pair, preferred_element_type=jnp.float32
    ).astype(jnp.bfloat16)
    enc_count = encoder.shape[1]
    cross_keys = enc_pair[0].reshape(batches, enc_count, head_count, HEAD_DIM)
    cross_values = enc_pair[1].reshape(batches, enc_count, head_count, HEAD_DIM)
    cross_four = cross_queries.reshape(head_shape)
    cross_probs = jax.nn.softmax(
        jnp.einsum("sqhe,skhe->sqhk", cross_four, cross_keys, preferred_element_type=jnp.float32)
        * factor,
        axis=-1,
    )
    cross_low = cross_probs.astype(jnp.bfloat16)
    context_two = (
        jnp.einsum("sqhk,skhe->sqhe", cross_low, cross_values, preferred_element_type=jnp.float32)
        .reshape(batches, row_count, local_width)
        .astype(jnp.bfloat16)
    )
    branch_two = finish_branch(context_two, back_cross)
    after_two = after_one + branch_two
    normed_three, unit_three, inverse_three = norm_rows(after_two, norm_gain[2], norm_bias[2])
    rows_ffn = spread_rows(normed_three.astype(jnp.bfloat16))
    pre_act = jnp.einsum("scd,df->scf", rows_ffn, expand_full, preferred_element_type=jnp.float32)
    activated, slopes = gelu_parts(pre_act)
    hidden_low = activated.astype(jnp.bfloat16)
    branch_three = finish_branch(hidden_low, shrink_full)
    final_sum = after_two + branch_three
    grad_three = spread_grads(cotangent)
    grad_shrink = jnp.einsum(
        "scf,scd->fd", hidden_low, grad_three, preferred_element_type=jnp.float32
    )
    grad_pre = (
        jnp.einsum("scd,fd->scf", grad_three, shrink_full, preferred_element_type=jnp.float32)
        * slopes
    ).astype(jnp.bfloat16)
    grad_expand = jnp.einsum("scd,scf->df", rows_ffn, grad_pre, preferred_element_type=jnp.float32)
    back_three, gain_three, shift_three = norm_back(
        finish_grad(grad_pre, expand_full), unit_three, inverse_three, norm_gain[2]
    )
    grad_after_two = cotangent.astype(jnp.float32) + back_three
    grad_two = spread_grads(grad_after_two.astype(jnp.bfloat16))
    grad_back_cross = jnp.einsum(
        "scw,scd->wd", context_two, grad_two, preferred_element_type=jnp.float32
    )
    grad_context_two = jnp.einsum(
        "scd,wd->scw", grad_two, back_cross, preferred_element_type=jnp.float32
    ).astype(jnp.bfloat16)
    grad_cross_four = grad_context_two.reshape(head_shape)
    grad_cross_probs = jnp.einsum(
        "sqhe,skhe->sqhk", grad_cross_four, cross_values, preferred_element_type=jnp.float32
    )
    grad_cross_scores = (
        cross_probs
        * (grad_cross_probs - jnp.sum(cross_probs * grad_cross_probs, -1, keepdims=True))
    ).astype(jnp.bfloat16)
    grad_cross_q = (
        (
            jnp.einsum(
                "sqhk,skhe->sqhe", grad_cross_scores, cross_keys, preferred_element_type=jnp.float32
            )
            * factor
        )
        .reshape(batches, row_count, local_width)
        .astype(jnp.bfloat16)
    )
    part_keys = (
        jnp.einsum(
            "sqhk,sqhe->skhe", grad_cross_scores, cross_four, preferred_element_type=jnp.float32
        )
        * factor
    ).reshape(batches, enc_count, local_width)
    part_values = jnp.einsum(
        "sqhk,sqhe->skhe", cross_low, grad_cross_four, preferred_element_type=jnp.float32
    ).reshape(batches, enc_count, local_width)
    enc_keys, enc_values = (
        lax.psum_scatter(part_keys, "ctx", scatter_dimension=1, tiled=True),
        lax.psum_scatter(part_values, "ctx", scatter_dimension=1, tiled=True),
    )
    enc_keys = enc_keys.astype(jnp.bfloat16)
    enc_values = enc_values.astype(jnp.bfloat16)
    enc_share = enc_keys.shape[1]
    enc_rows = lax.dynamic_slice_in_dim(encoder, ctx_index * enc_share, enc_share, 1)
    grad_pair = jnp.stack(
        [
            jnp.einsum("sed,sew->dw", enc_rows, enc_keys, preferred_element_type=jnp.float32),
            jnp.einsum("sed,sew->dw", enc_rows, enc_values, preferred_element_type=jnp.float32),
        ]
    )
    encoder_grad = lax.psum_scatter(
        jnp.einsum("sew,dw->sed", enc_keys, proj_pair[0], preferred_element_type=jnp.float32)
        + jnp.einsum("sew,dw->sed", enc_values, proj_pair[1], preferred_element_type=jnp.float32),
        "tp",
        scatter_dimension=1,
        tiled=True,
    )
    grad_query_proj = jnp.einsum(
        "scd,scw->dw", rows_cross, grad_cross_q, preferred_element_type=jnp.float32
    )
    back_two, gain_two, shift_two = norm_back(
        finish_grad(grad_cross_q, proj_query), unit_two, inverse_two, norm_gain[1]
    )
    grad_after_one = grad_after_two + back_two
    grad_one = spread_grads(grad_after_one.astype(jnp.bfloat16))
    grad_back_self = jnp.einsum(
        "scw,scd->wd", context_one, grad_one, preferred_element_type=jnp.float32
    )
    grad_context_one = jnp.einsum(
        "scd,wd->scw", grad_one, back_self, preferred_element_type=jnp.float32
    ).astype(jnp.bfloat16)
    grad_ctx_four = grad_context_one.reshape(head_shape)
    delta_rows = jnp.sum(grad_ctx_four.astype(jnp.float32) * attended, -1)
    grad_query, grad_key_all, grad_value_all = key_sweep(
        queries_four,
        grad_ctx_four,
        log_total,
        delta_rows,
        keys_four,
        values_four,
        query_pos,
        prefix,
        key_span,
        factor,
    )
    own_keys, own_values = (
        lax.psum_scatter(grad_key_all, "ctx", scatter_dimension=0, tiled=True),
        lax.psum_scatter(grad_value_all, "ctx", scatter_dimension=0, tiled=True),
    )
    own_keys = jnp.transpose(own_keys, (1, 0, 2))
    own_values = jnp.transpose(own_values, (1, 0, 2))
    grad_joined = jnp.concatenate(
        [grad_query.reshape(batches, row_count, local_width), own_keys, own_values], -1
    ).astype(jnp.bfloat16)
    grad_proj_self = jnp.transpose(
        jnp.einsum(
            "scd,scw->dw", rows_self, grad_joined, preferred_element_type=jnp.float32
        ).reshape(model_width, 3, local_width),
        (1, 0, 2),
    )
    back_one, gain_one, shift_one = norm_back(
        finish_grad(grad_joined, local_stack), unit_one, inverse_one, norm_gain[0]
    )
    input_grad = grad_after_one + back_one
    shard_grads = (
        lax.psum_scatter(grad_proj_self, "fsdp", scatter_dimension=1, tiled=True),
        lax.psum_scatter(grad_query_proj, "fsdp", scatter_dimension=0, tiled=True),
        lax.psum_scatter(grad_pair, "fsdp", scatter_dimension=1, tiled=True),
        lax.psum_scatter(grad_back_self, "fsdp", scatter_dimension=1, tiled=True),
        lax.psum_scatter(grad_back_cross, "fsdp", scatter_dimension=1, tiled=True),
        lax.psum_scatter(grad_expand, "fsdp", scatter_dimension=0, tiled=True),
        lax.psum_scatter(grad_shrink, "fsdp", scatter_dimension=1, tiled=True),
    )
    full_grads = lax.psum(
        (
            shard_grads[0],
            shard_grads[1],
            shard_grads[2],
            shard_grads[3],
            shard_grads[4],
            shard_grads[5],
            shard_grads[6],
        ),
        "ctx",
    )
    squares = jnp.stack(
        [
            jnp.sum(final_sum * final_sum),
            jnp.sum(branch_one * branch_one),
            jnp.sum(branch_two * branch_two),
            jnp.sum(branch_three * branch_three),
        ]
    )
    gain_grad, bias_grad, square_totals = lax.psum(
        (
            jnp.stack([gain_one, gain_two, gain_three]),
            jnp.stack([shift_one, shift_two, shift_three]),
            squares,
        ),
        ("fsdp", "ctx", "tp"),
    )
    entries = (
        tokens.shape[0]
        * tokens.shape[1]
        * tokens.shape[2]
        * lax.axis_size("fsdp")
        * lax.axis_size("ctx")
        * lax.axis_size("tp")
    )
    norms = jnp.sqrt(square_totals / entries)
    return (
        final_sum,
        input_grad,
        encoder_grad,
        full_grads[0],
        full_grads[1],
        full_grads[2],
        full_grads[3],
        full_grads[4],
        full_grads[5],
        full_grads[6],
        gain_grad,
        bias_grad[:2],
        bias_grad[2],
        norms,
    )


def dot_of(left, right, left_dim, right_dim):
    return lax.dot_general(
        left, right, (((left_dim,), (right_dim,)), ((), ())), preferred_element_type=jnp.float32
    )


def bounds(prefix, start, query_span, key_span):
    whole = jnp.maximum(prefix, start + 1) // key_span
    every = (jnp.maximum(prefix, start + query_span) + key_span - 1) // key_span
    return whole, every


def hide(scores, limit, offset):
    return jnp.where(lax.broadcasted_iota(jnp.int32, scores.shape, 0) < limit - offset, scores, NEG)


def low(value):
    return value.astype(jnp.bfloat16)


STRIP = 64


def in_strips(work, *values, strip=STRIP, axis=0):
    count = values[0].shape[axis] // strip
    cut = lambda v, n: lax.slice_in_dim(v, n * strip, (n + 1) * strip, axis=axis)
    parts = [work(*[cut(v, n) for v in values]) for n in range(count)]
    return tuple(jnp.concatenate(p, axis) for p in zip(*parts))


def gelu_strip(inputs):
    activated, slopes = gelu_parts(inputs)
    return low(activated), slopes


def rows_unit(hidden):
    centre = hidden - jnp.mean(hidden, -1, keepdims=True)
    inverse = lax.rsqrt(jnp.mean(centre * centre, -1, keepdims=True) + EPS)
    return centre * inverse, inverse


def rows_norm(hidden, scaling, offsets):
    def strip(rows):
        unit_rows, inverse = rows_unit(rows)
        return low(unit_rows * scaling + offsets), unit_rows, inverse

    return in_strips(strip, hidden)


def rows_back(upstream, unit_rows, inverse, scaling):
    sums = [jnp.zeros((8, upstream.shape[1]), jnp.float32)] * 2

    def strip(rows, units, inverses):
        scaled = rows * scaling
        for n, term in enumerate((rows * units, rows)):
            sums[n] = sums[n] + jnp.sum(term.reshape(-1, 8, term.shape[1]), 0)
        return (
            inverses
            * (
                scaled
                - jnp.mean(scaled, -1, keepdims=True)
                - units * jnp.mean(scaled * units, -1, keepdims=True)
            ),
        )

    (result,) = in_strips(strip, upstream, unit_rows, inverse)
    return result, jnp.sum(sums[0], 0, keepdims=True), jnp.sum(sums[1], 0, keepdims=True)


MESH = pl.DeviceIdType.MESH


def greet(group, tp, fsdp):
    here, core, chip = lax.axis_index("fsdp"), lax.axis_index("ctx"), lax.axis_index("tp")
    me = core * tp + chip
    barrier = pltpu.get_barrier_semaphore()
    for k in range(1, group):
        other = me ^ k
        pl.semaphore_signal(
            barrier, inc=1, device_id={"ctx": other // tp, "tp": other % tp}, device_id_type=MESH
        )
    for k in range(1, fsdp):
        pl.semaphore_signal(barrier, inc=1, device_id={"fsdp": here ^ k}, device_id_type=MESH)


def meet(group, fsdp):
    pl.semaphore_wait(pltpu.get_barrier_semaphore(), group - 1 + fsdp - 1)


def forward_kernel(
    prefix_ref,
    tokens_ref,
    step_ref,
    gain_ref,
    bias_ref,
    mine_ref,
    rows_out,
    qkv_ref,
    wide_ref,
    log_ref,
    ctx_ref,
    weight,
    rows_ref,
    other_ref,
    columns,
    pair_ref,
    keys_ref,
    values_ref,
    low_ref,
    landing,
    w_send,
    w_recv,
    v_send,
    v_recv,
    x_send,
    x_recv,
    c_send,
    c_recv,
    keep_sem,
    *,
    span,
    tp,
    fsdp,
):
    batches, chunk, width = tokens_ref.shape
    group = rows_ref.shape[0]
    length = group * chunk
    blocks, ratio = length // span, span // chunk
    wide_blocks = max(1, length // 2 // span)
    factor = HEAD_DIM**-0.5
    here, core, chip = lax.axis_index("fsdp"), lax.axis_index("ctx"), lax.axis_index("tp")
    me = core * tp + chip
    mine = chip // 2
    inner = (chip == 1) | (chip == 2)
    other_inner, other_outer = 2 - mine, 3 - 3 * mine
    greet(group, tp, fsdp)

    def send_to(source, target, send, recv, **place):
        return pltpu.make_async_remote_copy(
            src_ref=source,
            dst_ref=target,
            send_sem=send,
            recv_sem=recv,
            device_id=place,
            device_id_type=MESH,
        )

    def normalise(seq, target, at):
        start_sum = tokens_ref[seq].astype(jnp.float32) + step_ref[seq]
        target[at] = rows_norm(start_sum, gain_ref[0:1], bias_ref[0:1])[0]

    normalise(mine, rows_ref, me)
    normalise(1 - mine, other_ref, 0)
    meet(group, fsdp)

    v_core, v_chip = chip % 2, chip // 2 + 2 * core
    v_own = (v_core == core) & (v_chip == chip)
    v_copy = send_to(mine_ref, pair_ref, v_send.at[0], v_recv.at[0], ctx=v_core, tp=v_chip)

    @pl.when(v_own)
    def keep_pair():
        pair_ref[...] = mine_ref[...]

    @pl.when(jnp.logical_not(v_own))
    def send_pair():
        v_copy.start()

    comes = (chip // 2 != core) | (2 * (chip % 2) + core != chip)

    def w_copy(k):
        return send_to(pair_ref, columns.at[k], w_send.at[k], w_recv.at[k], fsdp=here ^ k)

    def x_copy(kind):
        block = rows_ref.at[me]
        near = rows_ref.at[core * tp + (chip ^ 1)]
        second = rows_ref.at[core * tp + other_inner]
        third = rows_ref.at[core * tp + other_outer]
        source, place, target = (
            (block, me, {"tp": chip ^ 1}),
            (other_ref.at[0], me, {"tp": other_inner}),
            (block, me, {"ctx": 1 - core}),
            (near, core * tp + (chip ^ 1), {"ctx": 1 - core}),
            (second, core * tp + other_inner, {"ctx": 1 - core}),
            (third, core * tp + other_outer, {"ctx": 1 - core}),
            (second, core * tp + other_inner, {"tp": chip ^ 1}),
            (third, core * tp + other_outer, {"tp": chip ^ 1}),
            (other_ref.at[0], me, {"tp": other_outer}),
        )[kind]
        return send_to(source, rows_ref.at[place], x_send.at[kind], x_recv.at[place], **target)

    def x_wait(place):
        send_to(
            rows_ref.at[place], rows_ref.at[place], x_send.at[0], x_recv.at[place], ctx=1 - core
        ).wait_recv()

    def arrive(number):
        x_wait(core * tp + (chip ^ 1, other_inner, other_outer)[number])
        if number:

            @pl.when(inner & (core == 0))
            def onward():
                x_copy(5 + number).start()

        x_copy(3 + number).start()


    @pl.when(core == 0)
    def first_half():
        x_copy(2).start()

        @pl.when(inner)
        def from_inner():
            x_copy(1).start()
            x_copy(0).start()

        @pl.when(jnp.logical_not(inner))
        def from_outer():
            x_copy(0).start()

    @pl.when(comes)
    def pair_here():
        v_copy.wait_recv()

    for k in range(1, fsdp):
        w_copy(k).start()
    values_ref[:, HEAD_DIM:, :] = jnp.ones_like(values_ref[:, HEAD_DIM:, :])

    def project(place, unused):
        rows = rows_ref[place]
        joined = low(dot_of(weight[...], rows, 1, 1))
        at = pl.ds(pl.multiple_of(place * chunk, chunk), chunk)
        for head in range(2):
            queries, keys, values = (
                joined[(3 * head + n) * HEAD_DIM : (3 * head + n + 1) * HEAD_DIM] for n in range(3)
            )
            qkv_ref[head, :HEAD_DIM, at] = queries * jnp.bfloat16(factor)
            qkv_ref[head, HEAD_DIM : 2 * HEAD_DIM, at] = keys
            qkv_ref[head, 2 * HEAD_DIM :, at] = values
            values_ref[head, :HEAD_DIM, at] = values
            keys_ref[head, at, :] = keys.T
        return unused

    @pl.when(core == 0)
    def first_lines():
        @pl.when(jnp.logical_not(inner))
        def then_other():
            x_copy(0).wait_send()
            x_copy(1).start()

        for number in range(3):
            arrive(number)

    @pl.when(core == 1)
    def second_lines():
        for place in range(tp):
            x_wait(place)
        for kind in (2, 1, 8, 0):
            x_copy(kind).start()

    piece = mine_ref.shape[1]
    for k in range(fsdp):
        if k:
            w_copy(k).wait_recv()
        part = columns[k] if k else pair_ref[...]
        for f in range(fsdp):

            @pl.when((here ^ k) == f)
            def place(f=f, part=part):
                weight[:, f * piece : (f + 1) * piece] = part

    lax.fori_loop(0, tp, project, 0)

    def c_copy(head, place):
        return send_to(
            low_ref.at[head, place],
            landing.at[head, me],
            c_send.at[head, place],
            c_recv.at[head, me],
            ctx=place // tp,
            tp=place % tp,
        )

    def c_wait(head, place):
        send_to(
            low_ref.at[head, place],
            landing.at[head, place],
            c_send.at[head, place],
            c_recv.at[head, place],
            ctx=place // tp,
            tp=place % tp,
        ).wait_recv()

    def attend(index, unused):
        block, head = (index // 2) ^ (1 - mine), index % 2

        @pl.when((core == 1) & (index == 3))
        def near_lines():
            arrive(0)

        @pl.when(index == 4)
        def second_half():
            @pl.when(core == 0)
            def wait_other():
                for place in range(tp, group):
                    x_wait(place)

            @pl.when(core == 1)
            def far_lines():
                arrive(1)
                arrive(2)

            def first_results(place, unused):
                @pl.when(place != me)
                def send():
                    for number in range(2):
                        c_copy(number, place).start()

                return unused

            lax.fori_loop(0, tp, first_results, 0)
            lax.fori_loop(tp, group, project, 0)

        start = pl.multiple_of(block * span, span)
        queries = qkv_ref[head, :HEAD_DIM, pl.ds(start, span)]
        limit = jnp.maximum(
            prefix_ref[mine], start + 1 + lax.broadcasted_iota(jnp.int32, (1, span), 1)
        )

        def advance(offset, count, carry, columns=None):
            highest, total = carry
            first = 0 if columns is None else columns
            scores = dot_of(keys_ref[head, pl.ds(offset, count), :], queries[:, first:], 1, 0)
            if columns is not None:
                scores = hide(scores, limit[:, first:], offset)
            higher = jnp.maximum(highest, jnp.max(scores, axis=0, keepdims=True))
            weights = low(jnp.exp(scores - higher))
            fading = jnp.exp(highest - higher)
            total = total * fading + dot_of(
                values_ref[head, :, pl.ds(offset, count)], weights, 1, 0
            )
            return higher, total

        def whole_step(other, carry):
            return advance(pl.multiple_of(other * span, span), span, carry)

        def masked_step(other, carry):
            return advance(pl.multiple_of(other * span, span), span, carry, 0)

        def diagonal_step(other, carry):
            half = span // 2
            carry = advance(start, half, carry, 0)
            offset = pl.multiple_of(start + half, half)
            upper = advance(offset, half, tuple(v[:, half:] for v in carry), half)
            return tuple(jnp.concatenate([v[:, :half], u], 1) for v, u in zip(carry, upper))

        carry = (
            jnp.full((1, span), NEG, jnp.float32),
            jnp.zeros((values_ref.shape[1], span), jnp.float32),
        )
        carry = lax.fori_loop(0, block, whole_step, carry)
        carry = lax.fori_loop(block, wide_blocks, masked_step, carry)
        highest, total = lax.fori_loop(
            0, jnp.where(block >= wide_blocks, 1, 0), diagonal_step, carry
        )
        weight_sum = total[HEAD_DIM : HEAD_DIM + 1, :]
        attended = total[:HEAD_DIM, :] / weight_sum
        wide_ref[head, :, pl.ds(start, span)] = attended
        log_ref[head, :, pl.ds(start, span)] = highest + jnp.log(weight_sum)
        attended = low(attended)
        for part in range(ratio):
            place = block * ratio + part
            low_ref[head, place] = attended[:, part * chunk : (part + 1) * chunk]

            @pl.when((place != me) & (index >= 4))
            def send(place=place):
                c_copy(head, place).start()

        return unused

    lax.fori_loop(0, 2 * blocks, attend, 0)
    keep = pltpu.make_async_copy(rows_ref, rows_out, keep_sem)
    keep.start()
    for head in range(2):

        def collect(k, unused, head=head):
            c_wait(head, me ^ k)
            ctx_ref[head, me ^ k] = landing[head, me ^ k]
            return unused

        lax.fori_loop(1, group, collect, 0)
        ctx_ref[head, me] = low_ref[head, me]
    for k in range(1, fsdp):
        w_copy(k).wait_send()

    @pl.when(jnp.logical_not(v_own))
    def pair_sent():
        v_copy.wait_send()

    for kind in range(1, 6):
        x_copy(kind).wait_send()

    @pl.when(inner | (core == 1))
    def own_sent():
        x_copy(0).wait_send()

    @pl.when(inner & (core == 0))
    def lines_sent():
        x_copy(6).wait_send()
        x_copy(7).wait_send()

    @pl.when(core == 1)
    def direct_sent():
        x_copy(8).wait_send()

    for head in range(2):

        def sent(k, unused, head=head):
            c_copy(head, me ^ k).wait_send()
            return unused

        lax.fori_loop(1, group, sent, 0)
    keep.wait()


def forward_group(prefix, tokens, steps, gain, bias, mine, span, group, tp, fsdp):
    batches, chunk, width = tokens.shape
    length = group * chunk
    bf16, f32 = jnp.bfloat16, jnp.float32
    struct = jax.ShapeDtypeStruct
    inside = pl.BlockSpec(memory_space=pltpu.VMEM)
    dma = pltpu.SemaphoreType.DMA
    return pl.pallas_call(
        functools.partial(forward_kernel, span=span, tp=tp, fsdp=fsdp),
        in_specs=[pl.BlockSpec(memory_space=pltpu.SMEM)] + [inside] * 5,
        out_specs=[pl.BlockSpec(memory_space=pl.ANY)] + [inside] * 5,
        out_shape=[
            struct((group, chunk, width), bf16),
            struct((2, 3 * HEAD_DIM, length), bf16),
            struct((2, HEAD_DIM, length), f32),
            struct((2, 1, length), f32),
            struct((2, group, HEAD_DIM, chunk), bf16),
            struct((6 * HEAD_DIM, width), bf16),
        ],
        scratch_shapes=[
            pltpu.VMEM((group, chunk, width), bf16),
            pltpu.VMEM((1, chunk, width), bf16),
            pltpu.VMEM((fsdp,) + mine.shape, bf16),
            pltpu.VMEM(mine.shape, bf16),
            pltpu.VMEM((2, length, HEAD_DIM), bf16),
            pltpu.VMEM((2, HEAD_DIM + 16, length), bf16),
            pltpu.VMEM((2, group, HEAD_DIM, chunk), bf16),
            pltpu.VMEM((2, group, HEAD_DIM, chunk), bf16),
            dma((fsdp,)),
            dma((fsdp,)),
            dma((1,)),
            dma((1,)),
            dma((9,)),
            dma((group,)),
            dma((2, group)),
            dma((2, group)),
            dma,
        ],
        compiler_params=pltpu.CompilerParams(
            vmem_limit_bytes=VMEM_LIMIT, collective_id=1, has_side_effects=True
        ),
        cost_estimate=pl.CostEstimate(
            flops=60_000_000_000, bytes_accessed=30_000_000, transcendentals=20_000_000
        ),
        name="forward_group",
    )(prefix, tokens, steps, gain, bias, mine)


QUERY, KEY, VALUE, SELF_OUT, CROSS_OUT, UP, DOWN = 0, 1, 2, 3, 4, 5, 9


def middle_kernel(
    gathered,
    tokens_ref,
    step_ref,
    enc_ref,
    cot_ref,
    gain_ref,
    bias_ref,
    ctx_ref,
    final_ref,
    after_ref,
    back_ref,
    enc_grad_ref,
    stats_ref,
    packed_ref,
    weights,
    hidden_all,
    pre_all,
    three_all,
    two_all,
    grad_two_all,
    grad_one_all,
    cross_all,
    query_all,
    context_all,
    queries,
    keys,
    values,
    probs,
    grad_heads,
    grad_keys,
    grad_values,
    back_rows,
    landing,
    d_send,
    d_recv,
    sem,
    *,
    tp,
    fsdp,
):
    batches, chunk, width = tokens_ref.shape
    group = landing.shape[1]
    core, chip = lax.axis_index("ctx"), lax.axis_index("tp")
    me = core * tp + chip
    mine = chip // 2
    greet(group, tp, fsdp)
    piece = gathered.shape[-1]
    factor = HEAD_DIM**-0.5
    heads = width // HEAD_DIM

    copies = []
    for f in range(width // piece):
        for c in range(group // tp):
            for t in range(tp):
                head = t * (group // tp) + c
                copies.append(
                    pltpu.make_async_copy(
                        gathered.at[f, c, t],
                        weights.at[:, pl.ds(head * HEAD_DIM, HEAD_DIM), pl.ds(f * piece, piece)],
                        sem.at[(f * group // tp + c) * tp + t],
                    )
                )
    for copy in copies:
        copy.start()
    stats_ref[...] = jnp.zeros_like(stats_ref)
    for copy in copies:
        copy.wait()

    owners = [(2 * (2 * z + c) + n, n, c * tp + z) for z in (0, 1) for c in (0, 1) for n in (0, 1)]

    def d_copy(turn, seq, head, number, owner):
        return pltpu.make_async_remote_copy(
            src_ref=back_rows.at[turn, pl.ds(head * HEAD_DIM, HEAD_DIM)],
            dst_ref=landing.at[number, me],
            send_sem=d_send.at[turn, head],
            recv_sem=d_recv.at[number, me],
            device_id={"ctx": owner // tp, "tp": owner % tp + 2 * seq},
            device_id_type=MESH,
        )

    def one_sequence(turn, unused):
        seq = jnp.where(turn == 0, 1 - mine, mine)
        at = pl.ds(pl.multiple_of(seq * chunk, chunk), chunk)
        for head, number, owner in owners:
            context_all[head * HEAD_DIM : (head + 1) * HEAD_DIM, at] = ctx_ref[number, owner + 2 * seq]
        start_sum = tokens_ref[seq].astype(jnp.float32) + step_ref[seq]
        branch_one = dot_of(context_all[:, at], weights[SELF_OUT], 0, 0)
        after_one = start_sum + branch_one
        stats_ref[1:2, :] += jnp.sum(branch_one * branch_one, 0, keepdims=True)
        normed_two, unit_two, inverse_two = rows_norm(after_one, gain_ref[1:2], bias_ref[1:2])
        two_all[at, :] = normed_two
        queries[...] = low(dot_of(weights[QUERY], normed_two, 1, 1))
        keys[...] = low(dot_of(weights[KEY], enc_ref[seq], 1, 1))
        values[...] = low(dot_of(weights[VALUE], enc_ref[seq], 1, 1))

        def attend(head, unused):
            rows = pl.ds(pl.multiple_of(head * HEAD_DIM, HEAD_DIM), HEAD_DIM)
            scores = dot_of(keys[rows, :].T, queries[rows, :], 1, 0) * factor

            def strip(columns):
                powers = jnp.exp(columns - jnp.max(columns, 0, keepdims=True))
                return (powers / jnp.sum(powers, 0, keepdims=True),)

            (attn,) = in_strips(strip, scores, strip=128, axis=1)
            probs[head] = attn
            cross_all[rows, at] = low(dot_of(values[rows, :], low(attn), 1, 0))
            return unused

        lax.fori_loop(0, heads, attend, 0, unroll=8)
        branch_two = dot_of(cross_all[:, at], weights[CROSS_OUT], 0, 0)
        after_two = after_one + branch_two
        stats_ref[2:3, :] += jnp.sum(branch_two * branch_two, 0, keepdims=True)
        normed_three, unit_three, inverse_three = rows_norm(after_two, gain_ref[2:3], bias_ref[2:3])
        three_all[at, :] = normed_three
        grad_three = cot_ref[seq]

        def feed(part, carry):
            branch, grad = carry
            up, down = weights[UP + part], weights[DOWN + part]
            inputs = dot_of(up, normed_three, 1, 1)
            hidden, slopes = in_strips(gelu_strip, inputs, strip=32)
            branch = branch + dot_of(hidden, down, 0, 0)
            hidden_all[part, :, at] = hidden
            grad_pre = low(dot_of(down, grad_three, 1, 1) * slopes)
            pre_all[part, :, at] = grad_pre
            return branch, grad + dot_of(grad_pre, up, 0, 0)

        blank = jnp.zeros((chunk, width), jnp.float32)
        branch_three, grad_norm = lax.fori_loop(0, DOWN - UP, feed, (blank, blank), unroll=4)
        final_sum = after_two + branch_three
        final_ref[seq] = final_sum
        stats_ref[0:1, :] += jnp.sum(final_sum * final_sum, 0, keepdims=True)
        stats_ref[3:4, :] += jnp.sum(branch_three * branch_three, 0, keepdims=True)
        back, gain_sum, bias_sum = rows_back(grad_norm, unit_three, inverse_three, gain_ref[2:3])
        stats_ref[6:7, :] += gain_sum
        stats_ref[7:8, :] += bias_sum
        grad_after_two = grad_three.astype(jnp.float32) + back
        grad_two = low(grad_after_two)
        grad_two_all[at, :] = grad_two
        grad_heads[...] = low(dot_of(weights[CROSS_OUT], grad_two, 1, 1))

        def attend_back(head, unused):
            rows = pl.ds(pl.multiple_of(head * HEAD_DIM, HEAD_DIM), HEAD_DIM)
            grads = grad_heads[rows, :]
            attn = probs[head]
            grad_probs = dot_of(values[rows, :].T, grads, 1, 0)

            def strip(ones, others):
                return (low(ones * (others - jnp.sum(ones * others, 0, keepdims=True))),)

            (grad_scores,) = in_strips(strip, attn, grad_probs, strip=128, axis=1)
            query_all[rows, at] = low(dot_of(keys[rows, :], grad_scores, 1, 0) * factor)
            grad_keys[rows, :] = dot_of(queries[rows, :], grad_scores, 1, 1) * factor
            grad_values[rows, :] = dot_of(grads, low(attn), 1, 1)
            return unused

        lax.fori_loop(0, heads, attend_back, 0, unroll=8)
        enc_grad_ref[seq, :, :width] = low(grad_keys[...].T)
        enc_grad_ref[seq, :, width:] = low(grad_values[...].T)
        upstream = dot_of(query_all[:, at], weights[QUERY], 0, 0)
        back, gain_sum, bias_sum = rows_back(upstream, unit_two, inverse_two, gain_ref[1:2])
        stats_ref[4:5, :] += gain_sum
        stats_ref[5:6, :] += bias_sum
        grad_after_one = grad_after_two + back
        after_ref[seq] = grad_after_one
        grad_one = low(grad_after_one)
        grad_one_all[at, :] = grad_one
        back_rows[turn] = low(dot_of(weights[SELF_OUT], grad_one, 1, 1))

        @pl.when(turn == 0)
        def all_here():
            meet(group, fsdp)

        for head, number, owner in owners:

            @pl.when(owner + 2 * seq != me)
            def give(head=head, number=number, owner=owner):
                d_copy(turn, seq, head, number, owner).start()

            @pl.when(owner + 2 * seq == me)
            def keep(head=head, number=number):
                back_ref[number, me] = back_rows[turn, head * HEAD_DIM : (head + 1) * HEAD_DIM, :]

        return unused


    lax.fori_loop(0, batches, one_sequence, 0)
    def pack(block, left, right):
        total = low(dot_of(left, right, 1, 0))
        for f in range(width // piece):
            for c in range(group // tp):
                for t in range(tp):
                    head = t * (group // tp) + c
                    packed_ref[c, f, t, block] = total[
                        head * HEAD_DIM : (head + 1) * HEAD_DIM, f * piece : (f + 1) * piece
                    ]

    grad_three_all = cot_ref[...].reshape(batches * chunk, width)
    pack(0, query_all[...], two_all[...])
    pack(1, context_all[...], grad_one_all[...])
    pack(2, cross_all[...], grad_two_all[...])

    def pack_feed(part, unused):
        pack(UP - 2 + part, pre_all[part], three_all[...])
        pack(DOWN - 2 + part, hidden_all[part], grad_three_all)
        return unused

    lax.fori_loop(0, DOWN - UP, pack_feed, 0)

    def collect(k, unused):
        place = me ^ k
        for number in range(2):
            pltpu.make_async_remote_copy(
                src_ref=landing.at[number, place],
                dst_ref=landing.at[number, place],
                send_sem=d_send.at[0, 0],
                recv_sem=d_recv.at[number, place],
                device_id={"ctx": place // tp, "tp": place % tp},
                device_id_type=MESH,
            ).wait_recv()
            back_ref[number, place] = landing[number, place]
        return unused

    lax.fori_loop(1, group, collect, 0)
    for turn in range(batches):
        seq = 1 - mine if turn == 0 else mine
        for head, number, owner in owners:

            @pl.when(owner + 2 * seq != me)
            def given(turn=turn, seq=seq, head=head, number=number, owner=owner):
                d_copy(turn, seq, head, number, owner).wait_send()


def middle(
    gathered, tokens, steps, encoder, cotangent, gains, biases, contexts, tp, fsdp
):
    batches, chunk, width = tokens.shape
    group = contexts.shape[1]
    enc_count = encoder.shape[1]
    heads = width // HEAD_DIM
    bf16, f32 = jnp.bfloat16, jnp.float32
    struct = jax.ShapeDtypeStruct
    inside = pl.BlockSpec(memory_space=pltpu.VMEM)
    dma = pltpu.SemaphoreType.DMA
    count = gathered.shape[3]
    packed = (group // tp, gathered.shape[0], tp, count - 2) + gathered.shape[4:]
    return pl.pallas_call(
        functools.partial(middle_kernel, tp=tp, fsdp=fsdp),
        in_specs=[pl.BlockSpec(memory_space=pl.ANY)] + [inside] * 7,
        out_specs=[inside] * 6,
        out_shape=[
            struct((batches, chunk, width), f32),
            struct((batches, chunk, width), f32),
            struct((2, group, HEAD_DIM, chunk), bf16),
            struct((batches, enc_count, 2 * width), bf16),
            struct((8, width), f32),
            struct(packed, bf16),
        ],
        scratch_shapes=[
            pltpu.VMEM((count, width, width), bf16),
            pltpu.VMEM((DOWN - UP, width, batches * chunk), bf16),
            pltpu.VMEM((DOWN - UP, width, batches * chunk), bf16),
            pltpu.VMEM((batches * chunk, width), bf16),
            pltpu.VMEM((batches * chunk, width), bf16),
            pltpu.VMEM((batches * chunk, width), bf16),
            pltpu.VMEM((batches * chunk, width), bf16),
            pltpu.VMEM((width, batches * chunk), bf16),
            pltpu.VMEM((width, batches * chunk), bf16),
            pltpu.VMEM((width, batches * chunk), bf16),
            pltpu.VMEM((width, chunk), bf16),
            pltpu.VMEM((width, enc_count), bf16),
            pltpu.VMEM((width, enc_count), bf16),
            pltpu.VMEM((heads, enc_count, chunk), f32),
            pltpu.VMEM((width, chunk), bf16),
            pltpu.VMEM((width, enc_count), f32),
            pltpu.VMEM((width, enc_count), f32),
            pltpu.VMEM((batches, width, chunk), bf16),
            pltpu.VMEM((2, group, HEAD_DIM, chunk), bf16),
            dma((batches, heads)),
            dma((2, group)),
            dma((32,)),
        ],
        compiler_params=pltpu.CompilerParams(
            vmem_limit_bytes=VMEM_LIMIT, collective_id=3, has_side_effects=True
        ),
        cost_estimate=pl.CostEstimate(
            flops=30_000_000_000, bytes_accessed=30_000_000, transcendentals=10_000_000
        ),
        name="middle",
    )(gathered, tokens, steps, encoder, cotangent, gains, biases, contexts)


def backward_kernel(
    prefix_ref,
    enc_parts,
    packed,
    gathered,
    rows_in,
    landing,
    weight,
    qkv_ref,
    wide_ref,
    log_ref,
    tokens_ref,
    step_ref,
    gain_ref,
    bias_ref,
    after_ref,
    enc_ref,
    stats_ref,
    input_ref,
    enc_out,
    self_out,
    query_out,
    pair_out,
    back_out,
    cross_out,
    up_out,
    down_out,
    sums_out,
    outgoing,
    core_rows,
    core_rows_landing,
    sum_rows,
    beside,
    incoming,
    queries_ref,
    pairs_ref,
    grad_ref,
    delta_ref,
    grad_pairs_ref,
    rows_ref,
    pair_weights,
    enc_own,
    enc_core,
    enc_sum,
    enc_landing,
    pair_ref,
    pair_landing,
    core_landing,
    partial_ref,
    fsdp_landing,
    line_ref,
    line_landing,
    shard_ref,
    head_ref,
    head_landing,
    head_pair,
    head_two,
    sums_ref,
    sums_landing,
    sums_two,
    e_send,
    e_recv,
    x_send,
    x_recv,
    i_send,
    i_recv,
    b_recv,
    r_send,
    r_recv,
    f_send,
    f_recv,
    t_send,
    t_recv,
    h_send,
    h_recv,
    p_send,
    p_recv,
    s_send,
    s_recv,
    local_sem,
    rows_sem,
    *,
    span,
    tp,
    fsdp,
):
    batches, chunk, width = tokens_ref.shape
    group = landing.shape[1]
    length = group * chunk
    blocks, ratio = length // span, span // chunk
    wide_blocks = max(1, length // 2 // span)
    factor = HEAD_DIM**-0.5
    here, core, chip = lax.axis_index("fsdp"), lax.axis_index("ctx"), lax.axis_index("tp")
    me = core * tp + chip
    mine = chip // 2
    inner = (chip == 1) | (chip == 2)
    cores = group // tp
    share = enc_landing.shape[2]
    piece = width // fsdp
    early = packed.shape[3]
    greet(group, tp, fsdp)

    def send_to(source, target, send, recv, **place):
        return pltpu.make_async_remote_copy(
            src_ref=source,
            dst_ref=target,
            send_sem=send,
            recv_sem=recv,
            device_id=place,
            device_id_type=MESH,
        )

    def member(place):
        return {"ctx": place // tp, "tp": place % tp}

    local = [
        pltpu.make_async_copy(
            packed.at[core], partial_ref.at[:, :, pl.ds(0, early)], local_sem.at[0]
        ),
        pltpu.make_async_copy(
            enc_parts.at[:, pl.ds(pl.multiple_of(core * tp * share, share), tp * share)],
            enc_own,
            local_sem.at[1],
        ),
    ]
    first = len(local)
    for f in range(fsdp):
        for c in range(cores):
            for t in range(tp):
                head = t * cores + c
                local.append(
                    pltpu.make_async_copy(
                        gathered.at[f, c, t, pl.ds(KEY, 2)],
                        pair_weights.at[
                            :, pl.ds(head * HEAD_DIM, HEAD_DIM), pl.ds(f * piece, piece)
                        ],
                        local_sem.at[first + (f * cores + c) * tp + t],
                    )
                )
    enc_copy = send_to(
        enc_parts.at[:, pl.ds(pl.multiple_of((1 - core) * tp * share, share), tp * share)],
        enc_core,
        e_send.at[0],
        e_recv.at[0],
        ctx=1 - core,
    )
    enc_line = [
        send_to(
            enc_sum.at[chip ^ n], enc_landing.at[n - 1], e_send.at[n], e_recv.at[n], tp=chip ^ n
        )
        for n in range(1, tp)
    ]

    core_copy = send_to(
        packed.at[1 - core], core_landing, r_send.at[0], r_recv.at[0], ctx=1 - core
    )
    pair_copy = send_to(
        pair_ref.at[1 - core], pair_landing, r_send.at[1], r_recv.at[1], ctx=1 - core
    )
    shard_copy = send_to(
        shard_ref.at[core], shard_ref.at[core], r_send.at[2], r_recv.at[2], ctx=1 - core
    )
    shard_wait = send_to(
        shard_ref.at[1 - core], shard_ref.at[1 - core], r_send.at[2], r_recv.at[2], ctx=1 - core
    )
    f_copies = [
        send_to(
            partial_ref.at[here ^ n, :, pl.ds(0, early)],
            fsdp_landing.at[n - 1, :, pl.ds(0, early)],
            f_send.at[n],
            f_recv.at[n],
            fsdp=here ^ n,
        )
        for n in range(1, fsdp)
    ]
    f_pairs = [
        send_to(
            partial_ref.at[here ^ n, :, pl.ds(early, 2)],
            fsdp_landing.at[n - 1, :, pl.ds(early, 2)],
            f_send.at[fsdp + n],
            f_recv.at[fsdp + n],
            fsdp=here ^ n,
        )
        for n in range(1, fsdp)
    ]
    t_copies = [
        send_to(line_ref.at[chip ^ k], line_landing.at[k - 1], t_send.at[k], t_recv.at[k], tp=chip ^ k)
        for k in range(1, tp)
    ]
    h_copies = [
        send_to(
            head_ref.at[here ^ k], head_landing.at[k - 1], h_send.at[k], h_recv.at[k], fsdp=here ^ k
        )
        for k in range(1, fsdp)
    ]

    pair_chip = 2 * (chip % 2) + core
    p_copies = [
        send_to(head_pair, head_two.at[mine], p_send.at[c], p_recv.at[mine], ctx=c, tp=pair_chip)
        for c in range(2)
    ]
    p_waits = [
        send_to(head_pair, head_two.at[n], p_send.at[0], p_recv.at[n], ctx=c, tp=t)
        for n, c, t in ((0, chip % 2, chip // 2), (1, chip % 2, chip // 2 + 2))
    ]
    p_here = [
        (core == chip % 2) & (chip == chip // 2 + 2 * n) for n in range(2)
    ]

    def s_copy(k):
        return send_to(
            sums_ref, sums_landing.at[k], s_send.at[k], s_recv.at[k], **member(me ^ k)
        )

    s_fsdp = [
        send_to(
            sums_two, sums_landing.at[group + k], s_send.at[group + k], s_recv.at[group + k], fsdp=here ^ k
        )
        for k in range(1, fsdp)
    ]

    def prepare(seq):
        def lay(place, unused):
            at = pl.ds(pl.multiple_of(place * chunk, chunk), chunk)
            grads = landing[seq, place]
            blank = jnp.zeros_like(grads)
            grad_ref[seq, at, :] = jnp.concatenate([blank, grads], 0).T
            delta_ref[seq, :, at] = jnp.sum(
                grads.astype(jnp.float32) * wide_ref[seq, :, at], axis=0, keepdims=True
            )
            queries_ref[seq, at, :] = jnp.concatenate([qkv_ref[seq, :HEAD_DIM, at], blank], 0).T
            pairs_ref[seq, at, :] = qkv_ref[seq, HEAD_DIM:, at].T
            return unused

        lax.fori_loop(0, group, lay, 0)
        grad_pairs_ref[seq] = jnp.zeros(grad_pairs_ref.shape[1:], jnp.float32)

    for copy in local:
        copy.start()
    for head in range(2):
        prepare(head)

    meet(group, fsdp)
    enc_copy.start()
    core_copy.start()

    def core_rows_copy(place):
        slot = place % tp
        return send_to(
            core_rows.at[slot], core_rows_landing.at[slot], x_send.at[slot], x_recv.at[slot], ctx=1 - core
        )

    def owner_copy(place):
        slot = place % tp
        return send_to(
            sum_rows.at[slot],
            incoming.at[mine, chip % 2],
            i_send.at[slot],
            i_recv.at[mine, chip % 2],
            tp=slot,
        )

    def spread(place):
        upstream = dot_of(outgoing[place].reshape(6 * HEAD_DIM, chunk), weight[...], 0, 0)
        slot = place % tp

        @pl.when(place // tp != core)
        def hand_over():
            core_rows[slot] = low(upstream)
            core_rows_copy(place).start()

        @pl.when(place // tp == core)
        def collect():
            core_rows_copy(place).wait_recv()
            total = low(upstream + core_rows_landing[slot].astype(jnp.float32))

            @pl.when(place == me)
            def own():
                incoming[mine, chip % 2] = total

            @pl.when(place != me)
            def send():
                sum_rows[slot] = total

                @pl.when((core == 0) & (slot // 2 != mine) & jnp.logical_not(inner))
                def to_inner():
                    beside_copy(slot).start()

                @pl.when((core == 1) | (slot // 2 == mine))
                def to_owner():
                    owner_copy(place).start()

    def beside_copy(slot):
        return send_to(
            sum_rows.at[slot], beside.at[slot % 2], i_send.at[slot], b_recv.at[slot % 2], tp=chip ^ 1
        )

    def pass_rows():
        for n in range(2):
            slot = 2 * (1 - mine) + n
            beside_copy(slot).wait_recv()
            sum_rows[slot] = low(
                sum_rows[slot].astype(jnp.float32) + beside[n].astype(jnp.float32)
            )
            owner_copy(slot).start()

    def encoder_cores():
        local[1].wait()
        enc_copy.wait_recv()
        for t in range(tp):
            lines = slice(t * share, (t + 1) * share)
            enc_sum[t] = low(
                enc_own[:, lines].astype(jnp.float32) + enc_core[:, lines].astype(jnp.float32)
            )
        for copy in enc_line:
            copy.start()

    def encoder_part():
        total = enc_sum[chip].astype(jnp.float32)
        for n, copy in enumerate(enc_line):
            copy.wait_recv()
            total = total + enc_landing[n].astype(jnp.float32)
        for copy in local[first:]:
            copy.wait()
        grads = low(total)
        enc_rows = enc_ref[:, pl.ds(pl.multiple_of(me * share, share), share), :]
        flat, enc_flat = grads.reshape(batches * share, 2 * width), enc_rows.reshape(
            batches * share, width
        )
        result = dot_of(flat[:, :width], pair_weights[0], 1, 0) + dot_of(
            flat[:, width:], pair_weights[1], 1, 0
        )
        enc_out[...] = result.reshape(batches, share, width)
        for which in range(2):
            grad = low(dot_of(flat[:, which * width : (which + 1) * width], enc_flat, 0, 0))
            for f in range(fsdp):
                for c in range(cores):
                    for t in range(tp):
                        head = t * cores + c
                        pair_ref[c, f, t, which] = grad[
                            head * HEAD_DIM : (head + 1) * HEAD_DIM, f * piece : (f + 1) * piece
                        ]
        pair_copy.start()

    def sum_cores():
        local[0].wait()
        core_copy.wait_recv()

        def one(f, unused):
            def two(t, unused):
                partial_ref[f, t, :early] = low(
                    partial_ref[f, t, :early].astype(jnp.float32)
                    + core_landing[f, t].astype(jnp.float32)
                )
                return unused

            return lax.fori_loop(0, tp, two, unused)

        lax.fori_loop(0, fsdp, one, 0)
        for copy in f_copies:
            copy.start()

    def sum_pairs():
        pair_copy.wait_recv()
        for f in range(fsdp):
            for t in range(tp):
                partial_ref[f, t, early:] = low(
                    pair_ref[core, f, t].astype(jnp.float32)
                    + pair_landing[f, t].astype(jnp.float32)
                )
        for copy in f_pairs:
            copy.start()

    def sum_fsdp():
        for copy in f_copies + f_pairs:
            copy.wait_recv()

        def one(t, unused):
            total = partial_ref[here, t].astype(jnp.float32)
            for k in range(fsdp - 1):
                total = total + fsdp_landing[k, t].astype(jnp.float32)
            line_ref[t] = low(total)
            return unused

        lax.fori_loop(0, tp, one, 0)
        for copy in t_copies:
            copy.start()

    def sum_line():
        for copy in t_copies:
            copy.wait_recv()
        total = line_ref[chip].astype(jnp.float32)
        for k in range(tp - 1):
            total = total + line_landing[k].astype(jnp.float32)
        shard_ref[core] = total
        shard_copy.start()

    def attend(index, unused):
        block, seq = blocks - 1 - index // 2, index % 2

        def hook(at, work):
            @pl.when(index == at)
            def run():
                work()

        hook(1, encoder_cores)
        hook(1, sum_cores)
        hook(2, encoder_part)
        hook(3, sum_pairs)
        hook(4, sum_fsdp)
        start = pl.multiple_of(block * span, span)
        at = pl.ds(start, span)
        blank = jnp.zeros((HEAD_DIM, span), jnp.bfloat16)
        queries_t = jnp.concatenate([qkv_ref[seq, :HEAD_DIM, at], blank], 0)
        queries = queries_ref[seq, at, :]
        grads = grad_ref[seq, at, :]
        grads_t = jnp.concatenate(
            [landing[seq, block * ratio + part] for part in range(ratio)], 1
        )
        grads_t = jnp.concatenate([blank, grads_t], 0)
        logs, deltas = log_ref[seq, :, at], delta_ref[seq, :, at]
        limit = jnp.maximum(
            prefix_ref[mine], start + 1 + lax.broadcasted_iota(jnp.int32, (1, span), 1)
        )

        def advance(offset, count, grad_queries, columns=None):
            first = 0 if columns is None else columns
            there = pl.ds(offset, count)
            pairs = pairs_ref[seq, there, :]
            scores = dot_of(pairs, queries_t[:, first:], 1, 0)
            if columns is not None:
                scores = hide(scores, limit[:, first:], offset)
            probs = jnp.exp(scores - logs[:, first:])
            grad_probs = dot_of(pairs, grads_t[:, first:], 1, 0)
            grad_scores = low(probs * (grad_probs - deltas[:, first:]))
            grad_pairs_ref[seq, there, :] += dot_of(low(probs), grads[first:], 1, 0) + dot_of(
                grad_scores, queries[first:], 1, 0
            )
            return grad_queries + dot_of(
                qkv_ref[seq, HEAD_DIM : 2 * HEAD_DIM, there], grad_scores, 1, 0
            )

        def whole_step(other, total):
            return advance(pl.multiple_of(other * span, span), span, total)

        def masked_step(other, total):
            return advance(pl.multiple_of(other * span, span), span, total, 0)

        def diagonal_step(other, total):
            half = span // 2
            total = advance(start, half, total, 0)
            offset = pl.multiple_of(start + half, half)
            upper = advance(offset, half, total[:, half:], half)
            return jnp.concatenate([total[:, :half], upper], 1)

        grad_queries = jnp.zeros((HEAD_DIM, span), jnp.float32)
        grad_queries = lax.fori_loop(0, block, whole_step, grad_queries)
        grad_queries = lax.fori_loop(block, wide_blocks, masked_step, grad_queries)
        grad_queries = lax.fori_loop(
            0, jnp.where(block >= wide_blocks, 1, 0), diagonal_step, grad_queries
        )
        done = low(grad_queries * factor)
        for part in range(ratio):
            place = block * ratio + part
            outgoing[place, seq, :HEAD_DIM, :] = done[:, part * chunk : (part + 1) * chunk]

        lowest = jnp.where(block == 0, 0, block)
        highest = jnp.where(
            block == 0, wide_blocks, jnp.where(block >= wide_blocks, block + 1, block)
        )

        def give(place, unused):
            at = pl.ds(pl.multiple_of(place * chunk, chunk), chunk)
            outgoing[place, seq, HEAD_DIM:, :] = low(grad_pairs_ref[seq, at, :].T)
            return unused

        lax.fori_loop(lowest * ratio, highest * ratio, give, 0)

        @pl.when(seq == 1)
        def both_heads():
            def one(place, unused):
                spread(place)
                return unused

            lax.fori_loop(lowest * ratio, highest * ratio, one, 0)

        return unused

    lax.fori_loop(0, 2 * blocks, attend, 0)

    sums_ref[...] = jnp.zeros_like(sums_ref)
    sums_ref[:8, :] = stats_ref[...]

    def rows_copy(number):
        return pltpu.make_async_copy(
            rows_in.at[number],
            rows_ref.at[number % rows_ref.shape[0]],
            rows_sem.at[number % rows_ref.shape[0]],
        )

    depth = rows_ref.shape[0]
    for number in range(depth):
        rows_copy(number).start()

    ones = jnp.ones((chunk, piece), jnp.bfloat16)

    def weigh(number, totals):
        rows_copy(number).wait()
        grads = outgoing[number].reshape(6 * HEAD_DIM, chunk)
        total = totals[0] + dot_of(grads, rows_ref[number % depth], 1, 0)

        @pl.when(number + depth < group)
        def more():
            rows_copy(number + depth).start()

        return total, totals[1] + dot_of(grads, ones, 1, 0)

    total, plain = lax.fori_loop(
        0,
        group,
        weigh,
        (
            jnp.zeros((6 * HEAD_DIM, width), jnp.float32),
            jnp.zeros((6 * HEAD_DIM, piece), jnp.float32),
        ),
    )
    token_copies = [
        pltpu.make_async_copy(tokens_ref.at[n], rows_ref.at[n], rows_sem.at[n])
        for n in range(batches)
    ]
    for copy in token_copies:
        copy.start()
    weights = weight[...].astype(jnp.float32)
    bias_sum = jnp.sum(weights * jnp.concatenate([plain] * (width // piece), 1), 0, keepdims=True)
    gain_sum = jnp.sum(weights * total, 0, keepdims=True) - bias_ref[0:1] * bias_sum
    sums_ref[8:9, :] = gain_sum / gain_ref[0:1]
    sums_ref[9:10, :] = bias_sum

    def start_sums(k, unused):
        s_copy(k).start()
        return unused

    lax.fori_loop(1, group, start_sums, 0)
    for f in range(fsdp):
        head_ref[f] = total[:, f * piece : (f + 1) * piece]
    for copy in h_copies:
        copy.start()

    @pl.when((core == 0) & inner)
    def last_rows():
        pass_rows()

    sum_line()

    for copy in h_copies:
        copy.wait_recv()
    total = head_ref[here]
    for k in range(fsdp - 1):
        total = total + head_landing[k]
    head_pair[...] = low(total)
    for c in range(2):
        there = (core == c) & (pair_chip == chip)

        @pl.when(there)
        def stay():
            head_two[mine] = head_pair[...]

        @pl.when(jnp.logical_not(there))
        def leave(c=c):
            p_copies[c].start()

    def arrive_sums(k, total):
        s_copy(k).wait_recv()
        return total + sums_landing[k]

    sums_two[...] = lax.fori_loop(1, group, arrive_sums, sums_ref[...])
    for copy in s_fsdp:
        copy.start()

    for copy in token_copies:
        copy.wait()

    def finish(seq, unused):
        for number in range(2):
            source = 2 * seq + number

            passed = (core == 0) & (seq != mine)

            @pl.when(passed & ((source == 0) | (source == 3)))
            def nothing(number=number):
                incoming[seq, number] = jnp.zeros((chunk, width), jnp.bfloat16)

            @pl.when((source != chip) & jnp.logical_not(passed & ((source == 0) | (source == 3))))
            def come(number=number, source=source):
                send_to(
                    incoming.at[seq, number],
                    incoming.at[seq, number],
                    i_send.at[0],
                    i_recv.at[seq, number],
                    tp=source,
                ).wait_recv()

        upstream = incoming[seq, 0].astype(jnp.float32) + incoming[seq, 1].astype(jnp.float32)
        start_sum = rows_ref[seq].astype(jnp.float32) + step_ref[seq]
        unit_rows, inverse = in_strips(rows_unit, start_sum)
        input_ref[seq] = after_ref[seq] + rows_back(
            upstream, unit_rows, inverse, gain_ref[0:1]
        )[0]
        return unused

    lax.fori_loop(0, batches, finish, 0)

    shard_wait.wait_recv()

    def whole(block):
        return jnp.concatenate([shard_ref[0, block], shard_ref[1, block]], 0)

    query_out[...] = whole(0).T
    back_out[...] = whole(1)
    cross_out[...] = whole(2)
    for part in range(4):
        up_out[:, part * piece : (part + 1) * piece] = whole(3 + part).T
        down_out[part * piece : (part + 1) * piece, :] = whole(7 + part)
    pair_out[0] = whole(11).T
    pair_out[1] = whole(12).T
    for n in range(2):

        @pl.when(jnp.logical_not(p_here[n]))
        def pair_come(n=n):
            p_waits[n].wait_recv()

    total = head_two[0].astype(jnp.float32) + head_two[1].astype(jnp.float32)
    for which in range(3):
        self_out[which] = jnp.concatenate(
            [
                total[(3 * n + which) * HEAD_DIM : (3 * n + which + 1) * HEAD_DIM]
                for n in range(2)
            ],
            0,
        ).T
    total = sums_two[...]
    for k, copy in enumerate(s_fsdp):
        copy.wait_recv()
        total = total + sums_landing[group + 1 + k]
    sums_out[...] = total
    core_copy.wait_send()
    pair_copy.wait_send()
    shard_copy.wait_send()
    for c in range(2):

        @pl.when(jnp.logical_not((core == c) & (pair_chip == chip)))
        def pair_sent(c=c):
            p_copies[c].wait_send()

    enc_copy.wait_send()
    for copy in enc_line + f_copies + f_pairs + t_copies + h_copies + s_fsdp:
        copy.wait_send()

    def sent(k, unused):
        s_copy(k).wait_send()
        return unused

    lax.fori_loop(1, group, sent, 0)

    def rows_sent(slot, unused):
        core_rows_copy((1 - core) * tp + slot).wait_send()

        @pl.when(slot != chip)
        def left():
            owner_copy(core * tp + slot).wait_send()

        return unused

    lax.fori_loop(0, tp, rows_sent, 0)


def backward_group(
    prefix,
    enc_parts,
    packed,
    gathered,
    rows,
    returned,
    weight,
    qkv,
    wide,
    logs,
    tokens,
    steps,
    gain,
    bias,
    after,
    encoder,
    stats,
    span,
    tp,
    fsdp,
):
    batches, chunk, width = tokens.shape
    group = returned.shape[1]
    length = group * chunk
    share = encoder.shape[1] // group
    piece = width // fsdp
    count = packed.shape[3]
    tail = packed.shape[4:]
    bf16, f32 = jnp.bfloat16, jnp.float32
    struct = jax.ShapeDtypeStruct
    inside = pl.BlockSpec(memory_space=pltpu.VMEM)
    outside = pl.BlockSpec(memory_space=pl.ANY)
    dma = pltpu.SemaphoreType.DMA
    vmem = pltpu.VMEM
    parts = group * fsdp
    return pl.pallas_call(
        functools.partial(backward_kernel, span=span, tp=tp, fsdp=fsdp),
        in_specs=[pl.BlockSpec(memory_space=pltpu.SMEM)] + [outside] * 4 + [inside] * 5 + [outside] + [inside] * 6,
        out_specs=[inside] * 10,
        out_shape=[
            struct((batches, chunk, width), f32),
            struct((batches, share, width), f32),
            struct((3, piece, piece), f32),
            struct((piece, piece), f32),
            struct((2, piece, piece), f32),
            struct((piece, piece), f32),
            struct((piece, piece), f32),
            struct((piece, width), f32),
            struct((width, piece), f32),
            struct((16, width), f32),
        ],
        scratch_shapes=[
            vmem((group, 2, 3 * HEAD_DIM, chunk), bf16),
            vmem((tp, chunk, width), bf16),
            vmem((tp, chunk, width), bf16),
            vmem((tp, chunk, width), bf16),
            vmem((2, chunk, width), bf16),
            vmem((batches, 2, chunk, width), bf16),
            vmem((2, length, 2 * HEAD_DIM), bf16),
            vmem((2, length, 2 * HEAD_DIM), bf16),
            vmem((2, length, 2 * HEAD_DIM), bf16),
            vmem((2, 1, length), f32),
            vmem((2, length, 2 * HEAD_DIM), f32),
            vmem((2, chunk, width), bf16),
            vmem((2, width, width), bf16),
            vmem((batches, tp * share, 2 * width), bf16),
            vmem((batches, tp * share, 2 * width), bf16),
            vmem((tp, batches, share, 2 * width), bf16),
            vmem((tp - 1, batches, share, 2 * width), bf16),
            vmem((group // tp, fsdp, tp, 2) + tail, bf16),
            vmem((fsdp, tp, 2) + tail, bf16),
            vmem((fsdp, tp, count) + tail, bf16),
            vmem((fsdp, tp, count + 2) + tail, bf16),
            vmem((fsdp - 1, tp, count + 2) + tail, bf16),
            vmem((tp, count + 2) + tail, bf16),
            vmem((tp - 1, count + 2) + tail, bf16),
            vmem((2, count + 2) + tail, f32),
            vmem((fsdp, 6 * HEAD_DIM, piece), f32),
            vmem((fsdp - 1, 6 * HEAD_DIM, piece), f32),
            vmem((6 * HEAD_DIM, piece), bf16),
            vmem((2, 6 * HEAD_DIM, piece), bf16),
            vmem((16, width), f32),
            vmem((group + fsdp, 16, width), f32),
            vmem((16, width), f32),
            dma((tp,)),
            dma((tp,)),
            dma((tp,)),
            dma((tp,)),
            dma((tp,)),
            dma((batches, 2)),
            dma((2,)),
            dma((4,)),
            dma((4,)),
            dma((2 * fsdp,)),
            dma((2 * fsdp,)),
            dma((tp,)),
            dma((tp,)),
            dma((fsdp,)),
            dma((fsdp,)),
            dma((2,)),
            dma((2,)),
            dma((group + fsdp,)),
            dma((group + fsdp,)),
            dma((2 + parts,)),
            dma((2,)),
        ],
        compiler_params=pltpu.CompilerParams(
            vmem_limit_bytes=VMEM_LIMIT, collective_id=2, has_side_effects=True
        ),
        cost_estimate=pl.CostEstimate(
            flops=100_000_000_000, bytes_accessed=40_000_000, transcendentals=20_000_000
        ),
        name="backward_group",
    )(
        prefix,
        enc_parts,
        packed,
        gathered,
        rows,
        returned,
        weight,
        qkv,
        wide,
        logs,
        tokens,
        steps,
        gain,
        bias,
        after,
        encoder,
        stats,
    )


def pack_kernel(
    scalars,
    table_ref,
    qkv_ref,
    query_ref,
    pair_ref,
    self_ref,
    cross_ref,
    up_ref,
    down_ref,
    half_ref,
    mine_ref,
    steps_ref,
    blocks,
):
    piece = query_ref.shape[0]
    blocks[0] = query_ref[...].T
    for n in range(2):
        blocks[1 + n] = pair_ref[n].T
    blocks[3] = self_ref[...]
    blocks[4] = cross_ref[...]
    for n in range(4):
        blocks[5 + n] = up_ref[:, n * piece : (n + 1) * piece].T
        blocks[9 + n] = down_ref[n * piece : (n + 1) * piece, :]
    half = piece // 2
    core = lax.axis_index("ctx")
    half_ref[...] = blocks[:, pl.ds(pl.multiple_of(core * half, half), half), :]
    for which in range(3):
        flipped = qkv_ref[which].T
        for head in range(2):
            mine_ref[(3 * head + which) * HEAD_DIM : (3 * head + which + 1) * HEAD_DIM, :] = (
                flipped[head * HEAD_DIM : (head + 1) * HEAD_DIM]
            )
    table = table_ref[...].astype(jnp.float32)
    rows = lax.broadcasted_iota(jnp.int32, table.shape, 0)
    for seq in range(steps_ref.shape[0]):
        chosen = jnp.where(rows == scalars[seq], table, 0.0)
        steps_ref[seq] = jnp.sum(chosen, 0, keepdims=True)


def pack_weights(scalars, table, self_qkv, cross_q, cross_kv, self_out, cross_out, up, down):
    piece = cross_q.shape[0]
    width = table.shape[1]
    batches = scalars.shape[0]
    bf16 = jnp.bfloat16
    struct = jax.ShapeDtypeStruct
    inside = pl.BlockSpec(memory_space=pltpu.VMEM)
    return pl.pallas_call(
        pack_kernel,
        in_specs=[pl.BlockSpec(memory_space=pltpu.SMEM)] + [inside] * 8,
        out_specs=[inside] * 3,
        out_shape=[
            struct((13, piece // 2, piece), bf16),
            struct((3 * piece, piece), bf16),
            struct((batches, 1, width), jnp.float32),
        ],
        scratch_shapes=[pltpu.VMEM((13, piece, piece), bf16)],
        name="pack_weights",
    )(scalars, table, self_qkv, cross_q, cross_kv, self_out, cross_out, up, down)


def collect_kernel(*refs, large, small, entries):
    ins, outs = refs[: large + small + 1], refs[large + small + 1 :]
    for n in range(large):
        outs[n][...] = ins[n][...]

    @pl.when(pl.program_id(0) == 0)
    def once():
        for n in range(large, large + small):
            outs[n][...] = ins[n][...]
        sums = ins[large + small]
        gain_ref, bias_ref, feed_ref, norms_ref = outs[large + small :]
        for n, row in enumerate((8, 4, 6)):
            gain_ref[n : n + 1, :] = sums[row : row + 1, :]
        for n, row in enumerate((9, 5)):
            bias_ref[n : n + 1, :] = sums[row : row + 1, :]
        feed_ref[...] = sums[7:8, :]
        totals = jnp.sum(sums[0:4, :], 1, keepdims=True) * (1.0 / entries)
        one = lax.broadcasted_iota(jnp.int32, (4, 128), 0) == lax.broadcasted_iota(
            jnp.int32, (4, 128), 1
        )
        norms_ref[...] = jnp.sqrt(jnp.sum(jnp.where(one, totals, 0.0), 0, keepdims=True))[:, :4]


def collect(large, small, sums, entries):
    width = sums.shape[1]
    f32 = jnp.float32
    struct = jax.ShapeDtypeStruct
    rest = [struct(v.shape, v.dtype) for v in small]
    extra = [struct((3, width), f32), struct((2, width), f32), struct((1, width), f32)]
    extra = extra + [struct((1, 4), f32)]
    still = lambda v: pl.BlockSpec(v.shape, lambda i, rank=len(v.shape): (0,) * rank)
    steps = 2
    moving = lambda v: pl.BlockSpec(
        (1, v.shape[0] * v.shape[1] // steps, v.shape[2]),
        lambda i, per=steps // v.shape[0]: (i // per, i % per, 0),
    )
    return pl.pallas_call(
        functools.partial(collect_kernel, large=len(large), small=len(small), entries=entries),
        grid=(steps,),
        in_specs=[moving(v) for v in large] + [still(v) for v in small] + [still(sums)],
        out_specs=[moving(v) for v in large] + [still(v) for v in rest + extra],
        out_shape=[struct(v.shape, v.dtype) for v in large] + rest + extra,
        name="collect",
    )(*large, *small, sums)


def local_heads(
    tokens,
    timesteps,
    time_table,
    prefix,
    encoder,
    self_qkv,
    cross_q,
    cross_kv,
    self_out,
    cross_out,
    ffn_up,
    ffn_down,
    norm_gain,
    norm_bias,
    cotangent,
):
    batches, chunk, width = tokens.shape
    group = 8
    length = group * chunk
    span = 1024
    own_half, mine, embedded = pack_weights(
        timesteps,
        time_table,
        self_qkv,
        cross_q,
        cross_kv,
        self_out,
        cross_out,
        ffn_up,
        ffn_down,
    )
    gathered = lax.all_gather(own_half, "tp", axis=0, tiled=False)
    gathered = lax.all_gather(gathered, ("fsdp", "ctx"), axis=0, tiled=False)
    gathered = gathered.reshape((4, 2, 4) + own_half.shape)
    rows, qkv, wide, logs, contexts, weight = forward_group(
        prefix, tokens, embedded, norm_gain, norm_bias, mine, span, group, 4, 4
    )
    final, grad_after, returned, enc_parts, stats, packed = middle(
        gathered,
        tokens,
        embedded,
        encoder,
        cotangent,
        norm_gain,
        norm_bias,
        contexts,
        4,
        4,
    )
    outs = backward_group(
        prefix,
        enc_parts,
        packed,
        gathered,
        rows,
        returned,
        weight,
        qkv,
        wide,
        logs,
        tokens,
        embedded,
        norm_gain,
        norm_bias,
        grad_after,
        encoder,
        stats,
        span,
        4,
        4,
    )
    sums = outs[9]
    entries = (
        tokens.shape[0]
        * tokens.shape[1]
        * tokens.shape[2]
        * lax.axis_size("fsdp")
        * lax.axis_size("ctx")
        * lax.axis_size("tp")
    )
    results = collect((final, *outs[:2]), outs[2:9], sums, entries)
    return (*results[:12], results[12].reshape(width), results[13].reshape(4))


def solution(mesh):
    placed = (
        P("fsdp", ("ctx", "tp"), None),
        P("fsdp"),
        P(),
        P("fsdp"),
        P("fsdp", None, None),
        P(None, "fsdp", "tp"),
        P("fsdp", "tp"),
        P(None, "fsdp", "tp"),
        P("tp", "fsdp"),
        P("tp", "fsdp"),
        P("fsdp", "tp"),
        P("tp", "fsdp"),
        P(),
        P(),
        P("fsdp", ("ctx", "tp"), None),
    )
    heads_fit = dict(mesh.shape) == {"fsdp": 4, "ctx": 2, "tp": 4}
    return jax.shard_map(
        local_heads if heads_fit else local,
        mesh=mesh,
        in_specs=placed,
        out_specs=(
            P("fsdp", ("ctx", "tp"), None),
            P("fsdp", ("ctx", "tp"), None),
            P("fsdp", ("ctx", "tp"), None),
            P(None, "fsdp", "tp"),
            P("fsdp", "tp"),
            P(None, "fsdp", "tp"),
            P("tp", "fsdp"),
            P("tp", "fsdp"),
            P("fsdp", "tp"),
            P("tp", "fsdp"),
            P(),
            P(),
            P(),
            P(),
        ),
        check_vma=False,
    )
```

```python
import functools
import math

import jax
import jax.numpy as jnp
from jax import lax
from jax.experimental import pallas as pl
from jax.experimental.pallas import tpu as pltpu
from jax.sharding import PartitionSpec as P

HEAD_DIM = 64


EPS = 1e-05
NEG = -1e30
ROOT_HALF = 1.0 / math.sqrt(2.0)
INV_ROOT_TWO_PI = 1.0 / math.sqrt(2.0 * math.pi)
VMEM_LIMIT = 63 * 2**20


def norm_rows(hidden, scaling, offsets):
    centre = hidden - jnp.mean(hidden, -1, keepdims=True)
    inverse = lax.rsqrt(jnp.mean(centre * centre, -1, keepdims=True) + EPS)
    unit_rows = centre * inverse
    return (unit_rows * scaling + offsets, unit_rows, inverse)


def norm_back(upstream, unit_rows, inverse, scaling):
    scaled = upstream * scaling
    result = inverse * (
        scaled
        - jnp.mean(scaled, -1, keepdims=True)
        - unit_rows * jnp.mean(scaled * unit_rows, -1, keepdims=True)
    )
    return (result, jnp.sum(upstream * unit_rows, (0, 1)), jnp.sum(upstream, (0, 1)))


def gelu_parts(inputs):
    normal_cdf = 0.5 * (1.0 + lax.erf(inputs * ROOT_HALF))
    return (
        inputs * normal_cdf,
        normal_cdf + inputs * jnp.exp(-0.5 * inputs * inputs) * INV_ROOT_TWO_PI,
    )


def spread_rows(rows):
    return lax.all_gather(rows, "tp", axis=1, tiled=True)


def spread_grads(grad_rows):
    return lax.all_gather(grad_rows, "tp", axis=1, tiled=True)


def finish_branch(local_in, local_weight):
    return lax.psum_scatter(
        jnp.einsum("scw,wd->scd", local_in, local_weight, preferred_element_type=jnp.float32),
        "tp",
        scatter_dimension=1,
        tiled=True,
    )


def finish_grad(local_grad, local_weight):
    return lax.psum_scatter(
        jnp.einsum("scw,dw->scd", local_grad, local_weight, preferred_element_type=jnp.float32),
        "tp",
        scatter_dimension=1,
        tiled=True,
    )


def block_scores(queries, key_block, query_pos, key_pos, lengths, factor):
    scores = (
        jnp.einsum("sqhe,skhe->sqhk", queries, key_block, preferred_element_type=jnp.float32)
        * factor
    )
    visible = (key_pos[None, None, :] <= query_pos[None, :, None]) | (
        key_pos[None, None, :] < lengths[:, None, None]
    )
    return jnp.where(visible[:, :, None, :], scores, NEG)


def attend_forward(queries, key_rows, value_rows, query_pos, lengths, key_span, factor):
    length = key_rows.shape[1]

    def attend_advance(running, offset):
        highest, totals, summed = running
        key_block = lax.dynamic_slice_in_dim(key_rows, offset, key_span, 1)
        value_block = lax.dynamic_slice_in_dim(value_rows, offset, key_span, 1)
        scores = block_scores(
            queries, key_block, query_pos, offset + lax.iota(jnp.int32, key_span), lengths, factor
        )
        new_high = jnp.maximum(highest, jnp.max(scores, -1))
        weights = jnp.exp(scores - new_high[..., None])
        fading = jnp.exp(highest - new_high)
        totals = totals * fading + jnp.sum(weights, -1)
        summed = summed * fading[..., None] + jnp.einsum(
            "sqhk,skhe->sqhe",
            weights.astype(jnp.bfloat16),
            value_block,
            preferred_element_type=jnp.float32,
        )
        return ((new_high, totals, summed), None)

    stat_shape = queries.shape[:3]
    initial = (
        jnp.full(stat_shape, NEG, jnp.float32),
        jnp.zeros(stat_shape, jnp.float32),
        jnp.zeros(queries.shape, jnp.float32),
    )
    offsets = jnp.arange(length // key_span, dtype=jnp.int32) * key_span
    (highest, totals, summed), unused = lax.scan(attend_advance, initial, offsets)
    return (summed / totals[..., None], highest + jnp.log(totals))


def attend_block(
    queries,
    grad_out,
    log_rows,
    delta_rows,
    key_block,
    value_block,
    query_pos,
    key_pos,
    lengths,
    factor,
):
    scores = block_scores(queries, key_block, query_pos, key_pos, lengths, factor)
    probs = jnp.exp(scores - log_rows[..., None])
    grad_probs = jnp.einsum(
        "sqhe,skhe->sqhk", grad_out, value_block, preferred_element_type=jnp.float32
    )
    grad_scores = (probs * (grad_probs - delta_rows[..., None])).astype(jnp.bfloat16)
    return (probs.astype(jnp.bfloat16), grad_scores)


def key_sweep(
    queries,
    grad_out,
    log_rows,
    delta_rows,
    key_rows,
    value_rows,
    query_pos,
    lengths,
    key_span,
    factor,
):
    batches, row_count, head_count, head_depth = queries.shape
    length = key_rows.shape[1]

    def key_advance(grad_query, offset):
        key_block = lax.dynamic_slice_in_dim(key_rows, offset, key_span, 1)
        value_block = lax.dynamic_slice_in_dim(value_rows, offset, key_span, 1)
        key_pos = offset + lax.iota(jnp.int32, key_span)
        probs_low, grad_scores = attend_block(
            queries,
            grad_out,
            log_rows,
            delta_rows,
            key_block,
            value_block,
            query_pos,
            key_pos,
            lengths,
            factor,
        )
        grad_query = (
            grad_query
            + jnp.einsum(
                "sqhk,skhe->sqhe", grad_scores, key_block, preferred_element_type=jnp.float32
            )
            * factor
        )
        grad_key = (
            jnp.einsum("sqhk,sqhe->kshe", grad_scores, queries, preferred_element_type=jnp.float32)
            * factor
        )
        grad_value = jnp.einsum(
            "sqhk,sqhe->kshe", probs_low, grad_out, preferred_element_type=jnp.float32
        )
        return (grad_query, (grad_key, grad_value))

    offsets = jnp.arange(length // key_span, dtype=jnp.int32) * key_span
    grad_query, stacked = lax.scan(key_advance, jnp.zeros(queries.shape, jnp.float32), offsets)
    flat_shape = (length, batches, head_count * head_depth)
    return (grad_query, stacked[0].reshape(flat_shape), stacked[1].reshape(flat_shape))


def local(
    tokens,
    timesteps,
    time_table,
    prefix,
    encoder,
    self_qkv,
    cross_q,
    cross_kv,
    self_out,
    cross_out,
    ffn_up,
    ffn_down,
    norm_gain,
    norm_bias,
    cotangent,
):
    proj_self, proj_query, proj_pair, back_self, back_cross, expand_full, shrink_full = (
        lax.all_gather(self_qkv, "fsdp", axis=1, tiled=True),
        lax.all_gather(cross_q, "fsdp", axis=0, tiled=True),
        lax.all_gather(cross_kv, "fsdp", axis=1, tiled=True),
        lax.all_gather(self_out, "fsdp", axis=1, tiled=True),
        lax.all_gather(cross_out, "fsdp", axis=1, tiled=True),
        lax.all_gather(ffn_up, "fsdp", axis=0, tiled=True),
        lax.all_gather(ffn_down, "fsdp", axis=1, tiled=True),
    )
    batches = tokens.shape[0]
    model_width = tokens.shape[2]
    local_width = proj_query.shape[1]
    head_count = local_width // HEAD_DIM
    factor = HEAD_DIM ** (-0.5)
    ctx_index = lax.axis_index("ctx")
    local_stack = jnp.transpose(proj_self, (1, 0, 2)).reshape(model_width, 3 * local_width)
    steps_onehot = (timesteps[:, None] == lax.iota(jnp.int32, time_table.shape[0])[None, :]).astype(
        jnp.bfloat16
    )
    embedded = jnp.dot(steps_onehot, time_table, preferred_element_type=jnp.float32)
    start_sum = tokens.astype(jnp.float32) + embedded[:, None, :]
    normed_one, unit_one, inverse_one = norm_rows(start_sum, norm_gain[0], norm_bias[0])
    rows_self = spread_rows(normed_one.astype(jnp.bfloat16))
    row_count = rows_self.shape[1]
    head_shape = (batches, row_count, head_count, HEAD_DIM)
    projected = jnp.einsum(
        "scd,kdw->kscw", rows_self, proj_self, preferred_element_type=jnp.float32
    ).astype(jnp.bfloat16)
    queries, key_local, value_local = (projected[0], projected[1], projected[2])
    key_all, value_all = (
        lax.all_gather(key_local, "ctx", axis=1, tiled=True),
        lax.all_gather(value_local, "ctx", axis=1, tiled=True),
    )
    length = key_all.shape[1]
    key_span = min(512, length)
    query_pos = ctx_index * row_count + lax.iota(jnp.int32, row_count)
    keys_four = key_all.reshape(batches, length, head_count, HEAD_DIM)
    values_four = value_all.reshape(batches, length, head_count, HEAD_DIM)
    queries_four = queries.reshape(head_shape)
    attended, log_total = attend_forward(
        queries_four, keys_four, values_four, query_pos, prefix, key_span, factor
    )
    context_one = attended.reshape(batches, row_count, local_width).astype(jnp.bfloat16)
    branch_one = finish_branch(context_one, back_self)
    after_one = start_sum + branch_one
    normed_two, unit_two, inverse_two = norm_rows(after_one, norm_gain[1], norm_bias[1])
    rows_cross = spread_rows(normed_two.astype(jnp.bfloat16))
    cross_queries = jnp.einsum(
        "scd,dw->scw", rows_cross, proj_query, preferred_element_type=jnp.float32
    ).astype(jnp.bfloat16)
    enc_pair = jnp.einsum(
        "sed,kdw->ksew", encoder, proj_pair, preferred_element_type=jnp.float32
    ).astype(jnp.bfloat16)
    enc_count = encoder.shape[1]
    cross_keys = enc_pair[0].reshape(batches, enc_count, head_count, HEAD_DIM)
    cross_values = enc_pair[1].reshape(batches, enc_count, head_count, HEAD_DIM)
    cross_four = cross_queries.reshape(head_shape)
    cross_probs = jax.nn.softmax(
        jnp.einsum("sqhe,skhe->sqhk", cross_four, cross_keys, preferred_element_type=jnp.float32)
        * factor,
        axis=-1,
    )
    cross_low = cross_probs.astype(jnp.bfloat16)
    context_two = (
        jnp.einsum("sqhk,skhe->sqhe", cross_low, cross_values, preferred_element_type=jnp.float32)
        .reshape(batches, row_count, local_width)
        .astype(jnp.bfloat16)
    )
    branch_two = finish_branch(context_two, back_cross)
    after_two = after_one + branch_two
    normed_three, unit_three, inverse_three = norm_rows(after_two, norm_gain[2], norm_bias[2])
    rows_ffn = spread_rows(normed_three.astype(jnp.bfloat16))
    pre_act = jnp.einsum("scd,df->scf", rows_ffn, expand_full, preferred_element_type=jnp.float32)
    activated, slopes = gelu_parts(pre_act)
    hidden_low = activated.astype(jnp.bfloat16)
    branch_three = finish_branch(hidden_low, shrink_full)
    final_sum = after_two + branch_three
    grad_three = spread_grads(cotangent)
    grad_shrink = jnp.einsum(
        "scf,scd->fd", hidden_low, grad_three, preferred_element_type=jnp.float32
    )
    grad_pre = (
        jnp.einsum("scd,fd->scf", grad_three, shrink_full, preferred_element_type=jnp.float32)
        * slopes
    ).astype(jnp.bfloat16)
    grad_expand = jnp.einsum("scd,scf->df", rows_ffn, grad_pre, preferred_element_type=jnp.float32)
    back_three, gain_three, shift_three = norm_back(
        finish_grad(grad_pre, expand_full), unit_three, inverse_three, norm_gain[2]
    )
    grad_after_two = cotangent.astype(jnp.float32) + back_three
    grad_two = spread_grads(grad_after_two.astype(jnp.bfloat16))
    grad_back_cross = jnp.einsum(
        "scw,scd->wd", context_two, grad_two, preferred_element_type=jnp.float32
    )
    grad_context_two = jnp.einsum(
        "scd,wd->scw", grad_two, back_cross, preferred_element_type=jnp.float32
    ).astype(jnp.bfloat16)
    grad_cross_four = grad_context_two.reshape(head_shape)
    grad_cross_probs = jnp.einsum(
        "sqhe,skhe->sqhk", grad_cross_four, cross_values, preferred_element_type=jnp.float32
    )
    grad_cross_scores = (
        cross_probs
        * (grad_cross_probs - jnp.sum(cross_probs * grad_cross_probs, -1, keepdims=True))
    ).astype(jnp.bfloat16)
    grad_cross_q = (
        (
            jnp.einsum(
                "sqhk,skhe->sqhe", grad_cross_scores, cross_keys, preferred_element_type=jnp.float32
            )
            * factor
        )
        .reshape(batches, row_count, local_width)
        .astype(jnp.bfloat16)
    )
    part_keys = (
        jnp.einsum(
            "sqhk,sqhe->skhe", grad_cross_scores, cross_four, preferred_element_type=jnp.float32
        )
        * factor
    ).reshape(batches, enc_count, local_width)
    part_values = jnp.einsum(
        "sqhk,sqhe->skhe", cross_low, grad_cross_four, preferred_element_type=jnp.float32
    ).reshape(batches, enc_count, local_width)
    enc_keys, enc_values = (
        lax.psum_scatter(part_keys, "ctx", scatter_dimension=1, tiled=True),
        lax.psum_scatter(part_values, "ctx", scatter_dimension=1, tiled=True),
    )
    enc_keys = enc_keys.astype(jnp.bfloat16)
    enc_values = enc_values.astype(jnp.bfloat16)
    enc_share = enc_keys.shape[1]
    enc_rows = lax.dynamic_slice_in_dim(encoder, ctx_index * enc_share, enc_share, 1)
    grad_pair = jnp.stack(
        [
            jnp.einsum("sed,sew->dw", enc_rows, enc_keys, preferred_element_type=jnp.float32),
            jnp.einsum("sed,sew->dw", enc_rows, enc_values, preferred_element_type=jnp.float32),
        ]
    )
    encoder_grad = lax.psum_scatter(
        jnp.einsum("sew,dw->sed", enc_keys, proj_pair[0], preferred_element_type=jnp.float32)
        + jnp.einsum("sew,dw->sed", enc_values, proj_pair[1], preferred_element_type=jnp.float32),
        "tp",
        scatter_dimension=1,
        tiled=True,
    )
    grad_query_proj = jnp.einsum(
        "scd,scw->dw", rows_cross, grad_cross_q, preferred_element_type=jnp.float32
    )
    back_two, gain_two, shift_two = norm_back(
        finish_grad(grad_cross_q, proj_query), unit_two, inverse_two, norm_gain[1]
    )
    grad_after_one = grad_after_two + back_two
    grad_one = spread_grads(grad_after_one.astype(jnp.bfloat16))
    grad_back_self = jnp.einsum(
        "scw,scd->wd", context_one, grad_one, preferred_element_type=jnp.float32
    )
    grad_context_one = jnp.einsum(
        "scd,wd->scw", grad_one, back_self, preferred_element_type=jnp.float32
    ).astype(jnp.bfloat16)
    grad_ctx_four = grad_context_one.reshape(head_shape)
    delta_rows = jnp.sum(grad_ctx_four.astype(jnp.float32) * attended, -1)
    grad_query, grad_key_all, grad_value_all = key_sweep(
        queries_four,
        grad_ctx_four,
        log_total,
        delta_rows,
        keys_four,
        values_four,
        query_pos,
        prefix,
        key_span,
        factor,
    )
    own_keys, own_values = (
        lax.psum_scatter(grad_key_all, "ctx", scatter_dimension=0, tiled=True),
        lax.psum_scatter(grad_value_all, "ctx", scatter_dimension=0, tiled=True),
    )
    own_keys = jnp.transpose(own_keys, (1, 0, 2))
    own_values = jnp.transpose(own_values, (1, 0, 2))
    grad_joined = jnp.concatenate(
        [grad_query.reshape(batches, row_count, local_width), own_keys, own_values], -1
    ).astype(jnp.bfloat16)
    grad_proj_self = jnp.transpose(
        jnp.einsum(
            "scd,scw->dw", rows_self, grad_joined, preferred_element_type=jnp.float32
        ).reshape(model_width, 3, local_width),
        (1, 0, 2),
    )
    back_one, gain_one, shift_one = norm_back(
        finish_grad(grad_joined, local_stack), unit_one, inverse_one, norm_gain[0]
    )
    input_grad = grad_after_one + back_one
    shard_grads = (
        lax.psum_scatter(grad_proj_self, "fsdp", scatter_dimension=1, tiled=True),
        lax.psum_scatter(grad_query_proj, "fsdp", scatter_dimension=0, tiled=True),
        lax.psum_scatter(grad_pair, "fsdp", scatter_dimension=1, tiled=True),
        lax.psum_scatter(grad_back_self, "fsdp", scatter_dimension=1, tiled=True),
        lax.psum_scatter(grad_back_cross, "fsdp", scatter_dimension=1, tiled=True),
        lax.psum_scatter(grad_expand, "fsdp", scatter_dimension=0, tiled=True),
        lax.psum_scatter(grad_shrink, "fsdp", scatter_dimension=1, tiled=True),
    )
    full_grads = lax.psum(
        (
            shard_grads[0],
            shard_grads[1],
            shard_grads[2],
            shard_grads[3],
            shard_grads[4],
            shard_grads[5],
            shard_grads[6],
        ),
        "ctx",
    )
    squares = jnp.stack(
        [
            jnp.sum(final_sum * final_sum),
            jnp.sum(branch_one * branch_one),
            jnp.sum(branch_two * branch_two),
            jnp.sum(branch_three * branch_three),
        ]
    )
    gain_grad, bias_grad, square_totals = lax.psum(
        (
            jnp.stack([gain_one, gain_two, gain_three]),
            jnp.stack([shift_one, shift_two, shift_three]),
            squares,
        ),
        ("fsdp", "ctx", "tp"),
    )
    entries = (
        tokens.shape[0]
        * tokens.shape[1]
        * tokens.shape[2]
        * lax.axis_size("fsdp")
        * lax.axis_size("ctx")
        * lax.axis_size("tp")
    )
    norms = jnp.sqrt(square_totals / entries)
    return (
        final_sum,
        input_grad,
        encoder_grad,
        full_grads[0],
        full_grads[1],
        full_grads[2],
        full_grads[3],
        full_grads[4],
        full_grads[5],
        full_grads[6],
        gain_grad,
        bias_grad[:2],
        bias_grad[2],
        norms,
    )


def dot_of(left, right, left_dim, right_dim):
    return lax.dot_general(
        left, right, (((left_dim,), (right_dim,)), ((), ())), preferred_element_type=jnp.float32
    )


def bounds(prefix, start, query_span, key_span):
    whole = jnp.maximum(prefix, start + 1) // key_span
    every = (jnp.maximum(prefix, start + query_span) + key_span - 1) // key_span
    return whole, every


def hide(scores, limit, offset):
    return jnp.where(lax.broadcasted_iota(jnp.int32, scores.shape, 0) < limit - offset, scores, NEG)


def low(value):
    return value.astype(jnp.bfloat16)


STRIP = 64


def in_strips(work, *values, strip=STRIP, axis=0):
    count = values[0].shape[axis] // strip
    cut = lambda v, n: lax.slice_in_dim(v, n * strip, (n + 1) * strip, axis=axis)
    parts = [work(*[cut(v, n) for v in values]) for n in range(count)]
    return tuple(jnp.concatenate(p, axis) for p in zip(*parts))


def gelu_strip(inputs):
    activated, slopes = gelu_parts(inputs)
    return low(activated), slopes


def rows_unit(hidden):
    centre = hidden - jnp.mean(hidden, -1, keepdims=True)
    inverse = lax.rsqrt(jnp.mean(centre * centre, -1, keepdims=True) + EPS)
    return centre * inverse, inverse


def rows_norm(hidden, scaling, offsets):
    def strip(rows):
        unit_rows, inverse = rows_unit(rows)
        return low(unit_rows * scaling + offsets), unit_rows, inverse

    return in_strips(strip, hidden)


def rows_back(upstream, unit_rows, inverse, scaling):
    sums = [jnp.zeros((8, upstream.shape[1]), jnp.float32)] * 2

    def strip(rows, units, inverses):
        scaled = rows * scaling
        for n, term in enumerate((rows * units, rows)):
            sums[n] = sums[n] + jnp.sum(term.reshape(-1, 8, term.shape[1]), 0)
        return (
            inverses
            * (
                scaled
                - jnp.mean(scaled, -1, keepdims=True)
                - units * jnp.mean(scaled * units, -1, keepdims=True)
            ),
        )

    (result,) = in_strips(strip, upstream, unit_rows, inverse)
    return result, jnp.sum(sums[0], 0, keepdims=True), jnp.sum(sums[1], 0, keepdims=True)


MESH = pl.DeviceIdType.MESH


def greet(group, tp, fsdp):
    here, core, chip = lax.axis_index("fsdp"), lax.axis_index("ctx"), lax.axis_index("tp")
    me = core * tp + chip
    barrier = pltpu.get_barrier_semaphore()
    for k in range(1, group):
        other = me ^ k
        pl.semaphore_signal(
            barrier, inc=1, device_id={"ctx": other // tp, "tp": other % tp}, device_id_type=MESH
        )
    for k in range(1, fsdp):
        pl.semaphore_signal(barrier, inc=1, device_id={"fsdp": here ^ k}, device_id_type=MESH)


def meet(group, fsdp):
    pl.semaphore_wait(pltpu.get_barrier_semaphore(), group - 1 + fsdp - 1)


def forward_kernel(
    prefix_ref,
    tokens_ref,
    step_ref,
    gain_ref,
    bias_ref,
    mine_ref,
    rows_out,
    qkv_ref,
    wide_ref,
    log_ref,
    ctx_ref,
    weight,
    rows_ref,
    other_ref,
    columns,
    pair_ref,
    keys_ref,
    values_ref,
    low_ref,
    landing,
    w_send,
    w_recv,
    v_send,
    v_recv,
    x_send,
    x_recv,
    c_send,
    c_recv,
    keep_sem,
    *,
    span,
    tp,
    fsdp,
):
    batches, chunk, width = tokens_ref.shape
    group = rows_ref.shape[0]
    length = group * chunk
    blocks, ratio = length // span, span // chunk
    wide_blocks = max(1, length // 2 // span)
    factor = HEAD_DIM**-0.5
    here, core, chip = lax.axis_index("fsdp"), lax.axis_index("ctx"), lax.axis_index("tp")
    me = core * tp + chip
    mine = chip // 2
    inner = (chip == 1) | (chip == 2)
    other_inner, other_outer = 2 - mine, 3 - 3 * mine
    greet(group, tp, fsdp)

    def send_to(source, target, send, recv, **place):
        return pltpu.make_async_remote_copy(
            src_ref=source,
            dst_ref=target,
            send_sem=send,
            recv_sem=recv,
            device_id=place,
            device_id_type=MESH,
        )

    def normalise(seq, target, at):
        start_sum = tokens_ref[seq].astype(jnp.float32) + step_ref[seq]
        target[at] = rows_norm(start_sum, gain_ref[0:1], bias_ref[0:1])[0]

    normalise(mine, rows_ref, me)
    normalise(1 - mine, other_ref, 0)
    meet(group, fsdp)

    v_core, v_chip = chip % 2, chip // 2 + 2 * core
    v_own = (v_core == core) & (v_chip == chip)
    v_copy = send_to(mine_ref, pair_ref, v_send.at[0], v_recv.at[0], ctx=v_core, tp=v_chip)

    @pl.when(v_own)
    def keep_pair():
        pair_ref[...] = mine_ref[...]

    @pl.when(jnp.logical_not(v_own))
    def send_pair():
        v_copy.start()

    comes = (chip // 2 != core) | (2 * (chip % 2) + core != chip)

    def w_copy(k):
        return send_to(pair_ref, columns.at[k], w_send.at[k], w_recv.at[k], fsdp=here ^ k)

    def x_copy(kind):
        block = rows_ref.at[me]
        near = rows_ref.at[core * tp + (chip ^ 1)]
        second = rows_ref.at[core * tp + other_inner]
        third = rows_ref.at[core * tp + other_outer]
        source, place, target = (
            (block, me, {"tp": chip ^ 1}),
            (other_ref.at[0], me, {"tp": other_inner}),
            (block, me, {"ctx": 1 - core}),
            (near, core * tp + (chip ^ 1), {"ctx": 1 - core}),
            (second, core * tp + other_inner, {"ctx": 1 - core}),
            (third, core * tp + other_outer, {"ctx": 1 - core}),
            (second, core * tp + other_inner, {"tp": chip ^ 1}),
            (third, core * tp + other_outer, {"tp": chip ^ 1}),
            (other_ref.at[0], me, {"tp": other_outer}),
        )[kind]
        return send_to(source, rows_ref.at[place], x_send.at[kind], x_recv.at[place], **target)

    def x_wait(place):
        send_to(
            rows_ref.at[place], rows_ref.at[place], x_send.at[0], x_recv.at[place], ctx=1 - core
        ).wait_recv()

    def arrive(number):
        x_wait(core * tp + (chip ^ 1, other_inner, other_outer)[number])
        if number:

            @pl.when(inner & (core == 0))
            def onward():
                x_copy(5 + number).start()

        x_copy(3 + number).start()


    @pl.when(core == 0)
    def first_half():
        x_copy(2).start()

        @pl.when(inner)
        def from_inner():
            x_copy(1).start()
            x_copy(0).start()

        @pl.when(jnp.logical_not(inner))
        def from_outer():
            x_copy(0).start()

    @pl.when(comes)
    def pair_here():
        v_copy.wait_recv()

    for k in range(1, fsdp):
        w_copy(k).start()
    values_ref[:, HEAD_DIM:, :] = jnp.ones_like(values_ref[:, HEAD_DIM:, :])

    def project(place, unused):
        rows = rows_ref[place]
        joined = low(dot_of(weight[...], rows, 1, 1))
        at = pl.ds(pl.multiple_of(place * chunk, chunk), chunk)
        for head in range(2):
            queries, keys, values = (
                joined[(3 * head + n) * HEAD_DIM : (3 * head + n + 1) * HEAD_DIM] for n in range(3)
            )
            qkv_ref[head, :HEAD_DIM, at] = queries * jnp.bfloat16(factor)
            qkv_ref[head, HEAD_DIM : 2 * HEAD_DIM, at] = keys
            qkv_ref[head, 2 * HEAD_DIM :, at] = values
            values_ref[head, :HEAD_DIM, at] = values
            keys_ref[head, at, :] = keys.T
        return unused

    @pl.when(core == 0)
    def first_lines():
        @pl.when(jnp.logical_not(inner))
        def then_other():
            x_copy(0).wait_send()
            x_copy(1).start()

        for number in range(3):
            arrive(number)

    @pl.when(core == 1)
    def second_lines():
        for place in range(tp):
            x_wait(place)
        for kind in (2, 1, 8, 0):
            x_copy(kind).start()

    piece = mine_ref.shape[1]
    for k in range(fsdp):
        if k:
            w_copy(k).wait_recv()
        part = columns[k] if k else pair_ref[...]
        for f in range(fsdp):

            @pl.when((here ^ k) == f)
            def place(f=f, part=part):
                weight[:, f * piece : (f + 1) * piece] = part

    lax.fori_loop(0, tp, project, 0)

    def c_copy(head, place):
        return send_to(
            low_ref.at[head, place],
            landing.at[head, me],
            c_send.at[head, place],
            c_recv.at[head, me],
            ctx=place // tp,
            tp=place % tp,
        )

    def c_wait(head, place):
        send_to(
            low_ref.at[head, place],
            landing.at[head, place],
            c_send.at[head, place],
            c_recv.at[head, place],
            ctx=place // tp,
            tp=place % tp,
        ).wait_recv()

    keep = pltpu.make_async_copy(rows_ref, rows_out, keep_sem)

    def attend(index, unused):
        block, head = (index // 2) ^ (1 - mine), index % 2

        @pl.when((core == 1) & (index == 3))
        def near_lines():
            arrive(0)

        @pl.when(index == 4)
        def second_half():
            @pl.when(core == 0)
            def wait_other():
                for place in range(tp, group):
                    x_wait(place)

            @pl.when(core == 1)
            def far_lines():
                arrive(1)
                arrive(2)

            def first_results(place, unused):
                @pl.when(place != me)
                def send():
                    for number in range(2):
                        c_copy(number, place).start()

                return unused

            lax.fori_loop(0, tp, first_results, 0)
            lax.fori_loop(tp, group, project, 0)
            keep.start()

        start = pl.multiple_of(block * span, span)
        queries = qkv_ref[head, :HEAD_DIM, pl.ds(start, span)]
        limit = jnp.maximum(
            prefix_ref[mine], start + 1 + lax.broadcasted_iota(jnp.int32, (1, span), 1)
        )

        def advance(offset, count, carry, columns=None):
            highest, total = carry
            first = 0 if columns is None else columns
            scores = dot_of(keys_ref[head, pl.ds(offset, count), :], queries[:, first:], 1, 0)
            if columns is not None:
                scores = hide(scores, limit[:, first:], offset)
            higher = jnp.maximum(highest, jnp.max(scores, axis=0, keepdims=True))
            weights = low(jnp.exp(scores - higher))
            fading = jnp.exp(highest - higher)
            total = total * fading + dot_of(
                values_ref[head, :, pl.ds(offset, count)], weights, 1, 0
            )
            return higher, total

        def whole_step(other, carry):
            return advance(pl.multiple_of(other * span, span), span, carry)

        def masked_step(other, carry):
            return advance(pl.multiple_of(other * span, span), span, carry, 0)

        def diagonal_step(other, carry):
            half = span // 2
            carry = advance(start, half, carry, 0)
            offset = pl.multiple_of(start + half, half)
            upper = advance(offset, half, tuple(v[:, half:] for v in carry), half)
            return tuple(jnp.concatenate([v[:, :half], u], 1) for v, u in zip(carry, upper))

        carry = (
            jnp.full((1, span), NEG, jnp.float32),
            jnp.zeros((values_ref.shape[1], span), jnp.float32),
        )
        carry = lax.fori_loop(0, block, whole_step, carry)
        carry = lax.fori_loop(block, wide_blocks, masked_step, carry)
        highest, total = lax.fori_loop(
            0, jnp.where(block >= wide_blocks, 1, 0), diagonal_step, carry
        )
        weight_sum = total[HEAD_DIM : HEAD_DIM + 1, :]
        attended = total[:HEAD_DIM, :] / weight_sum
        wide_ref[head, :, pl.ds(start, span)] = attended
        log_ref[head, :, pl.ds(start, span)] = highest + jnp.log(weight_sum)
        attended = low(attended)
        for part in range(ratio):
            place = block * ratio + part
            low_ref[head, place] = attended[:, part * chunk : (part + 1) * chunk]

            @pl.when((place != me) & (index >= 4))
            def send(place=place):
                c_copy(head, place).start()

        return unused

    lax.fori_loop(0, 2 * blocks, attend, 0)
    for head in range(2):

        def collect(k, unused, head=head):
            c_wait(head, me ^ k)
            ctx_ref[head, me ^ k] = landing[head, me ^ k]
            return unused

        lax.fori_loop(1, group, collect, 0)
        ctx_ref[head, me] = low_ref[head, me]
    for k in range(1, fsdp):
        w_copy(k).wait_send()

    @pl.when(jnp.logical_not(v_own))
    def pair_sent():
        v_copy.wait_send()

    for kind in range(1, 6):
        x_copy(kind).wait_send()

    @pl.when(inner | (core == 1))
    def own_sent():
        x_copy(0).wait_send()

    @pl.when(inner & (core == 0))
    def lines_sent():
        x_copy(6).wait_send()
        x_copy(7).wait_send()

    @pl.when(core == 1)
    def direct_sent():
        x_copy(8).wait_send()

    for head in range(2):

        def sent(k, unused, head=head):
            c_copy(head, me ^ k).wait_send()
            return unused

        lax.fori_loop(1, group, sent, 0)
    keep.wait()


def forward_group(prefix, tokens, steps, gain, bias, mine, span, group, tp, fsdp):
    batches, chunk, width = tokens.shape
    length = group * chunk
    bf16, f32 = jnp.bfloat16, jnp.float32
    struct = jax.ShapeDtypeStruct
    inside = pl.BlockSpec(memory_space=pltpu.VMEM)
    dma = pltpu.SemaphoreType.DMA
    return pl.pallas_call(
        functools.partial(forward_kernel, span=span, tp=tp, fsdp=fsdp),
        in_specs=[pl.BlockSpec(memory_space=pltpu.SMEM)] + [inside] * 5,
        out_specs=[pl.BlockSpec(memory_space=pl.ANY)] + [inside] * 5,
        out_shape=[
            struct((group, chunk, width), bf16),
            struct((2, 3 * HEAD_DIM, length), bf16),
            struct((2, HEAD_DIM, length), f32),
            struct((2, 1, length), f32),
            struct((2, group, HEAD_DIM, chunk), bf16),
            struct((6 * HEAD_DIM, width), bf16),
        ],
        scratch_shapes=[
            pltpu.VMEM((group, chunk, width), bf16),
            pltpu.VMEM((1, chunk, width), bf16),
            pltpu.VMEM((fsdp,) + mine.shape, bf16),
            pltpu.VMEM(mine.shape, bf16),
            pltpu.VMEM((2, length, HEAD_DIM), bf16),
            pltpu.VMEM((2, HEAD_DIM + 16, length), bf16),
            pltpu.VMEM((2, group, HEAD_DIM, chunk), bf16),
            pltpu.VMEM((2, group, HEAD_DIM, chunk), bf16),
            dma((fsdp,)),
            dma((fsdp,)),
            dma((1,)),
            dma((1,)),
            dma((9,)),
            dma((group,)),
            dma((2, group)),
            dma((2, group)),
            dma,
        ],
        compiler_params=pltpu.CompilerParams(
            vmem_limit_bytes=VMEM_LIMIT, collective_id=1, has_side_effects=True
        ),
        cost_estimate=pl.CostEstimate(
            flops=60_000_000_000, bytes_accessed=30_000_000, transcendentals=20_000_000
        ),
        name="forward_group",
    )(prefix, tokens, steps, gain, bias, mine)


QUERY, KEY, VALUE, SELF_OUT, CROSS_OUT, UP, DOWN = 0, 1, 2, 3, 4, 5, 9


def middle_kernel(
    gathered,
    tokens_ref,
    step_ref,
    enc_ref,
    cot_ref,
    gain_ref,
    bias_ref,
    ctx_ref,
    final_ref,
    after_ref,
    back_ref,
    enc_grad_ref,
    stats_ref,
    packed_ref,
    weights,
    hidden_all,
    pre_all,
    three_all,
    two_all,
    grad_two_all,
    grad_one_all,
    cross_all,
    query_all,
    context_all,
    queries,
    keys,
    values,
    probs,
    grad_heads,
    grad_keys,
    grad_values,
    back_rows,
    landing,
    d_send,
    d_recv,
    sem,
    *,
    tp,
    fsdp,
):
    batches, chunk, width = tokens_ref.shape
    group = landing.shape[1]
    core, chip = lax.axis_index("ctx"), lax.axis_index("tp")
    me = core * tp + chip
    mine = chip // 2
    greet(group, tp, fsdp)
    piece = gathered.shape[-1]
    factor = HEAD_DIM**-0.5
    heads = width // HEAD_DIM

    copies = [], []
    for f in range(width // piece):
        for c in range(group // tp):
            for t in range(tp):
                head = t * (group // tp) + c
                for n, blocks in enumerate((pl.ds(0, UP), pl.ds(UP, weights.shape[0] - UP))):
                    copies[n].append(
                        pltpu.make_async_copy(
                            gathered.at[f, c, t, blocks],
                            weights.at[
                                blocks, pl.ds(head * HEAD_DIM, HEAD_DIM), pl.ds(f * piece, piece)
                            ],
                            sem.at[n, (f * group // tp + c) * tp + t],
                        )
                    )
    for copy in copies[0] + copies[1]:
        copy.start()
    stats_ref[...] = jnp.zeros_like(stats_ref)
    for copy in copies[0]:
        copy.wait()

    owners = [(2 * (2 * z + c) + n, n, c * tp + z) for z in (0, 1) for c in (0, 1) for n in (0, 1)]

    def d_copy(turn, seq, head, number, owner):
        return pltpu.make_async_remote_copy(
            src_ref=back_rows.at[turn, pl.ds(head * HEAD_DIM, HEAD_DIM)],
            dst_ref=landing.at[number, me],
            send_sem=d_send.at[turn, head],
            recv_sem=d_recv.at[number, me],
            device_id={"ctx": owner // tp, "tp": owner % tp + 2 * seq},
            device_id_type=MESH,
        )

    def one_sequence(turn, unused):
        seq = jnp.where(turn == 0, 1 - mine, mine)
        at = pl.ds(pl.multiple_of(seq * chunk, chunk), chunk)
        for head, number, owner in owners:
            context_all[head * HEAD_DIM : (head + 1) * HEAD_DIM, at] = ctx_ref[number, owner + 2 * seq]
        start_sum = tokens_ref[seq].astype(jnp.float32) + step_ref[seq]
        branch_one = dot_of(context_all[:, at], weights[SELF_OUT], 0, 0)
        after_one = start_sum + branch_one
        stats_ref[1:2, :] += jnp.sum(branch_one * branch_one, 0, keepdims=True)
        normed_two, unit_two, inverse_two = rows_norm(after_one, gain_ref[1:2], bias_ref[1:2])
        two_all[at, :] = normed_two
        queries[...] = low(dot_of(weights[QUERY], normed_two, 1, 1))
        keys[...] = low(dot_of(weights[KEY], enc_ref[seq], 1, 1))
        values[...] = low(dot_of(weights[VALUE], enc_ref[seq], 1, 1))

        def attend(head, unused):
            rows = pl.ds(pl.multiple_of(head * HEAD_DIM, HEAD_DIM), HEAD_DIM)
            scores = dot_of(keys[rows, :].T, queries[rows, :], 1, 0) * factor

            def strip(columns):
                powers = jnp.exp(columns - jnp.max(columns, 0, keepdims=True))
                return (powers / jnp.sum(powers, 0, keepdims=True),)

            (attn,) = in_strips(strip, scores, strip=128, axis=1)
            probs[head] = attn
            cross_all[rows, at] = low(dot_of(values[rows, :], low(attn), 1, 0))
            return unused

        lax.fori_loop(0, heads, attend, 0, unroll=8)
        branch_two = dot_of(cross_all[:, at], weights[CROSS_OUT], 0, 0)
        after_two = after_one + branch_two
        stats_ref[2:3, :] += jnp.sum(branch_two * branch_two, 0, keepdims=True)
        normed_three, unit_three, inverse_three = rows_norm(after_two, gain_ref[2:3], bias_ref[2:3])
        three_all[at, :] = normed_three
        grad_three = cot_ref[seq]

        @pl.when(turn == 0)
        def feed_weights():
            for copy in copies[1]:
                copy.wait()


        def feed(part, carry):
            branch, grad = carry
            up, down = weights[UP + part], weights[DOWN + part]
            inputs = dot_of(up, normed_three, 1, 1)
            hidden, slopes = in_strips(gelu_strip, inputs, strip=32)
            branch = branch + dot_of(hidden, down, 0, 0)
            hidden_all[part, :, at] = hidden
            grad_pre = low(dot_of(down, grad_three, 1, 1) * slopes)
            pre_all[part, :, at] = grad_pre
            return branch, grad + dot_of(grad_pre, up, 0, 0)

        blank = jnp.zeros((chunk, width), jnp.float32)
        branch_three, grad_norm = lax.fori_loop(0, DOWN - UP, feed, (blank, blank), unroll=4)
        final_sum = after_two + branch_three
        final_ref[seq] = final_sum
        stats_ref[0:1, :] += jnp.sum(final_sum * final_sum, 0, keepdims=True)
        stats_ref[3:4, :] += jnp.sum(branch_three * branch_three, 0, keepdims=True)
        back, gain_sum, bias_sum = rows_back(grad_norm, unit_three, inverse_three, gain_ref[2:3])
        stats_ref[6:7, :] += gain_sum
        stats_ref[7:8, :] += bias_sum
        grad_after_two = grad_three.astype(jnp.float32) + back
        grad_two = low(grad_after_two)
        grad_two_all[at, :] = grad_two
        grad_heads[...] = low(dot_of(weights[CROSS_OUT], grad_two, 1, 1))

        def attend_back(head, unused):
            rows = pl.ds(pl.multiple_of(head * HEAD_DIM, HEAD_DIM), HEAD_DIM)
            grads = grad_heads[rows, :]
            attn = probs[head]
            grad_probs = dot_of(values[rows, :].T, grads, 1, 0)

            def strip(ones, others):
                return (low(ones * (others - jnp.sum(ones * others, 0, keepdims=True))),)

            (grad_scores,) = in_strips(strip, attn, grad_probs, strip=128, axis=1)
            query_all[rows, at] = low(dot_of(keys[rows, :], grad_scores, 1, 0) * factor)
            grad_keys[rows, :] = dot_of(queries[rows, :], grad_scores, 1, 1) * factor
            grad_values[rows, :] = dot_of(grads, low(attn), 1, 1)
            return unused

        lax.fori_loop(0, heads, attend_back, 0, unroll=8)
        enc_grad_ref[seq, :, :width] = low(grad_keys[...].T)
        enc_grad_ref[seq, :, width:] = low(grad_values[...].T)
        upstream = dot_of(query_all[:, at], weights[QUERY], 0, 0)
        back, gain_sum, bias_sum = rows_back(upstream, unit_two, inverse_two, gain_ref[1:2])
        stats_ref[4:5, :] += gain_sum
        stats_ref[5:6, :] += bias_sum
        grad_after_one = grad_after_two + back
        after_ref[seq] = grad_after_one
        grad_one = low(grad_after_one)
        grad_one_all[at, :] = grad_one
        back_rows[turn] = low(dot_of(weights[SELF_OUT], grad_one, 1, 1))

        @pl.when(turn == 0)
        def all_here():
            meet(group, fsdp)

        for head, number, owner in owners:

            @pl.when(owner + 2 * seq != me)
            def give(head=head, number=number, owner=owner):
                d_copy(turn, seq, head, number, owner).start()

            @pl.when(owner + 2 * seq == me)
            def keep(head=head, number=number):
                back_ref[number, me] = back_rows[turn, head * HEAD_DIM : (head + 1) * HEAD_DIM, :]

        return unused


    lax.fori_loop(0, batches, one_sequence, 0)
    def pack(block, left, right):
        total = low(dot_of(left, right, 1, 0))
        for f in range(width // piece):
            for c in range(group // tp):
                for t in range(tp):
                    head = t * (group // tp) + c
                    packed_ref[c, f, t, block] = total[
                        head * HEAD_DIM : (head + 1) * HEAD_DIM, f * piece : (f + 1) * piece
                    ]

    grad_three_all = cot_ref[...].reshape(batches * chunk, width)
    pack(0, query_all[...], two_all[...])
    pack(1, context_all[...], grad_one_all[...])
    pack(2, cross_all[...], grad_two_all[...])

    def pack_feed(part, unused):
        pack(UP - 2 + part, pre_all[part], three_all[...])
        pack(DOWN - 2 + part, hidden_all[part], grad_three_all)
        return unused

    lax.fori_loop(0, DOWN - UP, pack_feed, 0)

    def collect(k, unused):
        place = me ^ k
        for number in range(2):
            pltpu.make_async_remote_copy(
                src_ref=landing.at[number, place],
                dst_ref=landing.at[number, place],
                send_sem=d_send.at[0, 0],
                recv_sem=d_recv.at[number, place],
                device_id={"ctx": place // tp, "tp": place % tp},
                device_id_type=MESH,
            ).wait_recv()
            back_ref[number, place] = landing[number, place]
        return unused

    lax.fori_loop(1, group, collect, 0)
    for turn in range(batches):
        seq = 1 - mine if turn == 0 else mine
        for head, number, owner in owners:

            @pl.when(owner + 2 * seq != me)
            def given(turn=turn, seq=seq, head=head, number=number, owner=owner):
                d_copy(turn, seq, head, number, owner).wait_send()


def middle(
    gathered, tokens, steps, encoder, cotangent, gains, biases, contexts, tp, fsdp
):
    batches, chunk, width = tokens.shape
    group = contexts.shape[1]
    enc_count = encoder.shape[1]
    heads = width // HEAD_DIM
    bf16, f32 = jnp.bfloat16, jnp.float32
    struct = jax.ShapeDtypeStruct
    inside = pl.BlockSpec(memory_space=pltpu.VMEM)
    dma = pltpu.SemaphoreType.DMA
    count = gathered.shape[3]
    packed = (group // tp, gathered.shape[0], tp, count - 2) + gathered.shape[4:]
    return pl.pallas_call(
        functools.partial(middle_kernel, tp=tp, fsdp=fsdp),
        in_specs=[pl.BlockSpec(memory_space=pl.ANY)] + [inside] * 7,
        out_specs=[inside] * 6,
        out_shape=[
            struct((batches, chunk, width), f32),
            struct((batches, chunk, width), f32),
            struct((2, group, HEAD_DIM, chunk), bf16),
            struct((batches, enc_count, 2 * width), bf16),
            struct((8, width), f32),
            struct(packed, bf16),
        ],
        scratch_shapes=[
            pltpu.VMEM((count, width, width), bf16),
            pltpu.VMEM((DOWN - UP, width, batches * chunk), bf16),
            pltpu.VMEM((DOWN - UP, width, batches * chunk), bf16),
            pltpu.VMEM((batches * chunk, width), bf16),
            pltpu.VMEM((batches * chunk, width), bf16),
            pltpu.VMEM((batches * chunk, width), bf16),
            pltpu.VMEM((batches * chunk, width), bf16),
            pltpu.VMEM((width, batches * chunk), bf16),
            pltpu.VMEM((width, batches * chunk), bf16),
            pltpu.VMEM((width, batches * chunk), bf16),
            pltpu.VMEM((width, chunk), bf16),
            pltpu.VMEM((width, enc_count), bf16),
            pltpu.VMEM((width, enc_count), bf16),
            pltpu.VMEM((heads, enc_count, chunk), f32),
            pltpu.VMEM((width, chunk), bf16),
            pltpu.VMEM((width, enc_count), f32),
            pltpu.VMEM((width, enc_count), f32),
            pltpu.VMEM((batches, width, chunk), bf16),
            pltpu.VMEM((2, group, HEAD_DIM, chunk), bf16),
            dma((batches, heads)),
            dma((2, group)),
            dma((2, 32)),
        ],
        compiler_params=pltpu.CompilerParams(
            vmem_limit_bytes=VMEM_LIMIT, collective_id=3, has_side_effects=True
        ),
        cost_estimate=pl.CostEstimate(
            flops=30_000_000_000, bytes_accessed=30_000_000, transcendentals=10_000_000
        ),
        name="middle",
    )(gathered, tokens, steps, encoder, cotangent, gains, biases, contexts)


def backward_kernel(
    prefix_ref,
    enc_parts,
    packed,
    gathered,
    rows_in,
    landing,
    weight,
    qkv_ref,
    wide_ref,
    log_ref,
    tokens_ref,
    step_ref,
    gain_ref,
    bias_ref,
    after_ref,
    enc_ref,
    stats_ref,
    input_ref,
    enc_out,
    self_out,
    query_out,
    pair_out,
    back_out,
    cross_out,
    up_out,
    down_out,
    sums_out,
    outgoing,
    core_rows,
    core_rows_landing,
    sum_rows,
    beside,
    incoming,
    queries_ref,
    pairs_ref,
    grad_ref,
    delta_ref,
    grad_pairs_ref,
    rows_ref,
    pair_weights,
    enc_own,
    enc_core,
    enc_sum,
    enc_landing,
    pair_ref,
    pair_landing,
    core_landing,
    partial_ref,
    fsdp_landing,
    line_ref,
    line_landing,
    shard_ref,
    head_ref,
    head_landing,
    head_pair,
    head_two,
    sums_ref,
    sums_landing,
    sums_two,
    e_send,
    e_recv,
    x_send,
    x_recv,
    i_send,
    i_recv,
    b_recv,
    r_send,
    r_recv,
    f_send,
    f_recv,
    t_send,
    t_recv,
    h_send,
    h_recv,
    p_send,
    p_recv,
    s_send,
    s_recv,
    local_sem,
    rows_sem,
    *,
    span,
    tp,
    fsdp,
):
    batches, chunk, width = tokens_ref.shape
    group = landing.shape[1]
    length = group * chunk
    blocks, ratio = length // span, span // chunk
    wide_blocks = max(1, length // 2 // span)
    factor = HEAD_DIM**-0.5
    here, core, chip = lax.axis_index("fsdp"), lax.axis_index("ctx"), lax.axis_index("tp")
    me = core * tp + chip
    mine = chip // 2
    inner = (chip == 1) | (chip == 2)
    cores = group // tp
    share = enc_landing.shape[2]
    piece = width // fsdp
    early = packed.shape[3]
    greet(group, tp, fsdp)

    def send_to(source, target, send, recv, **place):
        return pltpu.make_async_remote_copy(
            src_ref=source,
            dst_ref=target,
            send_sem=send,
            recv_sem=recv,
            device_id=place,
            device_id_type=MESH,
        )

    def member(place):
        return {"ctx": place // tp, "tp": place % tp}

    local = [
        pltpu.make_async_copy(
            packed.at[core], partial_ref.at[:, :, pl.ds(0, early)], local_sem.at[0]
        ),
        pltpu.make_async_copy(
            enc_parts.at[:, pl.ds(pl.multiple_of(core * tp * share, share), tp * share)],
            enc_own,
            local_sem.at[1],
        ),
    ]
    first = len(local)
    for f in range(fsdp):
        for c in range(cores):
            for t in range(tp):
                head = t * cores + c
                local.append(
                    pltpu.make_async_copy(
                        gathered.at[f, c, t, pl.ds(KEY, 2)],
                        pair_weights.at[
                            :, pl.ds(head * HEAD_DIM, HEAD_DIM), pl.ds(f * piece, piece)
                        ],
                        local_sem.at[first + (f * cores + c) * tp + t],
                    )
                )
    enc_copy = send_to(
        enc_parts.at[:, pl.ds(pl.multiple_of((1 - core) * tp * share, share), tp * share)],
        enc_core,
        e_send.at[0],
        e_recv.at[0],
        ctx=1 - core,
    )
    enc_line = [
        send_to(
            enc_sum.at[chip ^ n], enc_landing.at[n - 1], e_send.at[n], e_recv.at[n], tp=chip ^ n
        )
        for n in range(1, tp)
    ]

    core_copy = send_to(
        packed.at[1 - core], core_landing, r_send.at[0], r_recv.at[0], ctx=1 - core
    )
    pair_copy = send_to(
        pair_ref.at[1 - core], pair_landing, r_send.at[1], r_recv.at[1], ctx=1 - core
    )
    shard_copy = send_to(
        shard_ref.at[core], shard_ref.at[core], r_send.at[2], r_recv.at[2], ctx=1 - core
    )
    shard_wait = send_to(
        shard_ref.at[1 - core], shard_ref.at[1 - core], r_send.at[2], r_recv.at[2], ctx=1 - core
    )
    f_copies = [
        send_to(
            partial_ref.at[here ^ n, :, pl.ds(0, early)],
            fsdp_landing.at[n - 1, :, pl.ds(0, early)],
            f_send.at[n],
            f_recv.at[n],
            fsdp=here ^ n,
        )
        for n in range(1, fsdp)
    ]
    f_pairs = [
        send_to(
            partial_ref.at[here ^ n, :, pl.ds(early, 2)],
            fsdp_landing.at[n - 1, :, pl.ds(early, 2)],
            f_send.at[fsdp + n],
            f_recv.at[fsdp + n],
            fsdp=here ^ n,
        )
        for n in range(1, fsdp)
    ]
    t_copies = [
        send_to(line_ref.at[chip ^ k], line_landing.at[k - 1], t_send.at[k], t_recv.at[k], tp=chip ^ k)
        for k in range(1, tp)
    ]
    h_copies = [
        send_to(
            head_ref.at[here ^ k], head_landing.at[k - 1], h_send.at[k], h_recv.at[k], fsdp=here ^ k
        )
        for k in range(1, fsdp)
    ]

    pair_chip = 2 * (chip % 2) + core
    p_copies = [
        send_to(head_pair, head_two.at[mine], p_send.at[c], p_recv.at[mine], ctx=c, tp=pair_chip)
        for c in range(2)
    ]
    p_waits = [
        send_to(head_pair, head_two.at[n], p_send.at[0], p_recv.at[n], ctx=c, tp=t)
        for n, c, t in ((0, chip % 2, chip // 2), (1, chip % 2, chip // 2 + 2))
    ]
    p_here = [
        (core == chip % 2) & (chip == chip // 2 + 2 * n) for n in range(2)
    ]

    def s_copy(k):
        return send_to(
            sums_ref, sums_landing.at[k], s_send.at[k], s_recv.at[k], **member(me ^ k)
        )

    s_fsdp = [
        send_to(
            sums_two, sums_landing.at[group + k], s_send.at[group + k], s_recv.at[group + k], fsdp=here ^ k
        )
        for k in range(1, fsdp)
    ]

    def prepare(seq):
        def lay(place, unused):
            at = pl.ds(pl.multiple_of(place * chunk, chunk), chunk)
            grads = landing[seq, place]
            blank = jnp.zeros_like(grads)
            grad_ref[seq, at, :] = jnp.concatenate([blank, grads], 0).T
            delta_ref[seq, :, at] = jnp.sum(
                grads.astype(jnp.float32) * wide_ref[seq, :, at], axis=0, keepdims=True
            )
            queries_ref[seq, at, :] = jnp.concatenate([qkv_ref[seq, :HEAD_DIM, at], blank], 0).T
            pairs_ref[seq, at, :] = qkv_ref[seq, HEAD_DIM:, at].T
            return unused

        lax.fori_loop(0, group, lay, 0)
        grad_pairs_ref[seq] = jnp.zeros(grad_pairs_ref.shape[1:], jnp.float32)

    for copy in local:
        copy.start()
    for head in range(2):
        prepare(head)

    meet(group, fsdp)
    enc_copy.start()
    core_copy.start()
    def rows_copy(number):
        return pltpu.make_async_copy(
            rows_in.at[number],
            rows_ref.at[number % rows_ref.shape[0]],
            rows_sem.at[number % rows_ref.shape[0]],
        )

    depth = rows_ref.shape[0]
    for number in range(depth):
        rows_copy(number).start()

    def core_rows_copy(place):
        slot = place % tp
        return send_to(
            core_rows.at[slot], core_rows_landing.at[slot], x_send.at[slot], x_recv.at[slot], ctx=1 - core
        )

    def owner_copy(place):
        slot = place % tp
        return send_to(
            sum_rows.at[slot],
            incoming.at[mine, chip % 2],
            i_send.at[slot],
            i_recv.at[mine, chip % 2],
            tp=slot,
        )

    def spread(place):
        upstream = dot_of(outgoing[place].reshape(6 * HEAD_DIM, chunk), weight[...], 0, 0)
        slot = place % tp

        @pl.when(place // tp != core)
        def hand_over():
            core_rows[slot] = low(upstream)
            core_rows_copy(place).start()

        @pl.when(place // tp == core)
        def collect():
            core_rows_copy(place).wait_recv()
            total = low(upstream + core_rows_landing[slot].astype(jnp.float32))

            @pl.when(place == me)
            def own():
                incoming[mine, chip % 2] = total

            @pl.when(place != me)
            def send():
                sum_rows[slot] = total

                @pl.when((core == 0) & (slot // 2 != mine) & jnp.logical_not(inner))
                def to_inner():
                    beside_copy(slot).start()

                @pl.when((core == 1) | (slot // 2 == mine))
                def to_owner():
                    owner_copy(place).start()

    def beside_copy(slot):
        return send_to(
            sum_rows.at[slot], beside.at[slot % 2], i_send.at[slot], b_recv.at[slot % 2], tp=chip ^ 1
        )

    def pass_rows():
        for n in range(2):
            slot = 2 * (1 - mine) + n
            beside_copy(slot).wait_recv()
            sum_rows[slot] = low(
                sum_rows[slot].astype(jnp.float32) + beside[n].astype(jnp.float32)
            )
            owner_copy(slot).start()

    def encoder_cores():
        local[1].wait()
        enc_copy.wait_recv()
        for t in range(tp):
            lines = slice(t * share, (t + 1) * share)
            enc_sum[t] = low(
                enc_own[:, lines].astype(jnp.float32) + enc_core[:, lines].astype(jnp.float32)
            )
        for copy in enc_line:
            copy.start()

    def encoder_part():
        total = enc_sum[chip].astype(jnp.float32)
        for n, copy in enumerate(enc_line):
            copy.wait_recv()
            total = total + enc_landing[n].astype(jnp.float32)
        for copy in local[first:]:
            copy.wait()
        grads = low(total)
        enc_rows = enc_ref[:, pl.ds(pl.multiple_of(me * share, share), share), :]
        flat, enc_flat = grads.reshape(batches * share, 2 * width), enc_rows.reshape(
            batches * share, width
        )
        result = dot_of(flat[:, :width], pair_weights[0], 1, 0) + dot_of(
            flat[:, width:], pair_weights[1], 1, 0
        )
        enc_out[...] = result.reshape(batches, share, width)
        for which in range(2):
            grad = low(dot_of(flat[:, which * width : (which + 1) * width], enc_flat, 0, 0))
            for f in range(fsdp):
                for c in range(cores):
                    for t in range(tp):
                        head = t * cores + c
                        pair_ref[c, f, t, which] = grad[
                            head * HEAD_DIM : (head + 1) * HEAD_DIM, f * piece : (f + 1) * piece
                        ]
        pair_copy.start()

    def sum_cores():
        local[0].wait()
        core_copy.wait_recv()

        def one(f, unused):
            def two(t, unused):
                partial_ref[f, t, :early] = low(
                    partial_ref[f, t, :early].astype(jnp.float32)
                    + core_landing[f, t].astype(jnp.float32)
                )
                return unused

            return lax.fori_loop(0, tp, two, unused)

        lax.fori_loop(0, fsdp, one, 0)
        for copy in f_copies:
            copy.start()

    def sum_pairs():
        pair_copy.wait_recv()
        for f in range(fsdp):
            for t in range(tp):
                partial_ref[f, t, early:] = low(
                    pair_ref[core, f, t].astype(jnp.float32)
                    + pair_landing[f, t].astype(jnp.float32)
                )
        for copy in f_pairs:
            copy.start()

    def sum_fsdp():
        for copy in f_copies + f_pairs:
            copy.wait_recv()

        def one(t, unused):
            total = partial_ref[here, t].astype(jnp.float32)
            for k in range(fsdp - 1):
                total = total + fsdp_landing[k, t].astype(jnp.float32)
            line_ref[t] = low(total)
            return unused

        lax.fori_loop(0, tp, one, 0)
        for copy in t_copies:
            copy.start()

    def sum_line():
        for copy in t_copies:
            copy.wait_recv()
        total = line_ref[chip].astype(jnp.float32)
        for k in range(tp - 1):
            total = total + line_landing[k].astype(jnp.float32)
        shard_ref[core] = total
        shard_copy.start()

    def attend(index, unused):
        block, seq = blocks - 1 - index // 2, index % 2

        def hook(at, work):
            @pl.when(index == at)
            def run():
                work()

        hook(1, encoder_cores)
        hook(1, sum_cores)
        hook(2, encoder_part)
        hook(3, sum_pairs)
        hook(4, sum_fsdp)
        start = pl.multiple_of(block * span, span)
        at = pl.ds(start, span)
        blank = jnp.zeros((HEAD_DIM, span), jnp.bfloat16)
        queries_t = jnp.concatenate([qkv_ref[seq, :HEAD_DIM, at], blank], 0)
        queries = queries_ref[seq, at, :]
        grads = grad_ref[seq, at, :]
        grads_t = jnp.concatenate(
            [landing[seq, block * ratio + part] for part in range(ratio)], 1
        )
        grads_t = jnp.concatenate([blank, grads_t], 0)
        logs, deltas = log_ref[seq, :, at], delta_ref[seq, :, at]
        limit = jnp.maximum(
            prefix_ref[mine], start + 1 + lax.broadcasted_iota(jnp.int32, (1, span), 1)
        )

        def advance(offset, count, grad_queries, columns=None):
            first = 0 if columns is None else columns
            there = pl.ds(offset, count)
            pairs = pairs_ref[seq, there, :]
            scores = dot_of(pairs, queries_t[:, first:], 1, 0)
            if columns is not None:
                scores = hide(scores, limit[:, first:], offset)
            probs = jnp.exp(scores - logs[:, first:])
            grad_probs = dot_of(pairs, grads_t[:, first:], 1, 0)
            grad_scores = low(probs * (grad_probs - deltas[:, first:]))
            grad_pairs_ref[seq, there, :] += dot_of(low(probs), grads[first:], 1, 0) + dot_of(
                grad_scores, queries[first:], 1, 0
            )
            return grad_queries + dot_of(
                qkv_ref[seq, HEAD_DIM : 2 * HEAD_DIM, there], grad_scores, 1, 0
            )

        def whole_step(other, total):
            return advance(pl.multiple_of(other * span, span), span, total)

        def masked_step(other, total):
            return advance(pl.multiple_of(other * span, span), span, total, 0)

        def diagonal_step(other, total):
            half = span // 2
            total = advance(start, half, total, 0)
            offset = pl.multiple_of(start + half, half)
            upper = advance(offset, half, total[:, half:], half)
            return jnp.concatenate([total[:, :half], upper], 1)

        grad_queries = jnp.zeros((HEAD_DIM, span), jnp.float32)
        grad_queries = lax.fori_loop(0, block, whole_step, grad_queries)
        grad_queries = lax.fori_loop(block, wide_blocks, masked_step, grad_queries)
        grad_queries = lax.fori_loop(
            0, jnp.where(block >= wide_blocks, 1, 0), diagonal_step, grad_queries
        )
        done = low(grad_queries * factor)
        for part in range(ratio):
            place = block * ratio + part
            outgoing[place, seq, :HEAD_DIM, :] = done[:, part * chunk : (part + 1) * chunk]

        lowest = jnp.where(block == 0, 0, block)
        highest = jnp.where(
            block == 0, wide_blocks, jnp.where(block >= wide_blocks, block + 1, block)
        )

        def give(place, unused):
            at = pl.ds(pl.multiple_of(place * chunk, chunk), chunk)
            outgoing[place, seq, HEAD_DIM:, :] = low(grad_pairs_ref[seq, at, :].T)
            return unused

        lax.fori_loop(lowest * ratio, highest * ratio, give, 0)

        @pl.when(seq == 1)
        def both_heads():
            def one(place, unused):
                spread(place)
                return unused

            lax.fori_loop(lowest * ratio, highest * ratio, one, 0)

        return unused

    lax.fori_loop(0, 2 * blocks, attend, 0)

    sums_ref[...] = jnp.zeros_like(sums_ref)
    sums_ref[:8, :] = stats_ref[...]

    ones = jnp.ones((chunk, piece), jnp.bfloat16)

    def weigh(number, totals):
        rows_copy(number).wait()
        grads = outgoing[number].reshape(6 * HEAD_DIM, chunk)
        total = totals[0] + dot_of(grads, rows_ref[number % depth], 1, 0)

        @pl.when(number + depth < group)
        def more():
            rows_copy(number + depth).start()

        return total, totals[1] + dot_of(grads, ones, 1, 0)

    total, plain = lax.fori_loop(
        0,
        group,
        weigh,
        (
            jnp.zeros((6 * HEAD_DIM, width), jnp.float32),
            jnp.zeros((6 * HEAD_DIM, piece), jnp.float32),
        ),
    )
    token_copies = [
        pltpu.make_async_copy(tokens_ref.at[n], rows_ref.at[n], rows_sem.at[n])
        for n in range(batches)
    ]
    for copy in token_copies:
        copy.start()
    weights = weight[...].astype(jnp.float32)
    bias_sum = jnp.sum(weights * jnp.concatenate([plain] * (width // piece), 1), 0, keepdims=True)
    gain_sum = jnp.sum(weights * total, 0, keepdims=True) - bias_ref[0:1] * bias_sum
    sums_ref[8:9, :] = gain_sum / gain_ref[0:1]
    sums_ref[9:10, :] = bias_sum

    def start_sums(k, unused):
        s_copy(k).start()
        return unused

    lax.fori_loop(1, group, start_sums, 0)
    for f in range(fsdp):
        head_ref[f] = total[:, f * piece : (f + 1) * piece]
    for copy in h_copies:
        copy.start()

    @pl.when((core == 0) & inner)
    def last_rows():
        pass_rows()

    sum_line()

    for copy in h_copies:
        copy.wait_recv()
    total = head_ref[here]
    for k in range(fsdp - 1):
        total = total + head_landing[k]
    head_pair[...] = low(total)
    for c in range(2):
        there = (core == c) & (pair_chip == chip)

        @pl.when(there)
        def stay():
            head_two[mine] = head_pair[...]

        @pl.when(jnp.logical_not(there))
        def leave(c=c):
            p_copies[c].start()

    def arrive_sums(k, total):
        s_copy(k).wait_recv()
        return total + sums_landing[k]

    sums_two[...] = lax.fori_loop(1, group, arrive_sums, sums_ref[...])
    for copy in s_fsdp:
        copy.start()

    for copy in token_copies:
        copy.wait()

    def finish(seq, unused):
        for number in range(2):
            source = 2 * seq + number

            passed = (core == 0) & (seq != mine)

            @pl.when(passed & ((source == 0) | (source == 3)))
            def nothing(number=number):
                incoming[seq, number] = jnp.zeros((chunk, width), jnp.bfloat16)

            @pl.when((source != chip) & jnp.logical_not(passed & ((source == 0) | (source == 3))))
            def come(number=number, source=source):
                send_to(
                    incoming.at[seq, number],
                    incoming.at[seq, number],
                    i_send.at[0],
                    i_recv.at[seq, number],
                    tp=source,
                ).wait_recv()

        upstream = incoming[seq, 0].astype(jnp.float32) + incoming[seq, 1].astype(jnp.float32)
        start_sum = rows_ref[seq].astype(jnp.float32) + step_ref[seq]
        unit_rows, inverse = in_strips(rows_unit, start_sum)
        input_ref[seq] = after_ref[seq] + rows_back(
            upstream, unit_rows, inverse, gain_ref[0:1]
        )[0]
        return unused

    lax.fori_loop(0, batches, finish, 0)

    shard_wait.wait_recv()

    def whole(block):
        return jnp.concatenate([shard_ref[0, block], shard_ref[1, block]], 0)

    query_out[...] = whole(0).T
    back_out[...] = whole(1)
    cross_out[...] = whole(2)
    for part in range(4):
        up_out[:, part * piece : (part + 1) * piece] = whole(3 + part).T
        down_out[part * piece : (part + 1) * piece, :] = whole(7 + part)
    pair_out[0] = whole(11).T
    pair_out[1] = whole(12).T
    for n in range(2):

        @pl.when(jnp.logical_not(p_here[n]))
        def pair_come(n=n):
            p_waits[n].wait_recv()

    total = head_two[0].astype(jnp.float32) + head_two[1].astype(jnp.float32)
    for which in range(3):
        self_out[which] = jnp.concatenate(
            [
                total[(3 * n + which) * HEAD_DIM : (3 * n + which + 1) * HEAD_DIM]
                for n in range(2)
            ],
            0,
        ).T
    total = sums_two[...]
    for k, copy in enumerate(s_fsdp):
        copy.wait_recv()
        total = total + sums_landing[group + 1 + k]
    sums_out[...] = total
    core_copy.wait_send()
    pair_copy.wait_send()
    shard_copy.wait_send()
    for c in range(2):

        @pl.when(jnp.logical_not((core == c) & (pair_chip == chip)))
        def pair_sent(c=c):
            p_copies[c].wait_send()

    enc_copy.wait_send()
    for copy in enc_line + f_copies + f_pairs + t_copies + h_copies + s_fsdp:
        copy.wait_send()

    def sent(k, unused):
        s_copy(k).wait_send()
        return unused

    lax.fori_loop(1, group, sent, 0)

    def rows_sent(slot, unused):
        core_rows_copy((1 - core) * tp + slot).wait_send()

        @pl.when(slot != chip)
        def left():
            owner_copy(core * tp + slot).wait_send()

        return unused

    lax.fori_loop(0, tp, rows_sent, 0)


def backward_group(
    prefix,
    enc_parts,
    packed,
    gathered,
    rows,
    returned,
    weight,
    qkv,
    wide,
    logs,
    tokens,
    steps,
    gain,
    bias,
    after,
    encoder,
    stats,
    span,
    tp,
    fsdp,
):
    batches, chunk, width = tokens.shape
    group = returned.shape[1]
    length = group * chunk
    share = encoder.shape[1] // group
    piece = width // fsdp
    count = packed.shape[3]
    tail = packed.shape[4:]
    bf16, f32 = jnp.bfloat16, jnp.float32
    struct = jax.ShapeDtypeStruct
    inside = pl.BlockSpec(memory_space=pltpu.VMEM)
    outside = pl.BlockSpec(memory_space=pl.ANY)
    dma = pltpu.SemaphoreType.DMA
    vmem = pltpu.VMEM
    parts = group * fsdp
    return pl.pallas_call(
        functools.partial(backward_kernel, span=span, tp=tp, fsdp=fsdp),
        in_specs=[pl.BlockSpec(memory_space=pltpu.SMEM)] + [outside] * 4 + [inside] * 5 + [outside] + [inside] * 6,
        out_specs=[inside] * 10,
        out_shape=[
            struct((batches, chunk, width), f32),
            struct((batches, share, width), f32),
            struct((3, piece, piece), f32),
            struct((piece, piece), f32),
            struct((2, piece, piece), f32),
            struct((piece, piece), f32),
            struct((piece, piece), f32),
            struct((piece, width), f32),
            struct((width, piece), f32),
            struct((16, width), f32),
        ],
        scratch_shapes=[
            vmem((group, 2, 3 * HEAD_DIM, chunk), bf16),
            vmem((tp, chunk, width), bf16),
            vmem((tp, chunk, width), bf16),
            vmem((tp, chunk, width), bf16),
            vmem((2, chunk, width), bf16),
            vmem((batches, 2, chunk, width), bf16),
            vmem((2, length, 2 * HEAD_DIM), bf16),
            vmem((2, length, 2 * HEAD_DIM), bf16),
            vmem((2, length, 2 * HEAD_DIM), bf16),
            vmem((2, 1, length), f32),
            vmem((2, length, 2 * HEAD_DIM), f32),
            vmem((2, chunk, width), bf16),
            vmem((2, width, width), bf16),
            vmem((batches, tp * share, 2 * width), bf16),
            vmem((batches, tp * share, 2 * width), bf16),
            vmem((tp, batches, share, 2 * width), bf16),
            vmem((tp - 1, batches, share, 2 * width), bf16),
            vmem((group // tp, fsdp, tp, 2) + tail, bf16),
            vmem((fsdp, tp, 2) + tail, bf16),
            vmem((fsdp, tp, count) + tail, bf16),
            vmem((fsdp, tp, count + 2) + tail, bf16),
            vmem((fsdp - 1, tp, count + 2) + tail, bf16),
            vmem((tp, count + 2) + tail, bf16),
            vmem((tp - 1, count + 2) + tail, bf16),
            vmem((2, count + 2) + tail, f32),
            vmem((fsdp, 6 * HEAD_DIM, piece), f32),
            vmem((fsdp - 1, 6 * HEAD_DIM, piece), f32),
            vmem((6 * HEAD_DIM, piece), bf16),
            vmem((2, 6 * HEAD_DIM, piece), bf16),
            vmem((16, width), f32),
            vmem((group + fsdp, 16, width), f32),
            vmem((16, width), f32),
            dma((tp,)),
            dma((tp,)),
            dma((tp,)),
            dma((tp,)),
            dma((tp,)),
            dma((batches, 2)),
            dma((2,)),
            dma((4,)),
            dma((4,)),
            dma((2 * fsdp,)),
            dma((2 * fsdp,)),
            dma((tp,)),
            dma((tp,)),
            dma((fsdp,)),
            dma((fsdp,)),
            dma((2,)),
            dma((2,)),
            dma((group + fsdp,)),
            dma((group + fsdp,)),
            dma((2 + parts,)),
            dma((2,)),
        ],
        compiler_params=pltpu.CompilerParams(
            vmem_limit_bytes=VMEM_LIMIT, collective_id=2, has_side_effects=True
        ),
        cost_estimate=pl.CostEstimate(
            flops=100_000_000_000, bytes_accessed=40_000_000, transcendentals=20_000_000
        ),
        name="backward_group",
    )(
        prefix,
        enc_parts,
        packed,
        gathered,
        rows,
        returned,
        weight,
        qkv,
        wide,
        logs,
        tokens,
        steps,
        gain,
        bias,
        after,
        encoder,
        stats,
    )


def pack_kernel(
    scalars,
    table_ref,
    qkv_ref,
    query_ref,
    pair_ref,
    self_ref,
    cross_ref,
    up_ref,
    down_ref,
    half_ref,
    mine_ref,
    steps_ref,
    blocks,
):
    piece = query_ref.shape[0]
    blocks[0] = query_ref[...].T
    for n in range(2):
        blocks[1 + n] = pair_ref[n].T
    blocks[3] = self_ref[...]
    blocks[4] = cross_ref[...]
    for n in range(4):
        blocks[5 + n] = up_ref[:, n * piece : (n + 1) * piece].T
        blocks[9 + n] = down_ref[n * piece : (n + 1) * piece, :]
    half = piece // 2
    core = lax.axis_index("ctx")
    half_ref[...] = blocks[:, pl.ds(pl.multiple_of(core * half, half), half), :]
    for which in range(3):
        flipped = qkv_ref[which].T
        for head in range(2):
            mine_ref[(3 * head + which) * HEAD_DIM : (3 * head + which + 1) * HEAD_DIM, :] = (
                flipped[head * HEAD_DIM : (head + 1) * HEAD_DIM]
            )
    table = table_ref[...].astype(jnp.float32)
    rows = lax.broadcasted_iota(jnp.int32, table.shape, 0)
    for seq in range(steps_ref.shape[0]):
        chosen = jnp.where(rows == scalars[seq], table, 0.0)
        steps_ref[seq] = jnp.sum(chosen, 0, keepdims=True)


def pack_weights(scalars, table, self_qkv, cross_q, cross_kv, self_out, cross_out, up, down):
    piece = cross_q.shape[0]
    width = table.shape[1]
    batches = scalars.shape[0]
    bf16 = jnp.bfloat16
    struct = jax.ShapeDtypeStruct
    inside = pl.BlockSpec(memory_space=pltpu.VMEM)
    return pl.pallas_call(
        pack_kernel,
        in_specs=[pl.BlockSpec(memory_space=pltpu.SMEM)] + [inside] * 8,
        out_specs=[inside] * 3,
        out_shape=[
            struct((13, piece // 2, piece), bf16),
            struct((3 * piece, piece), bf16),
            struct((batches, 1, width), jnp.float32),
        ],
        scratch_shapes=[pltpu.VMEM((13, piece, piece), bf16)],
        name="pack_weights",
    )(scalars, table, self_qkv, cross_q, cross_kv, self_out, cross_out, up, down)


def collect_kernel(*refs, large, small, entries):
    ins, outs = refs[: large + small + 1], refs[large + small + 1 :]
    for n in range(large):
        outs[n][...] = ins[n][...]

    @pl.when(pl.program_id(0) == 0)
    def once():
        for n in range(large, large + small):
            outs[n][...] = ins[n][...]
        sums = ins[large + small]
        gain_ref, bias_ref, feed_ref, norms_ref = outs[large + small :]
        for n, row in enumerate((8, 4, 6)):
            gain_ref[n : n + 1, :] = sums[row : row + 1, :]
        for n, row in enumerate((9, 5)):
            bias_ref[n : n + 1, :] = sums[row : row + 1, :]
        feed_ref[...] = sums[7:8, :]
        totals = jnp.sum(sums[0:4, :], 1, keepdims=True) * (1.0 / entries)
        one = lax.broadcasted_iota(jnp.int32, (4, 128), 0) == lax.broadcasted_iota(
            jnp.int32, (4, 128), 1
        )
        norms_ref[...] = jnp.sqrt(jnp.sum(jnp.where(one, totals, 0.0), 0, keepdims=True))[:, :4]


def collect(large, small, sums, entries):
    width = sums.shape[1]
    f32 = jnp.float32
    struct = jax.ShapeDtypeStruct
    rest = [struct(v.shape, v.dtype) for v in small]
    extra = [struct((3, width), f32), struct((2, width), f32), struct((1, width), f32)]
    extra = extra + [struct((1, 4), f32)]
    still = lambda v: pl.BlockSpec(v.shape, lambda i, rank=len(v.shape): (0,) * rank)
    steps = 2
    moving = lambda v: pl.BlockSpec(
        (1, v.shape[0] * v.shape[1] // steps, v.shape[2]),
        lambda i, per=steps // v.shape[0]: (i // per, i % per, 0),
    )
    return pl.pallas_call(
        functools.partial(collect_kernel, large=len(large), small=len(small), entries=entries),
        grid=(steps,),
        in_specs=[moving(v) for v in large] + [still(v) for v in small] + [still(sums)],
        out_specs=[moving(v) for v in large] + [still(v) for v in rest + extra],
        out_shape=[struct(v.shape, v.dtype) for v in large] + rest + extra,
        name="collect",
    )(*large, *small, sums)


def local_heads(
    tokens,
    timesteps,
    time_table,
    prefix,
    encoder,
    self_qkv,
    cross_q,
    cross_kv,
    self_out,
    cross_out,
    ffn_up,
    ffn_down,
    norm_gain,
    norm_bias,
    cotangent,
):
    batches, chunk, width = tokens.shape
    group = 8
    length = group * chunk
    span = 1024
    own_half, mine, embedded = pack_weights(
        timesteps,
        time_table,
        self_qkv,
        cross_q,
        cross_kv,
        self_out,
        cross_out,
        ffn_up,
        ffn_down,
    )
    gathered = lax.all_gather(own_half, "tp", axis=0, tiled=False)
    gathered = lax.all_gather(gathered, ("fsdp", "ctx"), axis=0, tiled=False)
    gathered = gathered.reshape((4, 2, 4) + own_half.shape)
    rows, qkv, wide, logs, contexts, weight = forward_group(
        prefix, tokens, embedded, norm_gain, norm_bias, mine, span, group, 4, 4
    )
    final, grad_after, returned, enc_parts, stats, packed = middle(
        gathered,
        tokens,
        embedded,
        encoder,
        cotangent,
        norm_gain,
        norm_bias,
        contexts,
        4,
        4,
    )
    outs = backward_group(
        prefix,
        enc_parts,
        packed,
        gathered,
        rows,
        returned,
        weight,
        qkv,
        wide,
        logs,
        tokens,
        embedded,
        norm_gain,
        norm_bias,
        grad_after,
        encoder,
        stats,
        span,
        4,
        4,
    )
    sums = outs[9]
    entries = (
        tokens.shape[0]
        * tokens.shape[1]
        * tokens.shape[2]
        * lax.axis_size("fsdp")
        * lax.axis_size("ctx")
        * lax.axis_size("tp")
    )
    results = collect((final, *outs[:2]), outs[2:9], sums, entries)
    return (*results[:12], results[12].reshape(width), results[13].reshape(4))


def solution(mesh):
    placed = (
        P("fsdp", ("ctx", "tp"), None),
        P("fsdp"),
        P(),
        P("fsdp"),
        P("fsdp", None, None),
        P(None, "fsdp", "tp"),
        P("fsdp", "tp"),
        P(None, "fsdp", "tp"),
        P("tp", "fsdp"),
        P("tp", "fsdp"),
        P("fsdp", "tp"),
        P("tp", "fsdp"),
        P(),
        P(),
        P("fsdp", ("ctx", "tp"), None),
    )
    heads_fit = dict(mesh.shape) == {"fsdp": 4, "ctx": 2, "tp": 4}
    return jax.shard_map(
        local_heads if heads_fit else local,
        mesh=mesh,
        in_specs=placed,
        out_specs=(
            P("fsdp", ("ctx", "tp"), None),
            P("fsdp", ("ctx", "tp"), None),
            P("fsdp", ("ctx", "tp"), None),
            P(None, "fsdp", "tp"),
            P("fsdp", "tp"),
            P(None, "fsdp", "tp"),
            P("tp", "fsdp"),
            P("tp", "fsdp"),
            P("fsdp", "tp"),
            P("tp", "fsdp"),
            P(),
            P(),
            P(),
            P(),
        ),
        check_vma=False,
    )
```
